32 devices in a mesh: gx: 2 (over y), gy: 4 (over x, core), gz: 4 (over z).
Axes of the slice: x: 2, y: 2, z: 4, core: 2. Of those that a mesh axis runs over, the one named last changes fastest.
Arguments:
- rhs: float32 [4, 32, 64, 1024], P(None, 'gz', 'gx', 'gy'), may hold values from -6 to 6
- coef_x: float32 [32, 64, 1024], P('gz', 'gx', 'gy'), may hold values from 0.3 to 3
- coef_y: float32 [32, 64, 1024], P('gz', 'gx', 'gy'), may hold values from 0.3 to 3
- coef_z: float32 [32, 64, 1024], P('gz', 'gx', 'gy'), may hold values from 0.3 to 3
- diag_term: float32 [32, 64, 1024], P('gz', 'gx', 'gy'), may hold values from 0.2 to 2
Outputs:
- ortho_basis: float32 [20, 32, 64, 1024], P(None, 'gz', 'gx', 'gy')
- triangle: float32 [20, 20], replicated
The draws below stay inside these ranges and needn't reach their ends.
All inputs are finite; a program needn't handle non-finite values.
Results may differ from the reference program's by a relative error of at most 0.0003.
Values sent between devices are 32-bit elements; how exact they have to be, the bound alone decides.
No kernel may reach another device: no remote copies, remote signals or barrier semaphores. Data moves between devices by JAX's collectives and lax.ppermute only.
A program may use at most 128 MiB of HBM per device.

```python
import math
import jax
import jax.numpy as jnp
from jax import lax

NRHS = 4
STEPS = 4
COLS = 20
NX = 64
NY = 1024
NZ = 32


def draw_rhs(key, part):
    common_key = jax.random.fold_in(key, 11)
    own_key = jax.random.fold_in(key, 12)
    common = jnp.clip(jax.random.normal(common_key, (1, NZ, NX, NY), jnp.float32), -6.0, 6.0)
    own = jnp.clip(jax.random.normal(own_key, (NRHS, NZ, NX, NY), jnp.float32), -6.0, 6.0)
    return jnp.clip(0.9 * common + 0.1 * own, -6.0, 6.0)


def shard_levels(key, dims, split, smallest, top_value):
    level = 1.0
    for position, blocks in split:
        heights = jax.random.uniform(jax.random.fold_in(jax.random.fold_in(key, 6), position), (blocks,), jnp.float32, smallest / len(split), top_value / len(split))
        level = level * jnp.repeat(jnp.exp(heights), dims[position] // blocks).reshape((-1,) + (1,) * (len(dims) - 1 - position))
    return level


def setup_inputs(seed: int = 0) -> dict:
    arg_keys = jax.random.split(jax.random.key(seed), 6)
    return {
        "rhs": draw_rhs(jax.random.fold_in(arg_keys[5], 71), 0),
        "coef_x": jnp.clip(jnp.exp(math.log(3.0) - 2.3025851 * jax.random.uniform(arg_keys[1], (NZ, NX, NY), jnp.float32) ** shard_levels(arg_keys[1], (NZ, NX, NY), ((0, 4), (1, 2), (2, 4)), -0.2, 0.2)), 0.3, 3.0),
        "coef_y": jnp.clip(jnp.exp(math.log(3.0) - 2.3025851 * jax.random.uniform(arg_keys[2], (NZ, NX, NY), jnp.float32) ** shard_levels(arg_keys[2], (NZ, NX, NY), ((0, 4), (1, 2), (2, 4)), -0.2, 0.2)), 0.3, 3.0),
        "coef_z": jnp.clip(jnp.exp(math.log(3.0) - 2.3025851 * jax.random.uniform(arg_keys[3], (NZ, NX, NY), jnp.float32) ** shard_levels(arg_keys[3], (NZ, NX, NY), ((0, 4), (1, 2), (2, 4)), -0.2, 0.2)), 0.3, 3.0),
        "diag_term": jnp.clip(0.2 + 1.8 * jax.random.uniform(arg_keys[4], (NZ, NX, NY), jnp.float32) ** shard_levels(arg_keys[4], (NZ, NX, NY), ((0, 4), (1, 2), (2, 4)), -0.2, 0.2), 0.2, 2.0),
    }


NEWTON_SHIFTS = (3.0, 11.0, 7.0, 1.5)
BASIS_SCALE = 1.0 / 6.0

def inner_part(array, off_z, off_x, off_y, margin=1):
    size_z, size_x, size_y = array.shape[-3:]
    return array[..., margin + off_z:size_z - margin + off_z, margin + off_x:size_x - margin + off_x, margin + off_y:size_y - margin + off_y]

def face_term(field, center, coef, off_z, off_x, off_y):
    upper = 0.5 * (inner_part(coef, 0, 0, 0) + inner_part(coef, off_z, off_x, off_y))
    lower = 0.5 * (inner_part(coef, 0, 0, 0) + inner_part(coef, -off_z, -off_x, -off_y))
    return upper * (center - inner_part(field, off_z, off_x, off_y)) + lower * (center - inner_part(field, -off_z, -off_x, -off_y))

def apply_operator(field, coef_z, coef_x, coef_y, diag_pad):
    center = inner_part(field, 0, 0, 0)
    image = inner_part(diag_pad, 0, 0, 0) * center
    image = image + face_term(field, center, coef_z, 1, 0, 0)
    image = image + face_term(field, center, coef_x, 0, 1, 0)
    image = image + face_term(field, center, coef_y, 0, 0, 1)
    return image

def pad_cells(array):
    widths = [(0, 0)] * (array.ndim - 3) + [(1, 1)] * 3
    return jnp.pad(array, widths)

def upper_cholesky(gram):
    order = gram.shape[0]
    column_ids = jnp.arange(order, dtype=jnp.int32)
    factor_rows = []
    for row_id in range(order):
        accum = gram[row_id]
        if factor_rows:
            earlier = jnp.stack(factor_rows, 0)
            accum = accum - lax.optimization_barrier(jnp.sum(earlier[:, row_id:row_id + 1] * earlier, 0))
        pivot = jnp.sqrt(accum[row_id])
        factor_rows.append(jnp.where(column_ids >= row_id, accum / pivot, jnp.zeros_like(accum)))
    return jnp.stack(factor_rows, 0)

def upper_inverse(factor):
    order = factor.shape[0]
    identity_mat = jnp.eye(order, dtype=factor.dtype)
    solved = [None] * order
    for row_id in range(order - 1, -1, -1):
        accum = identity_mat[row_id]
        if row_id < order - 1:
            later = jnp.stack(solved[row_id + 1:], 0)
            accum = accum - lax.optimization_barrier(jnp.sum(factor[row_id, row_id + 1:][:, None] * later, 0))
        solved[row_id] = accum / factor[row_id, row_id]
    return jnp.stack(solved, 0)

def orthonormalize(rows, count):
    gram = jnp.dot(rows, rows.T, precision=lax.Precision.HIGHEST)
    factor = upper_cholesky(gram / count)
    inverse = upper_inverse(factor)
    return (jnp.dot(inverse.T, rows, precision=lax.Precision.HIGHEST), factor)

def reference(rhs, coef_x, coef_y, coef_z, diag_term):
    pad_z = pad_cells(coef_z)
    pad_x = pad_cells(coef_x)
    pad_y = pad_cells(coef_y)
    pad_diag = pad_cells(diag_term)
    field = rhs
    blocks = [rhs]
    for section in range(STEPS):
        image = apply_operator(pad_cells(field), pad_z, pad_x, pad_y, pad_diag)
        field = (image - NEWTON_SHIFTS[section] * field) * BASIS_SCALE
        blocks.append(field)
    basis = jnp.concatenate(blocks, 0)
    count = float(NZ * NX * NY)
    rows = basis.reshape(COLS, -1)
    first, factor_one = orthonormalize(rows, count)
    second, factor_two = orthonormalize(first, count)
    return (second.reshape(basis.shape), jnp.dot(factor_two, factor_one, precision=lax.Precision.HIGHEST))
```

```python
import functools

import jax
import jax.numpy as jnp
from jax import lax
from jax.experimental import pallas as pl
from jax.experimental.pallas import tpu as pltpu
from jax.sharding import PartitionSpec as P

NRHS = 4
STEPS = 4
COLS = NRHS * (STEPS + 1)
SHIFTS = (3.0, 11.0, 7.0, 1.5)
SCALE = 1.0 / 6.0
FIELDS = NRHS + 4
AXES = ("gx", "gy", "gz")
HIGHEST = lax.Precision.HIGHEST

DEPTH = 4
NZ, NX, NY = 8, 32, 256
EZ = NZ + 2 * DEPTH
ROWS = NX + 8
EROWS = ROWS + 16
LT = 3
FACE = NRHS * 4 + 3 * 4 + 1
F32 = jnp.float32


def params(mb):
    return pltpu.CompilerParams(vmem_limit_bytes=mb << 20)


def vmem():
    return pl.BlockSpec(memory_space=pltpu.VMEM)


def smem():
    return pl.BlockSpec(memory_space=pltpu.SMEM)


def hbm():
    return pl.BlockSpec(memory_space=pl.ANY)


def row_ids(shape):
    return lax.broadcasted_iota(jnp.int32, shape, 0)


def lane_ids(shape):
    return lax.broadcasted_iota(jnp.int32, shape, 1)


def field_of(rhs, cz, cx, cy, dg, f, z):
    return rhs.at[f, z] if f < NRHS else (cz, cx, cy, dg)[f - NRHS].at[z]


def pack_faces(swap, place, rhs, cz, cx, cy, dg, zlo, zhi, *xmsgs):
    n = 0
    for f in range(FIELDS):
        depth = DEPTH if f <= NRHS else DEPTH - 1
        for d in range(depth):
            zlo[n] = field_of(rhs, cz, cx, cy, dg, f, d)[...]
            zhi[n] = field_of(rhs, cz, cx, cy, dg, f, NZ - depth + d)[...]
            n += 1
    low = row_ids((8, NY)) < 4
    up = place[0] == 0
    for f in range(FIELDS):
        for m in range(NZ // 2):
            a = field_of(rhs, cz, cx, cy, dg, f, 2 * m)
            b = field_of(rhs, cz, cx, cy, dg, f, 2 * m + 1)
            first = jnp.where(low, a[0:8], pltpu.roll(b[0:8], 4, 0))
            last = jnp.where(low, pltpu.roll(a[NX - 8 : NX], 4, 0), b[NX - 8 : NX])
            if swap:
                xmsgs[0][f, m] = jnp.where(up, last, first)
            else:
                xmsgs[0][f, m] = first
                xmsgs[1][f, m] = last


def halo_tile(above, below, odd, keep_up, keep_dn):
    low = row_ids(above.shape) < 4
    if odd:
        up, dn = pltpu.roll(above, 4, 0), below
    else:
        up, dn = above, pltpu.roll(below, 4, 0)
    return jnp.where(low, up * keep_up, dn * keep_dn)


def pack_rims(keep, rhs, cz, cx, cy, dg, above, below, ylo, yhi):
    lane = lane_ids((8, 128))
    keep_up, keep_dn = keep[0], keep[1]
    for t in range(ROWS // 8):
        for side, out in ((0, ylo), (1, yhi)):
            lanes = pl.ds(128 * side, 128)
            source = 124 * side
            for half in range(2):
                acc = jnp.zeros((8, 128), F32)
                for zz in range(4):
                    z = 4 * half + zz
                    for f in range(FIELDS):
                        if t < NX // 8:
                            tile = field_of(rhs, cz, cx, cy, dg, f, z)[8 * t : 8 * t + 8, lanes]
                        else:
                            tile = halo_tile(
                                above[f, z // 2, :, lanes], below[f, z // 2, :, lanes], z % 2, keep_up, keep_dn
                            )
                        spot = (zz * FIELDS + f) * 4
                        shift = (spot - source) % 128
                        if shift:
                            tile = pltpu.roll(tile, shift, 1)
                        acc = jnp.where((lane >= spot) & (lane < spot + 4), tile, acc)
                out[8 * t : 8 * t + 8, 128 * half : 128 * half + 128] = acc


def gram_message(read, count, parts, out, unroll=4):
    group = 5
    parts[...] = jnp.zeros_like(parts)
    for gi in range(COLS // group):
        for gj in range(gi, COLS // group):
            pairs = [
                (i, j)
                for i in range(group * gi, group * gi + group)
                for j in range(group * gj, group * gj + group)
                if i <= j
            ]

            def step(n, sums):
                sums = list(sums)
                rows = {i: read(i, n) for i in sorted({i for pair in pairs for i in pair})}
                for k, (i, j) in enumerate(pairs):
                    sums[k] = sums[k] + rows[i] * rows[j]
                return tuple(sums)

            sums = lax.fori_loop(
                0, count, step, tuple(jnp.zeros((8, 128), F32) for _ in pairs), unroll=unroll
            )
            for (i, j), total in zip(pairs, sums):
                line = jnp.sum(total, axis=0, keepdims=True)
                parts[32 * i + j : 32 * i + j + 1, :] = line
                if i != j:
                    parts[32 * j + i : 32 * j + i + 1, :] = line
    flat = lax.dot_general(
        jnp.ones((8, 128), F32), parts[...], (((1,), (1,)), ((), ())), precision=HIGHEST, preferred_element_type=F32
    )
    out[...] = jnp.zeros_like(out)
    for r in range(COLS * 32 // 128):
        out[r : r + 1, :] = flat[0:1, 128 * r : 128 * r + 128]


def krylov(
    keep, rhs, cz, cx, cy, dg, above, below, yup, ydn, facelo, facehi, rimlo, rimhi,
    basis, message,
    store, faces, ysrc, parts, sems,
):
    lane = lane_ids((8, 128))
    keep_up, keep_dn = keep[0], keep[1]
    n_x = 1 if above is below else 2

    def put(f, z, l, t, value):
        store[f, z, l, 8 + 8 * t : 16 + 8 * t, :] = value
        if t == 0:
            store[f, z, l, 8 + ROWS : 16 + ROWS, :] = value
        if t == ROWS // 8 - 1:
            store[f, z, l, 0:8, :] = value

    x_rows = FIELDS * 2 * 8
    for f in range(FIELDS):
        depth = DEPTH if f <= NRHS else DEPTH - 1
        start = f * DEPTH if f <= NRHS else NRHS * DEPTH + DEPTH + (f - NRHS - 1) * (DEPTH - 1)
        for z in range(EZ):
            own = DEPTH <= z < DEPTH + NZ
            if own:
                plane = field_of(rhs, cz, cx, cy, dg, f, z - DEPTH)
            elif z < DEPTH:
                d = z - (DEPTH - depth)
                plane = facelo.at[start + d] if d >= 0 else None
            else:
                d = z - DEPTH - NZ
                plane = facehi.at[start + d] if d < depth else None
            for l in range(2):
                lanes = pl.ds(128 * l, 128)
                for t in range(NX // 8):
                    if plane is None:
                        put(f, z, l, t, jnp.zeros((8, 128), F32))
                    else:
                        put(f, z, l, t, plane[8 * t : 8 * t + 8, lanes])
                if own:
                    m = (z - DEPTH) // 2
                    a, b = above[f, m, :, lanes], below[f, m, :, lanes]
                else:
                    rim, m = (rimlo, z // 2) if z < DEPTH else (rimhi, (z - DEPTH - NZ) // 2)
                    at = (f * 2 + m) * 8
                    a = rim[at : at + 8, lanes]
                    at += x_rows * (n_x - 1)
                    b = rim[at : at + 8, lanes]
                put(f, z, l, NX // 8, halo_tile(a, b, z % 2, keep_up, keep_dn))

    at = x_rows * n_x
    ysrc[0, 0] = rimlo[at : at + ROWS, 0:128]
    ysrc[1, 0] = rimlo[at : at + ROWS, 128:256]
    ysrc[0, 1] = yup[:, 0:128]
    ysrc[0, 2] = yup[:, 128:256]
    ysrc[1, 1] = ydn[:, 0:128]
    ysrc[1, 2] = ydn[:, 128:256]
    ysrc[0, 3] = rimhi[at : at + ROWS, 0:128]
    ysrc[1, 3] = rimhi[at : at + ROWS, 128:256]

    def place_y(q, carry):
        for t in range(ROWS // 8):
            up = ysrc[0, q, 8 * t : 8 * t + 8, :]
            dn = ysrc[1, q, 8 * t : 8 * t + 8, :]
            for zz in range(4):
                for f in range(FIELDS):
                    spot = (zz * FIELDS + f) * 4
                    u = pltpu.roll(up, (-spot) % 128, 1) if spot else up
                    d = pltpu.roll(dn, (124 - spot) % 128, 1) if spot != 124 else dn
                    put(f, 4 * q + zz, 2, t, jnp.where(lane < 4, u, jnp.where(lane >= 124, d, 0.0)))
        return carry

    lax.fori_loop(0, EZ // 4, place_y, 0)

    def tiles(f, z, t, off):
        return [store[f, z, l, pl.ds(8 + 8 * t + off, 8), :] for l in range(LT)]

    def lane_up(tri):
        rolled = [pltpu.roll(v, 127, 1) for v in tri]
        return [jnp.where(lane == 127, rolled[(l + 1) % LT], rolled[l]) for l in range(LT)]

    def lane_dn(tri):
        rolled = [pltpu.roll(v, 1, 1) for v in tri]
        return [jnp.where(lane == 0, rolled[(l - 1) % LT], rolled[l]) for l in range(LT)]

    def coefficients(z, carry):
        for t in range(ROWS // 8):
            kz, kx, ky, kd = (NRHS + i for i in range(4))
            center_z, center_x, center_y = (tiles(k, z, t, 0) for k in (kz, kx, ky))
            diag = tiles(kd, z, t, 0)
            sides = [
                (center_z, tiles(kz, z + 1, t, 0)),
                (center_z, tiles(kz, z - 1, t, 0)),
                (center_x, tiles(kx, z, t, 1)),
                (center_x, tiles(kx, z, t, -1)),
                (center_y, lane_up(center_y)),
                (center_y, lane_dn(center_y)),
            ]
            for l in range(LT):
                inside = diag[l] > 0.0
                total = diag[l] * SCALE
                for k, (mid, side) in enumerate(sides):
                    face = (mid[l] + side[l]) * (0.5 * SCALE)
                    total = total + face
                    faces[k, z, l, 8 * t : 8 * t + 8, :] = jnp.where(inside, face, 0.0)
                faces[6, z, l, 8 * t : 8 * t + 8, :] = jnp.where(inside, total, 0.0)
        return carry

    lax.fori_loop(1, EZ - 1, coefficients, 0)

    copies = []

    def send_block(k):
        copy = pltpu.make_async_copy(
            store.at[pl.ds(k * NRHS + (NRHS if k else 0) * 1, NRHS), pl.ds(DEPTH, NZ), pl.ds(0, 2), pl.ds(8, NX), :],
            basis.at[pl.ds(k * NRHS, NRHS)],
            sems.at[k],
        )
        copy.start()
        copies.append(copy)

    def slot(k):
        return k * NRHS + (NRHS if k else 0)

    send_block(0)
    for k in range(STEPS):

        def apply(z, carry):
            for t in range(ROWS // 8):
                face = [[faces[c, z, l, 8 * t : 8 * t + 8, :] for l in range(LT)] for c in range(7)]
                diag = [face[6][l] - SHIFTS[k] * SCALE for l in range(LT)]
                for r in range(NRHS):
                    f = slot(k) + r
                    mid = tiles(f, z, t, 0)
                    sides = [
                        tiles(f, z + 1, t, 0),
                        tiles(f, z - 1, t, 0),
                        tiles(f, z, t, 1),
                        tiles(f, z, t, -1),
                        lane_up(mid),
                        lane_dn(mid),
                    ]
                    for l in range(LT):
                        value = diag[l] * mid[l]
                        for c in range(6):
                            value = value - face[c][l] * sides[c][l]
                        put(slot(k + 1) + r, z, l, t, value)
            return carry

        lax.fori_loop(k + 1, EZ - 1 - k, apply, 0)
        send_block(k + 1)

    def read(i, n):
        f = slot(i // NRHS) + i % NRHS
        return store[f, DEPTH + n // 8, (n // 4) % 2, pl.ds(pl.multiple_of(8 + 8 * (n % 4), 8), 8), :]

    gram_message(read, NZ * 8, parts, message)
    for copy in copies:
        copy.wait()


def factor_gram(message, cells, gram, work):
    rows = row_ids((24, 128))
    lanes = lane_ids((24, 128))
    gram[...] = jnp.zeros_like(gram)
    for q in range(4):
        turned = pltpu.roll(message, (-32 * q) % 128, 1) if q else message
        for r in range(COLS // 4):
            i = 4 * r + q
            gram[i : i + 1, :] = turned[r : r + 1, :]
    a = jnp.where(lanes < COLS, gram[...] / cells, 0.0)
    a = jnp.where((lanes == rows + 32) & (rows < COLS), 1.0, a)
    for j in range(COLS - 1):
        column = jnp.broadcast_to(a[:, j : j + 1], (24, 128))
        row = jnp.broadcast_to(a[j : j + 1, :], (24, 128))
        pivot = jnp.broadcast_to(column[j : j + 1, :], (24, 128))
        a = a - jnp.where(rows > j, column / pivot, 0.0) * row
    diag = jnp.sum(jnp.where(lanes == rows, a, 0.0), axis=1, keepdims=True)
    diag = jnp.where(rows < COLS, jnp.broadcast_to(diag, (24, 128)), 1.0)
    a = a / jnp.sqrt(diag)
    return jnp.where((lanes >= rows) & (lanes < COLS) | (lanes >= 32) & (lanes <= rows + 32), a, 0.0)


def spread(factor, table):
    for j in range(COLS):
        table[j] = jnp.broadcast_to(factor[:, 32 + j : 33 + j], (24, 128))


def apply_rows(table, read, write):
    group = 5
    pieces = NX // 8
    for g in range(COLS // group):
        mine = range(group * g, group * g + group)
        sums = {i: None for i in mine}
        for j in range(group * g + group):
            value = [read(j, p) for p in range(pieces)]
            for i in mine:
                if j <= i:
                    weight = jnp.broadcast_to(table[j, i : i + 1, :], (8, 128))
                    terms = [weight * v for v in value]
                    sums[i] = terms if sums[i] is None else [s + t for s, t in zip(sums[i], terms)]
        for i in mine:
            for p in range(pieces):
                write(i, p, sums[i][p])


def first_pass(cells, message, basis_hbm, first_hbm, next_message, factor_out, basis, gram, table, parts, sems):
    load = pltpu.make_async_copy(basis_hbm, basis, sems.at[0])
    load.start()
    factor = factor_gram(message[...], cells, gram, None)
    factor_out[...] = factor
    spread(factor, table)
    load.wait()

    def chunk(n, carry):
        z, l = n // 2, n % 2

        def read(j, p):
            return basis[j, z, l, 8 * p : 8 * p + 8, :]

        pending = []
        apply_rows(table, read, lambda i, p, value: pending.append((i, p, value)))
        for i, p, value in pending:
            basis[i, z, l, 8 * p : 8 * p + 8, :] = value
        return carry

    lax.fori_loop(0, NZ * 2, chunk, 0)
    save = pltpu.make_async_copy(basis, first_hbm, sems.at[1])
    save.start()

    def read(i, n):
        return basis[i, n // 8, (n // 4) % 2, pl.ds(pl.multiple_of(8 * (n % 4), 8), 8), :]

    gram_message(read, NZ * 8, parts, next_message)
    save.wait()


def second_pass(cells, message, factor_one, first_hbm, out, triangle, first, gram, table, sems):
    load = pltpu.make_async_copy(first_hbm, first, sems.at[0])
    load.start()
    factor = factor_gram(message[...], cells, gram, None)
    spread(factor, table)
    lanes = lane_ids((24, 128))
    left = jnp.where(lanes < COLS, factor, 0.0)[:, 0:24]
    product = lax.dot_general(
        left, factor_one[...], (((1,), (0,)), ((), ())), precision=HIGHEST, preferred_element_type=F32
    )
    triangle[...] = product[0:COLS, 0:COLS]
    load.wait()

    def chunk(z, carry):
        for l in range(2):

            def read(j, p):
                return first[j, z, l, 8 * p : 8 * p + 8, :]

            def write(i, p, value):
                out[i, z, 8 * p : 8 * p + 8, 128 * l : 128 * l + 128] = value

            apply_rows(table, read, write)
        return carry

    lax.fori_loop(0, NZ, chunk, 0)


def shape(*dims):
    return jax.ShapeDtypeStruct(dims, F32)


def move(value, axis, delta):
    count = lax.axis_size(axis)
    pairs = [(i, i + delta) for i in range(count) if 0 <= i + delta < count]
    return lax.ppermute(value, axis, pairs)


def body(rhs, coef_x, coef_y, coef_z, diag_term):
    n_x = lax.axis_size("gx")
    cells = float(NZ * NX * NY * n_x * lax.axis_size("gy") * lax.axis_size("gz"))
    at_x = lax.axis_index("gx")
    swap = n_x == 2
    fields = (rhs, coef_z, coef_x, coef_y, diag_term)

    x_shape = shape(FIELDS, NZ // 2, 8, NY)
    face_shape = shape(FACE, NX, NY)
    zlo, zhi, *xmsgs = pl.pallas_call(
        functools.partial(pack_faces, swap),
        out_shape=(face_shape, face_shape) + (x_shape,) * (1 if swap else 2),
        in_specs=[smem()] + [vmem()] * 5,
        compiler_params=params(32),
    )(at_x.astype(jnp.int32).reshape(1), *fields)
    facehi = move(zlo, "gz", -1)
    facelo = move(zhi, "gz", 1)
    if swap:
        above = below = lax.ppermute(xmsgs[0], "gx", [(0, 1), (1, 0)])
        x_parts = (above,)
        keep = jnp.stack([1 - at_x, at_x]).astype(F32)
    else:
        above, below = move(xmsgs[0], "gx", -1), move(xmsgs[1], "gx", 1)
        x_parts = (above, below)
        keep = jnp.ones((2,), F32)

    rim_shape = shape(ROWS, NY)
    ylo, yhi = pl.pallas_call(
        pack_rims,
        out_shape=(rim_shape, rim_shape),
        in_specs=[smem()] + [vmem()] * 7,
        compiler_params=params(32),
    )(keep, *fields, above, below)
    yup, ydn = move(ylo, "gy", -1), move(yhi, "gy", 1)

    def rim(half):
        rows = [p[:, 2 * half : 2 * half + 2].reshape(-1, NY) for p in x_parts]
        lanes = slice(128 * half, 128 * half + 128)
        return jnp.concatenate(rows + [jnp.concatenate([yup[:, lanes], ydn[:, lanes]], 1)], 0)

    rimhi, rimlo = move(rim(0), "gz", -1), move(rim(1), "gz", 1)

    block = shape(COLS, NZ, 2, NX, 128)

    def krylov_entry(keep, rhs, cz, cx, cy, dg, *rest):
        if swap:
            rest = (rest[0],) + rest
        krylov(keep, rhs, cz, cx, cy, dg, *rest)

    basis, message = pl.pallas_call(
        krylov_entry,
        out_shape=(block, shape(8, 128)),
        in_specs=[smem()] + [vmem()] * (5 + len(x_parts) + 6),
        out_specs=(hbm(), vmem()),
        scratch_shapes=[
            pltpu.VMEM((COLS + NRHS, EZ, LT, EROWS, 128), F32),
            pltpu.VMEM((7, EZ, LT, ROWS, 128), F32),
            pltpu.VMEM((2, 4, ROWS, 128), F32),
            pltpu.VMEM((32 * COLS, 128), F32),
            pltpu.SemaphoreType.DMA((STEPS + 1,)),
        ],
        compiler_params=params(56),
    )(keep, *fields, *x_parts, yup, ydn, facelo, facehi, rimlo, rimhi)

    message = lax.psum(message, AXES)
    first, message, factor_one = pl.pallas_call(
        functools.partial(first_pass, cells),
        out_shape=(block, shape(8, 128), shape(24, 128)),
        in_specs=[vmem(), hbm()],
        out_specs=(hbm(), vmem(), vmem()),
        scratch_shapes=[
            pltpu.VMEM(block.shape, F32),
            pltpu.VMEM((24, 128), F32),
            pltpu.VMEM((COLS, 24, 128), F32),
            pltpu.VMEM((32 * COLS, 128), F32),
            pltpu.SemaphoreType.DMA((2,)),
        ],
        compiler_params=params(32),
    )(message, basis)

    message = lax.psum(message, AXES)
    return pl.pallas_call(
        functools.partial(second_pass, cells),
        out_shape=(shape(COLS, NZ, NX, NY), shape(COLS, COLS)),
        in_specs=[vmem(), vmem(), hbm()],
        out_specs=(vmem(), vmem()),
        scratch_shapes=[
            pltpu.VMEM(block.shape, F32),
            pltpu.VMEM((24, 128), F32),
            pltpu.VMEM((COLS, 24, 128), F32),
            pltpu.SemaphoreType.DMA((1,)),
        ],
        compiler_params=params(32),
    )(message, factor_one, first)


def solution(mesh):
    return jax.shard_map(
        body,
        mesh=mesh,
        in_specs=(
            P(None, "gz", "gx", "gy"),
            P("gz", "gx", "gy"),
            P("gz", "gx", "gy"),
            P("gz", "gx", "gy"),
            P("gz", "gx", "gy"),
        ),
        out_specs=(P(None, "gz", "gx", "gy"), P()),
        check_vma=False,
    )
```

```python
import functools

import jax
import jax.numpy as jnp
from jax import lax
from jax.experimental import pallas as pl
from jax.experimental.pallas import tpu as pltpu
from jax.sharding import PartitionSpec as P

NRHS = 4
STEPS = 4
COLS = NRHS * (STEPS + 1)
SHIFTS = (3.0, 11.0, 7.0, 1.5)
SCALE = 1.0 / 6.0
FIELDS = NRHS + 4
AXES = ("gx", "gy", "gz")
HIGHEST = lax.Precision.HIGHEST

DEPTH = 4
NZ, NX, NY = 8, 32, 256
EZ = NZ + 2 * DEPTH
ROWS = NX + 8
EROWS = ROWS + 16
LT = 3
FACE = NRHS * 4 + 3 * 4 + 1
F32 = jnp.float32


def params(mb):
    return pltpu.CompilerParams(vmem_limit_bytes=mb << 20)


def vmem():
    return pl.BlockSpec(memory_space=pltpu.VMEM)


def smem():
    return pl.BlockSpec(memory_space=pltpu.SMEM)


def hbm():
    return pl.BlockSpec(memory_space=pl.ANY)


def row_ids(shape):
    return lax.broadcasted_iota(jnp.int32, shape, 0)


def lane_ids(shape):
    return lax.broadcasted_iota(jnp.int32, shape, 1)


def field_of(rhs, cz, cx, cy, dg, f, z):
    return rhs.at[f, z] if f < NRHS else (cz, cx, cy, dg)[f - NRHS].at[z]


def pack_faces(swap, place, rhs, cz, cx, cy, dg, zlo, zhi, *xmsgs):
    n = 0
    for f in range(FIELDS):
        depth = DEPTH if f <= NRHS else DEPTH - 1
        for d in range(depth):
            zlo[n] = field_of(rhs, cz, cx, cy, dg, f, d)[...]
            zhi[n] = field_of(rhs, cz, cx, cy, dg, f, NZ - depth + d)[...]
            n += 1
    low = row_ids((8, NY)) < 4
    up = place[0] == 0
    for f in range(FIELDS):
        for m in range(NZ // 2):
            a = field_of(rhs, cz, cx, cy, dg, f, 2 * m)
            b = field_of(rhs, cz, cx, cy, dg, f, 2 * m + 1)
            first = jnp.where(low, a[0:8], pltpu.roll(b[0:8], 4, 0))
            last = jnp.where(low, pltpu.roll(a[NX - 8 : NX], 4, 0), b[NX - 8 : NX])
            if swap:
                xmsgs[0][f, m] = jnp.where(up, last, first)
            else:
                xmsgs[0][f, m] = first
                xmsgs[1][f, m] = last


def halo_tile(above, below, odd, keep_up, keep_dn):
    low = row_ids(above.shape) < 4
    if odd:
        up, dn = pltpu.roll(above, 4, 0), below
    else:
        up, dn = above, pltpu.roll(below, 4, 0)
    return jnp.where(low, up * keep_up, dn * keep_dn)


def pack_rims(keep, rhs, cz, cx, cy, dg, above, below, ylo, yhi):
    lane = lane_ids((8, 128))
    keep_up, keep_dn = keep[0], keep[1]
    for t in range(ROWS // 8):
        for side, out in ((0, ylo), (1, yhi)):
            lanes = pl.ds(128 * side, 128)
            source = 124 * side
            for half in range(2):
                acc = jnp.zeros((8, 128), F32)
                for zz in range(4):
                    z = 4 * half + zz
                    for f in range(FIELDS):
                        if t < NX // 8:
                            tile = field_of(rhs, cz, cx, cy, dg, f, z)[8 * t : 8 * t + 8, lanes]
                        else:
                            tile = halo_tile(
                                above[f, z // 2, :, lanes], below[f, z // 2, :, lanes], z % 2, keep_up, keep_dn
                            )
                        spot = (zz * FIELDS + f) * 4
                        shift = (spot - source) % 128
                        if shift:
                            tile = pltpu.roll(tile, shift, 1)
                        acc = jnp.where((lane >= spot) & (lane < spot + 4), tile, acc)
                out[8 * t : 8 * t + 8, 128 * half : 128 * half + 128] = acc


def gather_rows(values):
    rows = row_ids((8, 128))
    width = 1
    while len(values) > 1:
        low = (rows & width) == 0
        merged = []
        for a, b in zip(values[0::2], values[1::2]):
            if a is None and b is None:
                merged.append(None)
                continue
            a = jnp.zeros((8, 128), F32) if a is None else a
            b = jnp.zeros((8, 128), F32) if b is None else b
            merged.append(jnp.where(low, a, b) + pltpu.roll(jnp.where(low, b, a), width, 0))
        values = merged
        width *= 2
    return values[0]


def gram_message(read, count, out, unroll=2):
    lanes = lane_ids((8, 128))
    result = jnp.zeros((8, 128), F32)
    for tile in range(0, COLS, 8):
        mine = range(tile, min(tile + 8, COLS))
        columns = [mine] + [range(c, c + 4) for c in range(tile + 8, COLS, 4)]
        for group in columns:
            pairs = [(i, j) for j in group for i in mine if i <= j]

            def step(n, sums):
                rows = {i: read(i, n) for i in sorted({i for pair in pairs for i in pair})}
                return tuple(s + rows[i] * rows[j] for s, (i, j) in zip(sums, pairs))

            sums = lax.fori_loop(
                0, count, step, tuple(jnp.zeros((8, 128), F32) for _ in pairs), unroll=unroll
            )
            sums = dict(zip(pairs, sums))
            for j in group:
                total = gather_rows([sums.get((tile + s, j)) for s in range(8)])
                total = jnp.sum(total, axis=1, keepdims=True)
                result = jnp.where(lanes == 4 * tile + j, jnp.broadcast_to(total, (8, 128)), result)
    for n in range(out.shape[0]):
        out[n] = result


def krylov(
    keep, rhs, cz, cx, cy, dg, above, below, yup, ydn, facelo, facehi, rimlo, rimhi,
    basis, message,
    store, faces, ysrc, sems,
):
    lane = lane_ids((8, 128))
    keep_up, keep_dn = keep[0], keep[1]
    n_x = 1 if above is below else 2

    def put(f, z, l, t, value):
        store[f, z, l, 8 + 8 * t : 16 + 8 * t, :] = value
        if t == 0:
            store[f, z, l, 8 + ROWS : 16 + ROWS, :] = value
        if t == ROWS // 8 - 1:
            store[f, z, l, 0:8, :] = value

    x_rows = FIELDS * 2 * 8
    for f in range(FIELDS):
        depth = DEPTH if f <= NRHS else DEPTH - 1
        start = f * DEPTH if f <= NRHS else NRHS * DEPTH + DEPTH + (f - NRHS - 1) * (DEPTH - 1)
        for z in range(EZ):
            own = DEPTH <= z < DEPTH + NZ
            if own:
                plane = field_of(rhs, cz, cx, cy, dg, f, z - DEPTH)
            elif z < DEPTH:
                d = z - (DEPTH - depth)
                plane = facelo.at[start + d] if d >= 0 else None
            else:
                d = z - DEPTH - NZ
                plane = facehi.at[start + d] if d < depth else None
            for l in range(2):
                lanes = pl.ds(128 * l, 128)
                for t in range(NX // 8):
                    if plane is None:
                        put(f, z, l, t, jnp.zeros((8, 128), F32))
                    else:
                        put(f, z, l, t, plane[8 * t : 8 * t + 8, lanes])
                if own:
                    m = (z - DEPTH) // 2
                    a, b = above[f, m, :, lanes], below[f, m, :, lanes]
                else:
                    rim, m = (rimlo, z // 2) if z < DEPTH else (rimhi, (z - DEPTH - NZ) // 2)
                    at = (f * 2 + m) * 8
                    a = rim[at : at + 8, lanes]
                    at += x_rows * (n_x - 1)
                    b = rim[at : at + 8, lanes]
                put(f, z, l, NX // 8, halo_tile(a, b, z % 2, keep_up, keep_dn))

    at = x_rows * n_x
    ysrc[0, 0] = rimlo[at : at + ROWS, 0:128]
    ysrc[1, 0] = rimlo[at : at + ROWS, 128:256]
    ysrc[0, 1] = yup[:, 0:128]
    ysrc[0, 2] = yup[:, 128:256]
    ysrc[1, 1] = ydn[:, 0:128]
    ysrc[1, 2] = ydn[:, 128:256]
    ysrc[0, 3] = rimhi[at : at + ROWS, 0:128]
    ysrc[1, 3] = rimhi[at : at + ROWS, 128:256]

    def place_y(q, carry):
        for t in range(ROWS // 8):
            up = ysrc[0, q, 8 * t : 8 * t + 8, :]
            dn = ysrc[1, q, 8 * t : 8 * t + 8, :]
            for zz in range(4):
                for f in range(FIELDS):
                    spot = (zz * FIELDS + f) * 4
                    u = pltpu.roll(up, (-spot) % 128, 1) if spot else up
                    d = pltpu.roll(dn, (124 - spot) % 128, 1) if spot != 124 else dn
                    put(f, 4 * q + zz, 2, t, jnp.where(lane < 4, u, jnp.where(lane >= 124, d, 0.0)))
        return carry

    lax.fori_loop(0, EZ // 4, place_y, 0)

    def tiles(f, z, t, off):
        return [store[f, z, l, pl.ds(8 + 8 * t + off, 8), :] for l in range(LT)]

    def lane_up(tri):
        rolled = [pltpu.roll(v, 127, 1) for v in tri]
        return [jnp.where(lane == 127, rolled[(l + 1) % LT], rolled[l]) for l in range(LT)]

    def lane_dn(tri):
        rolled = [pltpu.roll(v, 1, 1) for v in tri]
        return [jnp.where(lane == 0, rolled[(l - 1) % LT], rolled[l]) for l in range(LT)]

    def coefficients(z, carry):
        for t in range(ROWS // 8):
            kz, kx, ky, kd = (NRHS + i for i in range(4))
            center_z, center_x, center_y = (tiles(k, z, t, 0) for k in (kz, kx, ky))
            diag = tiles(kd, z, t, 0)
            sides = [
                (center_z, tiles(kz, z + 1, t, 0)),
                (center_z, tiles(kz, z - 1, t, 0)),
                (center_x, tiles(kx, z, t, 1)),
                (center_x, tiles(kx, z, t, -1)),
                (center_y, lane_up(center_y)),
                (center_y, lane_dn(center_y)),
            ]
            for l in range(LT):
                inside = diag[l] > 0.0
                total = diag[l] * SCALE
                for k, (mid, side) in enumerate(sides):
                    face = (mid[l] + side[l]) * (0.5 * SCALE)
                    total = total + face
                    faces[k, z, l, 8 * t : 8 * t + 8, :] = jnp.where(inside, face, 0.0)
                faces[6, z, l, 8 * t : 8 * t + 8, :] = jnp.where(inside, total, 0.0)
        return carry

    lax.fori_loop(1, EZ - 1, coefficients, 0)

    copies = []

    def send_block(k):
        copy = pltpu.make_async_copy(
            store.at[pl.ds(k * NRHS + (NRHS if k else 0) * 1, NRHS), pl.ds(DEPTH, NZ), pl.ds(0, 2), pl.ds(8, NX), :],
            basis.at[pl.ds(k * NRHS, NRHS)],
            sems.at[k],
        )
        copy.start()
        copies.append(copy)

    def slot(k):
        return k * NRHS + (NRHS if k else 0)

    send_block(0)
    for k in range(STEPS):

        def apply(z, carry):
            for t in range(ROWS // 8):
                face = [[faces[c, z, l, 8 * t : 8 * t + 8, :] for l in range(LT)] for c in range(7)]
                diag = [face[6][l] - SHIFTS[k] * SCALE for l in range(LT)]
                for r in range(NRHS):
                    f = slot(k) + r
                    mid = tiles(f, z, t, 0)
                    sides = [
                        tiles(f, z + 1, t, 0),
                        tiles(f, z - 1, t, 0),
                        tiles(f, z, t, 1),
                        tiles(f, z, t, -1),
                        lane_up(mid),
                        lane_dn(mid),
                    ]
                    for l in range(LT):
                        value = diag[l] * mid[l]
                        for c in range(6):
                            value = value - face[c][l] * sides[c][l]
                        put(slot(k + 1) + r, z, l, t, value)
            return carry

        lax.fori_loop(k + 1, EZ - 1 - k, apply, 0)
        send_block(k + 1)

    def read(i, n):
        f = slot(i // NRHS) + i % NRHS
        return store[f, DEPTH + n // 8, (n // 4) % 2, pl.ds(pl.multiple_of(8 + 8 * (n % 4), 8), 8), :]

    gram_message(read, NZ * 8, message)
    for copy in copies:
        copy.wait()


def factor_gram(messages, cells):
    rows = row_ids((24, 128))
    lanes = lane_ids((24, 128))
    message = messages[0]
    for n in range(1, messages.shape[0]):
        message = message + messages[n]
    upper = jnp.concatenate([message] + [pltpu.roll(message, 128 - 32 * k, 1) for k in (1, 2)], 0)
    upper = jnp.where((lanes < COLS) & (rows < COLS), upper, 0.0)
    square = jnp.concatenate([upper, jnp.zeros((104, 128), F32)], 0)
    a = jnp.where(rows <= lanes, upper, square.T[0:24, :]) / cells
    a = jnp.where((lanes == rows + 32) & (rows < COLS), 1.0, a)
    for j in range(COLS - 1):
        column = jnp.broadcast_to(a[:, j : j + 1], (24, 128))
        row = jnp.broadcast_to(a[j : j + 1, :], (24, 128))
        pivot = jnp.broadcast_to(column[j : j + 1, :], (24, 128))
        a = a - jnp.where(rows > j, column / pivot, 0.0) * row
    diag = jnp.sum(jnp.where(lanes == rows, a, 0.0), axis=1, keepdims=True)
    diag = jnp.where(rows < COLS, jnp.broadcast_to(diag, (24, 128)), 1.0)
    a = a / jnp.sqrt(diag)
    return jnp.where((lanes >= rows) & (lanes < COLS) | (lanes >= 32) & (lanes <= rows + 32), a, 0.0)


def spread(factor, table):
    for j in range(COLS):
        table[j] = jnp.broadcast_to(factor[:, 32 + j : 33 + j], (24, 128))


def apply_rows(table, read, write):
    group = 5
    pieces = NX // 8
    for g in range(COLS // group):
        mine = range(group * g, group * g + group)
        sums = {i: None for i in mine}
        for j in range(group * g + group):
            value = [read(j, p) for p in range(pieces)]
            for i in mine:
                if j <= i:
                    weight = jnp.broadcast_to(table[j, i : i + 1, :], (8, 128))
                    terms = [weight * v for v in value]
                    sums[i] = terms if sums[i] is None else [s + t for s, t in zip(sums[i], terms)]
        for i in mine:
            for p in range(pieces):
                write(i, p, sums[i][p])


def first_pass(cells, message, basis_hbm, first_hbm, next_message, factor_out, basis, table, sems):
    load = pltpu.make_async_copy(basis_hbm, basis, sems.at[0])
    load.start()
    factor = factor_gram(message, cells)
    factor_out[...] = factor
    spread(factor, table)
    load.wait()

    def chunk(n, carry):
        z, l = n // 2, n % 2

        def read(j, p):
            return basis[j, z, l, 8 * p : 8 * p + 8, :]

        pending = []
        apply_rows(table, read, lambda i, p, value: pending.append((i, p, value)))
        for i, p, value in pending:
            basis[i, z, l, 8 * p : 8 * p + 8, :] = value
        return carry

    lax.fori_loop(0, NZ * 2, chunk, 0)
    save = pltpu.make_async_copy(basis, first_hbm, sems.at[1])
    save.start()

    def read(i, n):
        return basis[i, n // 8, (n // 4) % 2, pl.ds(pl.multiple_of(8 * (n % 4), 8), 8), :]

    gram_message(read, NZ * 8, next_message)
    save.wait()


def second_pass(cells, message, factor_one, first_hbm, out, triangle, first, table, sems):
    load = pltpu.make_async_copy(first_hbm, first, sems.at[0])
    load.start()
    factor = factor_gram(message, cells)
    spread(factor, table)
    lanes = lane_ids((24, 128))
    left = jnp.where(lanes < COLS, factor, 0.0)[:, 0:24]
    product = lax.dot_general(
        left, factor_one[...], (((1,), (0,)), ((), ())), precision=HIGHEST, preferred_element_type=F32
    )
    triangle[...] = product[0:COLS, 0:COLS]
    load.wait()

    def chunk(z, carry):
        for l in range(2):

            def read(j, p):
                return first[j, z, l, 8 * p : 8 * p + 8, :]

            def write(i, p, value):
                out[i, z, 8 * p : 8 * p + 8, 128 * l : 128 * l + 128] = value

            apply_rows(table, read, write)
        return carry

    lax.fori_loop(0, NZ, chunk, 0)


def shape(*dims):
    return jax.ShapeDtypeStruct(dims, F32)


def move(value, axis, delta):
    count = lax.axis_size(axis)
    pairs = [(i, i + delta) for i in range(count) if 0 <= i + delta < count]
    return lax.ppermute(value, axis, pairs)


def exchange(messages):
    return lax.all_to_all(messages, AXES, 0, 0, tiled=True)


def body(rhs, coef_x, coef_y, coef_z, diag_term):
    n_x = lax.axis_size("gx")
    devices = n_x * lax.axis_size("gy") * lax.axis_size("gz")
    cells = float(NZ * NX * NY * devices)
    at_x = lax.axis_index("gx")
    swap = n_x == 2
    fields = (rhs, coef_z, coef_x, coef_y, diag_term)

    x_shape = shape(FIELDS, NZ // 2, 8, NY)
    face_shape = shape(FACE, NX, NY)
    zlo, zhi, *xmsgs = pl.pallas_call(
        functools.partial(pack_faces, swap),
        out_shape=(face_shape, face_shape) + (x_shape,) * (1 if swap else 2),
        in_specs=[smem()] + [vmem()] * 5,
        compiler_params=params(60),
    )(at_x.astype(jnp.int32).reshape(1), *fields)
    facehi = move(zlo, "gz", -1)
    facelo = move(zhi, "gz", 1)
    if swap:
        above = below = lax.ppermute(xmsgs[0], "gx", [(0, 1), (1, 0)])
        x_parts = (above,)
        keep = jnp.stack([1 - at_x, at_x]).astype(F32)
    else:
        above, below = move(xmsgs[0], "gx", -1), move(xmsgs[1], "gx", 1)
        x_parts = (above, below)
        keep = jnp.ones((2,), F32)

    rim_shape = shape(ROWS, NY)
    ylo, yhi = pl.pallas_call(
        pack_rims,
        out_shape=(rim_shape, rim_shape),
        in_specs=[smem()] + [vmem()] * 7,
        compiler_params=params(60),
    )(keep, *fields, above, below)
    yup, ydn = move(ylo, "gy", -1), move(yhi, "gy", 1)

    def rim(half):
        rows = [p[:, 2 * half : 2 * half + 2].reshape(-1, NY) for p in x_parts]
        lanes = slice(128 * half, 128 * half + 128)
        return jnp.concatenate(rows + [jnp.concatenate([yup[:, lanes], ydn[:, lanes]], 1)], 0)

    rimhi, rimlo = move(rim(0), "gz", -1), move(rim(1), "gz", 1)

    block = shape(COLS, NZ, 2, NX, 128)

    def krylov_entry(keep, rhs, cz, cx, cy, dg, *rest):
        if swap:
            rest = (rest[0],) + rest
        krylov(keep, rhs, cz, cx, cy, dg, *rest)

    basis, message = pl.pallas_call(
        krylov_entry,
        out_shape=(block, shape(devices, 8, 128)),
        in_specs=[smem()] + [vmem()] * (5 + len(x_parts) + 6),
        out_specs=(hbm(), vmem()),
        scratch_shapes=[
            pltpu.VMEM((COLS + NRHS, EZ, LT, EROWS, 128), F32),
            pltpu.VMEM((7, EZ, LT, ROWS, 128), F32),
            pltpu.VMEM((2, 4, ROWS, 128), F32),
            pltpu.SemaphoreType.DMA((STEPS + 1,)),
        ],
        compiler_params=params(60),
    )(keep, *fields, *x_parts, yup, ydn, facelo, facehi, rimlo, rimhi)

    message = exchange(message)
    first, message, factor_one = pl.pallas_call(
        functools.partial(first_pass, cells),
        out_shape=(block, shape(devices, 8, 128), shape(24, 128)),
        in_specs=[vmem(), hbm()],
        out_specs=(hbm(), vmem(), vmem()),
        scratch_shapes=[
            pltpu.VMEM(block.shape, F32),
            pltpu.VMEM((COLS, 24, 128), F32),
            pltpu.SemaphoreType.DMA((2,)),
        ],
        compiler_params=params(60),
    )(message, basis)

    message = exchange(message)
    return pl.pallas_call(
        functools.partial(second_pass, cells),
        out_shape=(shape(COLS, NZ, NX, NY), shape(COLS, COLS)),
        in_specs=[vmem(), vmem(), hbm()],
        out_specs=(vmem(), vmem()),
        scratch_shapes=[
            pltpu.VMEM(block.shape, F32),
            pltpu.VMEM((COLS, 24, 128), F32),
            pltpu.SemaphoreType.DMA((1,)),
        ],
        compiler_params=params(60),
    )(message, factor_one, first)


def solution(mesh):
    return jax.shard_map(
        body,
        mesh=mesh,
        in_specs=(
            P(None, "gz", "gx", "gy"),
            P("gz", "gx", "gy"),
            P("gz", "gx", "gy"),
            P("gz", "gx", "gy"),
            P("gz", "gx", "gy"),
        ),
        out_specs=(P(None, "gz", "gx", "gy"), P()),
        check_vma=False,
    )
```

```python
import functools

import jax
import jax.numpy as jnp
from jax import lax
from jax.experimental import pallas as pl
from jax.experimental.pallas import tpu as pltpu
from jax.sharding import PartitionSpec as P

NRHS = 4
STEPS = 4
COLS = NRHS * (STEPS + 1)
SHIFTS = (3.0, 11.0, 7.0, 1.5)
SCALE = 1.0 / 6.0
FIELDS = NRHS + 4
AXES = ("gx", "gy", "gz")
HIGHEST = lax.Precision.HIGHEST

DEPTH = 4
NZ, NX, NY = 8, 32, 256
EZ = NZ + 2 * DEPTH
ROWS = NX + 8
EROWS = ROWS + 16
LT = 3
FACE = NRHS * 4 + 3 * 4 + 1
F32 = jnp.float32
LIMIT = 63


def params(mb):
    return pltpu.CompilerParams(vmem_limit_bytes=mb << 20)


def vmem():
    return pl.BlockSpec(memory_space=pltpu.VMEM)


def smem():
    return pl.BlockSpec(memory_space=pltpu.SMEM)


def hbm():
    return pl.BlockSpec(memory_space=pl.ANY)


def row_ids(shape):
    return lax.broadcasted_iota(jnp.int32, shape, 0)


def lane_ids(shape):
    return lax.broadcasted_iota(jnp.int32, shape, 1)


def field_of(rhs, cz, cx, cy, dg, f, z):
    return rhs.at[f, z] if f < NRHS else (cz, cx, cy, dg)[f - NRHS].at[z]


def pack_faces(swap, place, rhs, cz, cx, cy, dg, zlo, zhi, *rest):
    xmsgs, (first_rows, last_rows, sems) = rest[:-3], rest[-3:]
    edges = []
    planes = []
    n = at = 0
    for f in range(FIELDS):
        src = rhs.at[f] if f < NRHS else (cz, cx, cy, dg)[f - NRHS]
        depth = DEPTH if f <= NRHS else DEPTH - 1
        for side, rows, out in ((0, first_rows, zlo), (1, last_rows, zhi)):
            edges.append(pltpu.make_async_copy(src.at[:, pl.ds(side * (NX - 8), 8), :], rows.at[f], sems.at[n]))
            start = side * (NZ - depth)
            planes.append(
                pltpu.make_async_copy(src.at[pl.ds(start, depth)], out.at[pl.ds(at, depth)], sems.at[n + 1])
            )
            n += 2
        at += depth
    for copy in edges:
        copy.start()
    for copy in planes:
        copy.start()
    for copy in edges:
        copy.wait()
    low = row_ids((8, NY)) < 4
    up = place[0] == 0
    for f in range(FIELDS):
        for m in range(NZ // 2):
            first = jnp.where(low, first_rows[f, 2 * m], pltpu.roll(first_rows[f, 2 * m + 1], 4, 0))
            last = jnp.where(low, pltpu.roll(last_rows[f, 2 * m], 4, 0), last_rows[f, 2 * m + 1])
            if swap:
                xmsgs[0][f, m] = jnp.where(up, last, first)
            else:
                xmsgs[0][f, m] = first
                xmsgs[1][f, m] = last
    for copy in planes:
        copy.wait()


def halo_tile(above, below, odd, keep_up, keep_dn):
    low = row_ids(above.shape) < 4
    if odd:
        up, dn = pltpu.roll(above, 4, 0), below
    else:
        up, dn = above, pltpu.roll(below, 4, 0)
    return jnp.where(low, up * keep_up, dn * keep_dn)


def keep_sides(swap, place):
    if not swap:
        return 1.0, 1.0
    first = place[0] == 0
    return jnp.where(first, 1.0, 0.0), jnp.where(first, 0.0, 1.0)


def pack_lanes(tile_of, side):
    lane = lane_ids((8, 128))
    source = 124 * side
    acc = jnp.zeros((8, 128), F32)
    for zz in range(4):
        for f in range(FIELDS):
            tile = tile_of(f, zz)
            spot = (zz * FIELDS + f) * 4
            shift = (spot - source) % 128
            if shift:
                tile = pltpu.roll(tile, shift, 1)
            acc = jnp.where((lane >= spot) & (lane < spot + 4), tile, acc)
    return acc


def pack_own_rims(rhs, cz, cx, cy, dg, ylo, yhi):
    for t in range(NX // 8):
        for side, out in ((0, ylo), (1, yhi)):
            for half in range(2):
                out[8 * t : 8 * t + 8, 128 * half : 128 * half + 128] = pack_lanes(
                    lambda f, zz: field_of(rhs, cz, cx, cy, dg, f, 4 * half + zz)[
                        8 * t : 8 * t + 8, 128 * side : 128 * side + 128
                    ],
                    side,
                )


def pack_rims(swap, place, ylo_own, yhi_own, *refs):
    above, below, ylo, yhi = refs if not swap else (refs[0],) + refs
    keep_up, keep_dn = keep_sides(swap, place)
    for side, own, out in ((0, ylo_own, ylo), (1, yhi_own, yhi)):
        out[0:NX, :] = own[...]
        lanes = slice(128 * side, 128 * side + 128)
        for half in range(2):
            out[NX:ROWS, 128 * half : 128 * half + 128] = pack_lanes(
                lambda f, zz: halo_tile(
                    above[f, 2 * half + zz // 2, :, lanes], below[f, 2 * half + zz // 2, :, lanes], zz % 2, keep_up, keep_dn
                ),
                side,
            )


def gather_rows(values):
    rows = row_ids((8, 128))
    width = 1
    while len(values) > 1:
        low = (rows & width) == 0
        merged = []
        for a, b in zip(values[0::2], values[1::2]):
            if a is None and b is None:
                merged.append(None)
                continue
            a = jnp.zeros((8, 128), F32) if a is None else a
            b = jnp.zeros((8, 128), F32) if b is None else b
            merged.append(jnp.where(low, a, b) + pltpu.roll(jnp.where(low, b, a), width, 0))
        values = merged
        width *= 2
    return values[0]


def gram_message(read, count, out, unroll=8):
    lanes = lane_ids((8, 128))
    result = jnp.zeros((8, 128), F32)
    for tile in range(0, COLS, 8):
        mine = range(tile, min(tile + 8, COLS))
        columns = [mine] + [range(c, c + 4) for c in range(tile + 8, COLS, 4)]
        for group in columns:
            pairs = [(i, j) for j in group for i in mine if i <= j]

            def step(n, sums):
                rows = {i: read(i, n) for i in sorted({i for pair in pairs for i in pair})}
                return tuple(s + rows[i] * rows[j] for s, (i, j) in zip(sums, pairs))

            sums = lax.fori_loop(
                0, count, step, tuple(jnp.zeros((8, 128), F32) for _ in pairs), unroll=unroll
            )
            sums = dict(zip(pairs, sums))
            for j in group:
                total = gather_rows([sums.get((tile + s, j)) for s in range(8)])
                total = jnp.sum(total, axis=1, keepdims=True)
                result = jnp.where(lanes == 4 * tile + j, jnp.broadcast_to(total, (8, 128)), result)
    for n in range(out.shape[0]):
        out[n] = result


def krylov(
    swap, place, rhs, cz, cx, cy, dg, above, below, yup, ydn, facelo, facehi, rimlo, rimhi,
    basis, message,
    store, faces, ysrc, sems,
):
    lane = lane_ids((8, 128))
    keep_up, keep_dn = keep_sides(swap, place)
    n_x = 1 if swap else 2

    def put(f, z, l, t, value):
        store[f, z, l, 8 + 8 * t : 16 + 8 * t, :] = value
        if t == 0:
            store[f, z, l, 8 + ROWS : 16 + ROWS, :] = value
        if t == ROWS // 8 - 1:
            store[f, z, l, 0:8, :] = value

    x_rows = FIELDS * 2 * 8
    for f in range(FIELDS):
        depth = DEPTH if f <= NRHS else DEPTH - 1
        start = f * DEPTH if f <= NRHS else NRHS * DEPTH + DEPTH + (f - NRHS - 1) * (DEPTH - 1)
        for z in range(EZ):
            own = DEPTH <= z < DEPTH + NZ
            if own:
                plane = field_of(rhs, cz, cx, cy, dg, f, z - DEPTH)
            elif z < DEPTH:
                d = z - (DEPTH - depth)
                plane = facelo.at[start + d] if d >= 0 else None
            else:
                d = z - DEPTH - NZ
                plane = facehi.at[start + d] if d < depth else None
            for l in range(2):
                lanes = pl.ds(128 * l, 128)
                for t in range(NX // 8):
                    if plane is None:
                        put(f, z, l, t, jnp.zeros((8, 128), F32))
                    else:
                        put(f, z, l, t, plane[8 * t : 8 * t + 8, lanes])
                if own:
                    m = (z - DEPTH) // 2
                    a, b = above[f, m, :, lanes], below[f, m, :, lanes]
                else:
                    rim, m = (rimlo, z // 2) if z < DEPTH else (rimhi, (z - DEPTH - NZ) // 2)
                    at = (f * 2 + m) * 8
                    a = rim[at : at + 8, lanes]
                    at += x_rows * (n_x - 1)
                    b = rim[at : at + 8, lanes]
                put(f, z, l, NX // 8, halo_tile(a, b, z % 2, keep_up, keep_dn))

    at = x_rows * n_x
    ysrc[0, 0] = rimlo[at : at + ROWS, 0:128]
    ysrc[1, 0] = rimlo[at : at + ROWS, 128:256]
    ysrc[0, 1] = yup[:, 0:128]
    ysrc[0, 2] = yup[:, 128:256]
    ysrc[1, 1] = ydn[:, 0:128]
    ysrc[1, 2] = ydn[:, 128:256]
    ysrc[0, 3] = rimhi[at : at + ROWS, 0:128]
    ysrc[1, 3] = rimhi[at : at + ROWS, 128:256]

    def place_y(q, carry):
        for t in range(ROWS // 8):
            up = ysrc[0, q, 8 * t : 8 * t + 8, :]
            dn = ysrc[1, q, 8 * t : 8 * t + 8, :]
            for zz in range(4):
                for f in range(FIELDS):
                    spot = (zz * FIELDS + f) * 4
                    u = pltpu.roll(up, (-spot) % 128, 1) if spot else up
                    d = pltpu.roll(dn, (124 - spot) % 128, 1) if spot != 124 else dn
                    put(f, 4 * q + zz, 2, t, jnp.where(lane < 4, u, jnp.where(lane >= 124, d, 0.0)))
        return carry

    lax.fori_loop(0, EZ // 4, place_y, 0)

    def tiles(f, z, t, off):
        return [store[f, z, l, pl.ds(8 + 8 * t + off, 8), :] for l in range(LT)]

    def lane_up(tri):
        rolled = [pltpu.roll(v, 127, 1) for v in tri]
        return [jnp.where(lane == 127, rolled[(l + 1) % LT], rolled[l]) for l in range(LT)]

    def lane_dn(tri):
        rolled = [pltpu.roll(v, 1, 1) for v in tri]
        return [jnp.where(lane == 0, rolled[(l - 1) % LT], rolled[l]) for l in range(LT)]

    def coefficients(z, carry):
        for t in range(ROWS // 8):
            kz, kx, ky, kd = (NRHS + i for i in range(4))
            center_z, center_x, center_y = (tiles(k, z, t, 0) for k in (kz, kx, ky))
            diag = tiles(kd, z, t, 0)
            sides = [
                (center_z, tiles(kz, z + 1, t, 0)),
                (center_z, tiles(kz, z - 1, t, 0)),
                (center_x, tiles(kx, z, t, 1)),
                (center_x, tiles(kx, z, t, -1)),
                (center_y, lane_up(center_y)),
                (center_y, lane_dn(center_y)),
            ]
            for l in range(LT):
                inside = diag[l] > 0.0
                total = diag[l] * SCALE
                for k, (mid, side) in enumerate(sides):
                    face = (mid[l] + side[l]) * (0.5 * SCALE)
                    total = total + face
                    faces[k, z, l, 8 * t : 8 * t + 8, :] = jnp.where(inside, face, 0.0)
                faces[6, z, l, 8 * t : 8 * t + 8, :] = jnp.where(inside, total, 0.0)
        return carry

    lax.fori_loop(1, EZ - 1, coefficients, 0)

    def slot(k):
        return k * NRHS + (NRHS if k else 0)

    copies = []

    def send_block(k):
        copy = pltpu.make_async_copy(
            store.at[pl.ds(slot(k), NRHS), pl.ds(DEPTH, NZ), pl.ds(0, 2), pl.ds(8, NX), :],
            basis.at[pl.ds(k * NRHS, NRHS)],
            sems.at[k],
        )
        copy.start()
        copies.append(copy)

    send_block(0)
    for k in range(STEPS):

        def apply(z, carry):
            for t in range(ROWS // 8):
                face = [[faces[c, z, l, 8 * t : 8 * t + 8, :] for l in range(LT)] for c in range(7)]
                diag = [face[6][l] - SHIFTS[k] * SCALE for l in range(LT)]
                for r in range(NRHS):
                    f = slot(k) + r
                    mid = tiles(f, z, t, 0)
                    sides = [
                        tiles(f, z + 1, t, 0),
                        tiles(f, z - 1, t, 0),
                        tiles(f, z, t, 1),
                        tiles(f, z, t, -1),
                        lane_up(mid),
                        lane_dn(mid),
                    ]
                    for l in range(LT):
                        value = diag[l] * mid[l]
                        for c in range(6):
                            value = value - face[c][l] * sides[c][l]
                        put(slot(k + 1) + r, z, l, t, value)
            return carry

        lax.fori_loop(k + 1, EZ - 1 - k, apply, 0)
        send_block(k + 1)

    def read(i, n):
        f = slot(i // NRHS) + i % NRHS
        return store[f, DEPTH + n // 8, (n // 4) % 2, pl.ds(pl.multiple_of(8 + 8 * (n % 4), 8), 8), :]

    gram_message(read, NZ * 8, message)
    for copy in copies:
        copy.wait()


def factor_gram(messages, cells):
    rows = row_ids((24, 128))
    lanes = lane_ids((24, 128))
    message = messages[0]
    for n in range(1, messages.shape[0]):
        message = message + messages[n]
    upper = jnp.concatenate([message] + [pltpu.roll(message, 128 - 32 * k, 1) for k in (1, 2)], 0)
    upper = jnp.where((lanes < COLS) & (rows < COLS), upper, 0.0)
    square = jnp.concatenate([upper, jnp.zeros((104, 128), F32)], 0)
    a = jnp.where(rows <= lanes, upper, square.T[0:24, :]) / cells
    a = jnp.where((lanes == rows + 32) & (rows < COLS), 1.0, a)
    for j in range(COLS - 1):
        column = jnp.broadcast_to(a[:, j : j + 1], (24, 128))
        row = jnp.broadcast_to(a[j : j + 1, :], (24, 128))
        pivot = jnp.broadcast_to(column[j : j + 1, :], (24, 128))
        a = a - jnp.where(rows > j, column / pivot, 0.0) * row
    diag = jnp.sum(jnp.where(lanes == rows, a, 0.0), axis=1, keepdims=True)
    diag = jnp.where(rows < COLS, jnp.broadcast_to(diag, (24, 128)), 1.0)
    a = a / jnp.sqrt(diag)
    return jnp.where((lanes >= rows) & (lanes < COLS) | (lanes >= 32) & (lanes <= rows + 32), a, 0.0)


def spread(factor, table):
    for j in range(COLS):
        table[j] = jnp.broadcast_to(factor[:, 32 + j : 33 + j], (24, 128))


def apply_rows(table, read, write):
    group = 5
    pieces = NX // 8
    for g in reversed(range(COLS // group)):
        mine = range(group * g, group * g + group)
        sums = {i: None for i in mine}
        for j in range(group * g + group):
            value = [read(j, p) for p in range(pieces)]
            for i in mine:
                if j <= i:
                    weight = jnp.broadcast_to(table[j, i : i + 1, :], (8, 128))
                    terms = [weight * v for v in value]
                    sums[i] = terms if sums[i] is None else [s + t for s, t in zip(sums[i], terms)]
        for i in mine:
            for p in range(pieces):
                write(i, p, sums[i][p])


def plane_copy(src, dst, sems, z):
    return pltpu.make_async_copy(src.at[:, z], dst.at[:, z], sems.at[z])


def first_pass(cells, message, basis_hbm, first_hbm, next_message, factor_out, basis, table, loads, saves):
    for z in range(NZ):
        plane_copy(basis_hbm, basis, loads, z).start()
    factor = factor_gram(message, cells)
    factor_out[...] = factor
    spread(factor, table)

    def chunk(z, carry):
        plane_copy(basis_hbm, basis, loads, z).wait()
        for l in range(2):

            def read(j, p):
                return basis[j, z, l, 8 * p : 8 * p + 8, :]

            def write(i, p, value):
                basis[i, z, l, 8 * p : 8 * p + 8, :] = value

            apply_rows(table, read, write)
        plane_copy(basis, first_hbm, saves, z).start()
        return carry

    lax.fori_loop(0, NZ, chunk, 0)

    def read(i, n):
        return basis[i, n // 8, (n // 4) % 2, pl.ds(pl.multiple_of(8 * (n % 4), 8), 8), :]

    gram_message(read, NZ * 8, next_message)
    for z in range(NZ):
        plane_copy(basis, first_hbm, saves, z).wait()


def second_pass(cells, message, factor_one, first_hbm, out_hbm, triangle, first, out, table, loads, saves):
    for z in range(NZ):
        plane_copy(first_hbm, first, loads, z).start()
    factor = factor_gram(message, cells)
    spread(factor, table)
    lanes = lane_ids((24, 128))
    left = jnp.where(lanes < COLS, factor, 0.0)[:, 0:24]
    product = lax.dot_general(
        left, factor_one[...], (((1,), (0,)), ((), ())), precision=HIGHEST, preferred_element_type=F32
    )
    triangle[...] = product[0:COLS, 0:COLS]

    def chunk(z, carry):
        plane_copy(first_hbm, first, loads, z).wait()
        for l in range(2):

            def read(j, p):
                return first[j, z, l, 8 * p : 8 * p + 8, :]

            def write(i, p, value):
                out[i, z, 8 * p : 8 * p + 8, 128 * l : 128 * l + 128] = value

            apply_rows(table, read, write)
        plane_copy(out, out_hbm, saves, z).start()
        return carry

    lax.fori_loop(0, NZ, chunk, 0)
    for z in range(NZ):
        plane_copy(out, out_hbm, saves, z).wait()


def shape(*dims):
    return jax.ShapeDtypeStruct(dims, F32)


def move(value, axis, delta):
    count = lax.axis_size(axis)
    pairs = [(i, i + delta) for i in range(count) if 0 <= i + delta < count]
    return lax.ppermute(value, axis, pairs)


def exchange(messages):
    return lax.all_to_all(messages, AXES, 0, 0, tiled=True)


def body(rhs, coef_x, coef_y, coef_z, diag_term):
    n_x = lax.axis_size("gx")
    devices = n_x * lax.axis_size("gy") * lax.axis_size("gz")
    cells = float(NZ * NX * NY * devices)
    at_x = lax.axis_index("gx")
    swap = n_x == 2
    fields = (rhs, coef_z, coef_x, coef_y, diag_term)

    place = at_x.astype(jnp.int32).reshape(1)
    x_shape = shape(FIELDS, NZ // 2, 8, NY)
    face_shape = shape(FACE, NX, NY)
    zlo, zhi, *xmsgs = pl.pallas_call(
        functools.partial(pack_faces, swap),
        out_shape=(face_shape, face_shape) + (x_shape,) * (1 if swap else 2),
        in_specs=[smem()] + [hbm()] * 5,
        out_specs=(hbm(), hbm()) + (vmem(),) * (1 if swap else 2),
        scratch_shapes=[
            pltpu.VMEM((FIELDS, NZ, 8, NY), F32),
            pltpu.VMEM((FIELDS, NZ, 8, NY), F32),
            pltpu.SemaphoreType.DMA((4 * FIELDS,)),
        ],
        compiler_params=params(LIMIT),
    )(place, *fields)
    facehi = move(zlo, "gz", -1)
    facelo = move(zhi, "gz", 1)
    if swap:
        x_parts = (lax.ppermute(xmsgs[0], "gx", [(0, 1), (1, 0)]),)
    else:
        x_parts = (move(xmsgs[0], "gx", -1), move(xmsgs[1], "gx", 1))

    own_shape = shape(NX, NY)
    own_rims = pl.pallas_call(
        pack_own_rims,
        out_shape=(own_shape, own_shape),
        in_specs=[vmem()] * 5,
        compiler_params=params(LIMIT),
    )(*fields)
    rim_shape = shape(ROWS, NY)
    ylo, yhi = pl.pallas_call(
        functools.partial(pack_rims, swap),
        out_shape=(rim_shape, rim_shape),
        in_specs=[smem()] + [vmem()] * (2 + len(x_parts)),
        compiler_params=params(LIMIT),
    )(place, *own_rims, *x_parts)
    yup, ydn = move(ylo, "gy", -1), move(yhi, "gy", 1)

    def rim(half):
        rows = [p[:, 2 * half : 2 * half + 2].reshape(-1, NY) for p in x_parts]
        lanes = slice(128 * half, 128 * half + 128)
        return jnp.concatenate(rows + [jnp.concatenate([yup[:, lanes], ydn[:, lanes]], 1)], 0)

    rimhi, rimlo = move(rim(0), "gz", -1), move(rim(1), "gz", 1)

    block = shape(COLS, NZ, 2, NX, 128)

    def krylov_entry(place, rhs, cz, cx, cy, dg, *rest):
        if swap:
            rest = (rest[0],) + rest
        krylov(swap, place, rhs, cz, cx, cy, dg, *rest)

    basis, message = pl.pallas_call(
        krylov_entry,
        out_shape=(block, shape(devices, 8, 128)),
        in_specs=[smem()] + [vmem()] * (5 + len(x_parts) + 6),
        out_specs=(hbm(), vmem()),
        scratch_shapes=[
            pltpu.VMEM((COLS + NRHS, EZ, LT, EROWS, 128), F32),
            pltpu.VMEM((7, EZ, LT, ROWS, 128), F32),
            pltpu.VMEM((2, 4, ROWS, 128), F32),
            pltpu.SemaphoreType.DMA((STEPS + 1,)),
        ],
        compiler_params=params(LIMIT),
    )(place, *fields, *x_parts, yup, ydn, facelo, facehi, rimlo, rimhi)

    message = exchange(message)
    first, message, factor_one = pl.pallas_call(
        functools.partial(first_pass, cells),
        out_shape=(block, shape(devices, 8, 128), shape(24, 128)),
        in_specs=[vmem(), hbm()],
        out_specs=(hbm(), vmem(), vmem()),
        scratch_shapes=[
            pltpu.VMEM(block.shape, F32),
            pltpu.VMEM((COLS, 24, 128), F32),
            pltpu.SemaphoreType.DMA((NZ,)),
            pltpu.SemaphoreType.DMA((NZ,)),
        ],
        compiler_params=params(LIMIT),
    )(message, basis)

    message = exchange(message)
    return pl.pallas_call(
        functools.partial(second_pass, cells),
        out_shape=(shape(COLS, NZ, NX, NY), shape(COLS, COLS)),
        in_specs=[vmem(), vmem(), hbm()],
        out_specs=(hbm(), vmem()),
        scratch_shapes=[
            pltpu.VMEM(block.shape, F32),
            pltpu.VMEM((COLS, NZ, NX, NY), F32),
            pltpu.VMEM((COLS, 24, 128), F32),
            pltpu.SemaphoreType.DMA((NZ,)),
            pltpu.SemaphoreType.DMA((NZ,)),
        ],
        compiler_params=params(LIMIT),
    )(message, factor_one, first)


def solution(mesh):
    return jax.shard_map(
        body,
        mesh=mesh,
        in_specs=(
            P(None, "gz", "gx", "gy"),
            P("gz", "gx", "gy"),
            P("gz", "gx", "gy"),
            P("gz", "gx", "gy"),
            P("gz", "gx", "gy"),
        ),
        out_specs=(P(None, "gz", "gx", "gy"), P()),
        check_vma=False,
    )
```

```python
import functools

import jax
import jax.numpy as jnp
from jax import lax
from jax.experimental import pallas as pl
from jax.experimental.pallas import tpu as pltpu
from jax.sharding import PartitionSpec as P

NRHS = 4
STEPS = 4
COLS = NRHS * (STEPS + 1)
SHIFTS = (3.0, 11.0, 7.0, 1.5)
SCALE = 1.0 / 6.0
FIELDS = NRHS + 4
AXES = ("gx", "gy", "gz")
HIGHEST = lax.Precision.HIGHEST

DEPTH = 4
NZ, NX, NY = 8, 32, 256
EZ = NZ + 2 * DEPTH
ROWS = NX + 8
EROWS = ROWS + 16
LT = 3
FACE = NRHS * 4 + 3 * 4 + 1
F32 = jnp.float32
LIMIT = 63


def params(mb):
    return pltpu.CompilerParams(vmem_limit_bytes=mb << 20)


def vmem():
    return pl.BlockSpec(memory_space=pltpu.VMEM)


def smem():
    return pl.BlockSpec(memory_space=pltpu.SMEM)


def hbm():
    return pl.BlockSpec(memory_space=pl.ANY)


def row_ids(shape):
    return lax.broadcasted_iota(jnp.int32, shape, 0)


def lane_ids(shape):
    return lax.broadcasted_iota(jnp.int32, shape, 1)


def field_of(rhs, cz, cx, cy, dg, f, z):
    return rhs.at[f, z] if f < NRHS else (cz, cx, cy, dg)[f - NRHS].at[z]


def pack_faces(swap, place, rhs, cz, cx, cy, dg, zlo, zhi, *rest):
    xmsgs, (whole, loads, saves) = rest[:-3], rest[-3:]
    copies = []
    for f in range(FIELDS):
        src = rhs.at[f] if f < NRHS else (cz, cx, cy, dg)[f - NRHS]
        copies.append(pltpu.make_async_copy(src, whole.at[f], loads.at[f]))
        copies[-1].start()
    low = row_ids((8, NY)) < 4
    up = place[0] == 0
    planes = []
    at = 0
    for f in range(FIELDS):
        copies[f].wait()
        depth = DEPTH if f <= NRHS else DEPTH - 1
        for side, out in ((0, zlo), (1, zhi)):
            start = side * (NZ - depth)
            planes.append(
                pltpu.make_async_copy(
                    whole.at[f, pl.ds(start, depth)], out.at[pl.ds(at, depth)], saves.at[2 * f + side]
                )
            )
            planes[-1].start()
        at += depth
    for f in range(FIELDS):
        for m in range(NZ // 2):
            a, b = whole.at[f, 2 * m], whole.at[f, 2 * m + 1]
            first = jnp.where(low, a[0:8], pltpu.roll(b[0:8], 4, 0))
            last = jnp.where(low, pltpu.roll(a[NX - 8 : NX], 4, 0), b[NX - 8 : NX])
            if swap:
                xmsgs[0][f, m] = jnp.where(up, last, first)
            else:
                xmsgs[0][f, m] = first
                xmsgs[1][f, m] = last
    for copy in planes:
        copy.wait()


def halo_tile(above, below, odd, keep_up, keep_dn):
    low = row_ids(above.shape) < 4
    if odd:
        up, dn = pltpu.roll(above, 4, 0), below
    else:
        up, dn = above, pltpu.roll(below, 4, 0)
    return jnp.where(low, up * keep_up, dn * keep_dn)


def keep_sides(swap, place):
    if not swap:
        return 1.0, 1.0
    first = place[0] == 0
    return jnp.where(first, 1.0, 0.0), jnp.where(first, 0.0, 1.0)


def pack_lanes(tile_of, side):
    lane = lane_ids((8, 128))
    source = 124 * side
    acc = jnp.zeros((8, 128), F32)
    for zz in range(4):
        for f in range(FIELDS):
            tile = tile_of(f, zz)
            spot = (zz * FIELDS + f) * 4
            shift = (spot - source) % 128
            if shift:
                tile = pltpu.roll(tile, shift, 1)
            acc = jnp.where((lane >= spot) & (lane < spot + 4), tile, acc)
    return acc


def pack_own_rims(rhs, cz, cx, cy, dg, ylo, yhi):
    for t in range(NX // 8):
        for side, out in ((0, ylo), (1, yhi)):
            for half in range(2):
                out[8 * t : 8 * t + 8, 128 * half : 128 * half + 128] = pack_lanes(
                    lambda f, zz: field_of(rhs, cz, cx, cy, dg, f, 4 * half + zz)[
                        8 * t : 8 * t + 8, 128 * side : 128 * side + 128
                    ],
                    side,
                )


def pack_rims(swap, place, ylo_own, yhi_own, *refs):
    above, below, ylo, yhi = refs if not swap else (refs[0],) + refs
    keep_up, keep_dn = keep_sides(swap, place)
    for side, own, out in ((0, ylo_own, ylo), (1, yhi_own, yhi)):
        out[0:NX, :] = own[...]
        lanes = slice(128 * side, 128 * side + 128)
        for half in range(2):
            out[NX:ROWS, 128 * half : 128 * half + 128] = pack_lanes(
                lambda f, zz: halo_tile(
                    above[f, 2 * half + zz // 2, :, lanes], below[f, 2 * half + zz // 2, :, lanes], zz % 2, keep_up, keep_dn
                ),
                side,
            )


STACK = 8 * COLS


def gram_zero(accs):
    accs[...] = jnp.zeros_like(accs)


def gram_add(stacks, accs):
    left, right = [], []
    cross_left, cross_right = [], []
    for stack in stacks:
        high = stack.astype(jnp.bfloat16)
        rest = stack - high.astype(F32)
        mid = rest.astype(jnp.bfloat16)
        low = (rest - mid.astype(F32)).astype(jnp.bfloat16)
        left += [high, mid]
        cross_left += [high, high]
        cross_right += [mid, low]
    contract = (((1,), (1,)), ((), ()))

    def product(a, b):
        return lax.dot_general(jnp.concatenate(a, 1), jnp.concatenate(b, 1), contract, preferred_element_type=F32)

    accs[0] += product(left, left)
    accs[1] += product(cross_left, cross_right)


def gram_message(accs, out):
    same = (row_ids((STACK, STACK)) & 7) == (lane_ids((STACK, STACK)) & 7)
    pick = jnp.where((row_ids((STACK, 128)) >> 3) == lane_ids((STACK, 128)), 1.0, 0.0)

    def traces(product):
        picked = jnp.where(same, product, 0.0)
        rows = [jnp.sum(picked[8 * i : 8 * i + 8], axis=0, keepdims=True) for i in range(COLS)]
        rows = jnp.concatenate(rows + [jnp.zeros((128 - COLS, STACK), F32)], 0)
        return lax.dot_general(
            rows, pick, (((1,), (0,)), ((), ())), precision=HIGHEST, preferred_element_type=F32
        )

    cross = traces(accs[1])
    gram = traces(accs[0]) + cross + cross.T
    tops = [gram[8 * k : 8 * k + 8] for k in range(3)]
    rows, lanes = row_ids((8, 128)), lane_ids((8, 128))
    tile = jnp.where(lanes < COLS, tops[0], pltpu.roll(tops[1], 12, 1))
    corner = pltpu.roll(pltpu.roll(tops[2], 128 - 16, 1), 4, 0)
    tile = jnp.where((rows >= 4) & (lanes < 4), corner, tile)
    packed = tile
    for q in range(1, 4):
        turned = pltpu.roll(pltpu.roll(tile, 32 * q, 1), 8 - 2 * q, 0)
        packed = jnp.where((lanes >> 5) == q, turned, packed)
    packed = packed[0:2]
    for n in range(out.shape[0]):
        out[n] = packed


def gram_of(messages):
    total = messages[0]
    for n in range(1, messages.shape[0]):
        total = total + messages[n]
    total = jnp.concatenate([total] * 4, 0)
    rows, lanes = row_ids((8, 128)), lane_ids((8, 128))
    tile = total
    for q in range(1, 4):
        tile = jnp.where((rows >> 1) == q, pltpu.roll(total, 128 - 32 * q, 1), tile)
    corner = pltpu.roll(pltpu.roll(tile, 4, 0), 16, 1)
    tops = [
        jnp.where((lanes < COLS) & (lanes >= rows), tile, 0.0),
        jnp.where((lanes < COLS) & (lanes >= rows + 8), pltpu.roll(tile, 128 - 12, 1), 0.0),
        jnp.where((lanes < COLS) & (lanes >= rows + 16), corner, 0.0),
    ]
    return jnp.concatenate(tops, 0)


def krylov(
    swap, place, rhs, cz, cx, cy, dg, above, below, yup, ydn, facelo, facehi, rimlo, rimhi,
    basis, message,
    store, faces, ysrc, accs, sems,
):
    lane = lane_ids((8, 128))
    keep_up, keep_dn = keep_sides(swap, place)
    n_x = 1 if swap else 2

    def put(f, z, l, t, value):
        store[f, z, l, 8 + 8 * t : 16 + 8 * t, :] = value
        if t == 0:
            store[f, z, l, 8 + ROWS : 16 + ROWS, :] = value
        if t == ROWS // 8 - 1:
            store[f, z, l, 0:8, :] = value

    x_rows = FIELDS * 2 * 8
    for f in range(FIELDS):
        depth = DEPTH if f <= NRHS else DEPTH - 1
        start = f * DEPTH if f <= NRHS else NRHS * DEPTH + DEPTH + (f - NRHS - 1) * (DEPTH - 1)
        for z in range(EZ):
            own = DEPTH <= z < DEPTH + NZ
            if own:
                plane = field_of(rhs, cz, cx, cy, dg, f, z - DEPTH)
            elif z < DEPTH:
                d = z - (DEPTH - depth)
                plane = facelo.at[start + d] if d >= 0 else None
            else:
                d = z - DEPTH - NZ
                plane = facehi.at[start + d] if d < depth else None
            for l in range(2):
                lanes = pl.ds(128 * l, 128)
                for t in range(NX // 8):
                    if plane is None:
                        put(f, z, l, t, jnp.zeros((8, 128), F32))
                    else:
                        put(f, z, l, t, plane[8 * t : 8 * t + 8, lanes])
                if own:
                    m = (z - DEPTH) // 2
                    a, b = above[f, m, :, lanes], below[f, m, :, lanes]
                else:
                    rim, m = (rimlo, z // 2) if z < DEPTH else (rimhi, (z - DEPTH - NZ) // 2)
                    at = (f * 2 + m) * 8
                    a = rim[at : at + 8, lanes]
                    at += x_rows * (n_x - 1)
                    b = rim[at : at + 8, lanes]
                put(f, z, l, NX // 8, halo_tile(a, b, z % 2, keep_up, keep_dn))

    at = x_rows * n_x
    ysrc[0, 0] = rimlo[at : at + ROWS, 0:128]
    ysrc[1, 0] = rimlo[at : at + ROWS, 128:256]
    ysrc[0, 1] = yup[:, 0:128]
    ysrc[0, 2] = yup[:, 128:256]
    ysrc[1, 1] = ydn[:, 0:128]
    ysrc[1, 2] = ydn[:, 128:256]
    ysrc[0, 3] = rimhi[at : at + ROWS, 0:128]
    ysrc[1, 3] = rimhi[at : at + ROWS, 128:256]

    def place_y(q, carry):
        for t in range(ROWS // 8):
            up = ysrc[0, q, 8 * t : 8 * t + 8, :]
            dn = ysrc[1, q, 8 * t : 8 * t + 8, :]
            for zz in range(4):
                for f in range(FIELDS):
                    spot = (zz * FIELDS + f) * 4
                    u = pltpu.roll(up, (-spot) % 128, 1) if spot else up
                    d = pltpu.roll(dn, (124 - spot) % 128, 1) if spot != 124 else dn
                    put(f, 4 * q + zz, 2, t, jnp.where(lane < 4, u, jnp.where(lane >= 124, d, 0.0)))
        return carry

    lax.fori_loop(0, EZ // 4, place_y, 0)

    def tiles(f, z, t, off):
        return [store[f, z, l, pl.ds(8 + 8 * t + off, 8), :] for l in range(LT)]

    def lane_up(tri):
        rolled = [pltpu.roll(v, 127, 1) for v in tri]
        return [jnp.where(lane == 127, rolled[(l + 1) % LT], rolled[l]) for l in range(LT)]

    def lane_dn(tri):
        rolled = [pltpu.roll(v, 1, 1) for v in tri]
        return [jnp.where(lane == 0, rolled[(l - 1) % LT], rolled[l]) for l in range(LT)]

    def coefficients(z, carry):
        for t in range(ROWS // 8):
            kz, kx, ky, kd = (NRHS + i for i in range(4))
            center_z, center_x, center_y = (tiles(k, z, t, 0) for k in (kz, kx, ky))
            diag = tiles(kd, z, t, 0)
            sides = [
                (center_z, tiles(kz, z + 1, t, 0)),
                (center_z, tiles(kz, z - 1, t, 0)),
                (center_x, tiles(kx, z, t, 1)),
                (center_x, tiles(kx, z, t, -1)),
                (center_y, lane_up(center_y)),
                (center_y, lane_dn(center_y)),
            ]
            for l in range(LT):
                inside = diag[l] > 0.0
                total = diag[l] * SCALE
                for k, (mid, side) in enumerate(sides):
                    face = (mid[l] + side[l]) * (0.5 * SCALE)
                    total = total + face
                    faces[k, z, l, 8 * t : 8 * t + 8, :] = jnp.where(inside, face, 0.0)
                faces[6, z, l, 8 * t : 8 * t + 8, :] = jnp.where(inside, total, 0.0)
        return carry

    lax.fori_loop(1, EZ - 1, coefficients, 0)

    def slot(k):
        return k * NRHS + (NRHS if k else 0)

    copies = []

    def send_block(k):
        copy = pltpu.make_async_copy(
            store.at[pl.ds(slot(k), NRHS), pl.ds(DEPTH, NZ), pl.ds(0, 2), pl.ds(8, NX), :],
            basis.at[pl.ds(k * NRHS, NRHS)],
            sems.at[k],
        )
        copy.start()
        copies.append(copy)

    send_block(0)
    for k in range(STEPS):

        def apply(z, carry):
            for t in range(ROWS // 8):
                face = [[faces[c, z, l, 8 * t : 8 * t + 8, :] for l in range(LT)] for c in range(7)]
                diag = [face[6][l] - SHIFTS[k] * SCALE for l in range(LT)]
                for r in range(NRHS):
                    f = slot(k) + r
                    mid = tiles(f, z, t, 0)
                    sides = [
                        tiles(f, z + 1, t, 0),
                        tiles(f, z - 1, t, 0),
                        tiles(f, z, t, 1),
                        tiles(f, z, t, -1),
                        lane_up(mid),
                        lane_dn(mid),
                    ]
                    for l in range(LT):
                        value = diag[l] * mid[l]
                        for c in range(6):
                            value = value - face[c][l] * sides[c][l]
                        put(slot(k + 1) + r, z, l, t, value)
            return carry

        lax.fori_loop(k + 1, EZ - 1 - k, apply, 0)
        send_block(k + 1)

    gram_zero(accs)

    def products(z, carry):
        def tile(i, t):
            f = slot(i // NRHS) + i % NRHS
            return jnp.concatenate([store[f, z, l, 8 + 8 * t : 16 + 8 * t, :] for l in range(2)], 1)

        gram_add([jnp.concatenate([tile(i, t) for i in range(COLS)], 0) for t in range(NX // 8)], accs)
        return carry

    lax.fori_loop(DEPTH, DEPTH + NZ, products, 0)
    gram_message(accs, message)
    for copy in copies:
        copy.wait()


def factor_gram(messages, cells, table):
    rows = row_ids((24, 128))
    lanes = lane_ids((24, 128))
    upper = gram_of(messages) / cells
    square = jnp.concatenate([upper, jnp.zeros((104, 128), F32)], 0).T
    whole = jnp.where(rows <= lanes, upper, square[0:24, :])

    def splat(value):
        return jnp.broadcast_to(value, (24, 128))

    columns = [splat(whole[:, c : c + 1]) for c in range(COLS)]
    inverse = [jnp.where(rows == c, 1.0, 0.0) for c in range(COLS)]
    pivots = jnp.ones((24, 128), F32)
    factor = jnp.zeros((24, 128), F32)
    for j in range(COLS):
        pivot = splat(columns[j][j : j + 1, :])
        pivots = jnp.where(rows == j, pivot, pivots)
        below = jnp.where(rows > j, columns[j] / pivot, 0.0)
        for c in range(j, COLS):
            row = splat(columns[c][j : j + 1, :])
            factor = jnp.where((rows == j) & (lanes == c), row, factor)
            if c > j:
                columns[c] = columns[c] - below * row
        for c in range(j + 1):
            inverse[c] = inverse[c] - below * splat(inverse[c][j : j + 1, :])
    roots = jnp.sqrt(pivots)
    for c in range(COLS):
        table[c] = inverse[c] / roots
    return factor / roots


def apply_rows(table, read, write):
    group = 5
    pieces = NX // 8
    for g in reversed(range(COLS // group)):
        mine = range(group * g, group * g + group)
        sums = {i: None for i in mine}
        for j in range(group * g + group):
            value = [read(j, p) for p in range(pieces)]
            for i in mine:
                if j <= i:
                    weight = jnp.broadcast_to(table[j, i : i + 1, :], (8, 128))
                    terms = [weight * v for v in value]
                    sums[i] = terms if sums[i] is None else [s + t for s, t in zip(sums[i], terms)]
        for i in mine:
            for p in range(pieces):
                write(i, p, sums[i][p])


def plane_copy(src, dst, sems, z):
    return pltpu.make_async_copy(src.at[:, z], dst.at[:, z], sems.at[z])


def first_pass(cells, message, basis_hbm, first_hbm, next_message, factor_out, basis, table, accs, loads, saves):
    for z in range(NZ):
        plane_copy(basis_hbm, basis, loads, z).start()
    factor_out[...] = factor_gram(message, cells, table)
    gram_zero(accs)

    def chunk(z, carry):
        plane_copy(basis_hbm, basis, loads, z).wait()
        for l in range(2):

            def read(j, p):
                return basis[j, z, l, 8 * p : 8 * p + 8, :]

            def write(i, p, value):
                basis[i, z, l, 8 * p : 8 * p + 8, :] = value

            apply_rows(table, read, write)
        plane_copy(basis, first_hbm, saves, z).start()

        def tile(i, t):
            return jnp.concatenate([basis[i, z, l, 8 * t : 8 * t + 8, :] for l in range(2)], 1)

        gram_add([jnp.concatenate([tile(i, t) for i in range(COLS)], 0) for t in range(NX // 8)], accs)
        return carry

    lax.fori_loop(0, NZ, chunk, 0)

    gram_message(accs, next_message)
    for z in range(NZ):
        plane_copy(basis, first_hbm, saves, z).wait()


def second_pass(cells, message, factor_one, first_hbm, out_hbm, triangle, first, out, table, loads, saves):
    for z in range(NZ):
        plane_copy(first_hbm, first, loads, z).start()
    left = factor_gram(message, cells, table)[:, 0:24]
    product = lax.dot_general(
        left, factor_one[...], (((1,), (0,)), ((), ())), precision=HIGHEST, preferred_element_type=F32
    )
    triangle[...] = product[0:COLS, 0:COLS]

    def chunk(z, carry):
        plane_copy(first_hbm, first, loads, z).wait()
        for l in range(2):

            def read(j, p):
                return first[j, z, l, 8 * p : 8 * p + 8, :]

            def write(i, p, value):
                out[i, z, 8 * p : 8 * p + 8, 128 * l : 128 * l + 128] = value

            apply_rows(table, read, write)
        plane_copy(out, out_hbm, saves, z).start()
        return carry

    lax.fori_loop(0, NZ, chunk, 0)
    for z in range(NZ):
        plane_copy(out, out_hbm, saves, z).wait()


def shape(*dims):
    return jax.ShapeDtypeStruct(dims, F32)


def move(value, axis, delta):
    count = lax.axis_size(axis)
    pairs = [(i, i + delta) for i in range(count) if 0 <= i + delta < count]
    return lax.ppermute(value, axis, pairs)


def exchange(messages):
    return lax.all_to_all(messages, AXES, 0, 0, tiled=True)


def body(rhs, coef_x, coef_y, coef_z, diag_term):
    n_x = lax.axis_size("gx")
    devices = n_x * lax.axis_size("gy") * lax.axis_size("gz")
    cells = float(NZ * NX * NY * devices)
    at_x = lax.axis_index("gx")
    swap = n_x == 2
    fields = (rhs, coef_z, coef_x, coef_y, diag_term)

    place = at_x.astype(jnp.int32).reshape(1)
    x_shape = shape(FIELDS, NZ // 2, 8, NY)
    face_shape = shape(FACE, NX, NY)
    zlo, zhi, *xmsgs = pl.pallas_call(
        functools.partial(pack_faces, swap),
        out_shape=(face_shape, face_shape) + (x_shape,) * (1 if swap else 2),
        in_specs=[smem()] + [hbm()] * 5,
        out_specs=(hbm(), hbm()) + (vmem(),) * (1 if swap else 2),
        scratch_shapes=[
            pltpu.VMEM((FIELDS, NZ, NX, NY), F32),
            pltpu.SemaphoreType.DMA((FIELDS,)),
            pltpu.SemaphoreType.DMA((2 * FIELDS,)),
        ],
        compiler_params=params(LIMIT),
    )(place, *fields)
    facehi = move(zlo, "gz", -1)
    facelo = move(zhi, "gz", 1)
    if swap:
        x_parts = (lax.ppermute(xmsgs[0], "gx", [(0, 1), (1, 0)]),)
    else:
        x_parts = (move(xmsgs[0], "gx", -1), move(xmsgs[1], "gx", 1))

    own_shape = shape(NX, NY)
    own_rims = pl.pallas_call(
        pack_own_rims,
        out_shape=(own_shape, own_shape),
        in_specs=[vmem()] * 5,
        compiler_params=params(LIMIT),
    )(*fields)
    rim_shape = shape(ROWS, NY)
    ylo, yhi = pl.pallas_call(
        functools.partial(pack_rims, swap),
        out_shape=(rim_shape, rim_shape),
        in_specs=[smem()] + [vmem()] * (2 + len(x_parts)),
        compiler_params=params(LIMIT),
    )(place, *own_rims, *x_parts)
    yup, ydn = move(ylo, "gy", -1), move(yhi, "gy", 1)

    def rim(half):
        rows = [p[:, 2 * half : 2 * half + 2].reshape(-1, NY) for p in x_parts]
        lanes = slice(128 * half, 128 * half + 128)
        return jnp.concatenate(rows + [jnp.concatenate([yup[:, lanes], ydn[:, lanes]], 1)], 0)

    rimhi, rimlo = move(rim(0), "gz", -1), move(rim(1), "gz", 1)

    block = shape(COLS, NZ, 2, NX, 128)

    def krylov_entry(place, rhs, cz, cx, cy, dg, *rest):
        if swap:
            rest = (rest[0],) + rest
        krylov(swap, place, rhs, cz, cx, cy, dg, *rest)

    basis, message = pl.pallas_call(
        krylov_entry,
        out_shape=(block, shape(devices, 2, 128)),
        in_specs=[smem()] + [vmem()] * (5 + len(x_parts) + 6),
        out_specs=(hbm(), vmem()),
        scratch_shapes=[
            pltpu.VMEM((COLS + NRHS, EZ, LT, EROWS, 128), F32),
            pltpu.VMEM((7, EZ, LT, ROWS, 128), F32),
            pltpu.VMEM((2, 4, ROWS, 128), F32),
            pltpu.VMEM((2, STACK, STACK), F32),
            pltpu.SemaphoreType.DMA((STEPS + 1,)),
        ],
        compiler_params=params(LIMIT),
    )(place, *fields, *x_parts, yup, ydn, facelo, facehi, rimlo, rimhi)

    message = exchange(message)
    first, message, factor_one = pl.pallas_call(
        functools.partial(first_pass, cells),
        out_shape=(block, shape(devices, 2, 128), shape(24, 128)),
        in_specs=[vmem(), hbm()],
        out_specs=(hbm(), vmem(), vmem()),
        scratch_shapes=[
            pltpu.VMEM(block.shape, F32),
            pltpu.VMEM((COLS, 24, 128), F32),
            pltpu.VMEM((2, STACK, STACK), F32),
            pltpu.SemaphoreType.DMA((NZ,)),
            pltpu.SemaphoreType.DMA((NZ,)),
        ],
        compiler_params=params(LIMIT),
    )(message, basis)

    message = exchange(message)
    return pl.pallas_call(
        functools.partial(second_pass, cells),
        out_shape=(shape(COLS, NZ, NX, NY), shape(COLS, COLS)),
        in_specs=[vmem(), vmem(), hbm()],
        out_specs=(hbm(), vmem()),
        scratch_shapes=[
            pltpu.VMEM(block.shape, F32),
            pltpu.VMEM((COLS, NZ, NX, NY), F32),
            pltpu.VMEM((COLS, 24, 128), F32),
            pltpu.SemaphoreType.DMA((NZ,)),
            pltpu.SemaphoreType.DMA((NZ,)),
        ],
        compiler_params=params(LIMIT),
    )(message, factor_one, first)


def solution(mesh):
    return jax.shard_map(
        body,
        mesh=mesh,
        in_specs=(
            P(None, "gz", "gx", "gy"),
            P("gz", "gx", "gy"),
            P("gz", "gx", "gy"),
            P("gz", "gx", "gy"),
            P("gz", "gx", "gy"),
        ),
        out_specs=(P(None, "gz", "gx", "gy"), P()),
        check_vma=False,
    )
```

```python
import functools

import jax
import jax.numpy as jnp
from jax import lax
from jax.experimental import pallas as pl
from jax.experimental.pallas import tpu as pltpu
from jax.sharding import PartitionSpec as P

NRHS = 4
STEPS = 4
COLS = NRHS * (STEPS + 1)
SHIFTS = (3.0, 11.0, 7.0, 1.5)
SCALE = 1.0 / 6.0
FIELDS = NRHS + 4
AXES = ("gx", "gy", "gz")
HIGHEST = lax.Precision.HIGHEST

DEPTH = 4
NZ, NX, NY = 8, 32, 256
EZ = NZ + 2 * DEPTH
ROWS = NX + 8
EROWS = ROWS + 16
LT = 3
FACE = NRHS * 4 + 3 * 4 + 1
F32 = jnp.float32
LIMIT = 63


def params(mb):
    return pltpu.CompilerParams(vmem_limit_bytes=mb << 20)


def vmem():
    return pl.BlockSpec(memory_space=pltpu.VMEM)


def smem():
    return pl.BlockSpec(memory_space=pltpu.SMEM)


def hbm():
    return pl.BlockSpec(memory_space=pl.ANY)


def row_ids(shape):
    return lax.broadcasted_iota(jnp.int32, shape, 0)


def lane_ids(shape):
    return lax.broadcasted_iota(jnp.int32, shape, 1)


def field_of(rhs, cz, cx, cy, dg, f, z):
    return rhs.at[f, z] if f < NRHS else (cz, cx, cy, dg)[f - NRHS].at[z]


def pack_faces(rhs, cz, cx, cy, dg, zlo, zhi, token, whole, loads, saves):
    copies = []
    for f in range(FIELDS):
        src = rhs.at[f] if f < NRHS else (cz, cx, cy, dg)[f - NRHS]
        copies.append(pltpu.make_async_copy(src, whole.at[f], loads.at[f]))
        copies[-1].start()
    token[0] = 0
    planes = []
    at = 0
    for f in range(FIELDS):
        copies[f].wait()
        depth = DEPTH if f <= NRHS else DEPTH - 1
        for side, out in ((0, zlo), (1, zhi)):
            start = side * (NZ - depth)
            planes.append(
                pltpu.make_async_copy(
                    whole.at[f, pl.ds(start, depth)], out.at[pl.ds(at, depth)], saves.at[2 * f + side]
                )
            )
            planes[-1].start()
        at += depth
    for copy in planes:
        copy.wait()


def pack_rows(swap, place, token, rhs, cz, cx, cy, dg, *rest):
    xmsgs, (first_rows, last_rows, loads) = rest[:-3], rest[-3:]
    copies = []
    for f in range(FIELDS):
        src = rhs.at[f] if f < NRHS else (cz, cx, cy, dg)[f - NRHS]
        for side, rows in ((0, first_rows), (1, last_rows)):
            copies.append(
                pltpu.make_async_copy(
                    src.at[:, pl.ds(side * (NX - 8), 8), :], rows.at[f], loads.at[2 * f + side]
                )
            )
            copies[-1].start()
    low = row_ids((8, NY)) < 4
    up = place[0] + token[0] == 0
    for f in range(FIELDS):
        copies[2 * f].wait()
        copies[2 * f + 1].wait()
        for m in range(NZ // 2):
            first = jnp.where(low, first_rows[f, 2 * m], pltpu.roll(first_rows[f, 2 * m + 1], 4, 0))
            last = jnp.where(low, pltpu.roll(last_rows[f, 2 * m], 4, 0), last_rows[f, 2 * m + 1])
            if swap:
                xmsgs[0][f, m] = jnp.where(up, last, first)
            else:
                xmsgs[0][f, m] = first
                xmsgs[1][f, m] = last


def halo_tile(above, below, odd, keep_up, keep_dn):
    low = row_ids(above.shape) < 4
    if odd:
        up, dn = pltpu.roll(above, 4, 0), below
    else:
        up, dn = above, pltpu.roll(below, 4, 0)
    return jnp.where(low, up * keep_up, dn * keep_dn)


def keep_sides(swap, place):
    if not swap:
        return 1.0, 1.0
    first = place[0] == 0
    return jnp.where(first, 1.0, 0.0), jnp.where(first, 0.0, 1.0)


def pack_lanes(tile_of, side):
    lane = lane_ids((8, 128))
    source = 124 * side
    acc = jnp.zeros((8, 128), F32)
    for zz in range(4):
        for f in range(FIELDS):
            tile = tile_of(f, zz)
            spot = (zz * FIELDS + f) * 4
            shift = (spot - source) % 128
            if shift:
                tile = pltpu.roll(tile, shift, 1)
            acc = jnp.where((lane >= spot) & (lane < spot + 4), tile, acc)
    return acc


def pack_own_rims(rhs, cz, cx, cy, dg, ylo, yhi):
    for t in range(NX // 8):
        for side, out in ((0, ylo), (1, yhi)):
            for half in range(2):
                out[8 * t : 8 * t + 8, 128 * half : 128 * half + 128] = pack_lanes(
                    lambda f, zz: field_of(rhs, cz, cx, cy, dg, f, 4 * half + zz)[
                        8 * t : 8 * t + 8, 128 * side : 128 * side + 128
                    ],
                    side,
                )


def pack_rims(swap, place, ylo_own, yhi_own, *refs):
    above, below, ylo, yhi = refs if not swap else (refs[0],) + refs
    keep_up, keep_dn = keep_sides(swap, place)
    for side, own, out in ((0, ylo_own, ylo), (1, yhi_own, yhi)):
        out[0:NX, :] = own[...]
        lanes = slice(128 * side, 128 * side + 128)
        for half in range(2):
            out[NX:ROWS, 128 * half : 128 * half + 128] = pack_lanes(
                lambda f, zz: halo_tile(
                    above[f, 2 * half + zz // 2, :, lanes], below[f, 2 * half + zz // 2, :, lanes], zz % 2, keep_up, keep_dn
                ),
                side,
            )


STACK = 8 * COLS


def gram_zero(accs):
    accs[...] = jnp.zeros_like(accs)


def gram_add(stacks, accs):
    left, right = [], []
    cross_left, cross_right = [], []
    for stack in stacks:
        high = stack.astype(jnp.bfloat16)
        rest = stack - high.astype(F32)
        mid = rest.astype(jnp.bfloat16)
        low = (rest - mid.astype(F32)).astype(jnp.bfloat16)
        left += [high, mid]
        cross_left += [high, high]
        cross_right += [mid, low]
    contract = (((1,), (1,)), ((), ()))

    def product(a, b):
        return lax.dot_general(jnp.concatenate(a, 1), jnp.concatenate(b, 1), contract, preferred_element_type=F32)

    accs[0] += product(left, left)
    accs[1] += product(cross_left, cross_right)


def gram_message(accs, out):
    same = (row_ids((STACK, STACK)) & 7) == (lane_ids((STACK, STACK)) & 7)
    pick = jnp.where((row_ids((STACK, 128)) >> 3) == lane_ids((STACK, 128)), 1.0, 0.0)

    def traces(product):
        picked = jnp.where(same, product, 0.0)
        rows = [jnp.sum(picked[8 * i : 8 * i + 8], axis=0, keepdims=True) for i in range(COLS)]
        rows = jnp.concatenate(rows + [jnp.zeros((128 - COLS, STACK), F32)], 0)
        return lax.dot_general(
            rows, pick, (((1,), (0,)), ((), ())), precision=HIGHEST, preferred_element_type=F32
        )

    cross = traces(accs[1])
    gram = traces(accs[0]) + cross + cross.T
    tops = [gram[8 * k : 8 * k + 8] for k in range(3)]
    rows, lanes = row_ids((8, 128)), lane_ids((8, 128))
    tile = jnp.where(lanes < COLS, tops[0], pltpu.roll(tops[1], 12, 1))
    corner = pltpu.roll(pltpu.roll(tops[2], 128 - 16, 1), 4, 0)
    tile = jnp.where((rows >= 4) & (lanes < 4), corner, tile)
    packed = tile
    for q in range(1, 4):
        turned = pltpu.roll(pltpu.roll(tile, 32 * q, 1), 8 - 2 * q, 0)
        packed = jnp.where((lanes >> 5) == q, turned, packed)
    packed = packed[0:2]
    for n in range(out.shape[0]):
        out[n] = packed


def gram_of(messages):
    total = messages[0]
    for n in range(1, messages.shape[0]):
        total = total + messages[n]
    total = jnp.concatenate([total] * 4, 0)
    rows, lanes = row_ids((8, 128)), lane_ids((8, 128))
    tile = total
    for q in range(1, 4):
        tile = jnp.where((rows >> 1) == q, pltpu.roll(total, 128 - 32 * q, 1), tile)
    corner = pltpu.roll(pltpu.roll(tile, 4, 0), 16, 1)
    tops = [
        jnp.where((lanes < COLS) & (lanes >= rows), tile, 0.0),
        jnp.where((lanes < COLS) & (lanes >= rows + 8), pltpu.roll(tile, 128 - 12, 1), 0.0),
        jnp.where((lanes < COLS) & (lanes >= rows + 16), corner, 0.0),
    ]
    return jnp.concatenate(tops, 0)


def slot(k):
    return k * NRHS + (NRHS if k else 0)


class Block:
    def __init__(self, store, base, faces, faces_base):
        self.store, self.base, self.faces, self.faces_base = store, base, faces, faces_base
        self.lane = lane_ids((8, 128))

    def put(self, f, z, l, t, value):
        z = z - self.base
        self.store[f, z, l, 8 + 8 * t : 16 + 8 * t, :] = value
        if t == 0:
            self.store[f, z, l, 8 + ROWS : 16 + ROWS, :] = value
        if t == ROWS // 8 - 1:
            self.store[f, z, l, 0:8, :] = value

    def place_y(self, z, up, dn):
        for t in range(ROWS // 8):
            u_all, d_all = up[8 * t : 8 * t + 8, :], dn[8 * t : 8 * t + 8, :]
            for zz in range(4):
                for f in range(FIELDS):
                    spot = (zz * FIELDS + f) * 4
                    u = pltpu.roll(u_all, (-spot) % 128, 1) if spot else u_all
                    d = pltpu.roll(d_all, (124 - spot) % 128, 1) if spot != 124 else d_all
                    value = jnp.where(self.lane < 4, u, jnp.where(self.lane >= 124, d, 0.0))
                    self.put(f, z + zz, 2, t, value)

    def tiles(self, f, z, t, off):
        return [self.store[f, z - self.base, l, pl.ds(8 + 8 * t + off, 8), :] for l in range(LT)]

    def lane_up(self, tri):
        rolled = [pltpu.roll(v, 127, 1) for v in tri]
        return [jnp.where(self.lane == 127, rolled[(l + 1) % LT], rolled[l]) for l in range(LT)]

    def lane_dn(self, tri):
        rolled = [pltpu.roll(v, 1, 1) for v in tri]
        return [jnp.where(self.lane == 0, rolled[(l - 1) % LT], rolled[l]) for l in range(LT)]

    def coefficients(self, z):
        for t in range(ROWS // 8):
            kz, kx, ky, kd = (NRHS + i for i in range(4))
            center_z, center_x, center_y = (self.tiles(k, z, t, 0) for k in (kz, kx, ky))
            diag = self.tiles(kd, z, t, 0)
            sides = [
                (center_z, self.tiles(kz, z + 1, t, 0)),
                (center_z, self.tiles(kz, z - 1, t, 0)),
                (center_x, self.tiles(kx, z, t, 1)),
                (center_x, self.tiles(kx, z, t, -1)),
                (center_y, self.lane_up(center_y)),
                (center_y, self.lane_dn(center_y)),
            ]
            at = z - self.faces_base
            for l in range(LT):
                inside = diag[l] > 0.0
                total = diag[l] * SCALE
                for k, (mid, side) in enumerate(sides):
                    face = (mid[l] + side[l]) * (0.5 * SCALE)
                    total = total + face
                    self.faces[k, at, l, 8 * t : 8 * t + 8, :] = jnp.where(inside, face, 0.0)
                self.faces[6, at, l, 8 * t : 8 * t + 8, :] = jnp.where(inside, total, 0.0)

    def apply(self, k, z):
        last = k == STEPS - 1
        at = z - self.faces_base
        outs = 2 if last else LT
        for t in range(NX // 8 if last else ROWS // 8):
            face = [[self.faces[c, at, l, 8 * t : 8 * t + 8, :] for l in range(outs)] for c in range(7)]
            diag = [face[6][l] - SHIFTS[k] * SCALE for l in range(outs)]
            for r in range(NRHS):
                f = slot(k) + r
                mid = self.tiles(f, z, t, 0)
                sides = [
                    self.tiles(f, z + 1, t, 0),
                    self.tiles(f, z - 1, t, 0),
                    self.tiles(f, z, t, 1),
                    self.tiles(f, z, t, -1),
                    self.lane_up(mid),
                    self.lane_dn(mid),
                ]
                for l in range(outs):
                    value = diag[l] * mid[l]
                    for c in range(6):
                        value = value - face[c][l] * sides[c][l]
                    self.put(slot(k + 1) + r, z, l, t, value)


def loop(start, stop, do):
    def step(n, carry):
        do(n)
        return carry

    lax.fori_loop(start, stop, step, 0)


def inner_planes(k):
    return DEPTH + k, DEPTH + NZ - k


def inner_copies(inner, inner_faces, store, base, faces, faces_base, sems, out):
    def copy(n, there, here):
        src, dst = (here, there) if out else (there, here)
        return pltpu.make_async_copy(src, dst, sems.at[n])

    def planes(ref, f, start, stop, at):
        return ref.at[pl.ds(f, NRHS), pl.ds(start - at, stop - start)]

    result = []
    for n, (f, start, stop) in enumerate(
        [(0, DEPTH, DEPTH + NZ), (NRHS, DEPTH, DEPTH + 2), (NRHS, DEPTH + NZ - 2, DEPTH + NZ)]
        + [(slot(k), *inner_planes(k)) for k in range(1, STEPS)]
    ):
        result.append(copy(n, planes(inner, f, start, stop, DEPTH), planes(store, f, start, stop, base)))
    start, stop = inner_planes(1)
    result.append(copy(len(result), inner_faces, faces.at[:, pl.ds(start - faces_base, stop - start)]))
    return result


def krylov_inner(swap, place, rhs, cz, cx, cy, dg, *rest):
    above, below, yup, ydn, inner, inner_faces, store, faces, sems = rest if not swap else rest[:1] + rest
    keep_up, keep_dn = keep_sides(swap, place)
    block = Block(store, DEPTH, faces, DEPTH + 1)
    for f in range(FIELDS):
        for z in range(DEPTH, DEPTH + NZ):
            plane = field_of(rhs, cz, cx, cy, dg, f, z - DEPTH)
            m = (z - DEPTH) // 2
            for l in range(2):
                lanes = pl.ds(128 * l, 128)
                for t in range(NX // 8):
                    block.put(f, z, l, t, plane[8 * t : 8 * t + 8, lanes])
                tile = halo_tile(above[f, m, :, lanes], below[f, m, :, lanes], z % 2, keep_up, keep_dn)
                block.put(f, z, l, NX // 8, tile)
    for half in range(2):
        lanes = pl.ds(128 * half, 128)
        block.place_y(DEPTH + 4 * half, yup.at[:, lanes], ydn.at[:, lanes])
    copies = inner_copies(inner, inner_faces, store, DEPTH, faces, DEPTH + 1, sems, True)
    for n in range(3):
        copies[n].start()
    loop(*inner_planes(1), block.coefficients)
    copies[-1].start()
    for k in range(STEPS - 1):
        loop(*inner_planes(k + 1), functools.partial(block.apply, k))
        copies[3 + k].start()
    for copy in copies:
        copy.wait()


NEAR, FAR = 8 * FIELDS, 24


def krylov_outer(
    swap, place, inner, inner_faces, facelo, facehi, rimlo, rimhi,
    basis, message,
    store, faces, accs, loads, saves,
):
    keep_up, keep_dn = keep_sides(swap, place)
    n_x = 1 if swap else 2
    block = Block(store, 0, faces, 0)
    copies = inner_copies(inner, inner_faces, store, 0, faces, 0, loads, False)
    for copy in copies:
        copy.start()

    zero = jnp.zeros((8, 128), F32)
    for f in range(FIELDS):
        depth = DEPTH if f <= NRHS else DEPTH - 1
        start = f * DEPTH if f <= NRHS else NRHS * DEPTH + DEPTH + (f - NRHS - 1) * (DEPTH - 1)
        for face, rim, first in ((facelo, rimlo, 0), (facehi, rimhi, DEPTH + NZ)):
            for z in range(first, first + DEPTH):
                far = DEPTH - z if first == 0 else z - first + 1
                d = start + (depth - far if first == 0 else far - 1)
                for l in range(2):
                    lanes = pl.ds(128 * l, 128)
                    for t in range(NX // 8):
                        value = face[d, 8 * t : 8 * t + 8, lanes] if far <= depth else zero
                        block.put(f, z, l, t, value)
                    if far <= 2:
                        at, odd = 8 * f, z % 2
                    elif far == 3 and 8 * (f // 2) < FAR:
                        at, odd = NEAR + 8 * (f // 2), f % 2
                    else:
                        block.put(f, z, l, NX // 8, zero)
                        continue
                    other = at + (n_x - 1) * (NEAR + FAR)
                    tile = halo_tile(rim[at : at + 8, lanes], rim[other : other + 8, lanes], odd, keep_up, keep_dn)
                    block.put(f, z, l, NX // 8, tile)
    rows = pl.ds(n_x * (NEAR + FAR), ROWS)
    for rim, z in ((rimlo, 0), (rimhi, DEPTH + NZ)):
        block.place_y(z, rim.at[rows, pl.ds(0, 128)], rim.at[rows, pl.ds(128, 128)])

    for n in range(3):
        copies[n].wait()
    loop(1, DEPTH + 1, block.coefficients)
    loop(DEPTH + NZ - 1, EZ - 1, block.coefficients)

    sends = []

    def send_block(k):
        copy = pltpu.make_async_copy(
            store.at[pl.ds(slot(k), NRHS), pl.ds(DEPTH, NZ), pl.ds(0, 2), pl.ds(8, NX), :],
            basis.at[pl.ds(k * NRHS, NRHS)],
            saves.at[k],
        )
        copy.start()
        sends.append(copy)

    send_block(0)
    for k in range(STEPS):
        if k == 1:
            copies[-1].wait()
        loop(
            0,
            2 * DEPTH,
            lambda n, k=k: block.apply(k, n + k + 1 + jnp.where(n >= DEPTH, NZ - 2 - 2 * k, 0)),
        )
        if k < STEPS - 1:
            copies[3 + k].wait()
        send_block(k + 1)
    gram_zero(accs)

    def products(z):
        def tile(i, t):
            f = slot(i // NRHS) + i % NRHS
            return jnp.concatenate([store[f, z, l, 8 + 8 * t : 16 + 8 * t, :] for l in range(2)], 1)

        gram_add([jnp.concatenate([tile(i, t) for i in range(COLS)], 0) for t in range(NX // 8)], accs)

    loop(DEPTH, DEPTH + NZ, products)
    gram_message(accs, message)
    for copy in sends:
        copy.wait()


def factor_gram(messages, cells, table):
    rows = row_ids((24, 128))
    lanes = lane_ids((24, 128))
    upper = gram_of(messages) / cells
    square = jnp.concatenate([upper, jnp.zeros((104, 128), F32)], 0).T
    whole = jnp.where(rows <= lanes, upper, square[0:24, :])

    def splat(value):
        return jnp.broadcast_to(value, (24, 128))

    columns = [splat(whole[:, c : c + 1]) for c in range(COLS)]
    inverse = [jnp.where(rows == c, 1.0, 0.0) for c in range(COLS)]
    pivots = jnp.ones((24, 128), F32)
    factor = jnp.zeros((24, 128), F32)
    for j in range(COLS):
        pivot = splat(columns[j][j : j + 1, :])
        pivots = jnp.where(rows == j, pivot, pivots)
        below = jnp.where(rows > j, columns[j] / pivot, 0.0)
        for c in range(j, COLS):
            row = splat(columns[c][j : j + 1, :])
            factor = jnp.where((rows == j) & (lanes == c), row, factor)
            if c > j:
                columns[c] = columns[c] - below * row
        for c in range(j + 1):
            inverse[c] = inverse[c] - below * splat(inverse[c][j : j + 1, :])
    roots = jnp.sqrt(pivots)
    for c in range(COLS):
        table[c] = inverse[c] / roots
    return factor / roots


def apply_rows(table, read, write):
    group = 5
    pieces = NX // 8
    for g in reversed(range(COLS // group)):
        mine = range(group * g, group * g + group)
        sums = {i: None for i in mine}
        for j in range(group * g + group):
            value = [read(j, p) for p in range(pieces)]
            for i in mine:
                if j <= i:
                    weight = jnp.broadcast_to(table[j, i : i + 1, :], (8, 128))
                    terms = [weight * v for v in value]
                    sums[i] = terms if sums[i] is None else [s + t for s, t in zip(sums[i], terms)]
        for i in mine:
            for p in range(pieces):
                write(i, p, sums[i][p])


def plane_copy(src, dst, sems, z):
    return pltpu.make_async_copy(src.at[:, z], dst.at[:, z], sems.at[z])


def first_pass(cells, message, basis_hbm, first_hbm, next_message, factor_out, basis, table, accs, loads, saves):
    for z in range(NZ):
        plane_copy(basis_hbm, basis, loads, z).start()
    factor_out[...] = factor_gram(message, cells, table)
    gram_zero(accs)

    def chunk(z, carry):
        plane_copy(basis_hbm, basis, loads, z).wait()
        for l in range(2):

            def read(j, p):
                return basis[j, z, l, 8 * p : 8 * p + 8, :]

            def write(i, p, value):
                basis[i, z, l, 8 * p : 8 * p + 8, :] = value

            apply_rows(table, read, write)
        plane_copy(basis, first_hbm, saves, z).start()

        def tile(i, t):
            return jnp.concatenate([basis[i, z, l, 8 * t : 8 * t + 8, :] for l in range(2)], 1)

        gram_add([jnp.concatenate([tile(i, t) for i in range(COLS)], 0) for t in range(NX // 8)], accs)
        return carry

    lax.fori_loop(0, NZ, chunk, 0)

    gram_message(accs, next_message)
    for z in range(NZ):
        plane_copy(basis, first_hbm, saves, z).wait()


def second_pass(cells, message, factor_one, first_hbm, out_hbm, triangle, first, out, table, loads, saves):
    for z in range(NZ):
        plane_copy(first_hbm, first, loads, z).start()
    left = factor_gram(message, cells, table)[:, 0:24]
    product = lax.dot_general(
        left, factor_one[...], (((1,), (0,)), ((), ())), precision=HIGHEST, preferred_element_type=F32
    )
    triangle[...] = product[0:COLS, 0:COLS]

    def chunk(z, carry):
        plane_copy(first_hbm, first, loads, z).wait()
        for l in range(2):

            def read(j, p):
                return first[j, z, l, 8 * p : 8 * p + 8, :]

            def write(i, p, value):
                out[i, z, 8 * p : 8 * p + 8, 128 * l : 128 * l + 128] = value

            apply_rows(table, read, write)
        plane_copy(out, out_hbm, saves, z).start()
        return carry

    lax.fori_loop(0, NZ, chunk, 0)
    for z in range(NZ):
        plane_copy(out, out_hbm, saves, z).wait()


def shape(*dims):
    return jax.ShapeDtypeStruct(dims, F32)


def move(value, axis, delta):
    count = lax.axis_size(axis)
    pairs = [(i, i + delta) for i in range(count) if 0 <= i + delta < count]
    return lax.ppermute(value, axis, pairs)


def exchange(messages):
    return lax.all_to_all(messages, AXES, 0, 0, tiled=True)


def body(rhs, coef_x, coef_y, coef_z, diag_term):
    n_x = lax.axis_size("gx")
    devices = n_x * lax.axis_size("gy") * lax.axis_size("gz")
    cells = float(NZ * NX * NY * devices)
    at_x = lax.axis_index("gx")
    swap = n_x == 2
    fields = (rhs, coef_z, coef_x, coef_y, diag_term)

    place = at_x.astype(jnp.int32).reshape(1)
    face_shape = shape(FACE, NX, NY)
    zlo, zhi, token = pl.pallas_call(
        pack_faces,
        out_shape=(face_shape, face_shape, jax.ShapeDtypeStruct((1,), jnp.int32)),
        in_specs=[hbm()] * 5,
        out_specs=(hbm(), hbm(), smem()),
        scratch_shapes=[
            pltpu.VMEM((FIELDS, NZ, NX, NY), F32),
            pltpu.SemaphoreType.DMA((FIELDS,)),
            pltpu.SemaphoreType.DMA((2 * FIELDS,)),
        ],
        compiler_params=params(LIMIT),
    )(*fields)
    facehi = move(zlo, "gz", -1)
    facelo = move(zhi, "gz", 1)
    x_shape = shape(FIELDS, NZ // 2, 8, NY)
    xmsgs = pl.pallas_call(
        functools.partial(pack_rows, swap),
        out_shape=(x_shape,) * (1 if swap else 2),
        in_specs=[smem(), smem()] + [hbm()] * 5,
        scratch_shapes=[
            pltpu.VMEM((FIELDS, NZ, 8, NY), F32),
            pltpu.VMEM((FIELDS, NZ, 8, NY), F32),
            pltpu.SemaphoreType.DMA((2 * FIELDS,)),
        ],
        compiler_params=params(LIMIT),
    )(place, token, *fields)
    if swap:
        x_parts = (lax.ppermute(xmsgs[0], "gx", [(0, 1), (1, 0)]),)
    else:
        x_parts = (move(xmsgs[0], "gx", -1), move(xmsgs[1], "gx", 1))

    own_shape = shape(NX, NY)
    own_rims = pl.pallas_call(
        pack_own_rims,
        out_shape=(own_shape, own_shape),
        in_specs=[vmem()] * 5,
        compiler_params=params(LIMIT),
    )(*fields)
    rim_shape = shape(ROWS, NY)
    ylo, yhi = pl.pallas_call(
        functools.partial(pack_rims, swap),
        out_shape=(rim_shape, rim_shape),
        in_specs=[smem()] + [vmem()] * (2 + len(x_parts)),
        compiler_params=params(16),
    )(place, *own_rims, *x_parts)
    yup, ydn = move(ylo, "gy", -1), move(yhi, "gy", 1)

    def rim(half):
        near, far, odd = ((0, 1, 0), (3, 2, 1))[half]
        rows = []
        for part in x_parts:
            rows.append(part[:, near].reshape(NEAR, NY))
            rows.append(part[: FAR // 4, far, 4 * odd : 4 * odd + 4].reshape(FAR, NY))
        lanes = slice(128 * half, 128 * half + 128)
        return jnp.concatenate(rows + [jnp.concatenate([yup[:, lanes], ydn[:, lanes]], 1)], 0)

    rimhi, rimlo = move(rim(0), "gz", -1), move(rim(1), "gz", 1)

    inner_shape = shape(COLS, NZ, LT, EROWS, 128)
    inner_faces_shape = shape(7, NZ - 2, LT, ROWS, 128)
    inner, inner_faces = pl.pallas_call(
        functools.partial(krylov_inner, swap),
        out_shape=(inner_shape, inner_faces_shape),
        in_specs=[smem()] + [vmem()] * (5 + len(x_parts) + 2),
        out_specs=(hbm(), hbm()),
        scratch_shapes=[
            pltpu.VMEM(inner_shape.shape, F32),
            pltpu.VMEM(inner_faces_shape.shape, F32),
            pltpu.SemaphoreType.DMA((7,)),
        ],
        compiler_params=params(LIMIT),
        cost_estimate=pl.CostEstimate(flops=1 << 27, bytes_accessed=25 << 20, transcendentals=0),
    )(place, *fields, *x_parts, yup, ydn)

    block = shape(COLS, NZ, 2, NX, 128)
    basis, message = pl.pallas_call(
        functools.partial(krylov_outer, swap),
        out_shape=(block, shape(devices, 2, 128)),
        in_specs=[smem(), hbm(), hbm()] + [vmem()] * 4,
        out_specs=(hbm(), vmem()),
        scratch_shapes=[
            pltpu.VMEM((COLS + NRHS, EZ, LT, EROWS, 128), F32),
            pltpu.VMEM((7, EZ, LT, ROWS, 128), F32),
            pltpu.VMEM((2, STACK, STACK), F32),
            pltpu.SemaphoreType.DMA((7,)),
            pltpu.SemaphoreType.DMA((STEPS + 1,)),
        ],
        compiler_params=params(LIMIT),
    )(place, inner, inner_faces, facelo, facehi, rimlo, rimhi)

    message = exchange(message)
    first, message, factor_one = pl.pallas_call(
        functools.partial(first_pass, cells),
        out_shape=(block, shape(1, 2, 128), shape(24, 128)),
        in_specs=[vmem(), hbm()],
        out_specs=(hbm(), vmem(), vmem()),
        scratch_shapes=[
            pltpu.VMEM(block.shape, F32),
            pltpu.VMEM((COLS, 24, 128), F32),
            pltpu.VMEM((2, STACK, STACK), F32),
            pltpu.SemaphoreType.DMA((NZ,)),
            pltpu.SemaphoreType.DMA((NZ,)),
        ],
        compiler_params=params(LIMIT),
    )(message, basis)

    message = lax.all_gather(message[0], AXES)
    return pl.pallas_call(
        functools.partial(second_pass, cells),
        out_shape=(shape(COLS, NZ, NX, NY), shape(COLS, COLS)),
        in_specs=[vmem(), vmem(), hbm()],
        out_specs=(hbm(), vmem()),
        scratch_shapes=[
            pltpu.VMEM(block.shape, F32),
            pltpu.VMEM((COLS, NZ, NX, NY), F32),
            pltpu.VMEM((COLS, 24, 128), F32),
            pltpu.SemaphoreType.DMA((NZ,)),
            pltpu.SemaphoreType.DMA((NZ,)),
        ],
        compiler_params=params(LIMIT),
    )(message, factor_one, first)


def solution(mesh):
    return jax.shard_map(
        body,
        mesh=mesh,
        in_specs=(
            P(None, "gz", "gx", "gy"),
            P("gz", "gx", "gy"),
            P("gz", "gx", "gy"),
            P("gz", "gx", "gy"),
            P("gz", "gx", "gy"),
        ),
        out_specs=(P(None, "gz", "gx", "gy"), P()),
        check_vma=False,
    )
```

```python
import functools

import jax
import jax.numpy as jnp
from jax import lax
from jax.experimental import pallas as pl
from jax.experimental.pallas import tpu as pltpu
from jax.sharding import PartitionSpec as P

NRHS = 4
STEPS = 4
COLS = NRHS * (STEPS + 1)
SHIFTS = (3.0, 11.0, 7.0, 1.5)
SCALE = 1.0 / 6.0
FIELDS = NRHS + 4
AXES = ("gx", "gy", "gz")
HIGHEST = lax.Precision.HIGHEST

DEPTH = 4
NZ, NX, NY = 8, 32, 256
EZ = NZ + 2 * DEPTH
ROWS = NX + 8
EROWS = ROWS + 16
LT = 3
FACE = NRHS * 4 + 3 * 4 + 1
F32 = jnp.float32
LIMIT = 63


def params(mb):
    return pltpu.CompilerParams(vmem_limit_bytes=mb << 20)


def cost(us):
    return pl.CostEstimate(flops=0, bytes_accessed=int(us * 3.6e6), transcendentals=0)


def vmem():
    return pl.BlockSpec(memory_space=pltpu.VMEM)


def smem():
    return pl.BlockSpec(memory_space=pltpu.SMEM)


def hbm():
    return pl.BlockSpec(memory_space=pl.ANY)


def row_ids(shape):
    return lax.broadcasted_iota(jnp.int32, shape, 0)


def lane_ids(shape):
    return lax.broadcasted_iota(jnp.int32, shape, 1)


def field_of(rhs, cz, cx, cy, dg, f, z):
    return rhs.at[f, z] if f < NRHS else (cz, cx, cy, dg)[f - NRHS].at[z]


def pack_faces(swap, place, rhs, cz, cx, cy, dg, zlo, zhi, *rest):
    xmsgs, (whole, loads, saves) = rest[:-3], rest[-3:]
    copies = []
    for f in range(FIELDS):
        src = rhs.at[f] if f < NRHS else (cz, cx, cy, dg)[f - NRHS]
        copies.append(pltpu.make_async_copy(src, whole.at[f], loads.at[f]))
        copies[-1].start()
    low = row_ids((8, NY)) < 4
    up = place[0] == 0
    planes = []
    at = 0
    for f in range(FIELDS):
        copies[f].wait()
        depth = DEPTH if f <= NRHS else DEPTH - 1
        for side, out in ((0, zlo), (1, zhi)):
            start = side * (NZ - depth)
            planes.append(
                pltpu.make_async_copy(
                    whole.at[f, pl.ds(start, depth)], out.at[pl.ds(at, depth)], saves.at[2 * f + side]
                )
            )
            planes[-1].start()
        at += depth
        for m in range(NZ // 2):
            a, b = whole.at[f, 2 * m], whole.at[f, 2 * m + 1]
            first = jnp.where(low, a[0:8], pltpu.roll(b[0:8], 4, 0))
            last = jnp.where(low, pltpu.roll(a[NX - 8 : NX], 4, 0), b[NX - 8 : NX])
            if swap:
                xmsgs[0][f, m] = jnp.where(up, last, first)
            else:
                xmsgs[0][f, m] = first
                xmsgs[1][f, m] = last
    for copy in planes:
        copy.wait()


def halo_tile(above, below, odd, keep_up, keep_dn):
    low = row_ids(above.shape) < 4
    if odd:
        up, dn = pltpu.roll(above, 4, 0), below
    else:
        up, dn = above, pltpu.roll(below, 4, 0)
    return jnp.where(low, up * keep_up, dn * keep_dn)


def keep_sides(swap, place):
    if not swap:
        return 1.0, 1.0
    first = place[0] == 0
    return jnp.where(first, 1.0, 0.0), jnp.where(first, 0.0, 1.0)


def pack_lanes(tile_of, side):
    lane = lane_ids((8, 128))
    source = 124 * side
    acc = jnp.zeros((8, 128), F32)
    for zz in range(4):
        for f in range(FIELDS):
            tile = tile_of(f, zz)
            spot = (zz * FIELDS + f) * 4
            shift = (spot - source) % 128
            if shift:
                tile = pltpu.roll(tile, shift, 1)
            acc = jnp.where((lane >= spot) & (lane < spot + 4), tile, acc)
    return acc


def pack_own_rims(rhs, cz, cx, cy, dg, ylo, yhi):
    for t in range(NX // 8):
        for side, out in ((0, ylo), (1, yhi)):
            for half in range(2):
                out[8 * t : 8 * t + 8, 128 * half : 128 * half + 128] = pack_lanes(
                    lambda f, zz: field_of(rhs, cz, cx, cy, dg, f, 4 * half + zz)[
                        8 * t : 8 * t + 8, 128 * side : 128 * side + 128
                    ],
                    side,
                )


def pack_rims(swap, place, ylo_own, yhi_own, *refs):
    above, below, ylo, yhi = refs if not swap else (refs[0],) + refs
    keep_up, keep_dn = keep_sides(swap, place)
    for side, own, out in ((0, ylo_own, ylo), (1, yhi_own, yhi)):
        out[0:NX, :] = own[...]
        lanes = slice(128 * side, 128 * side + 128)
        for half in range(2):
            out[NX:ROWS, 128 * half : 128 * half + 128] = pack_lanes(
                lambda f, zz: halo_tile(
                    above[f, 2 * half + zz // 2, :, lanes], below[f, 2 * half + zz // 2, :, lanes], zz % 2, keep_up, keep_dn
                ),
                side,
            )


STACK = 8 * COLS


def gram_zero(accs):
    accs[...] = jnp.zeros_like(accs)


def gram_add(stacks, accs):
    left, right = [], []
    cross_left, cross_right = [], []
    for stack in stacks:
        high = stack.astype(jnp.bfloat16)
        rest = stack - high.astype(F32)
        mid = rest.astype(jnp.bfloat16)
        low = (rest - mid.astype(F32)).astype(jnp.bfloat16)
        left += [high, mid]
        cross_left += [high, high]
        cross_right += [mid, low]
    contract = (((1,), (1,)), ((), ()))

    def product(a, b):
        return lax.dot_general(jnp.concatenate(a, 1), jnp.concatenate(b, 1), contract, preferred_element_type=F32)

    accs[0] += product(left, left)
    accs[1] += product(cross_left, cross_right)


def gram_message(accs, out):
    same = (row_ids((STACK, STACK)) & 7) == (lane_ids((STACK, STACK)) & 7)
    pick = jnp.where((row_ids((STACK, 128)) >> 3) == lane_ids((STACK, 128)), 1.0, 0.0)

    def traces(product):
        picked = jnp.where(same, product, 0.0)
        rows = [jnp.sum(picked[8 * i : 8 * i + 8], axis=0, keepdims=True) for i in range(COLS)]
        rows = jnp.concatenate(rows + [jnp.zeros((128 - COLS, STACK), F32)], 0)
        return lax.dot_general(
            rows, pick, (((1,), (0,)), ((), ())), precision=HIGHEST, preferred_element_type=F32
        )

    cross = traces(accs[1])
    gram = traces(accs[0]) + cross + cross.T
    tops = [gram[8 * k : 8 * k + 8] for k in range(3)]
    rows, lanes = row_ids((8, 128)), lane_ids((8, 128))
    tile = jnp.where(lanes < COLS, tops[0], pltpu.roll(tops[1], 12, 1))
    corner = pltpu.roll(pltpu.roll(tops[2], 128 - 16, 1), 4, 0)
    tile = jnp.where((rows >= 4) & (lanes < 4), corner, tile)
    packed = tile
    for q in range(1, 4):
        turned = pltpu.roll(pltpu.roll(tile, 32 * q, 1), 8 - 2 * q, 0)
        packed = jnp.where((lanes >> 5) == q, turned, packed)
    packed = packed[0:2]
    for n in range(out.shape[0]):
        out[n] = packed


def gram_of(messages):
    total = messages[0]
    for n in range(1, messages.shape[0]):
        total = total + messages[n]
    total = jnp.concatenate([total] * 4, 0)
    rows, lanes = row_ids((8, 128)), lane_ids((8, 128))
    tile = total
    for q in range(1, 4):
        tile = jnp.where((rows >> 1) == q, pltpu.roll(total, 128 - 32 * q, 1), tile)
    corner = pltpu.roll(pltpu.roll(tile, 4, 0), 16, 1)
    tops = [
        jnp.where((lanes < COLS) & (lanes >= rows), tile, 0.0),
        jnp.where((lanes < COLS) & (lanes >= rows + 8), pltpu.roll(tile, 128 - 12, 1), 0.0),
        jnp.where((lanes < COLS) & (lanes >= rows + 16), corner, 0.0),
    ]
    return jnp.concatenate(tops, 0)


def slot(k):
    return k * NRHS + (NRHS if k else 0)


class Block:
    def __init__(self, store, base, faces, faces_base, one):
        self.one = one
        self.store, self.base, self.faces, self.faces_base = store, base, faces, faces_base
        self.lane = lane_ids((8, 128))

    def put(self, f, z, l, t, value):
        z = z - self.base
        self.store[f, z, l, 8 + 8 * t : 16 + 8 * t, :] = value
        if t == 0:
            self.store[f, z, l, 8 + ROWS : 16 + ROWS, :] = value
        if t == ROWS // 8 - 1:
            self.store[f, z, l, 0:8, :] = value

    def place_y(self, z, up, dn):
        for t in range(ROWS // 8):
            u_all, d_all = up[8 * t : 8 * t + 8, :], dn[8 * t : 8 * t + 8, :]
            for zz in range(4):
                for f in range(FIELDS):
                    spot = (zz * FIELDS + f) * 4
                    u = pltpu.roll(u_all, (-spot) % 128, 1) if spot else u_all
                    d = pltpu.roll(d_all, (124 - spot) % 128, 1) if spot != 124 else d_all
                    value = jnp.where(self.lane < 4, u, jnp.where(self.lane >= 124, d, 0.0))
                    self.put(f, z + zz, 2, t, value)

    def tiles(self, f, z, t, off):
        row = 8 + 8 * t + (off * self.one if off else 0)
        return [self.store[f, z - self.base, l, pl.ds(row, 8), :] for l in range(LT)]

    def close_ring(self, f, z):
        z = z - self.base
        for l in range(2):
            self.store[f, z, l, 8 + ROWS : 16 + ROWS, :] = self.store[f, z, l, 8:16, :]

    def lane_up(self, tri):
        rolled = [pltpu.roll(v, 127, 1) for v in tri]
        return [jnp.where(self.lane == 127, rolled[(l + 1) % LT], rolled[l]) for l in range(LT)]

    def lane_dn(self, tri):
        rolled = [pltpu.roll(v, 1, 1) for v in tri]
        return [jnp.where(self.lane == 0, rolled[(l - 1) % LT], rolled[l]) for l in range(LT)]

    def coefficients(self, z):
        for t in range(ROWS // 8):
            kz, kx, ky, kd = (NRHS + i for i in range(4))
            center_z, center_x, center_y = (self.tiles(k, z, t, 0) for k in (kz, kx, ky))
            diag = self.tiles(kd, z, t, 0)
            sides = [
                (center_z, self.tiles(kz, z + 1, t, 0)),
                (center_z, self.tiles(kz, z - 1, t, 0)),
                (center_x, self.tiles(kx, z, t, 1)),
                (center_x, self.tiles(kx, z, t, -1)),
                (center_y, self.lane_up(center_y)),
                (center_y, self.lane_dn(center_y)),
            ]
            at = z - self.faces_base
            for l in range(LT):
                inside = diag[l] > 0.0
                total = diag[l] * SCALE
                for k, (mid, side) in enumerate(sides):
                    face = (mid[l] + side[l]) * (0.5 * SCALE)
                    total = total + face
                    self.faces[k, at, l, 8 * t : 8 * t + 8, :] = jnp.where(inside, face, 0.0)
                self.faces[6, at, l, 8 * t : 8 * t + 8, :] = jnp.where(inside, total, 0.0)

    def apply(self, k, z):
        last = k == STEPS - 1
        at = z - self.faces_base
        outs = 2 if last else LT
        for t in range(NX // 8 if last else ROWS // 8):
            face = [[self.faces[c, at, l, 8 * t : 8 * t + 8, :] for l in range(outs)] for c in range(7)]
            diag = [face[6][l] - SHIFTS[k] * SCALE for l in range(outs)]
            for r in range(NRHS):
                f = slot(k) + r
                mid = self.tiles(f, z, t, 0)
                sides = [
                    self.tiles(f, z + 1, t, 0),
                    self.tiles(f, z - 1, t, 0),
                    self.tiles(f, z, t, 1),
                    self.tiles(f, z, t, -1),
                    self.lane_up(mid),
                    self.lane_dn(mid),
                ]
                for l in range(outs):
                    value = diag[l] * mid[l]
                    for c in range(6):
                        value = value - face[c][l] * sides[c][l]
                    self.put(slot(k + 1) + r, z, l, t, value)


def dynamic_one(place):
    return (place[0] >> 24) + 1


def loop(start, stop, do):
    def step(n, carry):
        do(n)
        return carry

    lax.fori_loop(start, stop, step, 0)


def inner_planes(k):
    return DEPTH + k, DEPTH + NZ - k


def inner_copies(inner, inner_faces, store, base, faces, faces_base, sems, out):
    def copy(n, there, here):
        src, dst = (here, there) if out else (there, here)
        return pltpu.make_async_copy(src, dst, sems.at[n])

    def planes(ref, f, start, stop, at):
        return ref.at[pl.ds(f, NRHS), pl.ds(start - at, stop - start)]

    result = []
    for n, (f, start, stop) in enumerate(
        [(0, DEPTH, DEPTH + NZ), (NRHS, DEPTH, DEPTH + 2), (NRHS, DEPTH + NZ - 2, DEPTH + NZ)]
        + [(slot(k), *inner_planes(k)) for k in range(1, STEPS)]
    ):
        result.append(copy(n, planes(inner, f, start, stop, DEPTH), planes(store, f, start, stop, base)))
    start, stop = inner_planes(1)
    result.append(copy(len(result), inner_faces, faces.at[:, pl.ds(start - faces_base, stop - start)]))
    return result


def krylov_inner(swap, place, rhs, cz, cx, cy, dg, *rest):
    above, below, yup, ydn, inner, inner_faces, store, faces, load_sems, sems = rest if not swap else rest[:1] + rest
    keep_up, keep_dn = keep_sides(swap, place)
    block = Block(store, DEPTH, faces, DEPTH + 1, dynamic_one(place))
    loads = []
    for n, src in enumerate((rhs, cz, cx, cy, dg)):
        for l in range(2):
            lanes = pl.ds(128 * l, 128)
            rows = pl.ds(8, NX)
            if n == 0:
                src_at, dst = src.at[:, :, :, lanes], store.at[pl.ds(0, NRHS), :, l, rows, :]
            else:
                src_at, dst = src.at[:, :, lanes], store.at[NRHS + n - 1, :, l, rows, :]
            loads.append(pltpu.make_async_copy(src_at, dst, load_sems.at[2 * n + l]))
            loads[-1].start()
    for f in range(FIELDS):
        for z in range(DEPTH, DEPTH + NZ):
            m = (z - DEPTH) // 2
            for l in range(2):
                lanes = pl.ds(128 * l, 128)
                tile = halo_tile(above[f, m, :, lanes], below[f, m, :, lanes], z % 2, keep_up, keep_dn)
                block.put(f, z, l, NX // 8, tile)
    for half in range(2):
        lanes = pl.ds(128 * half, 128)
        block.place_y(DEPTH + 4 * half, yup.at[:, lanes], ydn.at[:, lanes])
    for copy in loads:
        copy.wait()
    for f in range(FIELDS):
        for z in range(DEPTH, DEPTH + NZ):
            block.close_ring(f, z)
    copies = inner_copies(inner, inner_faces, store, DEPTH, faces, DEPTH + 1, sems, True)
    for n in range(3):
        copies[n].start()
    loop(*inner_planes(1), block.coefficients)
    copies[-1].start()
    for k in range(STEPS - 1):
        loop(*inner_planes(k + 1), functools.partial(block.apply, k))
        copies[3 + k].start()
    for copy in copies:
        copy.wait()


NEAR, FAR = 8 * FIELDS, 24


def krylov_outer(
    swap, facelo, facehi, place, inner, inner_faces, rimlo, rimhi,
    basis, message,
    store, faces, accs, plane_sems, loads, saves,
):
    keep_up, keep_dn = keep_sides(swap, place)
    n_x = 1 if swap else 2
    block = Block(store, 0, faces, 0, dynamic_one(place))
    copies = inner_copies(inner, inner_faces, store, 0, faces, 0, loads, False)
    planes = []
    start = 0
    for f in range(FIELDS):
        depth = DEPTH if f <= NRHS else DEPTH - 1
        for side, (face, z) in enumerate(((facelo, DEPTH - depth), (facehi, DEPTH + NZ))):
            for l in range(2):
                planes.append(
                    pltpu.make_async_copy(
                        face.at[pl.ds(start, depth), :, pl.ds(128 * l, 128)],
                        store.at[f, pl.ds(z, depth), l, pl.ds(8, NX), :],
                        plane_sems.at[4 * f + 2 * side + l],
                    )
                )
        start += depth
    for copy in copies[:3] + planes + copies[3:]:
        copy.start()

    zero = jnp.zeros((8, 128), F32)
    for f in range(FIELDS):
        for rim, first in ((rimlo, 0), (rimhi, DEPTH + NZ)):
            for z in range(first, first + DEPTH):
                far = DEPTH - z if first == 0 else z - first + 1
                for l in range(2):
                    lanes = pl.ds(128 * l, 128)
                    if far <= 2:
                        at, odd = 8 * f, z % 2
                    elif far == 3 and 8 * (f // 2) < FAR:
                        at, odd = NEAR + 8 * (f // 2), f % 2
                    else:
                        block.put(f, z, l, NX // 8, zero)
                        continue
                    other = at + (n_x - 1) * (NEAR + FAR)
                    tile = halo_tile(rim[at : at + 8, lanes], rim[other : other + 8, lanes], odd, keep_up, keep_dn)
                    block.put(f, z, l, NX // 8, tile)
    rows = pl.ds(n_x * (NEAR + FAR), ROWS)
    for rim, z in ((rimlo, 0), (rimhi, DEPTH + NZ)):
        block.place_y(z, rim.at[rows, pl.ds(0, 128)], rim.at[rows, pl.ds(128, 128)])

    for copy in copies[:3] + planes:
        copy.wait()
    for f in range(FIELDS):
        depth = DEPTH if f <= NRHS else DEPTH - 1
        for d in range(depth):
            block.close_ring(f, DEPTH - 1 - d)
            block.close_ring(f, DEPTH + NZ + d)
    loop(1, DEPTH + 1, block.coefficients)
    loop(DEPTH + NZ - 1, EZ - 1, block.coefficients)

    sends = []

    def send_block(k):
        copy = pltpu.make_async_copy(
            store.at[pl.ds(slot(k), NRHS), pl.ds(DEPTH, NZ), pl.ds(0, 2), pl.ds(8, NX), :],
            basis.at[pl.ds(k * NRHS, NRHS)],
            saves.at[k],
        )
        copy.start()
        sends.append(copy)

    send_block(0)
    for k in range(STEPS):
        if k == 1:
            copies[-1].wait()
        loop(
            0,
            2 * DEPTH,
            lambda n, k=k: block.apply(k, n + k + 1 + jnp.where(n >= DEPTH, NZ - 2 - 2 * k, 0)),
        )
        if k < STEPS - 1:
            copies[3 + k].wait()
        send_block(k + 1)
    gram_zero(accs)

    def products(z):
        def tile(i, t):
            f = slot(i // NRHS) + i % NRHS
            return jnp.concatenate([store[f, z, l, 8 + 8 * t : 16 + 8 * t, :] for l in range(2)], 1)

        gram_add([jnp.concatenate([tile(i, t) for i in range(COLS)], 0) for t in range(NX // 8)], accs)

    loop(DEPTH, DEPTH + NZ, products)
    gram_message(accs, message)
    for copy in sends:
        copy.wait()


def factor_gram(messages, cells, table):
    rows = row_ids((24, 128))
    lanes = lane_ids((24, 128))
    upper = gram_of(messages) / cells
    square = jnp.concatenate([upper, jnp.zeros((104, 128), F32)], 0).T
    whole = jnp.where(rows <= lanes, upper, square[0:24, :])

    def splat(value):
        return jnp.broadcast_to(value, (24, 128))

    columns = [splat(whole[:, c : c + 1]) for c in range(COLS)]
    inverse = [jnp.where(rows == c, 1.0, 0.0) for c in range(COLS)]
    pivots = jnp.ones((24, 128), F32)
    factor = jnp.zeros((24, 128), F32)
    for j in range(COLS):
        pivot = splat(columns[j][j : j + 1, :])
        pivots = jnp.where(rows == j, pivot, pivots)
        below = jnp.where(rows > j, columns[j] / pivot, 0.0)
        for c in range(j, COLS):
            row = splat(columns[c][j : j + 1, :])
            factor = jnp.where((rows == j) & (lanes == c), row, factor)
            if c > j:
                columns[c] = columns[c] - below * row
        for c in range(j + 1):
            inverse[c] = inverse[c] - below * splat(inverse[c][j : j + 1, :])
    roots = jnp.sqrt(pivots)
    for c in range(COLS):
        table[c] = inverse[c] / roots
    return factor / roots


def apply_rows(table, read, write):
    group = 5
    pieces = NX // 8
    for g in reversed(range(COLS // group)):
        mine = range(group * g, group * g + group)
        sums = {i: None for i in mine}
        for j in range(group * g + group):
            value = [read(j, p) for p in range(pieces)]
            for i in mine:
                if j <= i:
                    weight = jnp.broadcast_to(table[j, i : i + 1, :], (8, 128))
                    terms = [weight * v for v in value]
                    sums[i] = terms if sums[i] is None else [s + t for s, t in zip(sums[i], terms)]
        for i in mine:
            for p in range(pieces):
                write(i, p, sums[i][p])


def plane_copy(src, dst, sems, z):
    return pltpu.make_async_copy(src.at[:, z], dst.at[:, z], sems.at[z])


def first_pass(cells, message, basis_hbm, first_hbm, next_message, factor_out, basis, table, accs, loads, saves):
    for z in range(NZ):
        plane_copy(basis_hbm, basis, loads, z).start()
    factor_out[...] = factor_gram(message, cells, table)
    gram_zero(accs)

    def chunk(z, carry):
        plane_copy(basis_hbm, basis, loads, z).wait()
        for l in range(2):

            def read(j, p):
                return basis[j, z, l, 8 * p : 8 * p + 8, :]

            def write(i, p, value):
                basis[i, z, l, 8 * p : 8 * p + 8, :] = value

            apply_rows(table, read, write)
        plane_copy(basis, first_hbm, saves, z).start()

        def tile(i, t):
            return jnp.concatenate([basis[i, z, l, 8 * t : 8 * t + 8, :] for l in range(2)], 1)

        gram_add([jnp.concatenate([tile(i, t) for i in range(COLS)], 0) for t in range(NX // 8)], accs)
        return carry

    lax.fori_loop(0, NZ, chunk, 0)

    gram_message(accs, next_message)
    for z in range(NZ):
        plane_copy(basis, first_hbm, saves, z).wait()


def second_pass(cells, message, factor_one, first_hbm, out_hbm, triangle, first, out, table, loads, saves):
    for z in range(NZ):
        plane_copy(first_hbm, first, loads, z).start()
    left = factor_gram(message, cells, table)[:, 0:24]
    product = lax.dot_general(
        left, factor_one[...], (((1,), (0,)), ((), ())), precision=HIGHEST, preferred_element_type=F32
    )
    triangle[...] = product[0:COLS, 0:COLS]

    def chunk(z, carry):
        plane_copy(first_hbm, first, loads, z).wait()
        for l in range(2):

            def read(j, p):
                return first[j, z, l, 8 * p : 8 * p + 8, :]

            def write(i, p, value):
                out[i, z, 8 * p : 8 * p + 8, 128 * l : 128 * l + 128] = value

            apply_rows(table, read, write)
        plane_copy(out, out_hbm, saves, z).start()
        return carry

    lax.fori_loop(0, NZ, chunk, 0)
    for z in range(NZ):
        plane_copy(out, out_hbm, saves, z).wait()


def shape(*dims):
    return jax.ShapeDtypeStruct(dims, F32)


def move(value, axis, delta):
    count = lax.axis_size(axis)
    pairs = [(i, i + delta) for i in range(count) if 0 <= i + delta < count]
    return lax.ppermute(value, axis, pairs)


def exchange(messages):
    return lax.all_to_all(messages, AXES, 0, 0, tiled=True)


def body(rhs, coef_x, coef_y, coef_z, diag_term):
    n_x = lax.axis_size("gx")
    devices = n_x * lax.axis_size("gy") * lax.axis_size("gz")
    cells = float(NZ * NX * NY * devices)
    at_x = lax.axis_index("gx")
    swap = n_x == 2
    fields = (rhs, coef_z, coef_x, coef_y, diag_term)

    place = at_x.astype(jnp.int32).reshape(1)
    face_shape = shape(FACE, NX, NY)
    x_shape = shape(FIELDS, NZ // 2, 8, NY)
    zlo, zhi, *xmsgs = pl.pallas_call(
        functools.partial(pack_faces, swap),
        out_shape=(face_shape, face_shape) + (x_shape,) * (1 if swap else 2),
        in_specs=[smem()] + [hbm()] * 5,
        out_specs=(hbm(), hbm()) + (vmem(),) * (1 if swap else 2),
        scratch_shapes=[
            pltpu.VMEM((FIELDS, NZ, NX, NY), F32),
            pltpu.SemaphoreType.DMA((FIELDS,)),
            pltpu.SemaphoreType.DMA((2 * FIELDS,)),
        ],
        compiler_params=params(LIMIT),
        cost_estimate=cost(2.5),
    )(place, *fields)
    facehi = move(zlo, "gz", -1)
    facelo = move(zhi, "gz", 1)
    if swap:
        x_parts = (lax.ppermute(xmsgs[0], "gx", [(0, 1), (1, 0)]),)
    else:
        x_parts = (move(xmsgs[0], "gx", -1), move(xmsgs[1], "gx", 1))

    own_shape = shape(NX, NY)
    own_rims = pl.pallas_call(
        pack_own_rims,
        out_shape=(own_shape, own_shape),
        in_specs=[vmem()] * 5,
        compiler_params=params(LIMIT),
        cost_estimate=cost(2.5),
    )(*fields)
    rim_shape = shape(ROWS, NY)
    ylo, yhi = pl.pallas_call(
        functools.partial(pack_rims, swap),
        out_shape=(rim_shape, rim_shape),
        in_specs=[smem()] + [vmem()] * (2 + len(x_parts)),
        compiler_params=params(16),
        cost_estimate=cost(1),
    )(place, *own_rims, *x_parts)
    yup, ydn = move(ylo, "gy", -1), move(yhi, "gy", 1)

    def rim(half):
        near, far, odd = ((0, 1, 0), (3, 2, 1))[half]
        rows = []
        for part in x_parts:
            rows.append(part[:, near].reshape(NEAR, NY))
            rows.append(part[: FAR // 4, far, 4 * odd : 4 * odd + 4].reshape(FAR, NY))
        lanes = slice(128 * half, 128 * half + 128)
        return jnp.concatenate(rows + [jnp.concatenate([yup[:, lanes], ydn[:, lanes]], 1)], 0)

    rimhi, rimlo = move(rim(0), "gz", -1), move(rim(1), "gz", 1)

    inner_shape = shape(COLS, NZ, LT, EROWS, 128)
    inner_faces_shape = shape(7, NZ - 2, LT, ROWS, 128)
    inner, inner_faces = pl.pallas_call(
        functools.partial(krylov_inner, swap),
        out_shape=(inner_shape, inner_faces_shape),
        in_specs=[smem()] + [hbm()] * 5 + [vmem()] * (len(x_parts) + 2),
        out_specs=(hbm(), hbm()),
        scratch_shapes=[
            pltpu.VMEM(inner_shape.shape, F32),
            pltpu.VMEM(inner_faces_shape.shape, F32),
            pltpu.SemaphoreType.DMA((10,)),
            pltpu.SemaphoreType.DMA((7,)),
        ],
        compiler_params=params(LIMIT),
        cost_estimate=cost(7),
    )(place, *fields, *x_parts, yup, ydn)

    block = shape(COLS, NZ, 2, NX, 128)
    basis, message = pl.pallas_call(
        functools.partial(krylov_outer, swap),
        out_shape=(block, shape(devices, 2, 128)),
        in_specs=[hbm(), hbm(), smem(), hbm(), hbm(), vmem(), vmem()],
        out_specs=(hbm(), vmem()),
        scratch_shapes=[
            pltpu.VMEM((COLS + NRHS, EZ, LT, EROWS, 128), F32),
            pltpu.VMEM((7, EZ, LT, ROWS, 128), F32),
            pltpu.VMEM((2, STACK, STACK), F32),
            pltpu.SemaphoreType.DMA((4 * FIELDS,)),
            pltpu.SemaphoreType.DMA((7,)),
            pltpu.SemaphoreType.DMA((STEPS + 1,)),
        ],
        compiler_params=params(LIMIT),
        cost_estimate=cost(15),
    )(facelo, facehi, place, inner, inner_faces, rimlo, rimhi)

    message = exchange(message)
    first, message, factor_one = pl.pallas_call(
        functools.partial(first_pass, cells),
        out_shape=(block, shape(devices, 2, 128), shape(24, 128)),
        in_specs=[vmem(), hbm()],
        out_specs=(hbm(), vmem(), vmem()),
        scratch_shapes=[
            pltpu.VMEM(block.shape, F32),
            pltpu.VMEM((COLS, 24, 128), F32),
            pltpu.VMEM((2, STACK, STACK), F32),
            pltpu.SemaphoreType.DMA((NZ,)),
            pltpu.SemaphoreType.DMA((NZ,)),
        ],
        compiler_params=params(LIMIT),
    )(message, basis)

    message = exchange(message)
    return pl.pallas_call(
        functools.partial(second_pass, cells),
        out_shape=(shape(COLS, NZ, NX, NY), shape(COLS, COLS)),
        in_specs=[vmem(), vmem(), hbm()],
        out_specs=(hbm(), vmem()),
        scratch_shapes=[
            pltpu.VMEM(block.shape, F32),
            pltpu.VMEM((COLS, NZ, NX, NY), F32),
            pltpu.VMEM((COLS, 24, 128), F32),
            pltpu.SemaphoreType.DMA((NZ,)),
            pltpu.SemaphoreType.DMA((NZ,)),
        ],
        compiler_params=params(LIMIT),
    )(message, factor_one, first)


def solution(mesh):
    return jax.shard_map(
        body,
        mesh=mesh,
        in_specs=(
            P(None, "gz", "gx", "gy"),
            P("gz", "gx", "gy"),
            P("gz", "gx", "gy"),
            P("gz", "gx", "gy"),
            P("gz", "gx", "gy"),
        ),
        out_specs=(P(None, "gz", "gx", "gy"), P()),
        check_vma=False,
    )
```

```python
import functools

import jax
import jax.numpy as jnp
from jax import lax
from jax.experimental import pallas as pl
from jax.experimental.pallas import tpu as pltpu
from jax.sharding import PartitionSpec as P

NRHS = 4
STEPS = 4
COLS = NRHS * (STEPS + 1)
SHIFTS = (3.0, 11.0, 7.0, 1.5)
SCALE = 1.0 / 6.0
FIELDS = NRHS + 4
AXES = ("gx", "gy", "gz")
HIGHEST = lax.Precision.HIGHEST

DEPTH = 4
NZ, NX, NY = 8, 32, 256
EZ = NZ + 2 * DEPTH
ROWS = NX + 8
EROWS = ROWS + 16
LT = 3
FACE = NRHS * 4 + 3 * 4 + 1
F32 = jnp.float32
LIMIT = 63


def params(mb):
    return pltpu.CompilerParams(vmem_limit_bytes=mb << 20)


def cost(us):
    return pl.CostEstimate(flops=0, bytes_accessed=int(us * 3.6e6), transcendentals=0)


def vmem():
    return pl.BlockSpec(memory_space=pltpu.VMEM)


def smem():
    return pl.BlockSpec(memory_space=pltpu.SMEM)


def hbm():
    return pl.BlockSpec(memory_space=pl.ANY)


def row_ids(shape):
    return lax.broadcasted_iota(jnp.int32, shape, 0)


def lane_ids(shape):
    return lax.broadcasted_iota(jnp.int32, shape, 1)


def field_of(rhs, cz, cx, cy, dg, f, z):
    return rhs.at[f, z] if f < NRHS else (cz, cx, cy, dg)[f - NRHS].at[z]


def pack_faces(swap, place, rhs, cz, cx, cy, dg, zlo, zhi, *rest):
    xmsgs, (whole, loads, saves) = rest[:-3], rest[-3:]
    copies = []
    for f in range(FIELDS):
        src = rhs.at[f] if f < NRHS else (cz, cx, cy, dg)[f - NRHS]
        copies.append(pltpu.make_async_copy(src, whole.at[f], loads.at[f]))
        copies[-1].start()
    low = row_ids((8, NY)) < 4
    up = place[0] == 0
    planes = []
    at = 0
    for f in range(FIELDS):
        copies[f].wait()
        depth = DEPTH if f <= NRHS else DEPTH - 1
        for side, out in ((0, zlo), (1, zhi)):
            start = side * (NZ - depth)
            planes.append(
                pltpu.make_async_copy(
                    whole.at[f, pl.ds(start, depth)], out.at[pl.ds(at, depth)], saves.at[2 * f + side]
                )
            )
            planes[-1].start()
        at += depth
        for m in range(NZ // 2):
            a, b = whole.at[f, 2 * m], whole.at[f, 2 * m + 1]
            first = jnp.where(low, a[0:8], pltpu.roll(b[0:8], 4, 0))
            last = jnp.where(low, pltpu.roll(a[NX - 8 : NX], 4, 0), b[NX - 8 : NX])
            if swap:
                xmsgs[0][f, m] = jnp.where(up, last, first)
            else:
                xmsgs[0][f, m] = first
                xmsgs[1][f, m] = last
    for copy in planes:
        copy.wait()


def halo_tile(above, below, odd, keep_up, keep_dn):
    low = row_ids(above.shape) < 4
    if odd:
        up, dn = pltpu.roll(above, 4, 0), below
    else:
        up, dn = above, pltpu.roll(below, 4, 0)
    return jnp.where(low, up * keep_up, dn * keep_dn)


def keep_sides(swap, place):
    if not swap:
        return 1.0, 1.0
    first = place[0] == 0
    return jnp.where(first, 1.0, 0.0), jnp.where(first, 0.0, 1.0)


def pack_lanes(tile_of, side):
    lane = lane_ids((8, 128))
    source = 124 * side
    acc = jnp.zeros((8, 128), F32)
    for zz in range(4):
        for f in range(FIELDS):
            tile = tile_of(f, zz)
            spot = (zz * FIELDS + f) * 4
            shift = (spot - source) % 128
            if shift:
                tile = pltpu.roll(tile, shift, 1)
            acc = jnp.where((lane >= spot) & (lane < spot + 4), tile, acc)
    return acc


def pack_own_rims(rhs, cz, cx, cy, dg, ylo, yhi):
    for t in range(NX // 8):
        for side, out in ((0, ylo), (1, yhi)):
            for half in range(2):
                out[8 * t : 8 * t + 8, 128 * half : 128 * half + 128] = pack_lanes(
                    lambda f, zz: field_of(rhs, cz, cx, cy, dg, f, 4 * half + zz)[
                        8 * t : 8 * t + 8, 128 * side : 128 * side + 128
                    ],
                    side,
                )


def pack_rims(swap, place, ylo_own, yhi_own, *refs):
    above, below, ylo, yhi = refs if not swap else (refs[0],) + refs
    keep_up, keep_dn = keep_sides(swap, place)
    for side, own, out in ((0, ylo_own, ylo), (1, yhi_own, yhi)):
        out[0:NX, :] = own[...]
        lanes = slice(128 * side, 128 * side + 128)
        for half in range(2):
            out[NX:ROWS, 128 * half : 128 * half + 128] = pack_lanes(
                lambda f, zz: halo_tile(
                    above[f, 2 * half + zz // 2, :, lanes], below[f, 2 * half + zz // 2, :, lanes], zz % 2, keep_up, keep_dn
                ),
                side,
            )


STACK = 8 * COLS


def gram_zero(accs):
    accs[...] = jnp.zeros_like(accs)


def gram_add(stacks, accs):
    left, right = [], []
    cross_left, cross_right = [], []
    for stack in stacks:
        high = stack.astype(jnp.bfloat16)
        rest = stack - high.astype(F32)
        mid = rest.astype(jnp.bfloat16)
        low = (rest - mid.astype(F32)).astype(jnp.bfloat16)
        left += [high, mid]
        cross_left += [high, high]
        cross_right += [mid, low]
    contract = (((1,), (1,)), ((), ()))

    def product(a, b):
        return lax.dot_general(jnp.concatenate(a, 1), jnp.concatenate(b, 1), contract, preferred_element_type=F32)

    accs[0] += product(left, left)
    accs[1] += product(cross_left, cross_right)


def gram_message(accs, out):
    same = (row_ids((STACK, STACK)) & 7) == (lane_ids((STACK, STACK)) & 7)
    pick = jnp.where((row_ids((STACK, 128)) >> 3) == lane_ids((STACK, 128)), 1.0, 0.0)

    def traces(product):
        picked = jnp.where(same, product, 0.0)
        rows = [jnp.sum(picked[8 * i : 8 * i + 8], axis=0, keepdims=True) for i in range(COLS)]
        rows = jnp.concatenate(rows + [jnp.zeros((128 - COLS, STACK), F32)], 0)
        return lax.dot_general(
            rows, pick, (((1,), (0,)), ((), ())), precision=HIGHEST, preferred_element_type=F32
        )

    cross = traces(accs[1])
    gram = traces(accs[0]) + cross + cross.T
    tops = [gram[8 * k : 8 * k + 8] for k in range(3)]
    rows, lanes = row_ids((8, 128)), lane_ids((8, 128))
    tile = jnp.where(lanes < COLS, tops[0], pltpu.roll(tops[1], 12, 1))
    corner = pltpu.roll(pltpu.roll(tops[2], 128 - 16, 1), 4, 0)
    tile = jnp.where((rows >= 4) & (lanes < 4), corner, tile)
    packed = tile
    for q in range(1, 4):
        turned = pltpu.roll(pltpu.roll(tile, 32 * q, 1), 8 - 2 * q, 0)
        packed = jnp.where((lanes >> 5) == q, turned, packed)
    packed = packed[0:2]
    for n in range(out.shape[0]):
        out[n] = packed


def gram_of(messages):
    total = messages[0]
    for n in range(1, messages.shape[0]):
        total = total + messages[n]
    total = jnp.concatenate([total] * 4, 0)
    rows, lanes = row_ids((8, 128)), lane_ids((8, 128))
    tile = total
    for q in range(1, 4):
        tile = jnp.where((rows >> 1) == q, pltpu.roll(total, 128 - 32 * q, 1), tile)
    corner = pltpu.roll(pltpu.roll(tile, 4, 0), 16, 1)
    tops = [
        jnp.where((lanes < COLS) & (lanes >= rows), tile, 0.0),
        jnp.where((lanes < COLS) & (lanes >= rows + 8), pltpu.roll(tile, 128 - 12, 1), 0.0),
        jnp.where((lanes < COLS) & (lanes >= rows + 16), corner, 0.0),
    ]
    return jnp.concatenate(tops, 0)


def slot(k):
    return k * NRHS + (NRHS if k else 0)


class Block:
    def __init__(self, stores, base, faces, faces_base):
        self.stores, self.base, self.faces, self.faces_base = stores, base, faces, faces_base
        self.lane = lane_ids((8, 128))

    def put(self, f, z, l, t, value):
        store, f, z = self.stores[f // NRHS], f % NRHS, z - self.base
        store[f, z, l, 8 + 8 * t : 16 + 8 * t, :] = value
        if t == 0:
            store[f, z, l, 8 + ROWS : 16 + ROWS, :] = value
        if t == ROWS // 8 - 1:
            store[f, z, l, 0:8, :] = value

    def place_y(self, z, up, dn):
        for t in range(ROWS // 8):
            u_all, d_all = up[8 * t : 8 * t + 8, :], dn[8 * t : 8 * t + 8, :]
            for zz in range(4):
                for f in range(FIELDS):
                    spot = (zz * FIELDS + f) * 4
                    u = pltpu.roll(u_all, (-spot) % 128, 1) if spot else u_all
                    d = pltpu.roll(d_all, (124 - spot) % 128, 1) if spot != 124 else d_all
                    value = jnp.where(self.lane < 4, u, jnp.where(self.lane >= 124, d, 0.0))
                    self.put(f, z + zz, 2, t, value)

    def tiles(self, f, z, t, off):
        store, f, z = self.stores[f // NRHS], f % NRHS, z - self.base
        return [store[f, z, l, pl.ds(8 + 8 * t + off, 8), :] for l in range(LT)]

    def close_ring(self, f, z):
        store, f, z = self.stores[f // NRHS], f % NRHS, z - self.base
        for l in range(2):
            store[f, z, l, 8 + ROWS : 16 + ROWS, :] = store[f, z, l, 8:16, :]

    def lane_up(self, tri):
        rolled = [pltpu.roll(v, 127, 1) for v in tri]
        return [jnp.where(self.lane == 127, rolled[(l + 1) % LT], rolled[l]) for l in range(LT)]

    def lane_dn(self, tri):
        rolled = [pltpu.roll(v, 1, 1) for v in tri]
        return [jnp.where(self.lane == 0, rolled[(l - 1) % LT], rolled[l]) for l in range(LT)]

    def coefficients(self, z):
        for t in range(ROWS // 8):
            kz, kx, ky, kd = (NRHS + i for i in range(4))
            center_z, center_x, center_y = (self.tiles(k, z, t, 0) for k in (kz, kx, ky))
            diag = self.tiles(kd, z, t, 0)
            sides = [
                (center_z, self.tiles(kz, z + 1, t, 0)),
                (center_z, self.tiles(kz, z - 1, t, 0)),
                (center_x, self.tiles(kx, z, t, 1)),
                (center_x, self.tiles(kx, z, t, -1)),
                (center_y, self.lane_up(center_y)),
                (center_y, self.lane_dn(center_y)),
            ]
            at = z - self.faces_base
            for l in range(LT):
                inside = diag[l] > 0.0
                total = diag[l] * SCALE
                for k, (mid, side) in enumerate(sides):
                    face = (mid[l] + side[l]) * (0.5 * SCALE)
                    total = total + face
                    self.faces[k, at, l, 8 * t : 8 * t + 8, :] = jnp.where(inside, face, 0.0)
                self.faces[6, at, l, 8 * t : 8 * t + 8, :] = jnp.where(inside, total, 0.0)

    def apply(self, k, z):
        last = k == STEPS - 1
        at = z - self.faces_base
        outs = 2 if last else LT
        for t in range(NX // 8 if last else ROWS // 8):
            face = [[self.faces[c, at, l, 8 * t : 8 * t + 8, :] for l in range(outs)] for c in range(7)]
            diag = [face[6][l] - SHIFTS[k] * SCALE for l in range(outs)]
            for r in range(NRHS):
                f = slot(k) + r
                mid = self.tiles(f, z, t, 0)
                sides = [
                    self.tiles(f, z + 1, t, 0),
                    self.tiles(f, z - 1, t, 0),
                    self.tiles(f, z, t, 1),
                    self.tiles(f, z, t, -1),
                    self.lane_up(mid),
                    self.lane_dn(mid),
                ]
                for l in range(outs):
                    value = diag[l] * mid[l]
                    for c in range(6):
                        value = value - face[c][l] * sides[c][l]
                    self.put(slot(k + 1) + r, z, l, t, value)


def loop(start, stop, do):
    def step(n, carry):
        do(n)
        return carry

    lax.fori_loop(start, stop, step, 0)


def inner_planes(k):
    return DEPTH + k, DEPTH + NZ - k


def inner_copies(inner, inner_faces, stores, base, faces, faces_base, sems, out):
    def copy(n, there, here):
        src, dst = (here, there) if out else (there, here)
        return pltpu.make_async_copy(src, dst, sems.at[n])

    def planes(ref, f, start, stop, at):
        return ref.at[pl.ds(f, NRHS), pl.ds(start - at, stop - start)]

    result = []
    for n, (f, start, stop) in enumerate(
        [(0, DEPTH, DEPTH + NZ), (NRHS, DEPTH, DEPTH + 2), (NRHS, DEPTH + NZ - 2, DEPTH + NZ)]
        + [(slot(k), *inner_planes(k)) for k in range(1, STEPS)]
    ):
        there = planes(inner, f, start, stop, DEPTH)
        result.append(copy(n, there, stores[f // NRHS].at[:, pl.ds(start - base, stop - start)]))
    start, stop = inner_planes(1)
    result.append(copy(len(result), inner_faces, faces.at[:, pl.ds(start - faces_base, stop - start)]))
    return result


def krylov_inner(swap, place, rhs, cz, cx, cy, dg, *rest):
    above, below, yup, ydn, inner, inner_faces, *stores, faces, load_sems, sems = rest if not swap else rest[:1] + rest
    keep_up, keep_dn = keep_sides(swap, place)
    block = Block(stores, DEPTH, faces, DEPTH + 1)
    loads = []
    for n, src in enumerate((rhs, cz, cx, cy, dg)):
        for l in range(2):
            lanes = pl.ds(128 * l, 128)
            rows = pl.ds(8, NX)
            if n == 0:
                src_at, dst = src.at[:, :, :, lanes], stores[0].at[:, :, l, rows, :]
            else:
                src_at, dst = src.at[:, :, lanes], stores[1].at[n - 1, :, l, rows, :]
            loads.append(pltpu.make_async_copy(src_at, dst, load_sems.at[2 * n + l]))
            loads[-1].start()
    for f in range(FIELDS):
        for z in range(DEPTH, DEPTH + NZ):
            m = (z - DEPTH) // 2
            for l in range(2):
                lanes = pl.ds(128 * l, 128)
                tile = halo_tile(above[f, m, :, lanes], below[f, m, :, lanes], z % 2, keep_up, keep_dn)
                block.put(f, z, l, NX // 8, tile)
    for half in range(2):
        lanes = pl.ds(128 * half, 128)
        block.place_y(DEPTH + 4 * half, yup.at[:, lanes], ydn.at[:, lanes])
    for copy in loads:
        copy.wait()
    for f in range(FIELDS):
        for z in range(DEPTH, DEPTH + NZ):
            block.close_ring(f, z)
    copies = inner_copies(inner, inner_faces, stores, DEPTH, faces, DEPTH + 1, sems, True)
    for n in range(3):
        copies[n].start()
    loop(*inner_planes(1), block.coefficients)
    copies[-1].start()
    for k in range(STEPS - 1):
        loop(*inner_planes(k + 1), functools.partial(block.apply, k))
        copies[3 + k].start()
    for copy in copies:
        copy.wait()


NEAR, FAR = 8 * FIELDS, 24


def krylov_outer(
    swap, facelo, facehi, place, inner, inner_faces, rimlo, rimhi,
    basis, message,
    *rest,
):
    keep_up, keep_dn = keep_sides(swap, place)
    n_x = 1 if swap else 2
    *stores, faces, accs, plane_sems, loads, saves = rest
    block = Block(stores, 0, faces, 0)
    copies = inner_copies(inner, inner_faces, stores, 0, faces, 0, loads, False)
    planes = []
    start = 0
    for f in range(FIELDS):
        depth = DEPTH if f <= NRHS else DEPTH - 1
        for side, (face, z) in enumerate(((facelo, DEPTH - depth), (facehi, DEPTH + NZ))):
            for l in range(2):
                planes.append(
                    pltpu.make_async_copy(
                        face.at[pl.ds(start, depth), :, pl.ds(128 * l, 128)],
                        stores[f // NRHS].at[f % NRHS, pl.ds(z, depth), l, pl.ds(8, NX), :],
                        plane_sems.at[4 * f + 2 * side + l],
                    )
                )
        start += depth
    for copy in copies[:3] + planes:
        copy.start()

    zero = jnp.zeros((8, 128), F32)
    for f in range(FIELDS):
        for rim, first in ((rimlo, 0), (rimhi, DEPTH + NZ)):
            for z in range(first, first + DEPTH):
                far = DEPTH - z if first == 0 else z - first + 1
                for l in range(2):
                    lanes = pl.ds(128 * l, 128)
                    if far <= 2:
                        at, odd = 8 * f, z % 2
                    elif far == 3 and 8 * (f // 2) < FAR:
                        at, odd = NEAR + 8 * (f // 2), f % 2
                    else:
                        block.put(f, z, l, NX // 8, zero)
                        continue
                    other = at + (n_x - 1) * (NEAR + FAR)
                    tile = halo_tile(rim[at : at + 8, lanes], rim[other : other + 8, lanes], odd, keep_up, keep_dn)
                    block.put(f, z, l, NX // 8, tile)
    rows = pl.ds(n_x * (NEAR + FAR), ROWS)
    for rim, z in ((rimlo, 0), (rimhi, DEPTH + NZ)):
        block.place_y(z, rim.at[rows, pl.ds(0, 128)], rim.at[rows, pl.ds(128, 128)])

    for copy in copies[:3] + planes:
        copy.wait()
    for copy in copies[3:]:
        copy.start()
    for f in range(FIELDS):
        depth = DEPTH if f <= NRHS else DEPTH - 1
        for d in range(depth):
            block.close_ring(f, DEPTH - 1 - d)
            block.close_ring(f, DEPTH + NZ + d)
    loop(1, DEPTH + 1, block.coefficients)
    loop(DEPTH + NZ - 1, EZ - 1, block.coefficients)

    sends = []

    def send_block(k):
        copy = pltpu.make_async_copy(
            stores[slot(k) // NRHS].at[:, pl.ds(DEPTH, NZ), pl.ds(0, 2), pl.ds(8, NX), :],
            basis.at[pl.ds(k * NRHS, NRHS)],
            saves.at[k],
        )
        copy.start()
        sends.append(copy)

    send_block(0)
    for k in range(STEPS):
        if k == 1:
            copies[-1].wait()
        loop(
            0,
            2 * DEPTH,
            lambda n, k=k: block.apply(k, n + k + 1 + jnp.where(n >= DEPTH, NZ - 2 - 2 * k, 0)),
        )
        if k < STEPS - 1:
            copies[3 + k].wait()
        send_block(k + 1)
    gram_zero(accs)

    def products(z):
        def tile(i, t):
            store = stores[slot(i // NRHS) // NRHS]
            return jnp.concatenate([store[i % NRHS, z, l, 8 + 8 * t : 16 + 8 * t, :] for l in range(2)], 1)

        gram_add([jnp.concatenate([tile(i, t) for i in range(COLS)], 0) for t in range(NX // 8)], accs)

    loop(DEPTH, DEPTH + NZ, products)
    gram_message(accs, message)
    for copy in sends:
        copy.wait()


def factor_gram(messages, cells, table):
    rows = row_ids((24, 128))
    lanes = lane_ids((24, 128))
    upper = gram_of(messages) / cells
    square = jnp.concatenate([upper, jnp.zeros((104, 128), F32)], 0).T
    whole = jnp.where(rows <= lanes, upper, square[0:24, :])

    def splat(value):
        return jnp.broadcast_to(value, (24, 128))

    columns = [splat(whole[:, c : c + 1]) for c in range(COLS)]
    inverse = [jnp.where(rows == c, 1.0, 0.0) for c in range(COLS)]
    pivots = jnp.ones((24, 128), F32)
    factor = jnp.zeros((24, 128), F32)
    for j in range(COLS):
        pivot = splat(columns[j][j : j + 1, :])
        pivots = jnp.where(rows == j, pivot, pivots)
        below = jnp.where(rows > j, columns[j] / pivot, 0.0)
        for c in range(j, COLS):
            row = splat(columns[c][j : j + 1, :])
            factor = jnp.where((rows == j) & (lanes == c), row, factor)
            if c > j:
                columns[c] = columns[c] - below * row
        for c in range(j + 1):
            inverse[c] = inverse[c] - below * splat(inverse[c][j : j + 1, :])
    roots = jnp.sqrt(pivots)
    for c in range(COLS):
        table[c] = inverse[c] / roots
    return factor / roots


def apply_rows(table, read, write):
    group = 5
    pieces = NX // 8
    for g in reversed(range(COLS // group)):
        mine = range(group * g, group * g + group)
        sums = {i: None for i in mine}
        for j in range(group * g + group):
            value = [read(j, p) for p in range(pieces)]
            for i in mine:
                if j <= i:
                    weight = jnp.broadcast_to(table[j, i : i + 1, :], (8, 128))
                    terms = [weight * v for v in value]
                    sums[i] = terms if sums[i] is None else [s + t for s, t in zip(sums[i], terms)]
        for i in mine:
            for p in range(pieces):
                write(i, p, sums[i][p])


def plane_copy(src, dst, sems, z):
    return pltpu.make_async_copy(src.at[:, z], dst.at[:, z], sems.at[z])


def first_pass(
    cells, message, basis_hbm, first_hbm, next_message, factor_out, basis, first, table, accs, loads, saves
):
    for z in range(NZ):
        plane_copy(basis_hbm, basis, loads, z).start()
    factor_out[...] = factor_gram(message, cells, table)
    gram_zero(accs)

    def products(z):
        def tile(i, t):
            return jnp.concatenate([first[i, z, l, 8 * t : 8 * t + 8, :] for l in range(2)], 1)

        gram_add([jnp.concatenate([tile(i, t) for i in range(COLS)], 0) for t in range(NX // 8)], accs)

    def apply(z):
        for l in range(2):

            def read(j, p):
                return basis[j, z, l, 8 * p : 8 * p + 8, :]

            def write(i, p, value):
                first[i, z, l, 8 * p : 8 * p + 8, :] = value

            apply_rows(table, read, write)
        plane_copy(first, first_hbm, saves, z).start()

    def both(z):
        plane_copy(basis_hbm, basis, loads, z).wait()
        products(z - 1)
        apply(z)

    plane_copy(basis_hbm, basis, loads, 0).wait()
    apply(0)
    loop(1, NZ, both)
    products(NZ - 1)
    gram_message(accs, next_message)
    for z in range(NZ):
        plane_copy(first, first_hbm, saves, z).wait()


def second_pass(cells, message, factor_one, first_hbm, out_hbm, triangle, first, out, table, loads, saves):
    for z in range(NZ):
        plane_copy(first_hbm, first, loads, z).start()
    left = factor_gram(message, cells, table)[:, 0:24]
    product = lax.dot_general(
        left, factor_one[...], (((1,), (0,)), ((), ())), precision=HIGHEST, preferred_element_type=F32
    )
    triangle[...] = product[0:COLS, 0:COLS]

    def chunk(z, carry):
        plane_copy(first_hbm, first, loads, z).wait()
        for l in range(2):

            def read(j, p):
                return first[j, z, l, 8 * p : 8 * p + 8, :]

            def write(i, p, value):
                out[i, z, 8 * p : 8 * p + 8, 128 * l : 128 * l + 128] = value

            apply_rows(table, read, write)
        plane_copy(out, out_hbm, saves, z).start()
        return carry

    lax.fori_loop(0, NZ, chunk, 0)
    for z in range(NZ):
        plane_copy(out, out_hbm, saves, z).wait()


def shape(*dims):
    return jax.ShapeDtypeStruct(dims, F32)


def move(value, axis, delta):
    count = lax.axis_size(axis)
    pairs = [(i, i + delta) for i in range(count) if 0 <= i + delta < count]
    return lax.ppermute(value, axis, pairs)


def exchange(messages):
    return lax.all_to_all(messages, AXES, 0, 0, tiled=True)


def body(rhs, coef_x, coef_y, coef_z, diag_term):
    n_x = lax.axis_size("gx")
    devices = n_x * lax.axis_size("gy") * lax.axis_size("gz")
    cells = float(NZ * NX * NY * devices)
    at_x = lax.axis_index("gx")
    swap = n_x == 2
    fields = (rhs, coef_z, coef_x, coef_y, diag_term)

    place = at_x.astype(jnp.int32).reshape(1)
    face_shape = shape(FACE, NX, NY)
    x_shape = shape(FIELDS, NZ // 2, 8, NY)
    zlo, zhi, *xmsgs = pl.pallas_call(
        functools.partial(pack_faces, swap),
        out_shape=(face_shape, face_shape) + (x_shape,) * (1 if swap else 2),
        in_specs=[smem()] + [hbm()] * 5,
        out_specs=(hbm(), hbm()) + (vmem(),) * (1 if swap else 2),
        scratch_shapes=[
            pltpu.VMEM((FIELDS, NZ, NX, NY), F32),
            pltpu.SemaphoreType.DMA((FIELDS,)),
            pltpu.SemaphoreType.DMA((2 * FIELDS,)),
        ],
        compiler_params=params(LIMIT),
        cost_estimate=cost(2.5),
    )(place, *fields)
    facehi = move(zlo, "gz", -1)
    facelo = move(zhi, "gz", 1)
    if swap:
        x_parts = (lax.ppermute(xmsgs[0], "gx", [(0, 1), (1, 0)]),)
    else:
        x_parts = (move(xmsgs[0], "gx", -1), move(xmsgs[1], "gx", 1))

    own_shape = shape(NX, NY)
    own_rims = pl.pallas_call(
        pack_own_rims,
        out_shape=(own_shape, own_shape),
        in_specs=[vmem()] * 5,
        compiler_params=params(LIMIT),
        cost_estimate=cost(2.5),
    )(*fields)
    rim_shape = shape(ROWS, NY)
    ylo, yhi = pl.pallas_call(
        functools.partial(pack_rims, swap),
        out_shape=(rim_shape, rim_shape),
        in_specs=[smem()] + [vmem()] * (2 + len(x_parts)),
        compiler_params=params(16),
        cost_estimate=cost(1),
    )(place, *own_rims, *x_parts)
    yup, ydn = move(ylo, "gy", -1), move(yhi, "gy", 1)

    def rim(half):
        near, far, odd = ((0, 1, 0), (3, 2, 1))[half]
        rows = []
        for part in x_parts:
            rows.append(part[:, near].reshape(NEAR, NY))
            rows.append(part[: FAR // 4, far, 4 * odd : 4 * odd + 4].reshape(FAR, NY))
        lanes = slice(128 * half, 128 * half + 128)
        return jnp.concatenate(rows + [jnp.concatenate([yup[:, lanes], ydn[:, lanes]], 1)], 0)

    rimhi, rimlo = move(rim(0), "gz", -1), move(rim(1), "gz", 1)

    inner_shape = shape(COLS, NZ, LT, EROWS, 128)
    inner_faces_shape = shape(7, NZ - 2, LT, ROWS, 128)
    inner, inner_faces = pl.pallas_call(
        functools.partial(krylov_inner, swap),
        out_shape=(inner_shape, inner_faces_shape),
        in_specs=[smem()] + [hbm()] * 5 + [vmem()] * (len(x_parts) + 2),
        out_specs=(hbm(), hbm()),
        scratch_shapes=[
            *[pltpu.VMEM((NRHS,) + inner_shape.shape[1:], F32)] * (STEPS + 1),
            pltpu.VMEM(inner_faces_shape.shape, F32),
            pltpu.SemaphoreType.DMA((10,)),
            pltpu.SemaphoreType.DMA((7,)),
        ],
        compiler_params=params(LIMIT),
        cost_estimate=cost(7),
    )(place, *fields, *x_parts, yup, ydn)

    block = shape(COLS, NZ, 2, NX, 128)
    basis, message = pl.pallas_call(
        functools.partial(krylov_outer, swap),
        out_shape=(block, shape(devices, 2, 128)),
        in_specs=[hbm(), hbm(), smem(), hbm(), hbm(), vmem(), vmem()],
        out_specs=(hbm(), vmem()),
        scratch_shapes=[
            *[pltpu.VMEM((NRHS, EZ, LT, EROWS, 128), F32)] * (STEPS + 2),
            pltpu.VMEM((7, EZ, LT, ROWS, 128), F32),
            pltpu.VMEM((2, STACK, STACK), F32),
            pltpu.SemaphoreType.DMA((4 * FIELDS,)),
            pltpu.SemaphoreType.DMA((7,)),
            pltpu.SemaphoreType.DMA((STEPS + 1,)),
        ],
        compiler_params=params(LIMIT),
        cost_estimate=cost(15),
    )(facelo, facehi, place, inner, inner_faces, rimlo, rimhi)

    message = exchange(message)
    first, message, factor_one = pl.pallas_call(
        functools.partial(first_pass, cells),
        out_shape=(block, shape(devices, 2, 128), shape(24, 128)),
        in_specs=[vmem(), hbm()],
        out_specs=(hbm(), vmem(), vmem()),
        scratch_shapes=[
            pltpu.VMEM(block.shape, F32),
            pltpu.VMEM(block.shape, F32),
            pltpu.VMEM((COLS, 24, 128), F32),
            pltpu.VMEM((2, STACK, STACK), F32),
            pltpu.SemaphoreType.DMA((NZ,)),
            pltpu.SemaphoreType.DMA((NZ,)),
        ],
        compiler_params=params(LIMIT),
    )(message, basis)

    message = exchange(message)
    return pl.pallas_call(
        functools.partial(second_pass, cells),
        out_shape=(shape(COLS, NZ, NX, NY), shape(COLS, COLS)),
        in_specs=[vmem(), vmem(), hbm()],
        out_specs=(hbm(), vmem()),
        scratch_shapes=[
            pltpu.VMEM(block.shape, F32),
            pltpu.VMEM((COLS, NZ, NX, NY), F32),
            pltpu.VMEM((COLS, 24, 128), F32),
            pltpu.SemaphoreType.DMA((NZ,)),
            pltpu.SemaphoreType.DMA((NZ,)),
        ],
        compiler_params=params(LIMIT),
    )(message, factor_one, first)


def solution(mesh):
    return jax.shard_map(
        body,
        mesh=mesh,
        in_specs=(
            P(None, "gz", "gx", "gy"),
            P("gz", "gx", "gy"),
            P("gz", "gx", "gy"),
            P("gz", "gx", "gy"),
            P("gz", "gx", "gy"),
        ),
        out_specs=(P(None, "gz", "gx", "gy"), P()),
        check_vma=False,
    )
```

```python
import functools

import jax
import jax.numpy as jnp
from jax import lax
from jax.experimental import pallas as pl
from jax.experimental.pallas import tpu as pltpu
from jax.sharding import PartitionSpec as P

NRHS = 4
STEPS = 4
COLS = NRHS * (STEPS + 1)
SHIFTS = (3.0, 11.0, 7.0, 1.5)
SCALE = 1.0 / 6.0
FIELDS = NRHS + 4
AXES = ("gx", "gy", "gz")
HIGHEST = lax.Precision.HIGHEST

DEPTH = 4
NZ, NX, NY = 8, 32, 256
EZ = NZ + 2 * DEPTH
ROWS = NX + 8
EROWS = ROWS + 16
LT = 3
FACE = NRHS * 4 + 3 * 4 + 1
F32 = jnp.float32
LIMIT = 63


def params(mb):
    return pltpu.CompilerParams(vmem_limit_bytes=mb << 20)


def cost(us):
    return pl.CostEstimate(flops=0, bytes_accessed=int(us * 3.6e6), transcendentals=0)


def vmem():
    return pl.BlockSpec(memory_space=pltpu.VMEM)


def smem():
    return pl.BlockSpec(memory_space=pltpu.SMEM)


def hbm():
    return pl.BlockSpec(memory_space=pl.ANY)


def row_ids(shape):
    return lax.broadcasted_iota(jnp.int32, shape, 0)


def lane_ids(shape):
    return lax.broadcasted_iota(jnp.int32, shape, 1)


def field_of(rhs, cz, cx, cy, dg, f, z):
    return rhs.at[f, z] if f < NRHS else (cz, cx, cy, dg)[f - NRHS].at[z]


def pack_faces(swap, place, rhs, cz, cx, cy, dg, zlo, zhi, ylo, yhi, *rest):
    xmsgs, (whole, loads, saves) = rest[:-3], rest[-3:]
    copies = []
    for f in range(FIELDS):
        src = rhs.at[f] if f < NRHS else (cz, cx, cy, dg)[f - NRHS]
        copies.append(pltpu.make_async_copy(src, whole.at[f], loads.at[f]))
        copies[-1].start()
    low = row_ids((8, NY)) < 4
    up = place[0] == 0
    planes = []
    at = 0
    for f in range(FIELDS):
        copies[f].wait()
        depth = DEPTH if f <= NRHS else DEPTH - 1
        for side, out in ((0, zlo), (1, zhi)):
            start = side * (NZ - depth)
            planes.append(
                pltpu.make_async_copy(
                    whole.at[f, pl.ds(start, depth)], out.at[pl.ds(at, depth)], saves.at[2 * f + side]
                )
            )
            planes[-1].start()
        at += depth
        for m in range(NZ // 2):
            a, b = whole.at[f, 2 * m], whole.at[f, 2 * m + 1]
            first = jnp.where(low, a[0:8], pltpu.roll(b[0:8], 4, 0))
            last = jnp.where(low, pltpu.roll(a[NX - 8 : NX], 4, 0), b[NX - 8 : NX])
            if swap:
                xmsgs[0][f, m] = jnp.where(up, last, first)
            else:
                xmsgs[0][f, m] = first
                xmsgs[1][f, m] = last
    for t in range(NX // 8):
        for side, out in ((0, ylo), (1, yhi)):
            for half in range(2):
                out[8 * t : 8 * t + 8, 128 * half : 128 * half + 128] = pack_lanes(
                    lambda f, zz: whole[f, 4 * half + zz, 8 * t : 8 * t + 8, 128 * side : 128 * side + 128], side
                )
    for copy in planes:
        copy.wait()


def halo_tile(above, below, odd, keep_up, keep_dn):
    low = row_ids(above.shape) < 4
    if odd:
        up, dn = pltpu.roll(above, 4, 0), below
    else:
        up, dn = above, pltpu.roll(below, 4, 0)
    return jnp.where(low, up * keep_up, dn * keep_dn)


def keep_sides(swap, place):
    if not swap:
        return 1.0, 1.0
    first = place[0] == 0
    return jnp.where(first, 1.0, 0.0), jnp.where(first, 0.0, 1.0)


def pack_lanes(tile_of, side):
    lane = lane_ids((8, 128))
    source = 124 * side
    acc = jnp.zeros((8, 128), F32)
    for zz in range(4):
        for f in range(FIELDS):
            tile = tile_of(f, zz)
            spot = (zz * FIELDS + f) * 4
            shift = (spot - source) % 128
            if shift:
                tile = pltpu.roll(tile, shift, 1)
            acc = jnp.where((lane >= spot) & (lane < spot + 4), tile, acc)
    return acc


def pack_rims(swap, place, ylo_own, yhi_own, *refs):
    above, below, ylo, yhi = refs if not swap else (refs[0],) + refs
    keep_up, keep_dn = keep_sides(swap, place)
    for side, own, out in ((0, ylo_own, ylo), (1, yhi_own, yhi)):
        out[0:NX, :] = own[...]
        lanes = slice(128 * side, 128 * side + 128)
        for half in range(2):
            out[NX:ROWS, 128 * half : 128 * half + 128] = pack_lanes(
                lambda f, zz: halo_tile(
                    above[f, 2 * half + zz // 2, :, lanes], below[f, 2 * half + zz // 2, :, lanes], zz % 2, keep_up, keep_dn
                ),
                side,
            )


STACK = 8 * COLS


def gram_zero(accs):
    accs[...] = jnp.zeros_like(accs)


def gram_add(stacks, accs):
    left, right = [], []
    cross_left, cross_right = [], []
    for stack in stacks:
        high = stack.astype(jnp.bfloat16)
        rest = stack - high.astype(F32)
        mid = rest.astype(jnp.bfloat16)
        low = (rest - mid.astype(F32)).astype(jnp.bfloat16)
        left += [high, mid]
        cross_left += [high, high]
        cross_right += [mid, low]
    contract = (((1,), (1,)), ((), ()))

    def product(a, b):
        return lax.dot_general(jnp.concatenate(a, 1), jnp.concatenate(b, 1), contract, preferred_element_type=F32)

    accs[0] += product(left, left)
    accs[1] += product(cross_left, cross_right)


def gram_message(accs, out):
    same = (row_ids((STACK, STACK)) & 7) == (lane_ids((STACK, STACK)) & 7)
    pick = jnp.where((row_ids((STACK, 128)) >> 3) == lane_ids((STACK, 128)), 1.0, 0.0)

    def traces(product):
        picked = jnp.where(same, product, 0.0)
        rows = [jnp.sum(picked[8 * i : 8 * i + 8], axis=0, keepdims=True) for i in range(COLS)]
        rows = jnp.concatenate(rows + [jnp.zeros((128 - COLS, STACK), F32)], 0)
        return lax.dot_general(
            rows, pick, (((1,), (0,)), ((), ())), precision=HIGHEST, preferred_element_type=F32
        )

    cross = traces(accs[1])
    gram = traces(accs[0]) + cross + cross.T
    tops = [gram[8 * k : 8 * k + 8] for k in range(3)]
    rows, lanes = row_ids((8, 128)), lane_ids((8, 128))
    tile = jnp.where(lanes < COLS, tops[0], pltpu.roll(tops[1], 12, 1))
    corner = pltpu.roll(pltpu.roll(tops[2], 128 - 16, 1), 4, 0)
    tile = jnp.where((rows >= 4) & (lanes < 4), corner, tile)
    packed = tile
    for q in range(1, 4):
        turned = pltpu.roll(pltpu.roll(tile, 32 * q, 1), 8 - 2 * q, 0)
        packed = jnp.where((lanes >> 5) == q, turned, packed)
    packed = packed[0:2]
    for n in range(out.shape[0]):
        out[n] = packed


def gram_of(messages):
    total = messages[0]
    for n in range(1, messages.shape[0]):
        total = total + messages[n]
    total = jnp.concatenate([total] * 4, 0)
    rows, lanes = row_ids((8, 128)), lane_ids((8, 128))
    tile = total
    for q in range(1, 4):
        tile = jnp.where((rows >> 1) == q, pltpu.roll(total, 128 - 32 * q, 1), tile)
    corner = pltpu.roll(pltpu.roll(tile, 4, 0), 16, 1)
    tops = [
        jnp.where((lanes < COLS) & (lanes >= rows), tile, 0.0),
        jnp.where((lanes < COLS) & (lanes >= rows + 8), pltpu.roll(tile, 128 - 12, 1), 0.0),
        jnp.where((lanes < COLS) & (lanes >= rows + 16), corner, 0.0),
    ]
    return jnp.concatenate(tops, 0)


def slot(k):
    return k * NRHS + (NRHS if k else 0)


class Block:
    def __init__(self, stores, base, faces, faces_base, one):
        self.one = one
        self.stores, self.base, self.faces, self.faces_base = stores, base, faces, faces_base
        self.lane = lane_ids((8, 128))

    def put(self, f, z, l, t, value):
        store, f, z = self.stores[f // NRHS], f % NRHS, z - self.base
        store[f, z, l, 8 + 8 * t : 16 + 8 * t, :] = value
        if t == 0:
            store[f, z, l, 8 + ROWS : 16 + ROWS, :] = value
        if t == ROWS // 8 - 1:
            store[f, z, l, 0:8, :] = value

    def place_y(self, z, up, dn):
        for t in range(ROWS // 8):
            u_all, d_all = up[8 * t : 8 * t + 8, :], dn[8 * t : 8 * t + 8, :]
            for zz in range(4):
                for f in range(FIELDS):
                    spot = (zz * FIELDS + f) * 4
                    u = pltpu.roll(u_all, (-spot) % 128, 1) if spot else u_all
                    d = pltpu.roll(d_all, (124 - spot) % 128, 1) if spot != 124 else d_all
                    value = jnp.where(self.lane < 4, u, jnp.where(self.lane >= 124, d, 0.0))
                    self.put(f, z + zz, 2, t, value)

    def tiles(self, f, z, t, off):
        store, f, z = self.stores[f // NRHS], f % NRHS, z - self.base
        row = 8 + 8 * t + (off * self.one if off else 0)
        return [store[f, z, l, pl.ds(row, 8), :] for l in range(LT)]

    def close_ring(self, f, z):
        store, f, z = self.stores[f // NRHS], f % NRHS, z - self.base
        for l in range(2):
            store[f, z, l, 8 + ROWS : 16 + ROWS, :] = store[f, z, l, 8:16, :]

    def lane_up(self, tri):
        rolled = [pltpu.roll(v, 127, 1) for v in tri]
        return [jnp.where(self.lane == 127, rolled[(l + 1) % LT], rolled[l]) for l in range(LT)]

    def lane_dn(self, tri):
        rolled = [pltpu.roll(v, 1, 1) for v in tri]
        return [jnp.where(self.lane == 0, rolled[(l - 1) % LT], rolled[l]) for l in range(LT)]

    def coefficients(self, z):
        for t in range(ROWS // 8):
            kz, kx, ky, kd = (NRHS + i for i in range(4))
            center_z, center_x, center_y = (self.tiles(k, z, t, 0) for k in (kz, kx, ky))
            diag = self.tiles(kd, z, t, 0)
            sides = [
                (center_z, self.tiles(kz, z + 1, t, 0)),
                (center_z, self.tiles(kz, z - 1, t, 0)),
                (center_x, self.tiles(kx, z, t, 1)),
                (center_x, self.tiles(kx, z, t, -1)),
                (center_y, self.lane_up(center_y)),
                (center_y, self.lane_dn(center_y)),
            ]
            at = z - self.faces_base
            for l in range(LT):
                inside = diag[l] > 0.0
                total = diag[l] * SCALE
                for k, (mid, side) in enumerate(sides):
                    face = (mid[l] + side[l]) * (0.5 * SCALE)
                    total = total + face
                    self.faces[k, at, l, 8 * t : 8 * t + 8, :] = jnp.where(inside, face, 0.0)
                self.faces[6, at, l, 8 * t : 8 * t + 8, :] = jnp.where(inside, total, 0.0)

    def apply(self, k, z):
        last = k == STEPS - 1
        at = z - self.faces_base
        outs = 2 if last else LT
        for t in range(NX // 8 if last else ROWS // 8):
            face = [[self.faces[c, at, l, 8 * t : 8 * t + 8, :] for l in range(outs)] for c in range(7)]
            diag = [face[6][l] - SHIFTS[k] * SCALE for l in range(outs)]
            for r in range(NRHS):
                f = slot(k) + r
                mid = self.tiles(f, z, t, 0)
                sides = [
                    self.tiles(f, z + 1, t, 0),
                    self.tiles(f, z - 1, t, 0),
                    self.tiles(f, z, t, 1),
                    self.tiles(f, z, t, -1),
                    self.lane_up(mid),
                    self.lane_dn(mid),
                ]
                for l in range(outs):
                    value = diag[l] * mid[l]
                    for c in range(6):
                        value = value - face[c][l] * sides[c][l]
                    self.put(slot(k + 1) + r, z, l, t, value)


def dynamic_one(place):
    return (place[0] >> 24) + 1


def loop(start, stop, do):
    def step(n, carry):
        do(n)
        return carry

    lax.fori_loop(start, stop, step, 0)


def inner_planes(k):
    return DEPTH + k, DEPTH + NZ - k


def inner_copies(inner, inner_faces, stores, base, faces, faces_base, sems, out):
    def copy(n, there, here):
        src, dst = (here, there) if out else (there, here)
        return pltpu.make_async_copy(src, dst, sems.at[n])

    def planes(ref, f, start, stop, at):
        return ref.at[pl.ds(f, NRHS), pl.ds(start - at, stop - start)]

    result = []
    for n, (f, start, stop) in enumerate(
        [(f, z, z + 2) for f in (0, NRHS) for z in (DEPTH, DEPTH + NZ - 2)]
        + [(0, DEPTH + 2, DEPTH + NZ - 2)]
        + [(slot(k), *inner_planes(k)) for k in range(1, STEPS)]
    ):
        there = planes(inner, f, start, stop, DEPTH)
        result.append(copy(n, there, stores[f // NRHS].at[:, pl.ds(start - base, stop - start)]))
    start, stop = inner_planes(1)
    result.append(copy(len(result), inner_faces, faces.at[:, pl.ds(start - faces_base, stop - start)]))
    return result


def krylov_inner(swap, place, rhs, cz, cx, cy, dg, *rest):
    above, below, yup, ydn, inner, inner_faces, *stores, faces, load_sems, sems = rest if not swap else rest[:1] + rest
    keep_up, keep_dn = keep_sides(swap, place)
    block = Block(stores, DEPTH, faces, DEPTH + 1, dynamic_one(place))
    loads = []
    for n, src in enumerate((rhs, cz, cx, cy, dg)):
        for l in range(2):
            lanes = pl.ds(128 * l, 128)
            rows = pl.ds(8, NX)
            if n == 0:
                src_at, dst = src.at[:, :, :, lanes], stores[0].at[:, :, l, rows, :]
            else:
                src_at, dst = src.at[:, :, lanes], stores[1].at[n - 1, :, l, rows, :]
            loads.append(pltpu.make_async_copy(src_at, dst, load_sems.at[2 * n + l]))
            loads[-1].start()
    for f in range(FIELDS):
        for z in range(DEPTH, DEPTH + NZ):
            m = (z - DEPTH) // 2
            for l in range(2):
                lanes = pl.ds(128 * l, 128)
                tile = halo_tile(above[f, m, :, lanes], below[f, m, :, lanes], z % 2, keep_up, keep_dn)
                block.put(f, z, l, NX // 8, tile)
    for half in range(2):
        lanes = pl.ds(128 * half, 128)
        block.place_y(DEPTH + 4 * half, yup.at[:, lanes], ydn.at[:, lanes])
    for copy in loads:
        copy.wait()
    for f in range(FIELDS):
        for z in range(DEPTH, DEPTH + NZ):
            block.close_ring(f, z)
    copies = inner_copies(inner, inner_faces, stores, DEPTH, faces, DEPTH + 1, sems, True)
    for n in range(5):
        copies[n].start()
    loop(*inner_planes(1), block.coefficients)
    copies[-1].start()
    for k in range(STEPS - 1):
        loop(*inner_planes(k + 1), functools.partial(block.apply, k))
        copies[5 + k].start()
    for copy in copies:
        copy.wait()


NEAR, FAR = 8 * FIELDS, 24


def krylov_outer(
    swap, facelo, facehi, place, inner, inner_faces, rimlo, rimhi,
    basis, message,
    *rest,
):
    keep_up, keep_dn = keep_sides(swap, place)
    n_x = 1 if swap else 2
    *stores, faces, accs, plane_sems, loads, saves = rest
    block = Block(stores, 0, faces, 0, dynamic_one(place))
    copies = inner_copies(inner, inner_faces, stores, 0, faces, 0, loads, False)
    planes = []
    start = 0
    for f in range(FIELDS):
        depth = DEPTH if f <= NRHS else DEPTH - 1
        for side, (face, z) in enumerate(((facelo, DEPTH - depth), (facehi, DEPTH + NZ))):
            for l in range(2):
                planes.append(
                    pltpu.make_async_copy(
                        face.at[pl.ds(start, depth), :, pl.ds(128 * l, 128)],
                        stores[f // NRHS].at[f % NRHS, pl.ds(z, depth), l, pl.ds(8, NX), :],
                        plane_sems.at[4 * f + 2 * side + l],
                    )
                )
        start += depth
    for copy in copies[:4] + planes:
        copy.start()

    zero = jnp.zeros((8, 128), F32)
    for f in range(FIELDS):
        for rim, first in ((rimlo, 0), (rimhi, DEPTH + NZ)):
            for z in range(first, first + DEPTH):
                far = DEPTH - z if first == 0 else z - first + 1
                for l in range(2):
                    lanes = pl.ds(128 * l, 128)
                    if far <= 2:
                        at, odd = 8 * f, z % 2
                    elif far == 3 and 8 * (f // 2) < FAR:
                        at, odd = NEAR + 8 * (f // 2), f % 2
                    else:
                        block.put(f, z, l, NX // 8, zero)
                        continue
                    other = at + (n_x - 1) * (NEAR + FAR)
                    tile = halo_tile(rim[at : at + 8, lanes], rim[other : other + 8, lanes], odd, keep_up, keep_dn)
                    block.put(f, z, l, NX // 8, tile)
    rows = pl.ds(n_x * (NEAR + FAR), ROWS)
    for rim, z in ((rimlo, 0), (rimhi, DEPTH + NZ)):
        block.place_y(z, rim.at[rows, pl.ds(0, 128)], rim.at[rows, pl.ds(128, 128)])

    for copy in copies[:4] + planes:
        copy.wait()
    for copy in [copies[5], copies[-1], copies[6], copies[7], copies[4]]:
        copy.start()
    for f in range(FIELDS):
        depth = DEPTH if f <= NRHS else DEPTH - 1
        for d in range(depth):
            block.close_ring(f, DEPTH - 1 - d)
            block.close_ring(f, DEPTH + NZ + d)
    loop(1, DEPTH + 1, block.coefficients)
    loop(DEPTH + NZ - 1, EZ - 1, block.coefficients)

    sends = []

    def send_block(k):
        copy = pltpu.make_async_copy(
            stores[slot(k) // NRHS].at[:, pl.ds(DEPTH, NZ), pl.ds(0, 2), pl.ds(8, NX), :],
            basis.at[pl.ds(k * NRHS, NRHS)],
            saves.at[k],
        )
        copy.start()
        sends.append(copy)

    for k in range(STEPS):
        if k == 1:
            copies[-1].wait()
        loop(
            0,
            2 * DEPTH,
            lambda n, k=k: block.apply(k, n + k + 1 + jnp.where(n >= DEPTH, NZ - 2 - 2 * k, 0)),
        )
        if k < STEPS - 1:
            copies[5 + k].wait()
        send_block(k + 1)
    copies[4].wait()
    send_block(0)
    gram_zero(accs)

    def products(z):
        def tile(i, t):
            store = stores[slot(i // NRHS) // NRHS]
            return jnp.concatenate([store[i % NRHS, z, l, 8 + 8 * t : 16 + 8 * t, :] for l in range(2)], 1)

        gram_add([jnp.concatenate([tile(i, t) for i in range(COLS)], 0) for t in range(NX // 8)], accs)

    loop(DEPTH, DEPTH + NZ, products)
    gram_message(accs, message)
    for copy in sends:
        copy.wait()


def factor_gram(messages, cells, table):
    rows = row_ids((24, 128))
    lanes = lane_ids((24, 128))
    upper = gram_of(messages) / cells
    square = jnp.concatenate([upper, jnp.zeros((104, 128), F32)], 0).T
    whole = jnp.where(rows <= lanes, upper, square[0:24, :])

    def splat(value):
        return jnp.broadcast_to(value, (24, 128))

    columns = [splat(whole[:, c : c + 1]) for c in range(COLS)]
    inverse = [jnp.where(rows == c, 1.0, 0.0) for c in range(COLS)]
    pivots = jnp.ones((24, 128), F32)
    factor = jnp.zeros((24, 128), F32)
    for j in range(COLS):
        pivot = splat(columns[j][j : j + 1, :])
        pivots = jnp.where(rows == j, pivot, pivots)
        below = jnp.where(rows > j, columns[j] / pivot, 0.0)
        for c in range(j, COLS):
            row = splat(columns[c][j : j + 1, :])
            factor = jnp.where((rows == j) & (lanes == c), row, factor)
            if c > j:
                columns[c] = columns[c] - below * row
        for c in range(j + 1):
            inverse[c] = inverse[c] - below * splat(inverse[c][j : j + 1, :])
    roots = jnp.sqrt(pivots)
    for c in range(COLS):
        table[c] = inverse[c] / roots
    return factor / roots


def apply_rows(table, read, write):
    group = 5
    pieces = NX // 8
    for g in reversed(range(COLS // group)):
        mine = range(group * g, group * g + group)
        sums = {i: None for i in mine}
        for j in range(group * g + group):
            value = [read(j, p) for p in range(pieces)]
            for i in mine:
                if j <= i:
                    weight = jnp.broadcast_to(table[j, i : i + 1, :], (8, 128))
                    terms = [weight * v for v in value]
                    sums[i] = terms if sums[i] is None else [s + t for s, t in zip(sums[i], terms)]
        for i in mine:
            for p in range(pieces):
                write(i, p, sums[i][p])


def plane_copy(src, dst, sems, z):
    return pltpu.make_async_copy(src.at[:, z], dst.at[:, z], sems.at[z])


def first_pass(
    cells, message, basis_hbm, first_hbm, next_message, factor_out, basis, first, table, accs, loads, saves
):
    for z in range(NZ):
        plane_copy(basis_hbm, basis, loads, z).start()
    factor_out[...] = factor_gram(message, cells, table)
    gram_zero(accs)

    def products(z):
        def tile(i, t):
            return jnp.concatenate([first[i, z, l, 8 * t : 8 * t + 8, :] for l in range(2)], 1)

        gram_add([jnp.concatenate([tile(i, t) for i in range(COLS)], 0) for t in range(NX // 8)], accs)

    def apply(z):
        for l in range(2):

            def read(j, p):
                return basis[j, z, l, 8 * p : 8 * p + 8, :]

            def write(i, p, value):
                first[i, z, l, 8 * p : 8 * p + 8, :] = value

            apply_rows(table, read, write)
        plane_copy(first, first_hbm, saves, z).start()

    def both(z):
        plane_copy(basis_hbm, basis, loads, z).wait()
        products(z - 1)
        apply(z)

    plane_copy(basis_hbm, basis, loads, 0).wait()
    apply(0)
    loop(1, NZ, both)
    products(NZ - 1)
    gram_message(accs, next_message)
    for z in range(NZ):
        plane_copy(first, first_hbm, saves, z).wait()


def second_pass(cells, message, factor_one, first_hbm, out_hbm, triangle, first, out, table, loads, saves):
    for z in range(NZ):
        plane_copy(first_hbm, first, loads, z).start()
    left = factor_gram(message, cells, table)[:, 0:24]
    product = lax.dot_general(
        left, factor_one[...], (((1,), (0,)), ((), ())), precision=HIGHEST, preferred_element_type=F32
    )
    triangle[...] = product[0:COLS, 0:COLS]

    def chunk(z, carry):
        plane_copy(first_hbm, first, loads, z).wait()
        for l in range(2):

            def read(j, p):
                return first[j, z, l, 8 * p : 8 * p + 8, :]

            def write(i, p, value):
                out[i, z, 8 * p : 8 * p + 8, 128 * l : 128 * l + 128] = value

            apply_rows(table, read, write)
        plane_copy(out, out_hbm, saves, z).start()
        return carry

    lax.fori_loop(0, NZ, chunk, 0)
    for z in range(NZ):
        plane_copy(out, out_hbm, saves, z).wait()


def shape(*dims):
    return jax.ShapeDtypeStruct(dims, F32)


def move(value, axis, delta):
    count = lax.axis_size(axis)
    pairs = [(i, i + delta) for i in range(count) if 0 <= i + delta < count]
    return lax.ppermute(value, axis, pairs)


def exchange(messages):
    return lax.all_to_all(messages, AXES, 0, 0, tiled=True)


def body(rhs, coef_x, coef_y, coef_z, diag_term):
    n_x = lax.axis_size("gx")
    devices = n_x * lax.axis_size("gy") * lax.axis_size("gz")
    cells = float(NZ * NX * NY * devices)
    at_x = lax.axis_index("gx")
    swap = n_x == 2
    fields = (rhs, coef_z, coef_x, coef_y, diag_term)

    place = at_x.astype(jnp.int32).reshape(1)
    face_shape = shape(FACE, NX, NY)
    x_shape = shape(FIELDS, NZ // 2, 8, NY)
    own_shape = shape(NX, NY)
    zlo, zhi, ylo_own, yhi_own, *xmsgs = pl.pallas_call(
        functools.partial(pack_faces, swap),
        out_shape=(face_shape, face_shape, own_shape, own_shape) + (x_shape,) * (1 if swap else 2),
        in_specs=[smem()] + [hbm()] * 5,
        out_specs=(hbm(), hbm()) + (vmem(),) * (3 if swap else 4),
        scratch_shapes=[
            pltpu.VMEM((FIELDS, NZ, NX, NY), F32),
            pltpu.SemaphoreType.DMA((FIELDS,)),
            pltpu.SemaphoreType.DMA((2 * FIELDS,)),
        ],
        compiler_params=params(LIMIT),
        cost_estimate=cost(2.5),
    )(place, *fields)
    facehi = move(zlo, "gz", -1)
    facelo = move(zhi, "gz", 1)
    if swap:
        x_parts = (lax.ppermute(xmsgs[0], "gx", [(0, 1), (1, 0)]),)
    else:
        x_parts = (move(xmsgs[0], "gx", -1), move(xmsgs[1], "gx", 1))

    rim_shape = shape(ROWS, NY)
    ylo, yhi = pl.pallas_call(
        functools.partial(pack_rims, swap),
        out_shape=(rim_shape, rim_shape),
        in_specs=[smem()] + [vmem()] * (2 + len(x_parts)),
        compiler_params=params(16),
        cost_estimate=cost(1),
    )(place, ylo_own, yhi_own, *x_parts)
    yup, ydn = move(ylo, "gy", -1), move(yhi, "gy", 1)

    def rim(half):
        near, far, odd = ((0, 1, 0), (3, 2, 1))[half]
        rows = []
        for part in x_parts:
            rows.append(part[:, near].reshape(NEAR, NY))
            rows.append(part[: FAR // 4, far, 4 * odd : 4 * odd + 4].reshape(FAR, NY))
        lanes = slice(128 * half, 128 * half + 128)
        return jnp.concatenate(rows + [jnp.concatenate([yup[:, lanes], ydn[:, lanes]], 1)], 0)

    rimhi, rimlo = move(rim(0), "gz", -1), move(rim(1), "gz", 1)

    inner_shape = shape(COLS, NZ, LT, EROWS, 128)
    inner_faces_shape = shape(7, NZ - 2, LT, ROWS, 128)
    inner, inner_faces = pl.pallas_call(
        functools.partial(krylov_inner, swap),
        out_shape=(inner_shape, inner_faces_shape),
        in_specs=[smem()] + [hbm()] * 5 + [vmem()] * (len(x_parts) + 2),
        out_specs=(hbm(), hbm()),
        scratch_shapes=[
            *[pltpu.VMEM((NRHS,) + inner_shape.shape[1:], F32)] * (STEPS + 1),
            pltpu.VMEM(inner_faces_shape.shape, F32),
            pltpu.SemaphoreType.DMA((10,)),
            pltpu.SemaphoreType.DMA((9,)),
        ],
        compiler_params=params(LIMIT),
        cost_estimate=cost(7),
    )(place, *fields, *x_parts, yup, ydn)

    block = shape(COLS, NZ, 2, NX, 128)
    basis, message = pl.pallas_call(
        functools.partial(krylov_outer, swap),
        out_shape=(block, shape(devices, 2, 128)),
        in_specs=[hbm(), hbm(), smem(), hbm(), hbm(), vmem(), vmem()],
        out_specs=(hbm(), vmem()),
        scratch_shapes=[
            *[pltpu.VMEM((NRHS, EZ, LT, EROWS, 128), F32)] * (STEPS + 2),
            pltpu.VMEM((7, EZ, LT, ROWS, 128), F32),
            pltpu.VMEM((2, STACK, STACK), F32),
            pltpu.SemaphoreType.DMA((4 * FIELDS,)),
            pltpu.SemaphoreType.DMA((9,)),
            pltpu.SemaphoreType.DMA((STEPS + 1,)),
        ],
        compiler_params=params(LIMIT),
        cost_estimate=cost(15),
    )(facelo, facehi, place, inner, inner_faces, rimlo, rimhi)

    message = exchange(message)
    first, message, factor_one = pl.pallas_call(
        functools.partial(first_pass, cells),
        out_shape=(block, shape(devices, 2, 128), shape(24, 128)),
        in_specs=[vmem(), hbm()],
        out_specs=(hbm(), vmem(), vmem()),
        scratch_shapes=[
            pltpu.VMEM(block.shape, F32),
            pltpu.VMEM(block.shape, F32),
            pltpu.VMEM((COLS, 24, 128), F32),
            pltpu.VMEM((2, STACK, STACK), F32),
            pltpu.SemaphoreType.DMA((NZ,)),
            pltpu.SemaphoreType.DMA((NZ,)),
        ],
        compiler_params=params(LIMIT),
    )(message, basis)

    message = exchange(message)
    return pl.pallas_call(
        functools.partial(second_pass, cells),
        out_shape=(shape(COLS, NZ, NX, NY), shape(COLS, COLS)),
        in_specs=[vmem(), vmem(), hbm()],
        out_specs=(hbm(), vmem()),
        scratch_shapes=[
            pltpu.VMEM(block.shape, F32),
            pltpu.VMEM((COLS, NZ, NX, NY), F32),
            pltpu.VMEM((COLS, 24, 128), F32),
            pltpu.SemaphoreType.DMA((NZ,)),
            pltpu.SemaphoreType.DMA((NZ,)),
        ],
        compiler_params=params(LIMIT),
    )(message, factor_one, first)


def solution(mesh):
    return jax.shard_map(
        body,
        mesh=mesh,
        in_specs=(
            P(None, "gz", "gx", "gy"),
            P("gz", "gx", "gy"),
            P("gz", "gx", "gy"),
            P("gz", "gx", "gy"),
            P("gz", "gx", "gy"),
        ),
        out_specs=(P(None, "gz", "gx", "gy"), P()),
        check_vma=False,
    )
```

```python
import functools

import jax
import jax.numpy as jnp
from jax import lax
from jax.experimental import pallas as pl
from jax.experimental.pallas import tpu as pltpu
from jax.sharding import PartitionSpec as P

NRHS = 4
STEPS = 4
COLS = NRHS * (STEPS + 1)
SHIFTS = (3.0, 11.0, 7.0, 1.5)
SCALE = 1.0 / 6.0
FIELDS = NRHS + 4
AXES = ("gx", "gy", "gz")
HIGHEST = lax.Precision.HIGHEST

DEPTH = 4
NZ, NX, NY = 8, 32, 256
EZ = NZ + 2 * DEPTH
ROWS = NX + 8
EROWS = ROWS + 16
LT = 3
FACE = NRHS * 4 + 3 * 4 + 1
F32 = jnp.float32
LIMIT = 63


def params(mb):
    return pltpu.CompilerParams(vmem_limit_bytes=mb << 20)


def cost(us):
    return pl.CostEstimate(flops=0, bytes_accessed=int(us * 3.6e6), transcendentals=0)


def vmem():
    return pl.BlockSpec(memory_space=pltpu.VMEM)


def smem():
    return pl.BlockSpec(memory_space=pltpu.SMEM)


def hbm():
    return pl.BlockSpec(memory_space=pl.ANY)


def row_ids(shape):
    return lax.broadcasted_iota(jnp.int32, shape, 0)


def lane_ids(shape):
    return lax.broadcasted_iota(jnp.int32, shape, 1)


def field_of(rhs, cz, cx, cy, dg, f, z):
    return rhs.at[f, z] if f < NRHS else (cz, cx, cy, dg)[f - NRHS].at[z]


def pack_faces(swap, place, odd_z, rhs, cz, cx, cy, dg, z_one, z_two, ylo, yhi, *rest):
    xmsgs, (whole, loads, saves) = rest[:-3], rest[-3:]
    copies = []
    for f in range(FIELDS):
        src = rhs.at[f] if f < NRHS else (cz, cx, cy, dg)[f - NRHS]
        copies.append(pltpu.make_async_copy(src, whole.at[f], loads.at[f]))
        copies[-1].start()
    low = row_ids((8, NY)) < 4
    up = place[0] == 0
    planes = []
    at = 0
    for f in range(FIELDS):
        copies[f].wait()
        depth = DEPTH if f <= NRHS else DEPTH - 1
        for side, out in ((0, z_one), (1, z_two)):
            start = jnp.where(odd_z[0] == side, NZ - depth, 0)
            planes.append(
                pltpu.make_async_copy(
                    whole.at[f, pl.ds(start, depth)], out.at[pl.ds(at, depth)], saves.at[2 * f + side]
                )
            )
            planes[-1].start()
        at += depth
        for m in range(NZ // 2):
            a, b = whole.at[f, 2 * m], whole.at[f, 2 * m + 1]
            first = jnp.where(low, a[0:8], pltpu.roll(b[0:8], 4, 0))
            last = jnp.where(low, pltpu.roll(a[NX - 8 : NX], 4, 0), b[NX - 8 : NX])
            if swap:
                xmsgs[0][f, m] = jnp.where(up, last, first)
            else:
                xmsgs[0][f, m] = first
                xmsgs[1][f, m] = last
    for t in range(NX // 8):
        for side, out in ((0, ylo), (1, yhi)):
            for half in range(2):
                out[8 * t : 8 * t + 8, 128 * half : 128 * half + 128] = pack_lanes(
                    lambda f, zz: whole[f, 4 * half + zz, 8 * t : 8 * t + 8, 128 * side : 128 * side + 128], side
                )
    for copy in planes:
        copy.wait()


def halo_tile(above, below, odd, keep_up, keep_dn):
    low = row_ids(above.shape) < 4
    if odd:
        up, dn = pltpu.roll(above, 4, 0), below
    else:
        up, dn = above, pltpu.roll(below, 4, 0)
    return jnp.where(low, up * keep_up, dn * keep_dn)


def keep_sides(swap, place):
    if not swap:
        return 1.0, 1.0
    first = place[0] == 0
    return jnp.where(first, 1.0, 0.0), jnp.where(first, 0.0, 1.0)


def pack_lanes(tile_of, side):
    lane = lane_ids((8, 128))
    source = 124 * side
    acc = jnp.zeros((8, 128), F32)
    for zz in range(4):
        for f in range(FIELDS):
            tile = tile_of(f, zz)
            spot = (zz * FIELDS + f) * 4
            shift = (spot - source) % 128
            if shift:
                tile = pltpu.roll(tile, shift, 1)
            acc = jnp.where((lane >= spot) & (lane < spot + 4), tile, acc)
    return acc


def pack_rims(swap, place, odd_y, ylo_own, yhi_own, *refs):
    above, below, one, two = refs if not swap else (refs[0],) + refs
    keep_up, keep_dn = keep_sides(swap, place)
    odd = odd_y[0] == 1
    lo, hi = ylo_own[...], yhi_own[...]
    one[0:NX, :] = jnp.where(odd, lo, hi)
    two[0:NX, :] = jnp.where(odd, hi, lo)
    for half in range(2):
        halves = []
        for side in range(2):
            lanes = slice(128 * side, 128 * side + 128)
            halves.append(
                pack_lanes(
                    lambda f, zz: halo_tile(
                        above[f, 2 * half + zz // 2, :, lanes],
                        below[f, 2 * half + zz // 2, :, lanes],
                        zz % 2,
                        keep_up,
                        keep_dn,
                    ),
                    side,
                )
            )
        lo, hi = halves
        one[NX:ROWS, 128 * half : 128 * half + 128] = jnp.where(odd, lo, hi)
        two[NX:ROWS, 128 * half : 128 * half + 128] = jnp.where(odd, hi, lo)


STACK = 8 * COLS


def gram_zero(accs):
    accs[...] = jnp.zeros_like(accs)


def gram_add(stacks, accs):
    left, right = [], []
    cross_left, cross_right = [], []
    for stack in stacks:
        high = stack.astype(jnp.bfloat16)
        rest = stack - high.astype(F32)
        mid = rest.astype(jnp.bfloat16)
        low = (rest - mid.astype(F32)).astype(jnp.bfloat16)
        left += [high, mid]
        cross_left += [high, high]
        cross_right += [mid, low]
    contract = (((1,), (1,)), ((), ()))

    def product(a, b):
        return lax.dot_general(jnp.concatenate(a, 1), jnp.concatenate(b, 1), contract, preferred_element_type=F32)

    accs[0] += product(left, left)
    accs[1] += product(cross_left, cross_right)


def gram_message(accs, out):
    same = (row_ids((STACK, STACK)) & 7) == (lane_ids((STACK, STACK)) & 7)
    pick = jnp.where((row_ids((STACK, 128)) >> 3) == lane_ids((STACK, 128)), 1.0, 0.0)

    def traces(product):
        picked = jnp.where(same, product, 0.0)
        rows = [jnp.sum(picked[8 * i : 8 * i + 8], axis=0, keepdims=True) for i in range(COLS)]
        rows = jnp.concatenate(rows + [jnp.zeros((128 - COLS, STACK), F32)], 0)
        return lax.dot_general(
            rows, pick, (((1,), (0,)), ((), ())), precision=HIGHEST, preferred_element_type=F32
        )

    cross = traces(accs[1])
    gram = traces(accs[0]) + cross + cross.T
    tops = [gram[8 * k : 8 * k + 8] for k in range(3)]
    rows, lanes = row_ids((8, 128)), lane_ids((8, 128))
    tile = jnp.where(lanes < COLS, tops[0], pltpu.roll(tops[1], 12, 1))
    corner = pltpu.roll(pltpu.roll(tops[2], 128 - 16, 1), 4, 0)
    tile = jnp.where((rows >= 4) & (lanes < 4), corner, tile)
    packed = tile
    for q in range(1, 4):
        turned = pltpu.roll(pltpu.roll(tile, 32 * q, 1), 8 - 2 * q, 0)
        packed = jnp.where((lanes >> 5) == q, turned, packed)
    packed = packed[0:2]
    for n in range(out.shape[0]):
        out[n] = packed


def gram_of(messages):
    total = messages[0]
    for n in range(1, messages.shape[0]):
        total = total + messages[n]
    total = jnp.concatenate([total] * 4, 0)
    rows, lanes = row_ids((8, 128)), lane_ids((8, 128))
    tile = total
    for q in range(1, 4):
        tile = jnp.where((rows >> 1) == q, pltpu.roll(total, 128 - 32 * q, 1), tile)
    corner = pltpu.roll(pltpu.roll(tile, 4, 0), 16, 1)
    tops = [
        jnp.where((lanes < COLS) & (lanes >= rows), tile, 0.0),
        jnp.where((lanes < COLS) & (lanes >= rows + 8), pltpu.roll(tile, 128 - 12, 1), 0.0),
        jnp.where((lanes < COLS) & (lanes >= rows + 16), corner, 0.0),
    ]
    return jnp.concatenate(tops, 0)


def slot(k):
    return k * NRHS + (NRHS if k else 0)


class Block:
    def __init__(self, stores, base, faces, faces_base, one):
        self.one = one
        self.stores, self.base, self.faces, self.faces_base = stores, base, faces, faces_base
        self.lane = lane_ids((8, 128))

    def put(self, f, z, l, t, value):
        store, f, z = self.stores[f // NRHS], f % NRHS, z - self.base
        store[f, z, l, 8 + 8 * t : 16 + 8 * t, :] = value
        if t == 0:
            store[f, z, l, 8 + ROWS : 16 + ROWS, :] = value
        if t == ROWS // 8 - 1:
            store[f, z, l, 0:8, :] = value

    def place_y(self, z, up, dn):
        for t in range(ROWS // 8):
            u_all, d_all = up[8 * t : 8 * t + 8, :], dn[8 * t : 8 * t + 8, :]
            for zz in range(4):
                for f in range(FIELDS):
                    spot = (zz * FIELDS + f) * 4
                    u = pltpu.roll(u_all, (-spot) % 128, 1) if spot else u_all
                    d = pltpu.roll(d_all, (124 - spot) % 128, 1) if spot != 124 else d_all
                    value = jnp.where(self.lane < 4, u, jnp.where(self.lane >= 124, d, 0.0))
                    self.put(f, z + zz, 2, t, value)

    def tiles(self, f, z, t, off):
        store, f, z = self.stores[f // NRHS], f % NRHS, z - self.base
        row = 8 + 8 * t + (off * self.one if off else 0)
        return [store[f, z, l, pl.ds(row, 8), :] for l in range(LT)]

    def close_ring(self, f, z):
        store, f, z = self.stores[f // NRHS], f % NRHS, z - self.base
        for l in range(2):
            store[f, z, l, 8 + ROWS : 16 + ROWS, :] = store[f, z, l, 8:16, :]

    def lane_up(self, tri):
        rolled = [pltpu.roll(v, 127, 1) for v in tri]
        return [jnp.where(self.lane == 127, rolled[(l + 1) % LT], rolled[l]) for l in range(LT)]

    def lane_dn(self, tri):
        rolled = [pltpu.roll(v, 1, 1) for v in tri]
        return [jnp.where(self.lane == 0, rolled[(l - 1) % LT], rolled[l]) for l in range(LT)]

    def coefficients(self, z):
        for t in range(ROWS // 8):
            kz, kx, ky, kd = (NRHS + i for i in range(4))
            center_z, center_x, center_y = (self.tiles(k, z, t, 0) for k in (kz, kx, ky))
            diag = self.tiles(kd, z, t, 0)
            sides = [
                (center_z, self.tiles(kz, z + 1, t, 0)),
                (center_z, self.tiles(kz, z - 1, t, 0)),
                (center_x, self.tiles(kx, z, t, 1)),
                (center_x, self.tiles(kx, z, t, -1)),
                (center_y, self.lane_up(center_y)),
                (center_y, self.lane_dn(center_y)),
            ]
            at = z - self.faces_base
            for l in range(LT):
                inside = diag[l] > 0.0
                total = diag[l] * SCALE
                for k, (mid, side) in enumerate(sides):
                    face = (mid[l] + side[l]) * (0.5 * SCALE)
                    total = total + face
                    self.faces[k, at, l, 8 * t : 8 * t + 8, :] = jnp.where(inside, face, 0.0)
                self.faces[6, at, l, 8 * t : 8 * t + 8, :] = jnp.where(inside, total, 0.0)

    def apply(self, k, z):
        last = k == STEPS - 1
        at = z - self.faces_base
        outs = 2 if last else LT
        for t in range(NX // 8 if last else ROWS // 8):
            face = [[self.faces[c, at, l, 8 * t : 8 * t + 8, :] for l in range(outs)] for c in range(7)]
            diag = [face[6][l] - SHIFTS[k] * SCALE for l in range(outs)]
            for r in range(NRHS):
                f = slot(k) + r
                mid = self.tiles(f, z, t, 0)
                sides = [
                    self.tiles(f, z + 1, t, 0),
                    self.tiles(f, z - 1, t, 0),
                    self.tiles(f, z, t, 1),
                    self.tiles(f, z, t, -1),
                    self.lane_up(mid),
                    self.lane_dn(mid),
                ]
                for l in range(outs):
                    value = diag[l] * mid[l]
                    for c in range(6):
                        value = value - face[c][l] * sides[c][l]
                    self.put(slot(k + 1) + r, z, l, t, value)


def dynamic_one(place):
    return (place[0] >> 24) + 1


def loop(start, stop, do):
    def step(n, carry):
        do(n)
        return carry

    lax.fori_loop(start, stop, step, 0)


def inner_planes(k):
    return DEPTH + k, DEPTH + NZ - k


def inner_copies(inner, inner_faces, stores, base, faces, faces_base, sems, out):
    def copy(n, there, here):
        src, dst = (here, there) if out else (there, here)
        return pltpu.make_async_copy(src, dst, sems.at[n])

    def planes(ref, f, start, stop, at):
        return ref.at[pl.ds(f, NRHS), pl.ds(start - at, stop - start)]

    result = []
    for n, (f, start, stop) in enumerate(
        [(f, z, z + 2) for f in (0, NRHS) for z in (DEPTH, DEPTH + NZ - 2)]
        + [(0, DEPTH + 2, DEPTH + NZ - 2)]
        + [(slot(k), *inner_planes(k)) for k in range(1, STEPS)]
    ):
        there = planes(inner, f, start, stop, DEPTH)
        result.append(copy(n, there, stores[f // NRHS].at[:, pl.ds(start - base, stop - start)]))
    start, stop = inner_planes(1)
    result.append(copy(len(result), inner_faces, faces.at[:, pl.ds(start - faces_base, stop - start)]))
    return result


def krylov_inner(swap, place, rhs, cz, cx, cy, dg, *rest):
    above, below, yup, ydn, inner, inner_faces, *stores, faces, load_sems, sems = rest if not swap else rest[:1] + rest
    keep_up, keep_dn = keep_sides(swap, place)
    block = Block(stores, DEPTH, faces, DEPTH + 1, dynamic_one(place))
    loads = []
    for n, src in enumerate((rhs, cz, cx, cy, dg)):
        for l in range(2):
            lanes = pl.ds(128 * l, 128)
            rows = pl.ds(8, NX)
            if n == 0:
                src_at, dst = src.at[:, :, :, lanes], stores[0].at[:, :, l, rows, :]
            else:
                src_at, dst = src.at[:, :, lanes], stores[1].at[n - 1, :, l, rows, :]
            loads.append(pltpu.make_async_copy(src_at, dst, load_sems.at[2 * n + l]))
            loads[-1].start()
    for f in range(FIELDS):
        for z in range(DEPTH, DEPTH + NZ):
            m = (z - DEPTH) // 2
            for l in range(2):
                lanes = pl.ds(128 * l, 128)
                tile = halo_tile(above[f, m, :, lanes], below[f, m, :, lanes], z % 2, keep_up, keep_dn)
                block.put(f, z, l, NX // 8, tile)
    for half in range(2):
        lanes = pl.ds(128 * half, 128)
        block.place_y(DEPTH + 4 * half, yup.at[:, lanes], ydn.at[:, lanes])
    for copy in loads:
        copy.wait()
    for f in range(FIELDS):
        for z in range(DEPTH, DEPTH + NZ):
            block.close_ring(f, z)
    copies = inner_copies(inner, inner_faces, stores, DEPTH, faces, DEPTH + 1, sems, True)
    for n in range(5):
        copies[n].start()
    loop(*inner_planes(1), block.coefficients)
    copies[-1].start()
    for k in range(STEPS - 1):
        loop(*inner_planes(k + 1), functools.partial(block.apply, k))
        copies[5 + k].start()
    for copy in copies:
        copy.wait()


NEAR, FAR = 8 * FIELDS, 24


def krylov_outer(
    swap, face_one, face_two, place, odd_z, inner, inner_faces, rim_one, rim_two,
    basis, message,
    *rest,
):
    keep_up, keep_dn = keep_sides(swap, place)
    n_x = 1 if swap else 2
    *stores, faces, accs, rims, plane_sems, loads, saves = rest
    odd = odd_z[0] == 1
    block = Block(stores, 0, faces, 0, dynamic_one(place))
    copies = inner_copies(inner, inner_faces, stores, 0, faces, 0, loads, False)
    def plane_copies(lower, upper):
        planes = []
        start = 0
        for f in range(FIELDS):
            depth = DEPTH if f <= NRHS else DEPTH - 1
            for side, (face, z) in enumerate(((lower, DEPTH - depth), (upper, DEPTH + NZ))):
                for l in range(2):
                    planes.append(
                        pltpu.make_async_copy(
                            face.at[pl.ds(start, depth), :, pl.ds(128 * l, 128)],
                            stores[f // NRHS].at[f % NRHS, pl.ds(z, depth), l, pl.ds(8, NX), :],
                            plane_sems.at[4 * f + 2 * side + l],
                        )
                    )
            start += depth
        return planes

    for copy in copies[:4]:
        copy.start()

    @pl.when(odd)
    def _():
        for copy in plane_copies(face_one, face_two):
            copy.start()

    @pl.when(jnp.logical_not(odd))
    def _():
        for copy in plane_copies(face_two, face_one):
            copy.start()

    one, two = rim_one[...], rim_two[...]
    rims[0] = jnp.where(odd, one, two)
    rims[1] = jnp.where(odd, two, one)
    rimlo, rimhi = rims.at[0], rims.at[1]

    zero = jnp.zeros((8, 128), F32)
    for f in range(FIELDS):
        for rim, first in ((rimlo, 0), (rimhi, DEPTH + NZ)):
            for z in range(first, first + DEPTH):
                far = DEPTH - z if first == 0 else z - first + 1
                for l in range(2):
                    lanes = pl.ds(128 * l, 128)
                    if far <= 2:
                        at, odd = 8 * f, z % 2
                    elif far == 3 and 8 * (f // 2) < FAR:
                        at, odd = NEAR + 8 * (f // 2), f % 2
                    else:
                        block.put(f, z, l, NX // 8, zero)
                        continue
                    other = at + (n_x - 1) * (NEAR + FAR)
                    tile = halo_tile(rim[at : at + 8, lanes], rim[other : other + 8, lanes], odd, keep_up, keep_dn)
                    block.put(f, z, l, NX // 8, tile)
    rows = pl.ds(n_x * (NEAR + FAR), ROWS)
    for rim, z in ((rimlo, 0), (rimhi, DEPTH + NZ)):
        block.place_y(z, rim.at[rows, pl.ds(0, 128)], rim.at[rows, pl.ds(128, 128)])

    for copy in copies[:4] + plane_copies(face_one, face_two):
        copy.wait()
    for copy in [copies[5], copies[-1], copies[6], copies[7], copies[4]]:
        copy.start()
    for f in range(FIELDS):
        depth = DEPTH if f <= NRHS else DEPTH - 1
        for d in range(depth):
            block.close_ring(f, DEPTH - 1 - d)
            block.close_ring(f, DEPTH + NZ + d)
    loop(1, DEPTH + 1, block.coefficients)
    loop(DEPTH + NZ - 1, EZ - 1, block.coefficients)

    sends = []

    def send_block(k):
        copy = pltpu.make_async_copy(
            stores[slot(k) // NRHS].at[:, pl.ds(DEPTH, NZ), pl.ds(0, 2), pl.ds(8, NX), :],
            basis.at[pl.ds(k * NRHS, NRHS)],
            saves.at[k],
        )
        copy.start()
        sends.append(copy)

    for k in range(STEPS):
        if k == 1:
            copies[-1].wait()
        loop(
            0,
            2 * DEPTH,
            lambda n, k=k: block.apply(k, n + k + 1 + jnp.where(n >= DEPTH, NZ - 2 - 2 * k, 0)),
        )
        if k < STEPS - 1:
            copies[5 + k].wait()
        send_block(k + 1)
    copies[4].wait()
    send_block(0)
    gram_zero(accs)

    def products(z):
        def tile(i, t):
            store = stores[slot(i // NRHS) // NRHS]
            return jnp.concatenate([store[i % NRHS, z, l, 8 + 8 * t : 16 + 8 * t, :] for l in range(2)], 1)

        gram_add([jnp.concatenate([tile(i, t) for i in range(COLS)], 0) for t in range(NX // 8)], accs)

    loop(DEPTH, DEPTH + NZ, products)
    gram_message(accs, message)
    for copy in sends:
        copy.wait()


def factor_gram(messages, cells, table):
    rows = row_ids((24, 128))
    lanes = lane_ids((24, 128))
    upper = gram_of(messages) / cells
    square = jnp.concatenate([upper, jnp.zeros((104, 128), F32)], 0).T
    whole = jnp.where(rows <= lanes, upper, square[0:24, :])

    def splat(value):
        return jnp.broadcast_to(value, (24, 128))

    columns = [splat(whole[:, c : c + 1]) for c in range(COLS)]
    inverse = [jnp.where(rows == c, 1.0, 0.0) for c in range(COLS)]
    pivots = jnp.ones((24, 128), F32)
    factor = jnp.zeros((24, 128), F32)
    for j in range(COLS):
        pivot = splat(columns[j][j : j + 1, :])
        pivots = jnp.where(rows == j, pivot, pivots)
        below = jnp.where(rows > j, columns[j] / pivot, 0.0)
        for c in range(j, COLS):
            row = splat(columns[c][j : j + 1, :])
            factor = jnp.where((rows == j) & (lanes == c), row, factor)
            if c > j:
                columns[c] = columns[c] - below * row
        for c in range(j + 1):
            inverse[c] = inverse[c] - below * splat(inverse[c][j : j + 1, :])
    roots = jnp.sqrt(pivots)
    for c in range(COLS):
        table[c] = inverse[c] / roots
    return factor / roots


def apply_rows(table, read, write):
    group = 5
    pieces = NX // 8
    for g in reversed(range(COLS // group)):
        mine = range(group * g, group * g + group)
        sums = {i: None for i in mine}
        for j in range(group * g + group):
            value = [read(j, p) for p in range(pieces)]
            for i in mine:
                if j <= i:
                    weight = jnp.broadcast_to(table[j, i : i + 1, :], (8, 128))
                    terms = [weight * v for v in value]
                    sums[i] = terms if sums[i] is None else [s + t for s, t in zip(sums[i], terms)]
        for i in mine:
            for p in range(pieces):
                write(i, p, sums[i][p])


def plane_copy(src, dst, sems, z):
    return pltpu.make_async_copy(src.at[:, z], dst.at[:, z], sems.at[z])


def first_pass(
    cells, message, basis_hbm, first_hbm, next_message, factor_out, basis, first, table, accs, loads, saves
):
    for z in range(NZ):
        plane_copy(basis_hbm, basis, loads, z).start()
    factor_out[...] = factor_gram(message, cells, table)
    gram_zero(accs)

    def products(z):
        def tile(i, t):
            return jnp.concatenate([first[i, z, l, 8 * t : 8 * t + 8, :] for l in range(2)], 1)

        gram_add([jnp.concatenate([tile(i, t) for i in range(COLS)], 0) for t in range(NX // 8)], accs)

    def apply(z):
        for l in range(2):

            def read(j, p):
                return basis[j, z, l, 8 * p : 8 * p + 8, :]

            def write(i, p, value):
                first[i, z, l, 8 * p : 8 * p + 8, :] = value

            apply_rows(table, read, write)
        plane_copy(first, first_hbm, saves, z).start()

    def both(z):
        plane_copy(basis_hbm, basis, loads, z).wait()
        products(z - 1)
        apply(z)

    plane_copy(basis_hbm, basis, loads, 0).wait()
    apply(0)
    loop(1, NZ, both)
    products(NZ - 1)
    gram_message(accs, next_message)
    for z in range(NZ):
        plane_copy(first, first_hbm, saves, z).wait()


def second_pass(cells, message, factor_one, first_hbm, out_hbm, triangle, first, out, table, loads, saves):
    for z in range(NZ):
        plane_copy(first_hbm, first, loads, z).start()
    left = factor_gram(message, cells, table)[:, 0:24]
    product = lax.dot_general(
        left, factor_one[...], (((1,), (0,)), ((), ())), precision=HIGHEST, preferred_element_type=F32
    )
    triangle[...] = product[0:COLS, 0:COLS]

    def chunk(z, carry):
        plane_copy(first_hbm, first, loads, z).wait()
        for l in range(2):

            def read(j, p):
                return first[j, z, l, 8 * p : 8 * p + 8, :]

            def write(i, p, value):
                out[i, z, 8 * p : 8 * p + 8, 128 * l : 128 * l + 128] = value

            apply_rows(table, read, write)
        plane_copy(out, out_hbm, saves, z).start()
        return carry

    lax.fori_loop(0, NZ, chunk, 0)
    for z in range(NZ):
        plane_copy(out, out_hbm, saves, z).wait()


def shape(*dims):
    return jax.ShapeDtypeStruct(dims, F32)


def move(value, axis, delta):
    count = lax.axis_size(axis)
    pairs = [(i, i + delta) for i in range(count) if 0 <= i + delta < count]
    return lax.ppermute(value, axis, pairs)


def swap_pairs(value, axis, first):
    pairs = [(i, i + 1) for i in range(first, lax.axis_size(axis) - 1, 2)]
    return lax.ppermute(value, axis, pairs + [(j, i) for i, j in pairs])


def exchange(messages):
    return lax.all_to_all(messages, AXES, 0, 0, tiled=True)


def body(rhs, coef_x, coef_y, coef_z, diag_term):
    n_x = lax.axis_size("gx")
    devices = n_x * lax.axis_size("gy") * lax.axis_size("gz")
    cells = float(NZ * NX * NY * devices)
    at_x = lax.axis_index("gx")
    swap = n_x == 2
    fields = (rhs, coef_z, coef_x, coef_y, diag_term)

    place = at_x.astype(jnp.int32).reshape(1)
    odd_z, odd_y = ((lax.axis_index(axis) & 1).astype(jnp.int32).reshape(1) for axis in ("gz", "gy"))
    face_shape = shape(FACE, NX, NY)
    x_shape = shape(FIELDS, NZ // 2, 8, NY)
    own_shape = shape(NX, NY)
    z_one, z_two, ylo_own, yhi_own, *xmsgs = pl.pallas_call(
        functools.partial(pack_faces, swap),
        out_shape=(face_shape, face_shape, own_shape, own_shape) + (x_shape,) * (1 if swap else 2),
        in_specs=[smem()] * 2 + [hbm()] * 5,
        out_specs=(hbm(), hbm()) + (vmem(),) * (3 if swap else 4),
        scratch_shapes=[
            pltpu.VMEM((FIELDS, NZ, NX, NY), F32),
            pltpu.SemaphoreType.DMA((FIELDS,)),
            pltpu.SemaphoreType.DMA((2 * FIELDS,)),
        ],
        compiler_params=params(LIMIT),
        cost_estimate=cost(2.5),
    )(place, odd_z, *fields)
    face_one, face_two = swap_pairs(z_one, "gz", 0), swap_pairs(z_two, "gz", 1)
    if swap:
        x_parts = (lax.ppermute(xmsgs[0], "gx", [(0, 1), (1, 0)]),)
    else:
        x_parts = (move(xmsgs[0], "gx", -1), move(xmsgs[1], "gx", 1))

    rim_shape = shape(ROWS, NY)
    y_one, y_two = pl.pallas_call(
        functools.partial(pack_rims, swap),
        out_shape=(rim_shape, rim_shape),
        in_specs=[smem()] * 2 + [vmem()] * (2 + len(x_parts)),
        compiler_params=params(16),
        cost_estimate=cost(1),
    )(place, odd_y, ylo_own, yhi_own, *x_parts)
    y_one, y_two = swap_pairs(y_one, "gy", 0), swap_pairs(y_two, "gy", 1)
    yup, ydn = jnp.where(odd_y == 1, y_two, y_one), jnp.where(odd_y == 1, y_one, y_two)

    def rim(half):
        near, far, odd = ((0, 1, 0), (3, 2, 1))[half]
        rows = []
        for part in x_parts:
            rows.append(part[:, near].reshape(NEAR, NY))
            rows.append(part[: FAR // 4, far, 4 * odd : 4 * odd + 4].reshape(FAR, NY))
        lanes = slice(128 * half, 128 * half + 128)
        return jnp.concatenate(rows + [jnp.concatenate([yup[:, lanes], ydn[:, lanes]], 1)], 0)

    low, high = rim(0), rim(1)
    rim_one = swap_pairs(jnp.where(odd_z == 1, low, high), "gz", 0)
    rim_two = swap_pairs(jnp.where(odd_z == 1, high, low), "gz", 1)

    inner_shape = shape(COLS, NZ, LT, EROWS, 128)
    inner_faces_shape = shape(7, NZ - 2, LT, ROWS, 128)
    inner, inner_faces = pl.pallas_call(
        functools.partial(krylov_inner, swap),
        out_shape=(inner_shape, inner_faces_shape),
        in_specs=[smem()] + [hbm()] * 5 + [vmem()] * (len(x_parts) + 2),
        out_specs=(hbm(), hbm()),
        scratch_shapes=[
            *[pltpu.VMEM((NRHS,) + inner_shape.shape[1:], F32)] * (STEPS + 1),
            pltpu.VMEM(inner_faces_shape.shape, F32),
            pltpu.SemaphoreType.DMA((10,)),
            pltpu.SemaphoreType.DMA((9,)),
        ],
        compiler_params=params(LIMIT),
        cost_estimate=cost(7),
    )(place, *fields, *x_parts, yup, ydn)

    block = shape(COLS, NZ, 2, NX, 128)
    basis, message = pl.pallas_call(
        functools.partial(krylov_outer, swap),
        out_shape=(block, shape(devices, 2, 128)),
        in_specs=[hbm(), hbm(), smem(), smem(), hbm(), hbm(), vmem(), vmem()],
        out_specs=(hbm(), vmem()),
        scratch_shapes=[
            *[pltpu.VMEM((NRHS, EZ, LT, EROWS, 128), F32)] * (STEPS + 2),
            pltpu.VMEM((7, EZ, LT, ROWS, 128), F32),
            pltpu.VMEM((2, STACK, STACK), F32),
            pltpu.VMEM((2,) + rim_one.shape, F32),
            pltpu.SemaphoreType.DMA((4 * FIELDS,)),
            pltpu.SemaphoreType.DMA((9,)),
            pltpu.SemaphoreType.DMA((STEPS + 1,)),
        ],
        compiler_params=params(LIMIT),
        cost_estimate=cost(15),
    )(face_one, face_two, place, odd_z, inner, inner_faces, rim_one, rim_two)

    message = exchange(message)
    first, message, factor_one = pl.pallas_call(
        functools.partial(first_pass, cells),
        out_shape=(block, shape(devices, 2, 128), shape(24, 128)),
        in_specs=[vmem(), hbm()],
        out_specs=(hbm(), vmem(), vmem()),
        scratch_shapes=[
            pltpu.VMEM(block.shape, F32),
            pltpu.VMEM(block.shape, F32),
            pltpu.VMEM((COLS, 24, 128), F32),
            pltpu.VMEM((2, STACK, STACK), F32),
            pltpu.SemaphoreType.DMA((NZ,)),
            pltpu.SemaphoreType.DMA((NZ,)),
        ],
        compiler_params=params(LIMIT),
    )(message, basis)

    message = exchange(message)
    return pl.pallas_call(
        functools.partial(second_pass, cells),
        out_shape=(shape(COLS, NZ, NX, NY), shape(COLS, COLS)),
        in_specs=[vmem(), vmem(), hbm()],
        out_specs=(hbm(), vmem()),
        scratch_shapes=[
            pltpu.VMEM(block.shape, F32),
            pltpu.VMEM((COLS, NZ, NX, NY), F32),
            pltpu.VMEM((COLS, 24, 128), F32),
            pltpu.SemaphoreType.DMA((NZ,)),
            pltpu.SemaphoreType.DMA((NZ,)),
        ],
        compiler_params=params(LIMIT),
    )(message, factor_one, first)


def solution(mesh):
    return jax.shard_map(
        body,
        mesh=mesh,
        in_specs=(
            P(None, "gz", "gx", "gy"),
            P("gz", "gx", "gy"),
            P("gz", "gx", "gy"),
            P("gz", "gx", "gy"),
            P("gz", "gx", "gy"),
        ),
        out_specs=(P(None, "gz", "gx", "gy"), P()),
        check_vma=False,
    )
```

```python
import functools

import jax
import jax.numpy as jnp
from jax import lax
from jax.experimental import pallas as pl
from jax.experimental.pallas import tpu as pltpu
from jax.sharding import PartitionSpec as P

NRHS = 4
STEPS = 4
COLS = NRHS * (STEPS + 1)
SHIFTS = (3.0, 11.0, 7.0, 1.5)
SCALE = 1.0 / 6.0
FIELDS = NRHS + 4
AXES = ("gx", "gy", "gz")
HIGHEST = lax.Precision.HIGHEST

DEPTH = 4
NZ, NX, NY = 8, 32, 256
EZ = NZ + 2 * DEPTH
ROWS = NX + 8
EROWS = ROWS + 16
LT = 3
FACE = NRHS * 4 + 3 * 4 + 1
F32 = jnp.float32
LIMIT = 63


def params(mb):
    return pltpu.CompilerParams(vmem_limit_bytes=mb << 20)


def cost(us):
    return pl.CostEstimate(flops=0, bytes_accessed=int(us * 3.6e6), transcendentals=0)


def vmem():
    return pl.BlockSpec(memory_space=pltpu.VMEM)


def smem():
    return pl.BlockSpec(memory_space=pltpu.SMEM)


def hbm():
    return pl.BlockSpec(memory_space=pl.ANY)


def row_ids(shape):
    return lax.broadcasted_iota(jnp.int32, shape, 0)


def lane_ids(shape):
    return lax.broadcasted_iota(jnp.int32, shape, 1)


def field_of(rhs, cz, cx, cy, dg, f, z):
    return rhs.at[f, z] if f < NRHS else (cz, cx, cy, dg)[f - NRHS].at[z]


def pack_faces(swap, place, odd_z, odd_y, rhs, cz, cx, cy, dg, z_one, z_two, y_one, y_two, *rest):
    xmsgs, (whole, loads, saves) = rest[:-3], rest[-3:]
    copies = []
    for f in range(FIELDS):
        src = rhs.at[f] if f < NRHS else (cz, cx, cy, dg)[f - NRHS]
        copies.append(pltpu.make_async_copy(src, whole.at[f], loads.at[f]))
        copies[-1].start()
    low = row_ids((8, NY)) < 4
    up = place[0] == 0
    planes = []
    at = 0
    for f in range(FIELDS):
        copies[f].wait()
        depth = DEPTH if f <= NRHS else DEPTH - 1
        for side, out in ((0, z_one), (1, z_two)):
            start = jnp.where(odd_z[0] == side, NZ - depth, 0)
            planes.append(
                pltpu.make_async_copy(
                    whole.at[f, pl.ds(start, depth)], out.at[pl.ds(at, depth)], saves.at[2 * f + side]
                )
            )
            planes[-1].start()
        at += depth
        for m in range(NZ // 2):
            a, b = whole.at[f, 2 * m], whole.at[f, 2 * m + 1]
            first = jnp.where(low, a[0:8], pltpu.roll(b[0:8], 4, 0))
            last = jnp.where(low, pltpu.roll(a[NX - 8 : NX], 4, 0), b[NX - 8 : NX])
            if swap:
                xmsgs[0][f, m] = jnp.where(up, last, first)
            else:
                xmsgs[0][f, m] = first
                xmsgs[1][f, m] = last
    odd = odd_y[0] == 1
    for t in range(NX // 8):
        for half in range(2):
            lo, hi = (
                pack_lanes(
                    lambda f, zz: whole[f, 4 * half + zz, 8 * t : 8 * t + 8, 128 * side : 128 * side + 128], side
                )
                for side in range(2)
            )
            y_one[8 * t : 8 * t + 8, 128 * half : 128 * half + 128] = jnp.where(odd, lo, hi)
            y_two[8 * t : 8 * t + 8, 128 * half : 128 * half + 128] = jnp.where(odd, hi, lo)
    for copy in planes:
        copy.wait()


def halo_tile(above, below, odd, keep_up, keep_dn):
    low = row_ids(above.shape) < 4
    if odd:
        up, dn = pltpu.roll(above, 4, 0), below
    else:
        up, dn = above, pltpu.roll(below, 4, 0)
    return jnp.where(low, up * keep_up, dn * keep_dn)


def keep_sides(swap, place):
    if not swap:
        return 1.0, 1.0
    first = place[0] == 0
    return jnp.where(first, 1.0, 0.0), jnp.where(first, 0.0, 1.0)


def pack_lanes(tile_of, side):
    lane = lane_ids((8, 128))
    source = 124 * side
    acc = jnp.zeros((8, 128), F32)
    for zz in range(4):
        for f in range(FIELDS):
            tile = tile_of(f, zz)
            spot = (zz * FIELDS + f) * 4
            shift = (spot - source) % 128
            if shift:
                tile = pltpu.roll(tile, shift, 1)
            acc = jnp.where((lane >= spot) & (lane < spot + 4), tile, acc)
    return acc


def pack_rims(swap, place, odd_y, *refs):
    above, below, one, two = refs if not swap else (refs[0],) + refs
    keep_up, keep_dn = keep_sides(swap, place)
    odd = odd_y[0] == 1
    for half in range(2):
        halves = []
        for side in range(2):
            lanes = slice(128 * side, 128 * side + 128)
            halves.append(
                pack_lanes(
                    lambda f, zz: halo_tile(
                        above[f, 2 * half + zz // 2, :, lanes],
                        below[f, 2 * half + zz // 2, :, lanes],
                        zz % 2,
                        keep_up,
                        keep_dn,
                    ),
                    side,
                )
            )
        lo, hi = halves
        one[:, 128 * half : 128 * half + 128] = jnp.where(odd, lo, hi)
        two[:, 128 * half : 128 * half + 128] = jnp.where(odd, hi, lo)


STACK = 8 * COLS


def gram_zero(accs):
    accs[...] = jnp.zeros_like(accs)


def gram_add(stacks, accs):
    left, right = [], []
    cross_left, cross_right = [], []
    for stack in stacks:
        high = stack.astype(jnp.bfloat16)
        rest = stack - high.astype(F32)
        mid = rest.astype(jnp.bfloat16)
        low = (rest - mid.astype(F32)).astype(jnp.bfloat16)
        left += [high, mid]
        cross_left += [high, high]
        cross_right += [mid, low]
    contract = (((1,), (1,)), ((), ()))

    def product(a, b):
        return lax.dot_general(jnp.concatenate(a, 1), jnp.concatenate(b, 1), contract, preferred_element_type=F32)

    accs[0] += product(left, left)
    accs[1] += product(cross_left, cross_right)


def gram_message(accs, out):
    same = (row_ids((STACK, STACK)) & 7) == (lane_ids((STACK, STACK)) & 7)
    pick = jnp.where((row_ids((STACK, 128)) >> 3) == lane_ids((STACK, 128)), 1.0, 0.0)

    def traces(product):
        picked = jnp.where(same, product, 0.0)
        rows = [jnp.sum(picked[8 * i : 8 * i + 8], axis=0, keepdims=True) for i in range(COLS)]
        rows = jnp.concatenate(rows + [jnp.zeros((128 - COLS, STACK), F32)], 0)
        return lax.dot_general(
            rows, pick, (((1,), (0,)), ((), ())), precision=HIGHEST, preferred_element_type=F32
        )

    cross = traces(accs[1])
    gram = traces(accs[0]) + cross + cross.T
    tops = [gram[8 * k : 8 * k + 8] for k in range(3)]
    rows, lanes = row_ids((8, 128)), lane_ids((8, 128))
    tile = jnp.where(lanes < COLS, tops[0], pltpu.roll(tops[1], 12, 1))
    corner = pltpu.roll(pltpu.roll(tops[2], 128 - 16, 1), 4, 0)
    tile = jnp.where((rows >= 4) & (lanes < 4), corner, tile)
    packed = tile
    for q in range(1, 4):
        turned = pltpu.roll(pltpu.roll(tile, 32 * q, 1), 8 - 2 * q, 0)
        packed = jnp.where((lanes >> 5) == q, turned, packed)
    packed = packed[0:2]
    for n in range(out.shape[0]):
        out[n] = packed


def gram_of(messages):
    total = messages[0]
    for n in range(1, messages.shape[0]):
        total = total + messages[n]
    total = jnp.concatenate([total] * 4, 0)
    rows, lanes = row_ids((8, 128)), lane_ids((8, 128))
    tile = total
    for q in range(1, 4):
        tile = jnp.where((rows >> 1) == q, pltpu.roll(total, 128 - 32 * q, 1), tile)
    corner = pltpu.roll(pltpu.roll(tile, 4, 0), 16, 1)
    tops = [
        jnp.where((lanes < COLS) & (lanes >= rows), tile, 0.0),
        jnp.where((lanes < COLS) & (lanes >= rows + 8), pltpu.roll(tile, 128 - 12, 1), 0.0),
        jnp.where((lanes < COLS) & (lanes >= rows + 16), corner, 0.0),
    ]
    return jnp.concatenate(tops, 0)


def slot(k):
    return k * NRHS + (NRHS if k else 0)


class Block:
    def __init__(self, stores, base, faces, faces_base, one):
        self.one = one
        self.stores, self.base, self.faces, self.faces_base = stores, base, faces, faces_base
        self.lane = lane_ids((8, 128))

    def put(self, f, z, l, t, value):
        store, f, z = self.stores[f // NRHS], f % NRHS, z - self.base
        store[f, z, l, 8 + 8 * t : 16 + 8 * t, :] = value
        if t == 0:
            store[f, z, l, 8 + ROWS : 16 + ROWS, :] = value
        if t == ROWS // 8 - 1:
            store[f, z, l, 0:8, :] = value

    def place_y(self, z, up, dn):
        for t in range(ROWS // 8):
            u_all, d_all = up[8 * t : 8 * t + 8, :], dn[8 * t : 8 * t + 8, :]
            for zz in range(4):
                for f in range(FIELDS):
                    spot = (zz * FIELDS + f) * 4
                    u = pltpu.roll(u_all, (-spot) % 128, 1) if spot else u_all
                    d = pltpu.roll(d_all, (124 - spot) % 128, 1) if spot != 124 else d_all
                    value = jnp.where(self.lane < 4, u, jnp.where(self.lane >= 124, d, 0.0))
                    self.put(f, z + zz, 2, t, value)

    def tiles(self, f, z, t, off):
        store, f, z = self.stores[f // NRHS], f % NRHS, z - self.base
        row = 8 + 8 * t + (off * self.one if off else 0)
        return [store[f, z, l, pl.ds(row, 8), :] for l in range(LT)]

    def close_ring(self, f, z):
        store, f, z = self.stores[f // NRHS], f % NRHS, z - self.base
        for l in range(2):
            store[f, z, l, 8 + ROWS : 16 + ROWS, :] = store[f, z, l, 8:16, :]

    def lane_up(self, tri):
        rolled = [pltpu.roll(v, 127, 1) for v in tri]
        return [jnp.where(self.lane == 127, rolled[(l + 1) % LT], rolled[l]) for l in range(LT)]

    def lane_dn(self, tri):
        rolled = [pltpu.roll(v, 1, 1) for v in tri]
        return [jnp.where(self.lane == 0, rolled[(l - 1) % LT], rolled[l]) for l in range(LT)]

    def coefficients(self, z):
        for t in range(ROWS // 8):
            kz, kx, ky, kd = (NRHS + i for i in range(4))
            center_z, center_x, center_y = (self.tiles(k, z, t, 0) for k in (kz, kx, ky))
            diag = self.tiles(kd, z, t, 0)
            sides = [
                (center_z, self.tiles(kz, z + 1, t, 0)),
                (center_z, self.tiles(kz, z - 1, t, 0)),
                (center_x, self.tiles(kx, z, t, 1)),
                (center_x, self.tiles(kx, z, t, -1)),
                (center_y, self.lane_up(center_y)),
                (center_y, self.lane_dn(center_y)),
            ]
            at = z - self.faces_base
            for l in range(LT):
                inside = diag[l] > 0.0
                total = diag[l] * SCALE
                for k, (mid, side) in enumerate(sides):
                    face = (mid[l] + side[l]) * (0.5 * SCALE)
                    total = total + face
                    self.faces[k, at, l, 8 * t : 8 * t + 8, :] = jnp.where(inside, face, 0.0)
                self.faces[6, at, l, 8 * t : 8 * t + 8, :] = jnp.where(inside, total, 0.0)

    def apply(self, k, z):
        last = k == STEPS - 1
        at = z - self.faces_base
        outs = 2 if last else LT
        for t in range(NX // 8 if last else ROWS // 8):
            face = [[self.faces[c, at, l, 8 * t : 8 * t + 8, :] for l in range(outs)] for c in range(7)]
            diag = [face[6][l] - SHIFTS[k] * SCALE for l in range(outs)]
            for r in range(NRHS):
                f = slot(k) + r
                mid = self.tiles(f, z, t, 0)
                sides = [
                    self.tiles(f, z + 1, t, 0),
                    self.tiles(f, z - 1, t, 0),
                    self.tiles(f, z, t, 1),
                    self.tiles(f, z, t, -1),
                    self.lane_up(mid),
                    self.lane_dn(mid),
                ]
                for l in range(outs):
                    value = diag[l] * mid[l]
                    for c in range(6):
                        value = value - face[c][l] * sides[c][l]
                    self.put(slot(k + 1) + r, z, l, t, value)


def dynamic_one(place):
    return (place[0] >> 24) + 1


def loop(start, stop, do):
    def step(n, carry):
        do(n)
        return carry

    lax.fori_loop(start, stop, step, 0)


def inner_planes(k):
    return DEPTH + k, DEPTH + NZ - k


def inner_copies(inner, inner_faces, stores, base, faces, faces_base, sems, out):
    def copy(n, there, here):
        src, dst = (here, there) if out else (there, here)
        return pltpu.make_async_copy(src, dst, sems.at[n])

    def planes(ref, f, start, stop, at):
        return ref.at[pl.ds(f, NRHS), pl.ds(start - at, stop - start)]

    result = []
    for n, (f, start, stop) in enumerate(
        [(f, z, z + 2) for f in (0, NRHS) for z in (DEPTH, DEPTH + NZ - 2)]
        + [(0, DEPTH + 2, DEPTH + NZ - 2)]
        + [(slot(k), *inner_planes(k)) for k in range(1, STEPS)]
    ):
        there = planes(inner, f, start, stop, DEPTH)
        result.append(copy(n, there, stores[f // NRHS].at[:, pl.ds(start - base, stop - start)]))
    start, stop = inner_planes(1)
    result.append(copy(len(result), inner_faces, faces.at[:, pl.ds(start - faces_base, stop - start)]))
    return result


def krylov_inner(swap, place, rhs, cz, cx, cy, dg, *rest):
    above, below, yup, ydn, inner, inner_faces, *stores, faces, load_sems, sems = rest if not swap else rest[:1] + rest
    keep_up, keep_dn = keep_sides(swap, place)
    block = Block(stores, DEPTH, faces, DEPTH + 1, dynamic_one(place))
    loads = []
    for n, src in enumerate((rhs, cz, cx, cy, dg)):
        for l in range(2):
            lanes = pl.ds(128 * l, 128)
            rows = pl.ds(8, NX)
            if n == 0:
                src_at, dst = src.at[:, :, :, lanes], stores[0].at[:, :, l, rows, :]
            else:
                src_at, dst = src.at[:, :, lanes], stores[1].at[n - 1, :, l, rows, :]
            loads.append(pltpu.make_async_copy(src_at, dst, load_sems.at[2 * n + l]))
            loads[-1].start()
    for f in range(FIELDS):
        for z in range(DEPTH, DEPTH + NZ):
            m = (z - DEPTH) // 2
            for l in range(2):
                lanes = pl.ds(128 * l, 128)
                tile = halo_tile(above[f, m, :, lanes], below[f, m, :, lanes], z % 2, keep_up, keep_dn)
                block.put(f, z, l, NX // 8, tile)
    for half in range(2):
        lanes = pl.ds(128 * half, 128)
        block.place_y(DEPTH + 4 * half, yup.at[:, lanes], ydn.at[:, lanes])
    for copy in loads:
        copy.wait()
    for f in range(FIELDS):
        for z in range(DEPTH, DEPTH + NZ):
            block.close_ring(f, z)
    copies = inner_copies(inner, inner_faces, stores, DEPTH, faces, DEPTH + 1, sems, True)
    for n in range(5):
        copies[n].start()
    loop(*inner_planes(1), block.coefficients)
    copies[-1].start()
    for k in range(STEPS - 1):
        loop(*inner_planes(k + 1), functools.partial(block.apply, k))
        copies[5 + k].start()
    for copy in copies:
        copy.wait()


NEAR, FAR = 8 * FIELDS, 24


def krylov_outer(
    swap, face_one, face_two, place, odd_z, inner, inner_faces, rim_one, rim_two,
    basis, message,
    *rest,
):
    keep_up, keep_dn = keep_sides(swap, place)
    n_x = 1 if swap else 2
    *stores, faces, accs, rims, plane_sems, loads, saves = rest
    odd = odd_z[0] == 1
    block = Block(stores, 0, faces, 0, dynamic_one(place))
    copies = inner_copies(inner, inner_faces, stores, 0, faces, 0, loads, False)
    def plane_copies(lower, upper):
        planes = []
        start = 0
        for f in range(FIELDS):
            depth = DEPTH if f <= NRHS else DEPTH - 1
            for side, (face, z) in enumerate(((lower, DEPTH - depth), (upper, DEPTH + NZ))):
                for l in range(2):
                    planes.append(
                        pltpu.make_async_copy(
                            face.at[pl.ds(start, depth), :, pl.ds(128 * l, 128)],
                            stores[f // NRHS].at[f % NRHS, pl.ds(z, depth), l, pl.ds(8, NX), :],
                            plane_sems.at[4 * f + 2 * side + l],
                        )
                    )
            start += depth
        return planes

    for copy in copies[:4]:
        copy.start()

    @pl.when(odd)
    def _():
        for copy in plane_copies(face_one, face_two):
            copy.start()

    @pl.when(jnp.logical_not(odd))
    def _():
        for copy in plane_copies(face_two, face_one):
            copy.start()

    one, two = rim_one[...], rim_two[...]
    rims[0] = jnp.where(odd, one, two)
    rims[1] = jnp.where(odd, two, one)
    rimlo, rimhi = rims.at[0], rims.at[1]

    zero = jnp.zeros((8, 128), F32)
    for f in range(FIELDS):
        for rim, first in ((rimlo, 0), (rimhi, DEPTH + NZ)):
            for z in range(first, first + DEPTH):
                far = DEPTH - z if first == 0 else z - first + 1
                for l in range(2):
                    lanes = pl.ds(128 * l, 128)
                    if far <= 2:
                        at, odd = 8 * f, z % 2
                    elif far == 3 and 8 * (f // 2) < FAR:
                        at, odd = NEAR + 8 * (f // 2), f % 2
                    else:
                        block.put(f, z, l, NX // 8, zero)
                        continue
                    other = at + (n_x - 1) * (NEAR + FAR)
                    tile = halo_tile(rim[at : at + 8, lanes], rim[other : other + 8, lanes], odd, keep_up, keep_dn)
                    block.put(f, z, l, NX // 8, tile)
    rows = pl.ds(n_x * (NEAR + FAR), ROWS)
    for rim, z in ((rimlo, 0), (rimhi, DEPTH + NZ)):
        block.place_y(z, rim.at[rows, pl.ds(0, 128)], rim.at[rows, pl.ds(128, 128)])

    for copy in copies[:4] + plane_copies(face_one, face_two):
        copy.wait()
    for copy in [copies[5], copies[-1], copies[6], copies[7], copies[4]]:
        copy.start()
    for f in range(FIELDS):
        depth = DEPTH if f <= NRHS else DEPTH - 1
        for d in range(depth):
            block.close_ring(f, DEPTH - 1 - d)
            block.close_ring(f, DEPTH + NZ + d)
    loop(1, DEPTH + 1, block.coefficients)
    loop(DEPTH + NZ - 1, EZ - 1, block.coefficients)

    sends = []

    def send_block(k):
        copy = pltpu.make_async_copy(
            stores[slot(k) // NRHS].at[:, pl.ds(DEPTH, NZ), pl.ds(0, 2), pl.ds(8, NX), :],
            basis.at[pl.ds(k * NRHS, NRHS)],
            saves.at[k],
        )
        copy.start()
        sends.append(copy)

    for k in range(STEPS):
        if k == 1:
            copies[-1].wait()
        loop(
            0,
            2 * DEPTH,
            lambda n, k=k: block.apply(k, n + k + 1 + jnp.where(n >= DEPTH, NZ - 2 - 2 * k, 0)),
        )
        if k < STEPS - 1:
            copies[5 + k].wait()
        send_block(k + 1)
    copies[4].wait()
    send_block(0)
    gram_zero(accs)

    def products(z):
        def tile(i, t):
            store = stores[slot(i // NRHS) // NRHS]
            return jnp.concatenate([store[i % NRHS, z, l, 8 + 8 * t : 16 + 8 * t, :] for l in range(2)], 1)

        gram_add([jnp.concatenate([tile(i, t) for i in range(COLS)], 0) for t in range(NX // 8)], accs)

    loop(DEPTH, DEPTH + NZ, products)
    gram_message(accs, message)
    for copy in sends:
        copy.wait()


def factor_gram(messages, cells, table):
    rows = row_ids((24, 128))
    lanes = lane_ids((24, 128))
    upper = gram_of(messages) / cells
    square = jnp.concatenate([upper, jnp.zeros((104, 128), F32)], 0).T
    whole = jnp.where(rows <= lanes, upper, square[0:24, :])

    def splat(value):
        return jnp.broadcast_to(value, (24, 128))

    columns = [splat(whole[:, c : c + 1]) for c in range(COLS)]
    inverse = [jnp.where(rows == c, 1.0, 0.0) for c in range(COLS)]
    pivots = jnp.ones((24, 128), F32)
    factor = jnp.zeros((24, 128), F32)
    for j in range(COLS):
        pivot = splat(columns[j][j : j + 1, :])
        pivots = jnp.where(rows == j, pivot, pivots)
        below = jnp.where(rows > j, columns[j] / pivot, 0.0)
        for c in range(j, COLS):
            row = splat(columns[c][j : j + 1, :])
            factor = jnp.where((rows == j) & (lanes == c), row, factor)
            if c > j:
                columns[c] = columns[c] - below * row
        for c in range(j + 1):
            inverse[c] = inverse[c] - below * splat(inverse[c][j : j + 1, :])
    roots = jnp.sqrt(pivots)
    for c in range(COLS):
        table[c] = inverse[c] / roots
    return factor / roots


def apply_rows(table, read, write):
    group = 5
    pieces = NX // 8
    for g in reversed(range(COLS // group)):
        mine = range(group * g, group * g + group)
        sums = {i: None for i in mine}
        for j in range(group * g + group):
            value = [read(j, p) for p in range(pieces)]
            for i in mine:
                if j <= i:
                    weight = jnp.broadcast_to(table[j, i : i + 1, :], (8, 128))
                    terms = [weight * v for v in value]
                    sums[i] = terms if sums[i] is None else [s + t for s, t in zip(sums[i], terms)]
        for i in mine:
            for p in range(pieces):
                write(i, p, sums[i][p])


def plane_copy(src, dst, sems, z):
    return pltpu.make_async_copy(src.at[:, z], dst.at[:, z], sems.at[z])


def first_pass(
    cells, message, basis_hbm, first_hbm, next_message, factor_out, basis, first, table, accs, loads, saves
):
    for z in range(NZ):
        plane_copy(basis_hbm, basis, loads, z).start()
    factor_out[...] = factor_gram(message, cells, table)
    gram_zero(accs)

    def products(z):
        def tile(i, t):
            return jnp.concatenate([first[i, z, l, 8 * t : 8 * t + 8, :] for l in range(2)], 1)

        gram_add([jnp.concatenate([tile(i, t) for i in range(COLS)], 0) for t in range(NX // 8)], accs)

    def apply(z):
        for l in range(2):

            def read(j, p):
                return basis[j, z, l, 8 * p : 8 * p + 8, :]

            def write(i, p, value):
                first[i, z, l, 8 * p : 8 * p + 8, :] = value

            apply_rows(table, read, write)
        plane_copy(first, first_hbm, saves, z).start()

    def both(z):
        plane_copy(basis_hbm, basis, loads, z).wait()
        products(z - 1)
        apply(z)

    plane_copy(basis_hbm, basis, loads, 0).wait()
    apply(0)
    loop(1, NZ, both)
    products(NZ - 1)
    gram_message(accs, next_message)
    for z in range(NZ):
        plane_copy(first, first_hbm, saves, z).wait()


def second_pass(cells, message, factor_one, first_hbm, out_hbm, triangle, first, out, table, loads, saves):
    for z in range(NZ):
        plane_copy(first_hbm, first, loads, z).start()
    left = factor_gram(message, cells, table)[:, 0:24]
    product = lax.dot_general(
        left, factor_one[...], (((1,), (0,)), ((), ())), precision=HIGHEST, preferred_element_type=F32
    )
    triangle[...] = product[0:COLS, 0:COLS]

    def chunk(z, carry):
        plane_copy(first_hbm, first, loads, z).wait()
        for l in range(2):

            def read(j, p):
                return first[j, z, l, 8 * p : 8 * p + 8, :]

            def write(i, p, value):
                out[i, z, 8 * p : 8 * p + 8, 128 * l : 128 * l + 128] = value

            apply_rows(table, read, write)
        plane_copy(out, out_hbm, saves, z).start()
        return carry

    lax.fori_loop(0, NZ, chunk, 0)
    for z in range(NZ):
        plane_copy(out, out_hbm, saves, z).wait()


def shape(*dims):
    return jax.ShapeDtypeStruct(dims, F32)


def move(value, axis, delta):
    count = lax.axis_size(axis)
    pairs = [(i, i + delta) for i in range(count) if 0 <= i + delta < count]
    return lax.ppermute(value, axis, pairs)


def swap_pairs(value, axis, first):
    pairs = [(i, i + 1) for i in range(first, lax.axis_size(axis) - 1, 2)]
    return lax.ppermute(value, axis, pairs + [(j, i) for i, j in pairs])


def exchange(messages):
    return lax.all_to_all(messages, AXES, 0, 0, tiled=True)


def body(rhs, coef_x, coef_y, coef_z, diag_term):
    n_x = lax.axis_size("gx")
    devices = n_x * lax.axis_size("gy") * lax.axis_size("gz")
    cells = float(NZ * NX * NY * devices)
    at_x = lax.axis_index("gx")
    swap = n_x == 2
    fields = (rhs, coef_z, coef_x, coef_y, diag_term)

    place = at_x.astype(jnp.int32).reshape(1)
    odd_z = ((lax.axis_index("gz") + 1) & 1).astype(jnp.int32).reshape(1)
    odd_y = (lax.axis_index("gy") & 1).astype(jnp.int32).reshape(1)
    face_shape = shape(FACE, NX, NY)
    x_shape = shape(FIELDS, NZ // 2, 8, NY)
    own_shape = shape(NX, NY)
    z_one, z_two, own_one, own_two, *xmsgs = pl.pallas_call(
        functools.partial(pack_faces, swap),
        out_shape=(face_shape, face_shape, own_shape, own_shape) + (x_shape,) * (1 if swap else 2),
        in_specs=[smem()] * 3 + [hbm()] * 5,
        out_specs=(hbm(), hbm()) + (vmem(),) * (3 if swap else 4),
        scratch_shapes=[
            pltpu.VMEM((FIELDS, NZ, NX, NY), F32),
            pltpu.SemaphoreType.DMA((FIELDS,)),
            pltpu.SemaphoreType.DMA((2 * FIELDS,)),
        ],
        compiler_params=params(LIMIT),
        cost_estimate=cost(2.5),
    )(place, odd_z, odd_y, *fields)
    face_one, face_two = swap_pairs(z_one, "gz", 1), swap_pairs(z_two, "gz", 0)
    if swap:
        x_parts = (lax.ppermute(xmsgs[0], "gx", [(0, 1), (1, 0)]),)
    else:
        x_parts = (move(xmsgs[0], "gx", -1), move(xmsgs[1], "gx", 1))

    halo_shape = shape(ROWS - NX, NY)
    halo_one, halo_two = pl.pallas_call(
        functools.partial(pack_rims, swap),
        out_shape=(halo_shape, halo_shape),
        in_specs=[smem()] * 2 + [vmem()] * len(x_parts),
        compiler_params=params(16),
        cost_estimate=cost(1),
    )(place, odd_y, *x_parts)
    y_one = swap_pairs(jnp.concatenate([own_one, halo_one], 0), "gy", 0)
    y_two = swap_pairs(jnp.concatenate([own_two, halo_two], 0), "gy", 1)
    yup, ydn = jnp.where(odd_y == 1, y_two, y_one), jnp.where(odd_y == 1, y_one, y_two)

    def rim(half):
        near, far, odd = ((0, 1, 0), (3, 2, 1))[half]
        rows = []
        for part in x_parts:
            rows.append(part[:, near].reshape(NEAR, NY))
            rows.append(part[: FAR // 4, far, 4 * odd : 4 * odd + 4].reshape(FAR, NY))
        lanes = slice(128 * half, 128 * half + 128)
        return jnp.concatenate(rows + [jnp.concatenate([yup[:, lanes], ydn[:, lanes]], 1)], 0)

    low, high = rim(0), rim(1)
    rim_one = swap_pairs(jnp.where(odd_z == 1, low, high), "gz", 1)
    rim_two = swap_pairs(jnp.where(odd_z == 1, high, low), "gz", 0)

    inner_shape = shape(COLS, NZ, LT, EROWS, 128)
    inner_faces_shape = shape(7, NZ - 2, LT, ROWS, 128)
    inner, inner_faces = pl.pallas_call(
        functools.partial(krylov_inner, swap),
        out_shape=(inner_shape, inner_faces_shape),
        in_specs=[smem()] + [hbm()] * 5 + [vmem()] * (len(x_parts) + 2),
        out_specs=(hbm(), hbm()),
        scratch_shapes=[
            *[pltpu.VMEM((NRHS,) + inner_shape.shape[1:], F32)] * (STEPS + 1),
            pltpu.VMEM(inner_faces_shape.shape, F32),
            pltpu.SemaphoreType.DMA((10,)),
            pltpu.SemaphoreType.DMA((9,)),
        ],
        compiler_params=params(LIMIT),
        cost_estimate=cost(7),
    )(place, *fields, *x_parts, yup, ydn)

    block = shape(COLS, NZ, 2, NX, 128)
    basis, message = pl.pallas_call(
        functools.partial(krylov_outer, swap),
        out_shape=(block, shape(devices, 2, 128)),
        in_specs=[hbm(), hbm(), smem(), smem(), hbm(), hbm(), vmem(), vmem()],
        out_specs=(hbm(), vmem()),
        scratch_shapes=[
            *[pltpu.VMEM((NRHS, EZ, LT, EROWS, 128), F32)] * (STEPS + 2),
            pltpu.VMEM((7, EZ, LT, ROWS, 128), F32),
            pltpu.VMEM((2, STACK, STACK), F32),
            pltpu.VMEM((2,) + rim_one.shape, F32),
            pltpu.SemaphoreType.DMA((4 * FIELDS,)),
            pltpu.SemaphoreType.DMA((9,)),
            pltpu.SemaphoreType.DMA((STEPS + 1,)),
        ],
        compiler_params=params(LIMIT),
        cost_estimate=cost(15),
    )(face_one, face_two, place, odd_z, inner, inner_faces, rim_one, rim_two)

    message = exchange(message)
    first, message, factor_one = pl.pallas_call(
        functools.partial(first_pass, cells),
        out_shape=(block, shape(devices, 2, 128), shape(24, 128)),
        in_specs=[vmem(), hbm()],
        out_specs=(hbm(), vmem(), vmem()),
        scratch_shapes=[
            pltpu.VMEM(block.shape, F32),
            pltpu.VMEM(block.shape, F32),
            pltpu.VMEM((COLS, 24, 128), F32),
            pltpu.VMEM((2, STACK, STACK), F32),
            pltpu.SemaphoreType.DMA((NZ,)),
            pltpu.SemaphoreType.DMA((NZ,)),
        ],
        compiler_params=params(LIMIT),
    )(message, basis)

    message = exchange(message)
    return pl.pallas_call(
        functools.partial(second_pass, cells),
        out_shape=(shape(COLS, NZ, NX, NY), shape(COLS, COLS)),
        in_specs=[vmem(), vmem(), hbm()],
        out_specs=(hbm(), vmem()),
        scratch_shapes=[
            pltpu.VMEM(block.shape, F32),
            pltpu.VMEM((COLS, NZ, NX, NY), F32),
            pltpu.VMEM((COLS, 24, 128), F32),
            pltpu.SemaphoreType.DMA((NZ,)),
            pltpu.SemaphoreType.DMA((NZ,)),
        ],
        compiler_params=params(LIMIT),
    )(message, factor_one, first)


def solution(mesh):
    return jax.shard_map(
        body,
        mesh=mesh,
        in_specs=(
            P(None, "gz", "gx", "gy"),
            P("gz", "gx", "gy"),
            P("gz", "gx", "gy"),
            P("gz", "gx", "gy"),
            P("gz", "gx", "gy"),
        ),
        out_specs=(P(None, "gz", "gx", "gy"), P()),
        check_vma=False,
    )
```

```python
import functools

import jax
import jax.numpy as jnp
from jax import lax
from jax.experimental import pallas as pl
from jax.experimental.pallas import tpu as pltpu
from jax.sharding import PartitionSpec as P

NRHS = 4
STEPS = 4
COLS = NRHS * (STEPS + 1)
SHIFTS = (3.0, 11.0, 7.0, 1.5)
SCALE = 1.0 / 6.0
FIELDS = NRHS + 4
AXES = ("gx", "gy", "gz")
HIGHEST = lax.Precision.HIGHEST

DEPTH = 4
NZ, NX, NY = 8, 32, 256
EZ = NZ + 2 * DEPTH
ROWS = NX + 8
EROWS = ROWS + 16
LT = 3
FACE = NRHS * 4 + 3 * 4 + 1
F32 = jnp.float32
LIMIT = 63


def params(mb):
    return pltpu.CompilerParams(vmem_limit_bytes=mb << 20)


def cost(us):
    return pl.CostEstimate(flops=0, bytes_accessed=int(us * 3.6e6), transcendentals=0)


def vmem():
    return pl.BlockSpec(memory_space=pltpu.VMEM)


def smem():
    return pl.BlockSpec(memory_space=pltpu.SMEM)


def hbm():
    return pl.BlockSpec(memory_space=pl.ANY)


def row_ids(shape):
    return lax.broadcasted_iota(jnp.int32, shape, 0)


def lane_ids(shape):
    return lax.broadcasted_iota(jnp.int32, shape, 1)


def field_of(rhs, cz, cx, cy, dg, f, z):
    return rhs.at[f, z] if f < NRHS else (cz, cx, cy, dg)[f - NRHS].at[z]


def pack_faces(swap, place, odd_z, rhs, cz, cx, cy, dg, z_one, z_two, *rest):
    xmsgs, (whole, loads, saves) = rest[:-3], rest[-3:]
    copies = []
    for f in range(FIELDS):
        src = rhs.at[f] if f < NRHS else (cz, cx, cy, dg)[f - NRHS]
        copies.append(pltpu.make_async_copy(src, whole.at[f], loads.at[f]))
        copies[-1].start()
    low = row_ids((8, NY)) < 4
    up = place[0] == 0
    planes = []
    at = 0
    for f in range(FIELDS):
        copies[f].wait()
        depth = DEPTH if f <= NRHS else DEPTH - 1
        for side, out in ((0, z_one), (1, z_two)):
            start = jnp.where(odd_z[0] == side, NZ - depth, 0)
            planes.append(
                pltpu.make_async_copy(
                    whole.at[f, pl.ds(start, depth)], out.at[pl.ds(at, depth)], saves.at[2 * f + side]
                )
            )
            planes[-1].start()
        at += depth
        for m in range(NZ // 2):
            a, b = whole.at[f, 2 * m], whole.at[f, 2 * m + 1]
            first = jnp.where(low, a[0:8], pltpu.roll(b[0:8], 4, 0))
            last = jnp.where(low, pltpu.roll(a[NX - 8 : NX], 4, 0), b[NX - 8 : NX])
            if swap:
                xmsgs[0][f, m] = jnp.where(up, last, first)
            else:
                xmsgs[0][f, m] = first
                xmsgs[1][f, m] = last
    for copy in planes:
        copy.wait()


def halo_tile(above, below, odd, keep_up, keep_dn):
    low = row_ids(above.shape) < 4
    if odd:
        up, dn = pltpu.roll(above, 4, 0), below
    else:
        up, dn = above, pltpu.roll(below, 4, 0)
    return jnp.where(low, up * keep_up, dn * keep_dn)


def keep_sides(swap, place):
    if not swap:
        return 1.0, 1.0
    first = place[0] == 0
    return jnp.where(first, 1.0, 0.0), jnp.where(first, 0.0, 1.0)


def pack_lanes(tile_of, side):
    lane = lane_ids((8, 128))
    source = 124 * side
    acc = jnp.zeros((8, 128), F32)
    for zz in range(4):
        for f in range(FIELDS):
            tile = tile_of(f, zz)
            spot = (zz * FIELDS + f) * 4
            shift = (spot - source) % 128
            if shift:
                tile = pltpu.roll(tile, shift, 1)
            acc = jnp.where((lane >= spot) & (lane < spot + 4), tile, acc)
    return acc


def pack_own_rims(odd_y, rhs, cz, cx, cy, dg, one, two):
    odd = odd_y[0] == 1
    for t in range(NX // 8):
        for half in range(2):
            lo, hi = (
                pack_lanes(
                    lambda f, zz: field_of(rhs, cz, cx, cy, dg, f, 4 * half + zz)[
                        8 * t : 8 * t + 8, 128 * side : 128 * side + 128
                    ],
                    side,
                )
                for side in range(2)
            )
            one[8 * t : 8 * t + 8, 128 * half : 128 * half + 128] = jnp.where(odd, lo, hi)
            two[8 * t : 8 * t + 8, 128 * half : 128 * half + 128] = jnp.where(odd, hi, lo)


def pack_rims(swap, place, odd_y, *refs):
    above, below, one, two = refs if not swap else (refs[0],) + refs
    keep_up, keep_dn = keep_sides(swap, place)
    odd = odd_y[0] == 1
    for half in range(2):
        halves = []
        for side in range(2):
            lanes = slice(128 * side, 128 * side + 128)
            halves.append(
                pack_lanes(
                    lambda f, zz: halo_tile(
                        above[f, 2 * half + zz // 2, :, lanes],
                        below[f, 2 * half + zz // 2, :, lanes],
                        zz % 2,
                        keep_up,
                        keep_dn,
                    ),
                    side,
                )
            )
        lo, hi = halves
        one[:, 128 * half : 128 * half + 128] = jnp.where(odd, lo, hi)
        two[:, 128 * half : 128 * half + 128] = jnp.where(odd, hi, lo)


STACK = 8 * COLS


def gram_zero(accs):
    accs[...] = jnp.zeros_like(accs)


def gram_add(stacks, accs):
    left, right = [], []
    cross_left, cross_right = [], []
    for stack in stacks:
        high = stack.astype(jnp.bfloat16)
        rest = stack - high.astype(F32)
        mid = rest.astype(jnp.bfloat16)
        low = (rest - mid.astype(F32)).astype(jnp.bfloat16)
        left += [high, mid]
        cross_left += [high, high]
        cross_right += [mid, low]
    contract = (((1,), (1,)), ((), ()))

    def product(a, b):
        return lax.dot_general(jnp.concatenate(a, 1), jnp.concatenate(b, 1), contract, preferred_element_type=F32)

    accs[0] += product(left, left)
    accs[1] += product(cross_left, cross_right)


def gram_message(accs, out):
    same = (row_ids((STACK, STACK)) & 7) == (lane_ids((STACK, STACK)) & 7)
    pick = jnp.where((row_ids((STACK, 128)) >> 3) == lane_ids((STACK, 128)), 1.0, 0.0)

    def traces(product):
        picked = jnp.where(same, product, 0.0)
        rows = [jnp.sum(picked[8 * i : 8 * i + 8], axis=0, keepdims=True) for i in range(COLS)]
        rows = jnp.concatenate(rows + [jnp.zeros((128 - COLS, STACK), F32)], 0)
        return lax.dot_general(
            rows, pick, (((1,), (0,)), ((), ())), precision=HIGHEST, preferred_element_type=F32
        )

    cross = traces(accs[1])
    gram = traces(accs[0]) + cross + cross.T
    tops = [gram[8 * k : 8 * k + 8] for k in range(3)]
    rows, lanes = row_ids((8, 128)), lane_ids((8, 128))
    tile = jnp.where(lanes < COLS, tops[0], pltpu.roll(tops[1], 12, 1))
    corner = pltpu.roll(pltpu.roll(tops[2], 128 - 16, 1), 4, 0)
    tile = jnp.where((rows >= 4) & (lanes < 4), corner, tile)
    packed = tile
    for q in range(1, 4):
        turned = pltpu.roll(pltpu.roll(tile, 32 * q, 1), 8 - 2 * q, 0)
        packed = jnp.where((lanes >> 5) == q, turned, packed)
    packed = packed[0:2]
    for n in range(out.shape[0]):
        out[n] = packed


def gram_of(messages):
    total = messages[0]
    for n in range(1, messages.shape[0]):
        total = total + messages[n]
    total = jnp.concatenate([total] * 4, 0)
    rows, lanes = row_ids((8, 128)), lane_ids((8, 128))
    tile = total
    for q in range(1, 4):
        tile = jnp.where((rows >> 1) == q, pltpu.roll(total, 128 - 32 * q, 1), tile)
    corner = pltpu.roll(pltpu.roll(tile, 4, 0), 16, 1)
    tops = [
        jnp.where((lanes < COLS) & (lanes >= rows), tile, 0.0),
        jnp.where((lanes < COLS) & (lanes >= rows + 8), pltpu.roll(tile, 128 - 12, 1), 0.0),
        jnp.where((lanes < COLS) & (lanes >= rows + 16), corner, 0.0),
    ]
    return jnp.concatenate(tops, 0)


GROUPS = (9, 12, 9, 9, 9, 9)


def group(k):
    return k + 1 if k else 0


class Block:
    def __init__(self, stores, base, faces, faces_base, one):
        self.one = one
        self.stores, self.base, self.faces, self.faces_base = stores, base, faces, faces_base
        self.lane = lane_ids((8, 128))

    def where(self, f, l):
        return (0, 2 * f + l) if f < NRHS else (1, 3 * (f - NRHS) + l)

    def put(self, g, n, z, t, value):
        store, z = self.stores[g], z - self.base
        store[n, z, 8 + 8 * t : 16 + 8 * t, :] = value
        if t == 0:
            store[n, z, 8 + ROWS : 16 + ROWS, :] = value
        if t == ROWS // 8 - 1:
            store[n, z, 0:8, :] = value

    def get(self, g, n, z, t, off=0):
        row = 8 + 8 * t + (off * self.one if off else 0)
        return self.stores[g][n, z - self.base, pl.ds(row, 8), :]

    def close_ring(self, f, z):
        z = z - self.base
        for l in range(2):
            g, n = self.where(f, l)
            self.stores[g][n, z, 8 + ROWS : 16 + ROWS, :] = self.stores[g][n, z, 8:16, :]

    def place_y(self, z, up, dn):
        lane = self.lane
        for t in range(ROWS // 8):
            u_all, d_all = up[8 * t : 8 * t + 8, :], dn[8 * t : 8 * t + 8, :]

            def turned(value, shift):
                return pltpu.roll(value, shift % 128, 1) if shift % 128 else value

            def pair(f, zz, r, rest):
                spot = (zz * FIELDS + f) * 4
                u = turned(u_all, 32 * r - spot)
                d = turned(d_all, 32 * r + 28 - spot)
                rest = jnp.where((lane >= 32 * r) & (lane < 32 * r + 4), u, rest)
                return jnp.where((lane >= 32 * r + 28) & (lane < 32 * r + 32), d, rest)

            zero = jnp.zeros((8, 128), F32)
            for zz in range(4):
                value = zero
                for r in range(NRHS):
                    value = pair(r, zz, r, value)
                self.put(0, 2 * NRHS, z + zz, t, value)
                for c in range(4):
                    value = pair(NRHS + c, zz, 0, zero)
                    value = value + turned(value, 32)
                    value = value + turned(value, 64)
                    self.put(1, 3 * c + 2, z + zz, t, value)

    def coefficients(self, z):
        lane = self.lane
        for t in range(ROWS // 8):

            def tiles(c, z, off=0):
                return [self.get(1, 3 * c + l, z, t, off) for l in range(LT)]

            center_z, center_x, center_y, diag = (tiles(c, z) for c in range(4))
            up = [pltpu.roll(v, 127, 1) for v in center_y]
            dn = [pltpu.roll(v, 1, 1) for v in center_y]
            first = jnp.broadcast_to(center_y[0][:, 0:1], (8, 128))
            last = jnp.broadcast_to(center_y[1][:, 127:128], (8, 128))
            sides = [
                (center_z, tiles(0, z + 1)),
                (center_z, tiles(0, z - 1)),
                (center_x, tiles(1, z, 1)),
                (center_x, tiles(1, z, -1)),
                (
                    center_y,
                    [
                        jnp.where(lane == 127, up[1], up[0]),
                        jnp.where(lane == 127, up[2], up[1]),
                        jnp.where((lane & 31) == 31, first, up[2]),
                    ],
                ),
                (
                    center_y,
                    [
                        jnp.where(lane == 0, dn[2], dn[0]),
                        jnp.where(lane == 0, dn[0], dn[1]),
                        jnp.where((lane & 31) == 0, last, dn[2]),
                    ],
                ),
            ]
            at = z - self.faces_base
            for l in range(LT):
                inside = diag[l] > 0.0
                total = diag[l] * SCALE
                for k, (mid, side) in enumerate(sides):
                    face = (mid[l] + side[l]) * (0.5 * SCALE)
                    total = total + face
                    self.faces[k, at, l, 8 * t : 8 * t + 8, :] = jnp.where(inside, face, 0.0)
                self.faces[6, at, l, 8 * t : 8 * t + 8, :] = jnp.where(inside, total, 0.0)

    def apply(self, k, z):
        last = k == STEPS - 1
        at, lane, edge = z - self.faces_base, self.lane, 2 * NRHS
        src, dst = group(k), group(k + 1)
        for t in range(NX // 8 if last else ROWS // 8):
            face = [
                [self.faces[c, at, l, 8 * t : 8 * t + 8, :] for l in range(2 if last else LT)] for c in range(7)
            ]
            diag = [d - SHIFTS[k] * SCALE for d in face[6]]

            def image(n, l, mid, up, dn):
                sides = (
                    self.get(src, n, z + 1, t),
                    self.get(src, n, z - 1, t),
                    self.get(src, n, z, t, 1),
                    self.get(src, n, z, t, -1),
                    up,
                    dn,
                )
                value = diag[l] * mid
                for c, side in enumerate(sides):
                    value = value - face[c][l] * side
                self.put(dst, n, z, t, value)

            rim = self.get(src, edge, z, t)
            rim_up, rim_dn = pltpu.roll(rim, 127, 1), pltpu.roll(rim, 1, 1)
            edge_up, edge_dn = rim_up, rim_dn
            for r in range(NRHS):
                one, two = self.get(src, 2 * r, z, t), self.get(src, 2 * r + 1, z, t)
                one_up, two_up = pltpu.roll(one, 127, 1), pltpu.roll(two, 127, 1)
                one_dn, two_dn = pltpu.roll(one, 1, 1), pltpu.roll(two, 1, 1)
                above = rim_up if r == 0 else pltpu.roll(rim, 127 - 32 * r, 1)
                below = rim_dn if r == NRHS - 1 else pltpu.roll(rim, 97 - 32 * r, 1)
                image(2 * r, 0, one, jnp.where(lane == 127, two_up, one_up), jnp.where(lane == 0, below, one_dn))
                image(2 * r + 1, 1, two, jnp.where(lane == 127, above, two_up), jnp.where(lane == 0, one_dn, two_dn))
                if not last:
                    start = one_up if r == NRHS - 1 else pltpu.roll(one, 32 * r + 31, 1)
                    end = two_dn if r == 0 else pltpu.roll(two, 32 * r + 1, 1)
                    edge_up = jnp.where(lane == 32 * r + 31, start, edge_up)
                    edge_dn = jnp.where(lane == 32 * r, end, edge_dn)
            if not last:
                image(edge, 2, rim, edge_up, edge_dn)


def dynamic_one(place):
    return (place[0] >> 24) + 1


def loop(start, stop, do):
    def step(n, carry):
        do(n)
        return carry

    lax.fori_loop(start, stop, step, 0)


def inner_planes(k):
    return DEPTH + k, DEPTH + NZ - k


def inner_copies(inner, inner_faces, stores, base, faces, faces_base, sems, out):
    def copy(n, there, here):
        src, dst = (here, there) if out else (there, here)
        return pltpu.make_async_copy(src, dst, sems.at[n])

    result = []
    for n, (g, start, stop) in enumerate(
        [(g, z, z + 2) for g in (0, 1) for z in (DEPTH, DEPTH + NZ - 2)]
        + [(0, DEPTH + 2, DEPTH + NZ - 2)]
        + [(group(k), *inner_planes(k)) for k in range(1, STEPS)]
    ):
        there = inner.at[pl.ds(sum(GROUPS[:g]), GROUPS[g]), pl.ds(start - DEPTH, stop - start)]
        result.append(copy(n, there, stores[g].at[:, pl.ds(start - base, stop - start)]))
    start, stop = inner_planes(1)
    result.append(copy(len(result), inner_faces, faces.at[:, pl.ds(start - faces_base, stop - start)]))
    return result


def krylov_inner(swap, place, rhs, cz, cx, cy, dg, *rest):
    above, below, yup, ydn, inner, inner_faces, *stores, faces, load_sems, sems = rest if not swap else rest[:1] + rest
    keep_up, keep_dn = keep_sides(swap, place)
    block = Block(stores, DEPTH, faces, DEPTH + 1, dynamic_one(place))
    loads = []
    for f in range(FIELDS):
        src = rhs.at[f] if f < NRHS else (cz, cx, cy, dg)[f - NRHS]
        for l in range(2):
            g, n = block.where(f, l)
            loads.append(
                pltpu.make_async_copy(
                    src.at[:, :, pl.ds(128 * l, 128)], stores[g].at[n, :, pl.ds(8, NX), :], load_sems.at[2 * f + l]
                )
            )
            loads[-1].start()
    for f in range(FIELDS):
        for z in range(DEPTH, DEPTH + NZ):
            m = (z - DEPTH) // 2
            for l in range(2):
                lanes = pl.ds(128 * l, 128)
                tile = halo_tile(above[f, m, :, lanes], below[f, m, :, lanes], z % 2, keep_up, keep_dn)
                block.put(*block.where(f, l), z, NX // 8, tile)
    for half in range(2):
        lanes = pl.ds(128 * half, 128)
        block.place_y(DEPTH + 4 * half, yup.at[:, lanes], ydn.at[:, lanes])
    for copy in loads:
        copy.wait()
    for f in range(FIELDS):
        for z in range(DEPTH, DEPTH + NZ):
            block.close_ring(f, z)
    copies = inner_copies(inner, inner_faces, stores, DEPTH, faces, DEPTH + 1, sems, True)
    for n in range(5):
        copies[n].start()
    loop(*inner_planes(1), block.coefficients)
    copies[-1].start()
    for k in range(STEPS - 1):
        loop(*inner_planes(k + 1), functools.partial(block.apply, k))
        copies[5 + k].start()
    for copy in copies:
        copy.wait()


NEAR, FAR = 8 * FIELDS, 24


def krylov_outer(
    swap, face_one, face_two, place, odd_z, inner, inner_faces, rim_one, rim_two,
    basis, message,
    *rest,
):
    keep_up, keep_dn = keep_sides(swap, place)
    n_x = 1 if swap else 2
    *stores, faces, accs, rims, plane_sems, loads, saves = rest
    odd = odd_z[0] == 1
    block = Block(stores, 0, faces, 0, dynamic_one(place))
    copies = inner_copies(inner, inner_faces, stores, 0, faces, 0, loads, False)
    def plane_copies(lower, upper):
        planes = []
        start = 0
        for f in range(FIELDS):
            depth = DEPTH if f <= NRHS else DEPTH - 1
            for side, (face, z) in enumerate(((lower, DEPTH - depth), (upper, DEPTH + NZ))):
                for l in range(2):
                    g, n = block.where(f, l)
                    planes.append(
                        pltpu.make_async_copy(
                            face.at[pl.ds(start, depth), :, pl.ds(128 * l, 128)],
                            stores[g].at[n, pl.ds(z, depth), pl.ds(8, NX), :],
                            plane_sems.at[4 * f + 2 * side + l],
                        )
                    )
            start += depth
        return planes

    for copy in copies[:4]:
        copy.start()

    @pl.when(odd)
    def _():
        for copy in plane_copies(face_one, face_two):
            copy.start()

    @pl.when(jnp.logical_not(odd))
    def _():
        for copy in plane_copies(face_two, face_one):
            copy.start()

    one, two = rim_one[...], rim_two[...]
    rims[0] = jnp.where(odd, one, two)
    rims[1] = jnp.where(odd, two, one)
    rimlo, rimhi = rims.at[0], rims.at[1]

    zero = jnp.zeros((8, 128), F32)
    for f in range(FIELDS):
        for rim, first in ((rimlo, 0), (rimhi, DEPTH + NZ)):
            for z in range(first, first + DEPTH):
                far = DEPTH - z if first == 0 else z - first + 1
                for l in range(2):
                    lanes = pl.ds(128 * l, 128)
                    if far <= 2:
                        at, odd = 8 * f, z % 2
                    elif far == 3 and 8 * (f // 2) < FAR:
                        at, odd = NEAR + 8 * (f // 2), f % 2
                    else:
                        block.put(*block.where(f, l), z, NX // 8, zero)
                        continue
                    other = at + (n_x - 1) * (NEAR + FAR)
                    tile = halo_tile(rim[at : at + 8, lanes], rim[other : other + 8, lanes], odd, keep_up, keep_dn)
                    block.put(*block.where(f, l), z, NX // 8, tile)
    rows = pl.ds(n_x * (NEAR + FAR), ROWS)
    for rim, z in ((rimlo, 0), (rimhi, DEPTH + NZ)):
        block.place_y(z, rim.at[rows, pl.ds(0, 128)], rim.at[rows, pl.ds(128, 128)])

    for copy in copies[:4] + plane_copies(face_one, face_two):
        copy.wait()
    for copy in [copies[5], copies[-1], copies[6], copies[7], copies[4]]:
        copy.start()
    for f in range(FIELDS):
        depth = DEPTH if f <= NRHS else DEPTH - 1
        for d in range(depth):
            block.close_ring(f, DEPTH - 1 - d)
            block.close_ring(f, DEPTH + NZ + d)
    loop(1, DEPTH + 1, block.coefficients)
    loop(DEPTH + NZ - 1, EZ - 1, block.coefficients)

    sends = []

    def send_block(k):
        copy = pltpu.make_async_copy(
            stores[group(k)].at[pl.ds(0, 2 * NRHS), pl.ds(DEPTH, NZ), pl.ds(8, NX), :],
            basis.at[pl.ds(k * 2 * NRHS, 2 * NRHS)],
            saves.at[k],
        )
        copy.start()
        sends.append(copy)

    for k in range(STEPS):
        if k == 1:
            copies[-1].wait()
        loop(
            0,
            2 * DEPTH,
            lambda n, k=k: block.apply(k, n + k + 1 + jnp.where(n >= DEPTH, NZ - 2 - 2 * k, 0)),
        )
        if k < STEPS - 1:
            copies[5 + k].wait()
        send_block(k + 1)
    copies[4].wait()
    send_block(0)
    gram_zero(accs)

    def products(z):
        def tile(i, t):
            store = stores[group(i // NRHS)]
            return jnp.concatenate([store[2 * (i % NRHS) + l, z, 8 + 8 * t : 16 + 8 * t, :] for l in range(2)], 1)

        gram_add([jnp.concatenate([tile(i, t) for i in range(COLS)], 0) for t in range(NX // 8)], accs)

    loop(DEPTH, DEPTH + NZ, products)
    gram_message(accs, message)
    for copy in sends:
        copy.wait()


def factor_gram(messages, cells, table):
    rows = row_ids((24, 128))
    lanes = lane_ids((24, 128))
    upper = gram_of(messages) / cells
    square = jnp.concatenate([upper, jnp.zeros((104, 128), F32)], 0).T
    whole = jnp.where(rows <= lanes, upper, square[0:24, :])

    tile_rows = row_ids((8, 128))
    tiles = range(3)

    def split(value):
        return [value[8 * k : 8 * k + 8] for k in tiles]

    def row_of(column, j):
        return jnp.broadcast_to(column[j // 8][j % 8 : j % 8 + 1, :], (8, 128))

    columns = [split(jnp.broadcast_to(whole[:, c : c + 1], (24, 128))) for c in range(COLS)]
    inverse = [[jnp.where(tile_rows + 8 * k == c, 1.0, 0.0) for k in tiles] for c in range(COLS)]
    pivots = [jnp.ones((8, 128), F32) for k in tiles]
    for j in range(COLS):
        pivot = row_of(columns[j], j)
        first = j // 8
        pivots[first] = jnp.where(tile_rows == j % 8, pivot, pivots[first])
        below = {k: columns[j][k] / pivot for k in tiles if k >= first}
        below[first] = jnp.where(tile_rows > j % 8, below[first], 0.0)
        for c in range(COLS):
            change = columns[c] if c > j else inverse[c]
            row = row_of(change, j)
            for k in below:
                change[k] = change[k] - below[k] * row
    scales = [1.0 / jnp.sqrt(p) for p in pivots]
    factor = jnp.zeros((24, 128), F32)
    for c in range(COLS):
        table[c] = jnp.concatenate([inverse[c][k] * scales[k] for k in tiles], 0)
        factor = jnp.where(lanes == c, jnp.concatenate(columns[c], 0), factor)
    return jnp.where((rows <= lanes) & (rows < COLS), factor * jnp.concatenate(scales, 0), 0.0)


def apply_rows(table, read, write):
    group = 5
    pieces = NX // 8
    for g in reversed(range(COLS // group)):
        mine = range(group * g, group * g + group)
        sums = {i: None for i in mine}
        for j in range(group * g + group):
            value = [read(j, p) for p in range(pieces)]
            for i in mine:
                if j <= i:
                    weight = jnp.broadcast_to(table[j, i : i + 1, :], (8, 128))
                    terms = [weight * v for v in value]
                    sums[i] = terms if sums[i] is None else [s + t for s, t in zip(sums[i], terms)]
        for i in mine:
            for p in range(pieces):
                write(i, p, sums[i][p])


def plane_copy(src, dst, sems, z):
    return pltpu.make_async_copy(src.at[:, z], dst.at[:, z], sems.at[z])


def first_pass(
    cells, message, basis_hbm, first_hbm, next_message, factor_out, basis, first, table, accs, loads, saves
):
    for z in range(NZ):
        plane_copy(basis_hbm, basis, loads, z).start()
    factor_out[...] = factor_gram(message, cells, table)
    gram_zero(accs)

    def products(z):
        def tile(i, t):
            return jnp.concatenate([first[2 * i + l, z, 8 * t : 8 * t + 8, :] for l in range(2)], 1)

        gram_add([jnp.concatenate([tile(i, t) for i in range(COLS)], 0) for t in range(NX // 8)], accs)

    def apply(z):
        for l in range(2):

            def read(j, p):
                return basis[2 * j + l, z, 8 * p : 8 * p + 8, :]

            def write(i, p, value):
                first[2 * i + l, z, 8 * p : 8 * p + 8, :] = value

            apply_rows(table, read, write)
        plane_copy(first, first_hbm, saves, z).start()

    def both(z):
        plane_copy(basis_hbm, basis, loads, z).wait()
        products(z - 1)
        apply(z)

    plane_copy(basis_hbm, basis, loads, 0).wait()
    apply(0)
    loop(1, NZ, both)
    products(NZ - 1)
    gram_message(accs, next_message)
    for z in range(NZ):
        plane_copy(first, first_hbm, saves, z).wait()


def second_pass(cells, message, factor_one, first_hbm, out_hbm, triangle, first, out, table, loads, saves):
    for z in range(NZ):
        plane_copy(first_hbm, first, loads, z).start()
    left = factor_gram(message, cells, table)[:, 0:24]
    product = lax.dot_general(
        left, factor_one[...], (((1,), (0,)), ((), ())), precision=HIGHEST, preferred_element_type=F32
    )
    triangle[...] = product[0:COLS, 0:COLS]

    def chunk(z, carry):
        plane_copy(first_hbm, first, loads, z).wait()
        for l in range(2):

            def read(j, p):
                return first[2 * j + l, z, 8 * p : 8 * p + 8, :]

            def write(i, p, value):
                out[i, z, 8 * p : 8 * p + 8, 128 * l : 128 * l + 128] = value

            apply_rows(table, read, write)
        plane_copy(out, out_hbm, saves, z).start()
        return carry

    lax.fori_loop(0, NZ, chunk, 0)
    for z in range(NZ):
        plane_copy(out, out_hbm, saves, z).wait()


def shape(*dims):
    return jax.ShapeDtypeStruct(dims, F32)


def move(value, axis, delta):
    count = lax.axis_size(axis)
    pairs = [(i, i + delta) for i in range(count) if 0 <= i + delta < count]
    return lax.ppermute(value, axis, pairs)


def swap_pairs(value, axis, first):
    pairs = [(i, i + 1) for i in range(first, lax.axis_size(axis) - 1, 2)]
    return lax.ppermute(value, axis, pairs + [(j, i) for i, j in pairs])


def exchange(messages):
    return lax.all_to_all(messages, AXES, 0, 0, tiled=True)


def body(rhs, coef_x, coef_y, coef_z, diag_term):
    n_x = lax.axis_size("gx")
    devices = n_x * lax.axis_size("gy") * lax.axis_size("gz")
    cells = float(NZ * NX * NY * devices)
    at_x = lax.axis_index("gx")
    swap = n_x == 2
    fields = (rhs, coef_z, coef_x, coef_y, diag_term)

    place = at_x.astype(jnp.int32).reshape(1)
    odd_z, odd_y = ((lax.axis_index(axis) & 1).astype(jnp.int32).reshape(1) for axis in ("gz", "gy"))
    face_shape = shape(FACE, NX, NY)
    x_shape = shape(FIELDS, NZ // 2, 8, NY)
    z_one, z_two, *xmsgs = pl.pallas_call(
        functools.partial(pack_faces, swap),
        out_shape=(face_shape, face_shape) + (x_shape,) * (1 if swap else 2),
        in_specs=[smem()] * 2 + [hbm()] * 5,
        out_specs=(hbm(), hbm()) + (vmem(),) * (1 if swap else 2),
        scratch_shapes=[
            pltpu.VMEM((FIELDS, NZ, NX, NY), F32),
            pltpu.SemaphoreType.DMA((FIELDS,)),
            pltpu.SemaphoreType.DMA((2 * FIELDS,)),
        ],
        compiler_params=params(LIMIT),
        cost_estimate=cost(2.5),
    )(place, odd_z, *fields)
    face_one, face_two = swap_pairs(z_one, "gz", 0), swap_pairs(z_two, "gz", 1)
    if swap:
        x_parts = (lax.ppermute(xmsgs[0], "gx", [(0, 1), (1, 0)]),)
    else:
        x_parts = (move(xmsgs[0], "gx", -1), move(xmsgs[1], "gx", 1))

    own_shape, halo_shape = shape(NX, NY), shape(ROWS - NX, NY)
    own_one, own_two = pl.pallas_call(
        pack_own_rims,
        out_shape=(own_shape, own_shape),
        in_specs=[smem()] + [vmem()] * 5,
        compiler_params=params(LIMIT),
        cost_estimate=cost(2.5),
    )(odd_y, *fields)
    halo_one, halo_two = pl.pallas_call(
        functools.partial(pack_rims, swap),
        out_shape=(halo_shape, halo_shape),
        in_specs=[smem()] * 2 + [vmem()] * len(x_parts),
        compiler_params=params(16),
        cost_estimate=cost(1),
    )(place, odd_y, *x_parts)
    y_one = swap_pairs(jnp.concatenate([own_one, halo_one], 0), "gy", 0)
    y_two = swap_pairs(jnp.concatenate([own_two, halo_two], 0), "gy", 1)
    yup, ydn = jnp.where(odd_y == 1, y_two, y_one), jnp.where(odd_y == 1, y_one, y_two)

    def rim(half):
        near, far, odd = ((0, 1, 0), (3, 2, 1))[half]
        rows = []
        for part in x_parts:
            rows.append(part[:, near].reshape(NEAR, NY))
            rows.append(part[: FAR // 4, far, 4 * odd : 4 * odd + 4].reshape(FAR, NY))
        lanes = slice(128 * half, 128 * half + 128)
        return jnp.concatenate(rows + [jnp.concatenate([yup[:, lanes], ydn[:, lanes]], 1)], 0)

    low, high = rim(0), rim(1)
    rim_one = swap_pairs(jnp.where(odd_z == 1, low, high), "gz", 0)
    rim_two = swap_pairs(jnp.where(odd_z == 1, high, low), "gz", 1)

    inner_shape = shape(sum(GROUPS[:-1]), NZ, EROWS, 128)
    inner_faces_shape = shape(7, NZ - 2, LT, ROWS, 128)
    inner, inner_faces = pl.pallas_call(
        functools.partial(krylov_inner, swap),
        out_shape=(inner_shape, inner_faces_shape),
        in_specs=[smem()] + [hbm()] * 5 + [vmem()] * (len(x_parts) + 2),
        out_specs=(hbm(), hbm()),
        scratch_shapes=[
            *[pltpu.VMEM((tiles, NZ, EROWS, 128), F32) for tiles in GROUPS[:-1]],
            pltpu.VMEM(inner_faces_shape.shape, F32),
            pltpu.SemaphoreType.DMA((2 * FIELDS,)),
            pltpu.SemaphoreType.DMA((9,)),
        ],
        compiler_params=params(LIMIT),
        cost_estimate=cost(7),
    )(place, *fields, *x_parts, yup, ydn)

    block = shape(2 * COLS, NZ, NX, 128)
    basis, message = pl.pallas_call(
        functools.partial(krylov_outer, swap),
        out_shape=(block, shape(devices, 2, 128)),
        in_specs=[hbm(), hbm(), smem(), smem(), hbm(), hbm(), vmem(), vmem()],
        out_specs=(hbm(), vmem()),
        scratch_shapes=[
            *[pltpu.VMEM((tiles, EZ, EROWS, 128), F32) for tiles in GROUPS],
            pltpu.VMEM((7, EZ, LT, ROWS, 128), F32),
            pltpu.VMEM((2, STACK, STACK), F32),
            pltpu.VMEM((2,) + rim_one.shape, F32),
            pltpu.SemaphoreType.DMA((4 * FIELDS,)),
            pltpu.SemaphoreType.DMA((9,)),
            pltpu.SemaphoreType.DMA((STEPS + 1,)),
        ],
        compiler_params=params(LIMIT),
        cost_estimate=cost(15),
    )(face_one, face_two, place, odd_z, inner, inner_faces, rim_one, rim_two)

    message = exchange(message)
    first, message, factor_one = pl.pallas_call(
        functools.partial(first_pass, cells),
        out_shape=(block, shape(devices, 2, 128), shape(24, 128)),
        in_specs=[vmem(), hbm()],
        out_specs=(hbm(), vmem(), vmem()),
        scratch_shapes=[
            pltpu.VMEM(block.shape, F32),
            pltpu.VMEM(block.shape, F32),
            pltpu.VMEM((COLS, 24, 128), F32),
            pltpu.VMEM((2, STACK, STACK), F32),
            pltpu.SemaphoreType.DMA((NZ,)),
            pltpu.SemaphoreType.DMA((NZ,)),
        ],
        compiler_params=params(LIMIT),
    )(message, basis)

    message = exchange(message)
    return pl.pallas_call(
        functools.partial(second_pass, cells),
        out_shape=(shape(COLS, NZ, NX, NY), shape(COLS, COLS)),
        in_specs=[vmem(), vmem(), hbm()],
        out_specs=(hbm(), vmem()),
        scratch_shapes=[
            pltpu.VMEM(block.shape, F32),
            pltpu.VMEM((COLS, NZ, NX, NY), F32),
            pltpu.VMEM((COLS, 24, 128), F32),
            pltpu.SemaphoreType.DMA((NZ,)),
            pltpu.SemaphoreType.DMA((NZ,)),
        ],
        compiler_params=params(LIMIT),
    )(message, factor_one, first)


def solution(mesh):
    return jax.shard_map(
        body,
        mesh=mesh,
        in_specs=(
            P(None, "gz", "gx", "gy"),
            P("gz", "gx", "gy"),
            P("gz", "gx", "gy"),
            P("gz", "gx", "gy"),
            P("gz", "gx", "gy"),
        ),
        out_specs=(P(None, "gz", "gx", "gy"), P()),
        check_vma=False,
    )
```

```python
import functools

import jax
import jax.numpy as jnp
from jax import lax
from jax.experimental import pallas as pl
from jax.experimental.pallas import tpu as pltpu
from jax.sharding import PartitionSpec as P

NRHS = 4
STEPS = 4
COLS = NRHS * (STEPS + 1)
SHIFTS = (3.0, 11.0, 7.0, 1.5)
SCALE = 1.0 / 6.0
FIELDS = NRHS + 4
AXES = ("gx", "gy", "gz")
HIGHEST = lax.Precision.HIGHEST

DEPTH = 4
NZ, NX, NY = 8, 32, 256
EZ = NZ + 2 * DEPTH
ROWS = NX + 8
EROWS = ROWS + 16
LT = 3
FACE = NRHS * 4 + 3 * 4 + 1
F32 = jnp.float32
LIMIT = 63


def params(mb):
    return pltpu.CompilerParams(vmem_limit_bytes=mb << 20)


def cost(us):
    return pl.CostEstimate(flops=0, bytes_accessed=int(us * 3.6e6), transcendentals=0)


def vmem():
    return pl.BlockSpec(memory_space=pltpu.VMEM)


def smem():
    return pl.BlockSpec(memory_space=pltpu.SMEM)


def hbm():
    return pl.BlockSpec(memory_space=pl.ANY)


def row_ids(shape):
    return lax.broadcasted_iota(jnp.int32, shape, 0)


def lane_ids(shape):
    return lax.broadcasted_iota(jnp.int32, shape, 1)


def field_of(rhs, cz, cx, cy, dg, f, z):
    return rhs.at[f, z] if f < NRHS else (cz, cx, cy, dg)[f - NRHS].at[z]


def pack_faces(swap, place, odd_z, rhs, cz, cx, cy, dg, z_one, z_two, *rest):
    xmsgs, (whole, loads, saves) = rest[:-3], rest[-3:]
    copies = []
    for f in range(FIELDS):
        src = rhs.at[f] if f < NRHS else (cz, cx, cy, dg)[f - NRHS]
        copies.append(pltpu.make_async_copy(src, whole.at[f], loads.at[f]))
        copies[-1].start()
    low = row_ids((8, NY)) < 4
    up = place[0] == 0
    planes = []
    at = 0
    for f in range(FIELDS):
        copies[f].wait()
        depth = DEPTH if f <= NRHS else DEPTH - 1
        for side, out in ((0, z_one), (1, z_two)):
            start = jnp.where(odd_z[0] == side, NZ - depth, 0)
            planes.append(
                pltpu.make_async_copy(
                    whole.at[f, pl.ds(start, depth)], out.at[pl.ds(at, depth)], saves.at[2 * f + side]
                )
            )
            planes[-1].start()
        at += depth
        for m in range(NZ // 2):
            a, b = whole.at[f, 2 * m], whole.at[f, 2 * m + 1]
            first = jnp.where(low, a[0:8], pltpu.roll(b[0:8], 4, 0))
            last = jnp.where(low, pltpu.roll(a[NX - 8 : NX], 4, 0), b[NX - 8 : NX])
            if swap:
                xmsgs[0][f, m] = jnp.where(up, last, first)
            else:
                xmsgs[0][f, m] = first
                xmsgs[1][f, m] = last
    for copy in planes:
        copy.wait()


def halo_tile(above, below, odd, keep_up, keep_dn):
    low = row_ids(above.shape) < 4
    if odd:
        up, dn = pltpu.roll(above, 4, 0), below
    else:
        up, dn = above, pltpu.roll(below, 4, 0)
    return jnp.where(low, up * keep_up, dn * keep_dn)


def keep_sides(swap, place):
    if not swap:
        return 1.0, 1.0
    first = place[0] == 0
    return jnp.where(first, 1.0, 0.0), jnp.where(first, 0.0, 1.0)


def pack_lanes(tile_of, side):
    lane = lane_ids((8, 128))
    source = 124 * side
    acc = jnp.zeros((8, 128), F32)
    for zz in range(4):
        for f in range(FIELDS):
            tile = tile_of(f, zz)
            spot = (zz * FIELDS + f) * 4
            shift = (spot - source) % 128
            if shift:
                tile = pltpu.roll(tile, shift, 1)
            acc = jnp.where((lane >= spot) & (lane < spot + 4), tile, acc)
    return acc


def pack_own_rims(odd_y, rhs, cz, cx, cy, dg, one, two):
    odd = odd_y[0] == 1
    for t in range(NX // 8):
        for half in range(2):
            lo, hi = (
                pack_lanes(
                    lambda f, zz: field_of(rhs, cz, cx, cy, dg, f, 4 * half + zz)[
                        8 * t : 8 * t + 8, 128 * side : 128 * side + 128
                    ],
                    side,
                )
                for side in range(2)
            )
            one[8 * t : 8 * t + 8, 128 * half : 128 * half + 128] = jnp.where(odd, lo, hi)
            two[8 * t : 8 * t + 8, 128 * half : 128 * half + 128] = jnp.where(odd, hi, lo)


def pack_rims(swap, place, odd_y, *refs):
    above, below, one, two = refs if not swap else (refs[0],) + refs
    keep_up, keep_dn = keep_sides(swap, place)
    odd = odd_y[0] == 1
    for half in range(2):
        halves = []
        for side in range(2):
            lanes = slice(128 * side, 128 * side + 128)
            halves.append(
                pack_lanes(
                    lambda f, zz: halo_tile(
                        above[f, 2 * half + zz // 2, :, lanes],
                        below[f, 2 * half + zz // 2, :, lanes],
                        zz % 2,
                        keep_up,
                        keep_dn,
                    ),
                    side,
                )
            )
        lo, hi = halves
        one[:, 128 * half : 128 * half + 128] = jnp.where(odd, lo, hi)
        two[:, 128 * half : 128 * half + 128] = jnp.where(odd, hi, lo)


STACK = 8 * COLS


def gram_zero(accs):
    accs[...] = jnp.zeros_like(accs)


def gram_add(stacks, accs):
    left, right = [], []
    cross_left, cross_right = [], []
    for stack in stacks:
        high = stack.astype(jnp.bfloat16)
        rest = stack - high.astype(F32)
        mid = rest.astype(jnp.bfloat16)
        low = (rest - mid.astype(F32)).astype(jnp.bfloat16)
        left += [high, mid]
        cross_left += [high, high]
        cross_right += [mid, low]
    contract = (((1,), (1,)), ((), ()))

    def product(a, b):
        return lax.dot_general(jnp.concatenate(a, 1), jnp.concatenate(b, 1), contract, preferred_element_type=F32)

    accs[0] += product(left, left)
    accs[1] += product(cross_left, cross_right)


def gram_message(accs, out):
    same = (row_ids((STACK, STACK)) & 7) == (lane_ids((STACK, STACK)) & 7)
    pick = jnp.where((row_ids((STACK, 128)) >> 3) == lane_ids((STACK, 128)), 1.0, 0.0)

    def traces(product):
        picked = jnp.where(same, product, 0.0)
        rows = [jnp.sum(picked[8 * i : 8 * i + 8], axis=0, keepdims=True) for i in range(COLS)]
        rows = jnp.concatenate(rows + [jnp.zeros((128 - COLS, STACK), F32)], 0)
        return lax.dot_general(
            rows, pick, (((1,), (0,)), ((), ())), precision=HIGHEST, preferred_element_type=F32
        )

    cross = traces(accs[1])
    gram = traces(accs[0]) + cross + cross.T
    tops = [gram[8 * k : 8 * k + 8] for k in range(3)]
    rows, lanes = row_ids((8, 128)), lane_ids((8, 128))
    tile = jnp.where(lanes < COLS, tops[0], pltpu.roll(tops[1], 12, 1))
    corner = pltpu.roll(pltpu.roll(tops[2], 128 - 16, 1), 4, 0)
    tile = jnp.where((rows >= 4) & (lanes < 4), corner, tile)
    packed = tile
    for q in range(1, 4):
        turned = pltpu.roll(pltpu.roll(tile, 32 * q, 1), 8 - 2 * q, 0)
        packed = jnp.where((lanes >> 5) == q, turned, packed)
    packed = packed[0:2]
    for n in range(out.shape[0]):
        out[n] = packed


def gram_of(messages):
    total = messages[0]
    for n in range(1, messages.shape[0]):
        total = total + messages[n]
    total = jnp.concatenate([total] * 4, 0)
    rows, lanes = row_ids((8, 128)), lane_ids((8, 128))
    tile = total
    for q in range(1, 4):
        tile = jnp.where((rows >> 1) == q, pltpu.roll(total, 128 - 32 * q, 1), tile)
    corner = pltpu.roll(pltpu.roll(tile, 4, 0), 16, 1)
    tops = [
        jnp.where((lanes < COLS) & (lanes >= rows), tile, 0.0),
        jnp.where((lanes < COLS) & (lanes >= rows + 8), pltpu.roll(tile, 128 - 12, 1), 0.0),
        jnp.where((lanes < COLS) & (lanes >= rows + 16), corner, 0.0),
    ]
    return jnp.concatenate(tops, 0)


GROUPS = (9, 12, 9, 9, 9, 9)


def group(k):
    return k + 1 if k else 0


class Block:
    def __init__(self, stores, base, faces, faces_base, one):
        self.one = one
        self.stores, self.base, self.faces, self.faces_base = stores, base, faces, faces_base
        self.lane = lane_ids((8, 128))

    def where(self, f, l):
        return (0, 2 * f + l) if f < NRHS else (1, 3 * (f - NRHS) + l)

    def put(self, g, n, z, t, value):
        store, z = self.stores[g], z - self.base
        store[n, z, 8 + 8 * t : 16 + 8 * t, :] = value
        if t == 0:
            store[n, z, 8 + ROWS : 16 + ROWS, :] = value
        if t == ROWS // 8 - 1:
            store[n, z, 0:8, :] = value

    def get(self, g, n, z, t, off=0):
        row = 8 + 8 * t + (off * self.one if off else 0)
        return self.stores[g][n, z - self.base, pl.ds(row, 8), :]

    def close_ring(self, f, z):
        z = z - self.base
        for l in range(2):
            g, n = self.where(f, l)
            self.stores[g][n, z, 8 + ROWS : 16 + ROWS, :] = self.stores[g][n, z, 8:16, :]

    def place_y(self, z, up, dn):
        part, place = self.lane & 31, self.lane >> 5
        upper, lower = part < 4, part >= 28
        for t in range(ROWS // 8):
            u_all, d_all = up[8 * t : 8 * t + 8, :], dn[8 * t : 8 * t + 8, :]

            def turned(value, shift):
                return pltpu.roll(value, shift % 128, 1) if shift % 128 else value

            def copies(f):
                result = []
                for m in range(4):
                    u, d = turned(u_all, 32 * m - 4 * f), turned(d_all, 32 * m + 28 - 4 * f)
                    result.append(jnp.where(upper, u, jnp.where(lower, d, 0.0)))
                return result

            def pick(tiles):
                value = tiles[0]
                for r in range(1, 4):
                    value = jnp.where(place == r, tiles[r], value)
                return value

            fields = [copies(r) for r in range(NRHS)]
            for zz in range(4):
                self.put(0, 2 * NRHS, z + zz, t, pick([fields[r][(r - zz) % 4] for r in range(4)]))
            for c in range(4):
                mine = copies(NRHS + c)
                for zz in range(4):
                    self.put(1, 3 * c + 2, z + zz, t, pick([mine[(r - zz) % 4] for r in range(4)]))

    def coefficients(self, z):
        lane = self.lane
        for t in range(ROWS // 8):

            def tiles(c, z, off=0):
                return [self.get(1, 3 * c + l, z, t, off) for l in range(LT)]

            center_z, center_x, center_y, diag = (tiles(c, z) for c in range(4))
            up = [pltpu.roll(v, 127, 1) for v in center_y]
            dn = [pltpu.roll(v, 1, 1) for v in center_y]
            first = jnp.broadcast_to(center_y[0][:, 0:1], (8, 128))
            last = jnp.broadcast_to(center_y[1][:, 127:128], (8, 128))
            sides = [
                (center_z, tiles(0, z + 1)),
                (center_z, tiles(0, z - 1)),
                (center_x, tiles(1, z, 1)),
                (center_x, tiles(1, z, -1)),
                (
                    center_y,
                    [
                        jnp.where(lane == 127, up[1], up[0]),
                        jnp.where(lane == 127, up[2], up[1]),
                        jnp.where((lane & 31) == 31, first, up[2]),
                    ],
                ),
                (
                    center_y,
                    [
                        jnp.where(lane == 0, dn[2], dn[0]),
                        jnp.where(lane == 0, dn[0], dn[1]),
                        jnp.where((lane & 31) == 0, last, dn[2]),
                    ],
                ),
            ]
            at = z - self.faces_base
            for l in range(LT):
                inside = diag[l] > 0.0
                total = diag[l] * SCALE
                for k, (mid, side) in enumerate(sides):
                    face = (mid[l] + side[l]) * (0.5 * SCALE)
                    total = total + face
                    self.faces[k, at, l, 8 * t : 8 * t + 8, :] = jnp.where(inside, face, 0.0)
                self.faces[6, at, l, 8 * t : 8 * t + 8, :] = jnp.where(inside, total, 0.0)

    def apply(self, k, z):
        last = k == STEPS - 1
        at, lane, edge = z - self.faces_base, self.lane, 2 * NRHS
        src, dst = group(k), group(k + 1)
        for t in range(NX // 8 if last else ROWS // 8):
            face = [
                [self.faces[c, at, l, 8 * t : 8 * t + 8, :] for l in range(2 if last else LT)] for c in range(7)
            ]
            diag = [d - SHIFTS[k] * SCALE for d in face[6]]

            def image(n, l, mid, up, dn):
                sides = (
                    self.get(src, n, z + 1, t),
                    self.get(src, n, z - 1, t),
                    self.get(src, n, z, t, 1),
                    self.get(src, n, z, t, -1),
                    up,
                    dn,
                )
                value = diag[l] * mid
                for c, side in enumerate(sides):
                    value = value - face[c][l] * side
                self.put(dst, n, z, t, value)

            rim = self.get(src, edge, z, t)
            rim_up, rim_dn = pltpu.roll(rim, 127, 1), pltpu.roll(rim, 1, 1)
            edge_up, edge_dn = rim_up, rim_dn
            for r in range(NRHS):
                one, two = self.get(src, 2 * r, z, t), self.get(src, 2 * r + 1, z, t)
                one_up, two_up = pltpu.roll(one, 127, 1), pltpu.roll(two, 127, 1)
                one_dn, two_dn = pltpu.roll(one, 1, 1), pltpu.roll(two, 1, 1)
                above = rim_up if r == 0 else pltpu.roll(rim, 127 - 32 * r, 1)
                below = rim_dn if r == NRHS - 1 else pltpu.roll(rim, 97 - 32 * r, 1)
                image(2 * r, 0, one, jnp.where(lane == 127, two_up, one_up), jnp.where(lane == 0, below, one_dn))
                image(2 * r + 1, 1, two, jnp.where(lane == 127, above, two_up), jnp.where(lane == 0, one_dn, two_dn))
                if not last:
                    start = one_up if r == NRHS - 1 else pltpu.roll(one, 32 * r + 31, 1)
                    end = two_dn if r == 0 else pltpu.roll(two, 32 * r + 1, 1)
                    edge_up = jnp.where(lane == 32 * r + 31, start, edge_up)
                    edge_dn = jnp.where(lane == 32 * r, end, edge_dn)
            if not last:
                image(edge, 2, rim, edge_up, edge_dn)


def dynamic_one(place):
    return (place[0] >> 24) + 1


def loop(start, stop, do):
    def step(n, carry):
        do(n)
        return carry

    lax.fori_loop(start, stop, step, 0)


def inner_planes(k):
    return DEPTH + k, DEPTH + NZ - k


def inner_copies(inner, inner_faces, stores, base, faces, faces_base, sems, out):
    def copy(n, there, here):
        src, dst = (here, there) if out else (there, here)
        return pltpu.make_async_copy(src, dst, sems.at[n])

    result = []
    for n, (g, start, stop) in enumerate(
        [(g, z, z + 2) for g in (0, 1) for z in (DEPTH, DEPTH + NZ - 2)]
        + [(0, DEPTH + 2, DEPTH + NZ - 2)]
        + [(group(k), *inner_planes(k)) for k in range(1, STEPS)]
    ):
        there = inner.at[pl.ds(sum(GROUPS[:g]), GROUPS[g]), pl.ds(start - DEPTH, stop - start)]
        result.append(copy(n, there, stores[g].at[:, pl.ds(start - base, stop - start)]))
    start, stop = inner_planes(1)
    result.append(copy(len(result), inner_faces, faces.at[:, pl.ds(start - faces_base, stop - start)]))
    return result


def krylov_inner(swap, place, rhs, cz, cx, cy, dg, *rest):
    above, below, yup, ydn, inner, inner_faces, *stores, faces, load_sems, sems = rest if not swap else rest[:1] + rest
    keep_up, keep_dn = keep_sides(swap, place)
    block = Block(stores, DEPTH, faces, DEPTH + 1, dynamic_one(place))
    loads = []
    for f in range(FIELDS):
        src = rhs.at[f] if f < NRHS else (cz, cx, cy, dg)[f - NRHS]
        for l in range(2):
            g, n = block.where(f, l)
            loads.append(
                pltpu.make_async_copy(
                    src.at[:, :, pl.ds(128 * l, 128)], stores[g].at[n, :, pl.ds(8, NX), :], load_sems.at[2 * f + l]
                )
            )
            loads[-1].start()
    for f in range(FIELDS):
        for z in range(DEPTH, DEPTH + NZ):
            m = (z - DEPTH) // 2
            for l in range(2):
                lanes = pl.ds(128 * l, 128)
                tile = halo_tile(above[f, m, :, lanes], below[f, m, :, lanes], z % 2, keep_up, keep_dn)
                block.put(*block.where(f, l), z, NX // 8, tile)
    for half in range(2):
        lanes = pl.ds(128 * half, 128)
        block.place_y(DEPTH + 4 * half, yup.at[:, lanes], ydn.at[:, lanes])
    for copy in loads:
        copy.wait()
    for f in range(FIELDS):
        for z in range(DEPTH, DEPTH + NZ):
            block.close_ring(f, z)
    copies = inner_copies(inner, inner_faces, stores, DEPTH, faces, DEPTH + 1, sems, True)
    for n in range(5):
        copies[n].start()
    loop(*inner_planes(1), block.coefficients)
    copies[-1].start()
    for k in range(STEPS - 1):
        loop(*inner_planes(k + 1), functools.partial(block.apply, k))
        copies[5 + k].start()
    for copy in copies:
        copy.wait()


NEAR, FAR = 8 * FIELDS, 24


def krylov_outer(
    swap, face_one, face_two, place, odd_z, inner, inner_faces, rim_one, rim_two,
    basis, message,
    *rest,
):
    keep_up, keep_dn = keep_sides(swap, place)
    n_x = 1 if swap else 2
    *stores, faces, accs, rims, plane_sems, loads, saves = rest
    odd = odd_z[0] == 1
    block = Block(stores, 0, faces, 0, dynamic_one(place))
    copies = inner_copies(inner, inner_faces, stores, 0, faces, 0, loads, False)
    def plane_copies(lower, upper):
        planes = []
        start = 0
        for f in range(FIELDS):
            depth = DEPTH if f <= NRHS else DEPTH - 1
            for side, (face, z) in enumerate(((lower, DEPTH - depth), (upper, DEPTH + NZ))):
                for l in range(2):
                    g, n = block.where(f, l)
                    planes.append(
                        pltpu.make_async_copy(
                            face.at[pl.ds(start, depth), :, pl.ds(128 * l, 128)],
                            stores[g].at[n, pl.ds(z, depth), pl.ds(8, NX), :],
                            plane_sems.at[4 * f + 2 * side + l],
                        )
                    )
            start += depth
        return planes

    for copy in copies[:4]:
        copy.start()

    @pl.when(odd)
    def _():
        for copy in plane_copies(face_one, face_two):
            copy.start()

    @pl.when(jnp.logical_not(odd))
    def _():
        for copy in plane_copies(face_two, face_one):
            copy.start()

    one, two = rim_one[...], rim_two[...]
    rims[0] = jnp.where(odd, one, two)
    rims[1] = jnp.where(odd, two, one)
    rimlo, rimhi = rims.at[0], rims.at[1]

    zero = jnp.zeros((8, 128), F32)
    for f in range(FIELDS):
        for rim, first in ((rimlo, 0), (rimhi, DEPTH + NZ)):
            for z in range(first, first + DEPTH):
                far = DEPTH - z if first == 0 else z - first + 1
                for l in range(2):
                    lanes = pl.ds(128 * l, 128)
                    if far <= 2:
                        at, odd = 8 * f, z % 2
                    elif far == 3 and 8 * (f // 2) < FAR:
                        at, odd = NEAR + 8 * (f // 2), f % 2
                    else:
                        block.put(*block.where(f, l), z, NX // 8, zero)
                        continue
                    other = at + (n_x - 1) * (NEAR + FAR)
                    tile = halo_tile(rim[at : at + 8, lanes], rim[other : other + 8, lanes], odd, keep_up, keep_dn)
                    block.put(*block.where(f, l), z, NX // 8, tile)
    rows = pl.ds(n_x * (NEAR + FAR), ROWS)
    for rim, z in ((rimlo, 0), (rimhi, DEPTH + NZ)):
        block.place_y(z, rim.at[rows, pl.ds(0, 128)], rim.at[rows, pl.ds(128, 128)])

    for copy in copies[:4] + plane_copies(face_one, face_two):
        copy.wait()
    for copy in [copies[5], copies[-1], copies[6], copies[7], copies[4]]:
        copy.start()
    for f in range(FIELDS):
        depth = DEPTH if f <= NRHS else DEPTH - 1
        for d in range(depth):
            block.close_ring(f, DEPTH - 1 - d)
            block.close_ring(f, DEPTH + NZ + d)
    loop(1, DEPTH + 1, block.coefficients)
    loop(DEPTH + NZ - 1, EZ - 1, block.coefficients)

    sends = []

    def send_block(k):
        copy = pltpu.make_async_copy(
            stores[group(k)].at[pl.ds(0, 2 * NRHS), pl.ds(DEPTH, NZ), pl.ds(8, NX), :],
            basis.at[pl.ds(k * 2 * NRHS, 2 * NRHS)],
            saves.at[k],
        )
        copy.start()
        sends.append(copy)

    for k in range(STEPS):
        if k == 1:
            copies[-1].wait()
        loop(
            0,
            2 * DEPTH,
            lambda n, k=k: block.apply(k, n + k + 1 + jnp.where(n >= DEPTH, NZ - 2 - 2 * k, 0)),
        )
        if k < STEPS - 1:
            copies[5 + k].wait()
        send_block(k + 1)
    copies[4].wait()
    send_block(0)
    gram_zero(accs)

    def products(z):
        def tile(i, t):
            store = stores[group(i // NRHS)]
            return jnp.concatenate([store[2 * (i % NRHS) + l, z, 8 + 8 * t : 16 + 8 * t, :] for l in range(2)], 1)

        gram_add([jnp.concatenate([tile(i, t) for i in range(COLS)], 0) for t in range(NX // 8)], accs)

    loop(DEPTH, DEPTH + NZ, products)
    gram_message(accs, message)
    for copy in sends:
        copy.wait()


def factor_gram(messages, cells, table):
    rows = row_ids((24, 128))
    lanes = lane_ids((24, 128))
    upper = gram_of(messages) / cells
    square = jnp.concatenate([upper, jnp.zeros((104, 128), F32)], 0).T
    whole = jnp.where(rows <= lanes, upper, square[0:24, :])

    tile_rows = row_ids((8, 128))
    tiles = range(3)

    def split(value):
        return [value[8 * k : 8 * k + 8] for k in tiles]

    def row_of(column, j):
        return jnp.broadcast_to(column[j // 8][j % 8 : j % 8 + 1, :], (8, 128))

    columns = [split(jnp.broadcast_to(whole[:, c : c + 1], (24, 128))) for c in range(COLS)]
    inverse = [[jnp.where(tile_rows + 8 * k == c, 1.0, 0.0) for k in tiles] for c in range(COLS)]
    pivots = [jnp.ones((8, 128), F32) for k in tiles]
    for j in range(COLS):
        pivot = row_of(columns[j], j)
        first = j // 8
        pivots[first] = jnp.where(tile_rows == j % 8, pivot, pivots[first])
        below = {k: columns[j][k] / pivot for k in tiles if k >= first}
        below[first] = jnp.where(tile_rows > j % 8, below[first], 0.0)
        for c in range(COLS):
            change = columns[c] if c > j else inverse[c]
            row = row_of(change, j)
            for k in below:
                change[k] = change[k] - below[k] * row
    scales = [1.0 / jnp.sqrt(p) for p in pivots]
    factor = jnp.zeros((24, 128), F32)
    for c in range(COLS):
        table[c] = jnp.concatenate([inverse[c][k] * scales[k] for k in tiles], 0)
        factor = jnp.where(lanes == c, jnp.concatenate(columns[c], 0), factor)
    return jnp.where((rows <= lanes) & (rows < COLS), factor * jnp.concatenate(scales, 0), 0.0)


def apply_rows(table, read, write):
    group = 5
    pieces = NX // 8
    for g in reversed(range(COLS // group)):
        mine = range(group * g, group * g + group)
        sums = {i: None for i in mine}
        for j in range(group * g + group):
            value = [read(j, p) for p in range(pieces)]
            for i in mine:
                if j <= i:
                    weight = jnp.broadcast_to(table[j, i : i + 1, :], (8, 128))
                    terms = [weight * v for v in value]
                    sums[i] = terms if sums[i] is None else [s + t for s, t in zip(sums[i], terms)]
        for i in mine:
            for p in range(pieces):
                write(i, p, sums[i][p])


def plane_copy(src, dst, sems, z):
    return pltpu.make_async_copy(src.at[:, z], dst.at[:, z], sems.at[z])


def first_pass(
    cells, message, basis_hbm, first_hbm, next_message, factor_out, basis, first, table, accs, loads, saves
):
    for z in range(NZ):
        plane_copy(basis_hbm, basis, loads, z).start()
    factor_out[...] = factor_gram(message, cells, table)
    gram_zero(accs)

    def products(z):
        def tile(i, t):
            return jnp.concatenate([first[2 * i + l, z, 8 * t : 8 * t + 8, :] for l in range(2)], 1)

        gram_add([jnp.concatenate([tile(i, t) for i in range(COLS)], 0) for t in range(NX // 8)], accs)

    def apply(z):
        for l in range(2):

            def read(j, p):
                return basis[2 * j + l, z, 8 * p : 8 * p + 8, :]

            def write(i, p, value):
                first[2 * i + l, z, 8 * p : 8 * p + 8, :] = value

            apply_rows(table, read, write)
        plane_copy(first, first_hbm, saves, z).start()

    def both(z):
        plane_copy(basis_hbm, basis, loads, z).wait()
        products(z - 1)
        apply(z)

    plane_copy(basis_hbm, basis, loads, 0).wait()
    apply(0)
    loop(1, NZ, both)
    products(NZ - 1)
    gram_message(accs, next_message)
    for z in range(NZ):
        plane_copy(first, first_hbm, saves, z).wait()


def second_pass(cells, message, factor_one, first_hbm, out_hbm, triangle, first, out, table, loads, saves):
    for z in range(NZ):
        plane_copy(first_hbm, first, loads, z).start()
    left = factor_gram(message, cells, table)[:, 0:24]
    product = lax.dot_general(
        left, factor_one[...], (((1,), (0,)), ((), ())), precision=HIGHEST, preferred_element_type=F32
    )
    triangle[...] = product[0:COLS, 0:COLS]

    def chunk(z, carry):
        plane_copy(first_hbm, first, loads, z).wait()
        for l in range(2):

            def read(j, p):
                return first[2 * j + l, z, 8 * p : 8 * p + 8, :]

            def write(i, p, value):
                out[i, z, 8 * p : 8 * p + 8, 128 * l : 128 * l + 128] = value

            apply_rows(table, read, write)
        plane_copy(out, out_hbm, saves, z).start()
        return carry

    lax.fori_loop(0, NZ, chunk, 0)
    for z in range(NZ):
        plane_copy(out, out_hbm, saves, z).wait()


def shape(*dims):
    return jax.ShapeDtypeStruct(dims, F32)


def move(value, axis, delta):
    count = lax.axis_size(axis)
    pairs = [(i, i + delta) for i in range(count) if 0 <= i + delta < count]
    return lax.ppermute(value, axis, pairs)


def swap_pairs(value, axis, first):
    pairs = [(i, i + 1) for i in range(first, lax.axis_size(axis) - 1, 2)]
    return lax.ppermute(value, axis, pairs + [(j, i) for i, j in pairs])


def exchange(messages):
    return lax.all_to_all(messages, AXES, 0, 0, tiled=True)


def body(rhs, coef_x, coef_y, coef_z, diag_term):
    n_x = lax.axis_size("gx")
    devices = n_x * lax.axis_size("gy") * lax.axis_size("gz")
    cells = float(NZ * NX * NY * devices)
    at_x = lax.axis_index("gx")
    swap = n_x == 2
    fields = (rhs, coef_z, coef_x, coef_y, diag_term)

    place = at_x.astype(jnp.int32).reshape(1)
    odd_z, odd_y = ((lax.axis_index(axis) & 1).astype(jnp.int32).reshape(1) for axis in ("gz", "gy"))
    face_shape = shape(FACE, NX, NY)
    x_shape = shape(FIELDS, NZ // 2, 8, NY)
    z_one, z_two, *xmsgs = pl.pallas_call(
        functools.partial(pack_faces, swap),
        out_shape=(face_shape, face_shape) + (x_shape,) * (1 if swap else 2),
        in_specs=[smem()] * 2 + [hbm()] * 5,
        out_specs=(hbm(), hbm()) + (vmem(),) * (1 if swap else 2),
        scratch_shapes=[
            pltpu.VMEM((FIELDS, NZ, NX, NY), F32),
            pltpu.SemaphoreType.DMA((FIELDS,)),
            pltpu.SemaphoreType.DMA((2 * FIELDS,)),
        ],
        compiler_params=params(LIMIT),
        cost_estimate=cost(2.5),
    )(place, odd_z, *fields)
    face_one, face_two = swap_pairs(z_one, "gz", 0), swap_pairs(z_two, "gz", 1)
    if swap:
        x_parts = (lax.ppermute(xmsgs[0], "gx", [(0, 1), (1, 0)]),)
    else:
        x_parts = (move(xmsgs[0], "gx", -1), move(xmsgs[1], "gx", 1))

    own_shape, halo_shape = shape(NX, NY), shape(ROWS - NX, NY)
    own_one, own_two = pl.pallas_call(
        pack_own_rims,
        out_shape=(own_shape, own_shape),
        in_specs=[smem()] + [vmem()] * 5,
        compiler_params=params(LIMIT),
        cost_estimate=cost(2.5),
    )(odd_y, *fields)
    halo_one, halo_two = pl.pallas_call(
        functools.partial(pack_rims, swap),
        out_shape=(halo_shape, halo_shape),
        in_specs=[smem()] * 2 + [vmem()] * len(x_parts),
        compiler_params=params(16),
        cost_estimate=cost(1),
    )(place, odd_y, *x_parts)
    y_one = swap_pairs(jnp.concatenate([own_one, halo_one], 0), "gy", 0)
    y_two = swap_pairs(jnp.concatenate([own_two, halo_two], 0), "gy", 1)
    yup, ydn = jnp.where(odd_y == 1, y_two, y_one), jnp.where(odd_y == 1, y_one, y_two)

    def rim(half):
        near, far, odd = ((0, 1, 0), (3, 2, 1))[half]
        rows = []
        for part in x_parts:
            rows.append(part[:, near].reshape(NEAR, NY))
            rows.append(part[: FAR // 4, far, 4 * odd : 4 * odd + 4].reshape(FAR, NY))
        lanes = slice(128 * half, 128 * half + 128)
        return jnp.concatenate(rows + [jnp.concatenate([yup[:, lanes], ydn[:, lanes]], 1)], 0)

    low, high = rim(0), rim(1)
    rim_one = swap_pairs(jnp.where(odd_z == 1, low, high), "gz", 0)
    rim_two = swap_pairs(jnp.where(odd_z == 1, high, low), "gz", 1)

    inner_shape = shape(sum(GROUPS[:-1]), NZ, EROWS, 128)
    inner_faces_shape = shape(7, NZ - 2, LT, ROWS, 128)
    inner, inner_faces = pl.pallas_call(
        functools.partial(krylov_inner, swap),
        out_shape=(inner_shape, inner_faces_shape),
        in_specs=[smem()] + [hbm()] * 5 + [vmem()] * (len(x_parts) + 2),
        out_specs=(hbm(), hbm()),
        scratch_shapes=[
            *[pltpu.VMEM((tiles, NZ, EROWS, 128), F32) for tiles in GROUPS[:-1]],
            pltpu.VMEM(inner_faces_shape.shape, F32),
            pltpu.SemaphoreType.DMA((2 * FIELDS,)),
            pltpu.SemaphoreType.DMA((9,)),
        ],
        compiler_params=params(LIMIT),
        cost_estimate=cost(7),
    )(place, *fields, *x_parts, yup, ydn)

    block = shape(2 * COLS, NZ, NX, 128)
    basis, message = pl.pallas_call(
        functools.partial(krylov_outer, swap),
        out_shape=(block, shape(devices, 2, 128)),
        in_specs=[hbm(), hbm(), smem(), smem(), hbm(), hbm(), vmem(), vmem()],
        out_specs=(hbm(), vmem()),
        scratch_shapes=[
            *[pltpu.VMEM((tiles, EZ, EROWS, 128), F32) for tiles in GROUPS],
            pltpu.VMEM((7, EZ, LT, ROWS, 128), F32),
            pltpu.VMEM((2, STACK, STACK), F32),
            pltpu.VMEM((2,) + rim_one.shape, F32),
            pltpu.SemaphoreType.DMA((4 * FIELDS,)),
            pltpu.SemaphoreType.DMA((9,)),
            pltpu.SemaphoreType.DMA((STEPS + 1,)),
        ],
        compiler_params=params(LIMIT),
        cost_estimate=cost(15),
    )(face_one, face_two, place, odd_z, inner, inner_faces, rim_one, rim_two)

    message = exchange(message)
    first, message, factor_one = pl.pallas_call(
        functools.partial(first_pass, cells),
        out_shape=(block, shape(devices, 2, 128), shape(24, 128)),
        in_specs=[vmem(), hbm()],
        out_specs=(hbm(), vmem(), vmem()),
        scratch_shapes=[
            pltpu.VMEM(block.shape, F32),
            pltpu.VMEM(block.shape, F32),
            pltpu.VMEM((COLS, 24, 128), F32),
            pltpu.VMEM((2, STACK, STACK), F32),
            pltpu.SemaphoreType.DMA((NZ,)),
            pltpu.SemaphoreType.DMA((NZ,)),
        ],
        compiler_params=params(LIMIT),
    )(message, basis)

    message = exchange(message)
    return pl.pallas_call(
        functools.partial(second_pass, cells),
        out_shape=(shape(COLS, NZ, NX, NY), shape(COLS, COLS)),
        in_specs=[vmem(), vmem(), hbm()],
        out_specs=(hbm(), vmem()),
        scratch_shapes=[
            pltpu.VMEM(block.shape, F32),
            pltpu.VMEM((COLS, NZ, NX, NY), F32),
            pltpu.VMEM((COLS, 24, 128), F32),
            pltpu.SemaphoreType.DMA((NZ,)),
            pltpu.SemaphoreType.DMA((NZ,)),
        ],
        compiler_params=params(LIMIT),
    )(message, factor_one, first)


def solution(mesh):
    return jax.shard_map(
        body,
        mesh=mesh,
        in_specs=(
            P(None, "gz", "gx", "gy"),
            P("gz", "gx", "gy"),
            P("gz", "gx", "gy"),
            P("gz", "gx", "gy"),
            P("gz", "gx", "gy"),
        ),
        out_specs=(P(None, "gz", "gx", "gy"), P()),
        check_vma=False,
    )
```

```python
import functools

import jax
import jax.numpy as jnp
from jax import lax
from jax.experimental import pallas as pl
from jax.experimental.pallas import tpu as pltpu
from jax.sharding import PartitionSpec as P

NRHS = 4
STEPS = 4
COLS = NRHS * (STEPS + 1)
SHIFTS = (3.0, 11.0, 7.0, 1.5)
SCALE = 1.0 / 6.0
FIELDS = NRHS + 4
AXES = ("gx", "gy", "gz")
HIGHEST = lax.Precision.HIGHEST

DEPTH = 4
NZ, NX, NY = 8, 32, 256
EZ = NZ + 2 * DEPTH
ROWS = NX + 8
EROWS = ROWS + 16
LT = 3
FACE = NRHS * 4 + 3 * 4 + 1
F32 = jnp.float32
LIMIT, ROOMY = 63, 52


def params(mb):
    return pltpu.CompilerParams(vmem_limit_bytes=mb << 20)


def cost(us):
    return pl.CostEstimate(flops=0, bytes_accessed=int(us * 3.6e6), transcendentals=0)


def vmem():
    return pl.BlockSpec(memory_space=pltpu.VMEM)


def smem():
    return pl.BlockSpec(memory_space=pltpu.SMEM)


def hbm():
    return pl.BlockSpec(memory_space=pl.ANY)


def row_ids(shape):
    return lax.broadcasted_iota(jnp.int32, shape, 0)


def lane_ids(shape):
    return lax.broadcasted_iota(jnp.int32, shape, 1)


def field_of(rhs, cz, cx, cy, dg, f, z):
    return rhs.at[f, z] if f < NRHS else (cz, cx, cy, dg)[f - NRHS].at[z]


def pack_faces(swap, place, odd_z, rhs, cz, cx, cy, dg, z_one, z_two, *rest):
    xmsgs, (whole, loads, saves) = rest[:-3], rest[-3:]
    copies = []
    for f in range(FIELDS):
        src = rhs.at[f] if f < NRHS else (cz, cx, cy, dg)[f - NRHS]
        copies.append(pltpu.make_async_copy(src, whole.at[f], loads.at[f]))
        copies[-1].start()
    low = row_ids((8, NY)) < 4
    up = place[0] == 0
    planes = []
    at = 0
    for f in range(FIELDS):
        copies[f].wait()
        depth = DEPTH if f <= NRHS else DEPTH - 1
        for side, out in ((0, z_one), (1, z_two)):
            start = jnp.where(odd_z[0] == side, NZ - depth, 0)
            planes.append(
                pltpu.make_async_copy(
                    whole.at[f, pl.ds(start, depth)], out.at[pl.ds(at, depth)], saves.at[2 * f + side]
                )
            )
            planes[-1].start()
        at += depth
        for m in range(NZ // 2):
            a, b = whole.at[f, 2 * m], whole.at[f, 2 * m + 1]
            first = jnp.where(low, a[0:8], pltpu.roll(b[0:8], 4, 0))
            last = jnp.where(low, pltpu.roll(a[NX - 8 : NX], 4, 0), b[NX - 8 : NX])
            if swap:
                xmsgs[0][f, m] = jnp.where(up, last, first)
            else:
                xmsgs[0][f, m] = first
                xmsgs[1][f, m] = last
    for copy in planes:
        copy.wait()


def halo_tile(above, below, odd, keep_up, keep_dn):
    low = row_ids(above.shape) < 4
    if odd:
        up, dn = pltpu.roll(above, 4, 0), below
    else:
        up, dn = above, pltpu.roll(below, 4, 0)
    return jnp.where(low, up * keep_up, dn * keep_dn)


def keep_sides(swap, place):
    if not swap:
        return 1.0, 1.0
    first = place[0] == 0
    return jnp.where(first, 1.0, 0.0), jnp.where(first, 0.0, 1.0)


def pack_lanes(tile_of, side):
    lane = lane_ids((8, 128))
    source = 124 * side
    acc = jnp.zeros((8, 128), F32)
    for zz in range(4):
        for f in range(FIELDS):
            tile = tile_of(f, zz)
            spot = (zz * FIELDS + f) * 4
            shift = (spot - source) % 128
            if shift:
                tile = pltpu.roll(tile, shift, 1)
            acc = jnp.where((lane >= spot) & (lane < spot + 4), tile, acc)
    return acc


def pack_own_rims(odd_y, rhs, cz, cx, cy, dg, one, two):
    odd = odd_y[0] == 1
    for t in range(NX // 8):
        for half in range(2):
            lo, hi = (
                pack_lanes(
                    lambda f, zz: field_of(rhs, cz, cx, cy, dg, f, 4 * half + zz)[
                        8 * t : 8 * t + 8, 128 * side : 128 * side + 128
                    ],
                    side,
                )
                for side in range(2)
            )
            one[8 * t : 8 * t + 8, 128 * half : 128 * half + 128] = jnp.where(odd, lo, hi)
            two[8 * t : 8 * t + 8, 128 * half : 128 * half + 128] = jnp.where(odd, hi, lo)


def pack_rims(swap, place, odd_y, *refs):
    above, below, one, two = refs if not swap else (refs[0],) + refs
    keep_up, keep_dn = keep_sides(swap, place)
    odd = odd_y[0] == 1
    for half in range(2):
        halves = []
        for side in range(2):
            lanes = slice(128 * side, 128 * side + 128)
            halves.append(
                pack_lanes(
                    lambda f, zz: halo_tile(
                        above[f, 2 * half + zz // 2, :, lanes],
                        below[f, 2 * half + zz // 2, :, lanes],
                        zz % 2,
                        keep_up,
                        keep_dn,
                    ),
                    side,
                )
            )
        lo, hi = halves
        one[:, 128 * half : 128 * half + 128] = jnp.where(odd, lo, hi)
        two[:, 128 * half : 128 * half + 128] = jnp.where(odd, hi, lo)


STACK = 8 * COLS


def gram_zero(accs):
    accs[...] = jnp.zeros_like(accs)


def gram_add(stacks, accs):
    left, right = [], []
    cross_left, cross_right = [], []
    for stack in stacks:
        high = stack.astype(jnp.bfloat16)
        rest = stack - high.astype(F32)
        mid = rest.astype(jnp.bfloat16)
        low = (rest - mid.astype(F32)).astype(jnp.bfloat16)
        left += [high, mid]
        cross_left += [high, high]
        cross_right += [mid, low]
    contract = (((1,), (1,)), ((), ()))

    def product(a, b):
        return lax.dot_general(jnp.concatenate(a, 1), jnp.concatenate(b, 1), contract, preferred_element_type=F32)

    accs[0] += product(left, left)
    accs[1] += product(cross_left, cross_right)


def gram_message(accs, out):
    same = (row_ids((STACK, STACK)) & 7) == (lane_ids((STACK, STACK)) & 7)
    pick = jnp.where((row_ids((STACK, 128)) >> 3) == lane_ids((STACK, 128)), 1.0, 0.0)

    def traces(product):
        picked = jnp.where(same, product, 0.0)
        rows = [jnp.sum(picked[8 * i : 8 * i + 8], axis=0, keepdims=True) for i in range(COLS)]
        rows = jnp.concatenate(rows + [jnp.zeros((128 - COLS, STACK), F32)], 0)
        return lax.dot_general(
            rows, pick, (((1,), (0,)), ((), ())), precision=HIGHEST, preferred_element_type=F32
        )

    cross = traces(accs[1])
    gram = traces(accs[0]) + cross + cross.T
    tops = [gram[8 * k : 8 * k + 8] for k in range(3)]
    rows, lanes = row_ids((8, 128)), lane_ids((8, 128))
    tile = jnp.where(lanes < COLS, tops[0], pltpu.roll(tops[1], 12, 1))
    corner = pltpu.roll(pltpu.roll(tops[2], 128 - 16, 1), 4, 0)
    tile = jnp.where((rows >= 4) & (lanes < 4), corner, tile)
    packed = tile
    for q in range(1, 4):
        turned = pltpu.roll(pltpu.roll(tile, 32 * q, 1), 8 - 2 * q, 0)
        packed = jnp.where((lanes >> 5) == q, turned, packed)
    packed = packed[0:2]
    for n in range(out.shape[0]):
        out[n] = packed


def gram_of(messages):
    total = messages[0]
    for n in range(1, messages.shape[0]):
        total = total + messages[n]
    total = jnp.concatenate([total] * 4, 0)
    rows, lanes = row_ids((8, 128)), lane_ids((8, 128))
    tile = total
    for q in range(1, 4):
        tile = jnp.where((rows >> 1) == q, pltpu.roll(total, 128 - 32 * q, 1), tile)
    corner = pltpu.roll(pltpu.roll(tile, 4, 0), 16, 1)
    tops = [
        jnp.where((lanes < COLS) & (lanes >= rows), tile, 0.0),
        jnp.where((lanes < COLS) & (lanes >= rows + 8), pltpu.roll(tile, 128 - 12, 1), 0.0),
        jnp.where((lanes < COLS) & (lanes >= rows + 16), corner, 0.0),
    ]
    return jnp.concatenate(tops, 0)


GROUPS = (9, 12, 9, 9, 9, 9)


def group(k):
    return k + 1 if k else 0


class Block:
    def __init__(self, stores, base, faces, faces_base, one):
        self.one = one
        self.stores, self.base, self.faces, self.faces_base = stores, base, faces, faces_base
        self.lane = lane_ids((8, 128))

    def where(self, f, l):
        return (0, 2 * f + l) if f < NRHS else (1, 3 * (f - NRHS) + l)

    def put(self, g, n, z, t, value):
        store, z = self.stores[g], z - self.base
        store[n, z, 8 + 8 * t : 16 + 8 * t, :] = value
        if t == 0:
            store[n, z, 8 + ROWS : 16 + ROWS, :] = value
        if t == ROWS // 8 - 1:
            store[n, z, 0:8, :] = value

    def get(self, g, n, z, t, off=0):
        row = 8 + 8 * t + (off * self.one if off else 0)
        return self.stores[g][n, z - self.base, pl.ds(row, 8), :]

    def close_ring(self, f, z):
        z = z - self.base
        for l in range(2):
            g, n = self.where(f, l)
            self.stores[g][n, z, 8 + ROWS : 16 + ROWS, :] = self.stores[g][n, z, 8:16, :]

    def place_y(self, z, up, dn):
        part, place = self.lane & 31, self.lane >> 5
        upper, lower = part < 4, part >= 28
        for t in range(ROWS // 8):
            u_all, d_all = up[8 * t : 8 * t + 8, :], dn[8 * t : 8 * t + 8, :]

            def turned(value, shift):
                return pltpu.roll(value, shift % 128, 1) if shift % 128 else value

            def copies(f):
                result = []
                for m in range(4):
                    u, d = turned(u_all, 32 * m - 4 * f), turned(d_all, 32 * m + 28 - 4 * f)
                    result.append(jnp.where(upper, u, jnp.where(lower, d, 0.0)))
                return result

            def pick(tiles):
                value = tiles[0]
                for r in range(1, 4):
                    value = jnp.where(place == r, tiles[r], value)
                return value

            fields = [copies(r) for r in range(NRHS)]
            for zz in range(4):
                self.put(0, 2 * NRHS, z + zz, t, pick([fields[r][(r - zz) % 4] for r in range(4)]))
            for c in range(4):
                mine = copies(NRHS + c)
                for zz in range(4):
                    self.put(1, 3 * c + 2, z + zz, t, pick([mine[(r - zz) % 4] for r in range(4)]))

    def coefficients(self, z):
        lane = self.lane
        for t in range(ROWS // 8):

            def tiles(c, z, off=0):
                return [self.get(1, 3 * c + l, z, t, off) for l in range(LT)]

            center_z, center_x, center_y, diag = (tiles(c, z) for c in range(4))
            up = [pltpu.roll(v, 127, 1) for v in center_y]
            dn = [pltpu.roll(v, 1, 1) for v in center_y]
            first = jnp.broadcast_to(center_y[0][:, 0:1], (8, 128))
            last = jnp.broadcast_to(center_y[1][:, 127:128], (8, 128))
            sides = [
                (center_z, tiles(0, z + 1)),
                (center_z, tiles(0, z - 1)),
                (center_x, tiles(1, z, 1)),
                (center_x, tiles(1, z, -1)),
                (
                    center_y,
                    [
                        jnp.where(lane == 127, up[1], up[0]),
                        jnp.where(lane == 127, up[2], up[1]),
                        jnp.where((lane & 31) == 31, first, up[2]),
                    ],
                ),
                (
                    center_y,
                    [
                        jnp.where(lane == 0, dn[2], dn[0]),
                        jnp.where(lane == 0, dn[0], dn[1]),
                        jnp.where((lane & 31) == 0, last, dn[2]),
                    ],
                ),
            ]
            at = z - self.faces_base
            for l in range(LT):
                inside = diag[l] > 0.0
                total = diag[l] * SCALE
                for k, (mid, side) in enumerate(sides):
                    face = (mid[l] + side[l]) * (0.5 * SCALE)
                    total = total + face
                    self.faces[k, at, l, 8 * t : 8 * t + 8, :] = jnp.where(inside, face, 0.0)
                self.faces[6, at, l, 8 * t : 8 * t + 8, :] = jnp.where(inside, total, 0.0)

    def apply(self, k, z):
        last = k == STEPS - 1
        at, lane, edge = z - self.faces_base, self.lane, 2 * NRHS
        src, dst = group(k), group(k + 1)
        for t in range(NX // 8 if last else ROWS // 8):
            face = [
                [self.faces[c, at, l, 8 * t : 8 * t + 8, :] for l in range(2 if last else LT)] for c in range(7)
            ]
            diag = [d - SHIFTS[k] * SCALE for d in face[6]]

            def image(n, l, mid, up, dn):
                sides = (
                    self.get(src, n, z + 1, t),
                    self.get(src, n, z - 1, t),
                    self.get(src, n, z, t, 1),
                    self.get(src, n, z, t, -1),
                    up,
                    dn,
                )
                value = diag[l] * mid
                for c, side in enumerate(sides):
                    value = value - face[c][l] * side
                self.put(dst, n, z, t, value)

            rim = self.get(src, edge, z, t)
            rim_up, rim_dn = pltpu.roll(rim, 127, 1), pltpu.roll(rim, 1, 1)
            edge_up, edge_dn = rim_up, rim_dn
            for r in range(NRHS):
                one, two = self.get(src, 2 * r, z, t), self.get(src, 2 * r + 1, z, t)
                one_up, two_up = pltpu.roll(one, 127, 1), pltpu.roll(two, 127, 1)
                one_dn, two_dn = pltpu.roll(one, 1, 1), pltpu.roll(two, 1, 1)
                above = rim_up if r == 0 else pltpu.roll(rim, 127 - 32 * r, 1)
                below = rim_dn if r == NRHS - 1 else pltpu.roll(rim, 97 - 32 * r, 1)
                image(2 * r, 0, one, jnp.where(lane == 127, two_up, one_up), jnp.where(lane == 0, below, one_dn))
                image(2 * r + 1, 1, two, jnp.where(lane == 127, above, two_up), jnp.where(lane == 0, one_dn, two_dn))
                if not last:
                    start = one_up if r == NRHS - 1 else pltpu.roll(one, 32 * r + 31, 1)
                    end = two_dn if r == 0 else pltpu.roll(two, 32 * r + 1, 1)
                    edge_up = jnp.where(lane == 32 * r + 31, start, edge_up)
                    edge_dn = jnp.where(lane == 32 * r, end, edge_dn)
            if not last:
                image(edge, 2, rim, edge_up, edge_dn)


def dynamic_one(place):
    return (place[0] >> 24) + 1


def loop(start, stop, do):
    def step(n, carry):
        do(n)
        return carry

    lax.fori_loop(start, stop, step, 0)


def inner_planes(k):
    return DEPTH + k, DEPTH + NZ - k


def inner_copies(inner, inner_faces, stores, base, faces, faces_base, sems, out):
    def copy(n, there, here):
        src, dst = (here, there) if out else (there, here)
        return pltpu.make_async_copy(src, dst, sems.at[n])

    result = []
    for n, (g, start, stop) in enumerate(
        [(g, z, z + 2) for g in (0, 1) for z in (DEPTH, DEPTH + NZ - 2)]
        + [(0, DEPTH + 2, DEPTH + NZ - 2)]
        + [(group(k), *inner_planes(k)) for k in range(1, STEPS)]
    ):
        there = inner.at[pl.ds(sum(GROUPS[:g]), GROUPS[g]), pl.ds(start - DEPTH, stop - start)]
        result.append(copy(n, there, stores[g].at[:, pl.ds(start - base, stop - start)]))
    start, stop = inner_planes(1)
    result.append(copy(len(result), inner_faces, faces.at[:, pl.ds(start - faces_base, stop - start)]))
    return result


def krylov_inner(swap, place, rhs, cz, cx, cy, dg, *rest):
    above, below, yup, ydn, inner, inner_faces, *stores, faces, load_sems, sems = rest if not swap else rest[:1] + rest
    keep_up, keep_dn = keep_sides(swap, place)
    block = Block(stores, DEPTH, faces, DEPTH + 1, dynamic_one(place))
    loads = []
    for f in range(FIELDS):
        src = rhs.at[f] if f < NRHS else (cz, cx, cy, dg)[f - NRHS]
        for l in range(2):
            g, n = block.where(f, l)
            loads.append(
                pltpu.make_async_copy(
                    src.at[:, :, pl.ds(128 * l, 128)], stores[g].at[n, :, pl.ds(8, NX), :], load_sems.at[2 * f + l]
                )
            )
            loads[-1].start()
    for f in range(FIELDS):
        for z in range(DEPTH, DEPTH + NZ):
            m = (z - DEPTH) // 2
            for l in range(2):
                lanes = pl.ds(128 * l, 128)
                tile = halo_tile(above[f, m, :, lanes], below[f, m, :, lanes], z % 2, keep_up, keep_dn)
                block.put(*block.where(f, l), z, NX // 8, tile)
    for half in range(2):
        lanes = pl.ds(128 * half, 128)
        block.place_y(DEPTH + 4 * half, yup.at[:, lanes], ydn.at[:, lanes])
    for copy in loads:
        copy.wait()
    for f in range(FIELDS):
        for z in range(DEPTH, DEPTH + NZ):
            block.close_ring(f, z)
    copies = inner_copies(inner, inner_faces, stores, DEPTH, faces, DEPTH + 1, sems, True)
    for n in range(5):
        copies[n].start()
    loop(*inner_planes(1), block.coefficients)
    copies[-1].start()
    for k in range(STEPS - 1):
        loop(*inner_planes(k + 1), functools.partial(block.apply, k))
        copies[5 + k].start()
    for copy in copies:
        copy.wait()


NEAR, FAR = 8 * FIELDS, 24


def krylov_outer(
    swap, face_one, face_two, place, odd_z, inner, inner_faces, rim_one, rim_two,
    basis, message,
    *rest,
):
    keep_up, keep_dn = keep_sides(swap, place)
    n_x = 1 if swap else 2
    *stores, faces, accs, rims, plane_sems, loads, saves = rest
    odd = odd_z[0] == 1
    block = Block(stores, 0, faces, 0, dynamic_one(place))
    copies = inner_copies(inner, inner_faces, stores, 0, faces, 0, loads, False)
    def plane_copies(lower, upper):
        planes = []
        start = 0
        for f in range(FIELDS):
            depth = DEPTH if f <= NRHS else DEPTH - 1
            for side, (face, z) in enumerate(((lower, DEPTH - depth), (upper, DEPTH + NZ))):
                for l in range(2):
                    g, n = block.where(f, l)
                    planes.append(
                        pltpu.make_async_copy(
                            face.at[pl.ds(start, depth), :, pl.ds(128 * l, 128)],
                            stores[g].at[n, pl.ds(z, depth), pl.ds(8, NX), :],
                            plane_sems.at[4 * f + 2 * side + l],
                        )
                    )
            start += depth
        return planes

    for copy in copies[:4]:
        copy.start()

    @pl.when(odd)
    def _():
        for copy in plane_copies(face_one, face_two):
            copy.start()

    @pl.when(jnp.logical_not(odd))
    def _():
        for copy in plane_copies(face_two, face_one):
            copy.start()

    one, two = rim_one[...], rim_two[...]
    rims[0] = jnp.where(odd, one, two)
    rims[1] = jnp.where(odd, two, one)
    rimlo, rimhi = rims.at[0], rims.at[1]

    zero = jnp.zeros((8, 128), F32)
    for f in range(FIELDS):
        for rim, first in ((rimlo, 0), (rimhi, DEPTH + NZ)):
            for z in range(first, first + DEPTH):
                far = DEPTH - z if first == 0 else z - first + 1
                for l in range(2):
                    lanes = pl.ds(128 * l, 128)
                    if far <= 2:
                        at, odd = 8 * f, z % 2
                    elif far == 3 and 8 * (f // 2) < FAR:
                        at, odd = NEAR + 8 * (f // 2), f % 2
                    else:
                        block.put(*block.where(f, l), z, NX // 8, zero)
                        continue
                    other = at + (n_x - 1) * (NEAR + FAR)
                    tile = halo_tile(rim[at : at + 8, lanes], rim[other : other + 8, lanes], odd, keep_up, keep_dn)
                    block.put(*block.where(f, l), z, NX // 8, tile)
    rows = pl.ds(n_x * (NEAR + FAR), ROWS)
    for rim, z in ((rimlo, 0), (rimhi, DEPTH + NZ)):
        block.place_y(z, rim.at[rows, pl.ds(0, 128)], rim.at[rows, pl.ds(128, 128)])

    for copy in copies[:4] + plane_copies(face_one, face_two):
        copy.wait()
    for copy in [copies[5], copies[-1], copies[6], copies[7], copies[4]]:
        copy.start()
    for f in range(FIELDS):
        depth = DEPTH if f <= NRHS else DEPTH - 1
        for d in range(depth):
            block.close_ring(f, DEPTH - 1 - d)
            block.close_ring(f, DEPTH + NZ + d)
    loop(1, DEPTH + 1, block.coefficients)
    loop(DEPTH + NZ - 1, EZ - 1, block.coefficients)

    sends = []

    def send_block(k):
        copy = pltpu.make_async_copy(
            stores[group(k)].at[pl.ds(0, 2 * NRHS), pl.ds(DEPTH, NZ), pl.ds(8, NX), :],
            basis.at[pl.ds(k * 2 * NRHS, 2 * NRHS)],
            saves.at[k],
        )
        copy.start()
        sends.append(copy)

    for k in range(STEPS):
        if k == 1:
            copies[-1].wait()
        loop(
            0,
            2 * DEPTH,
            lambda n, k=k: block.apply(k, n + k + 1 + jnp.where(n >= DEPTH, NZ - 2 - 2 * k, 0)),
        )
        if k < STEPS - 1:
            copies[5 + k].wait()
        send_block(k + 1)
    copies[4].wait()
    send_block(0)
    gram_zero(accs)

    def products(z):
        def tile(i, t):
            store = stores[group(i // NRHS)]
            return jnp.concatenate([store[2 * (i % NRHS) + l, z, 8 + 8 * t : 16 + 8 * t, :] for l in range(2)], 1)

        gram_add([jnp.concatenate([tile(i, t) for i in range(COLS)], 0) for t in range(NX // 8)], accs)

    loop(DEPTH, DEPTH + NZ, products)
    gram_message(accs, message)
    for copy in sends:
        copy.wait()


def factor_gram(messages, cells, table):
    rows = row_ids((24, 128))
    lanes = lane_ids((24, 128))
    upper = gram_of(messages) / cells
    square = jnp.concatenate([upper, jnp.zeros((104, 128), F32)], 0).T
    whole = jnp.where(rows <= lanes, upper, square[0:24, :])

    tile_rows = row_ids((8, 128))
    tiles = range(3)

    def split(value):
        return [value[8 * k : 8 * k + 8] for k in tiles]

    def row_of(column, j):
        return jnp.broadcast_to(column[j // 8][j % 8 : j % 8 + 1, :], (8, 128))

    columns = [split(jnp.broadcast_to(whole[:, c : c + 1], (24, 128))) for c in range(COLS)]
    inverse = [[jnp.where(tile_rows + 8 * k == c, 1.0, 0.0) for k in tiles] for c in range(COLS)]
    pivots = [jnp.ones((8, 128), F32) for k in tiles]
    for j in range(COLS):
        pivot = row_of(columns[j], j)
        first = j // 8
        pivots[first] = jnp.where(tile_rows == j % 8, pivot, pivots[first])
        below = {k: columns[j][k] / pivot for k in tiles if k >= first}
        below[first] = jnp.where(tile_rows > j % 8, below[first], 0.0)
        for c in range(COLS):
            change = columns[c] if c > j else inverse[c]
            row = row_of(change, j)
            for k in below:
                change[k] = change[k] - below[k] * row
    scales = [1.0 / jnp.sqrt(p) for p in pivots]
    factor = jnp.zeros((24, 128), F32)
    for c in range(COLS):
        table[c] = jnp.concatenate([inverse[c][k] * scales[k] for k in tiles], 0)
        factor = jnp.where(lanes == c, jnp.concatenate(columns[c], 0), factor)
    return jnp.where((rows <= lanes) & (rows < COLS), factor * jnp.concatenate(scales, 0), 0.0)


def apply_rows(table, read, write):
    group = 5
    pieces = NX // 8
    for g in reversed(range(COLS // group)):
        mine = range(group * g, group * g + group)
        sums = {i: None for i in mine}
        for j in range(group * g + group):
            value = [read(j, p) for p in range(pieces)]
            for i in mine:
                if j <= i:
                    weight = jnp.broadcast_to(table[j, i : i + 1, :], (8, 128))
                    terms = [weight * v for v in value]
                    sums[i] = terms if sums[i] is None else [s + t for s, t in zip(sums[i], terms)]
        for i in mine:
            for p in range(pieces):
                write(i, p, sums[i][p])


def plane_copy(src, dst, sems, z):
    return pltpu.make_async_copy(src.at[:, z], dst.at[:, z], sems.at[z])


def first_pass(
    cells, message, basis_hbm, first_hbm, next_message, factor_out, basis, first, table, accs, loads, saves
):
    for z in range(NZ):
        plane_copy(basis_hbm, basis, loads, z).start()
    factor_out[...] = factor_gram(message, cells, table)
    gram_zero(accs)

    def products(z):
        def tile(i, t):
            return jnp.concatenate([first[2 * i + l, z, 8 * t : 8 * t + 8, :] for l in range(2)], 1)

        gram_add([jnp.concatenate([tile(i, t) for i in range(COLS)], 0) for t in range(NX // 8)], accs)

    def apply(z):
        for l in range(2):

            def read(j, p):
                return basis[2 * j + l, z, 8 * p : 8 * p + 8, :]

            def write(i, p, value):
                first[2 * i + l, z, 8 * p : 8 * p + 8, :] = value

            apply_rows(table, read, write)
        plane_copy(first, first_hbm, saves, z).start()

    def both(z):
        plane_copy(basis_hbm, basis, loads, z).wait()
        products(z - 1)
        apply(z)

    plane_copy(basis_hbm, basis, loads, 0).wait()
    apply(0)
    loop(1, NZ, both)
    products(NZ - 1)
    gram_message(accs, next_message)
    for z in range(NZ):
        plane_copy(first, first_hbm, saves, z).wait()


def second_pass(cells, message, factor_one, first_hbm, out_hbm, triangle, first, out, table, loads, saves):
    for z in range(NZ):
        plane_copy(first_hbm, first, loads, z).start()
    left = factor_gram(message, cells, table)[:, 0:24]
    product = lax.dot_general(
        left, factor_one[...], (((1,), (0,)), ((), ())), precision=HIGHEST, preferred_element_type=F32
    )
    triangle[...] = product[0:COLS, 0:COLS]

    def chunk(z, carry):
        plane_copy(first_hbm, first, loads, z).wait()
        for l in range(2):

            def read(j, p):
                return first[2 * j + l, z, 8 * p : 8 * p + 8, :]

            def write(i, p, value):
                out[i, z, 8 * p : 8 * p + 8, 128 * l : 128 * l + 128] = value

            apply_rows(table, read, write)
        plane_copy(out, out_hbm, saves, z).start()
        return carry

    lax.fori_loop(0, NZ, chunk, 0)
    for z in range(NZ):
        plane_copy(out, out_hbm, saves, z).wait()


def shape(*dims):
    return jax.ShapeDtypeStruct(dims, F32)


def move(value, axis, delta):
    count = lax.axis_size(axis)
    pairs = [(i, i + delta) for i in range(count) if 0 <= i + delta < count]
    return lax.ppermute(value, axis, pairs)


def swap_pairs(value, axis, first):
    pairs = [(i, i + 1) for i in range(first, lax.axis_size(axis) - 1, 2)]
    return lax.ppermute(value, axis, pairs + [(j, i) for i, j in pairs])


def exchange(messages):
    return lax.all_to_all(messages, AXES, 0, 0, tiled=True)


def body(rhs, coef_x, coef_y, coef_z, diag_term):
    n_x = lax.axis_size("gx")
    devices = n_x * lax.axis_size("gy") * lax.axis_size("gz")
    cells = float(NZ * NX * NY * devices)
    at_x = lax.axis_index("gx")
    swap = n_x == 2
    fields = (rhs, coef_z, coef_x, coef_y, diag_term)

    place = at_x.astype(jnp.int32).reshape(1)
    odd_z, odd_y = ((lax.axis_index(axis) & 1).astype(jnp.int32).reshape(1) for axis in ("gz", "gy"))
    face_shape = shape(FACE, NX, NY)
    x_shape = shape(FIELDS, NZ // 2, 8, NY)
    z_one, z_two, *xmsgs = pl.pallas_call(
        functools.partial(pack_faces, swap),
        out_shape=(face_shape, face_shape) + (x_shape,) * (1 if swap else 2),
        in_specs=[smem()] * 2 + [hbm()] * 5,
        out_specs=(hbm(), hbm()) + (vmem(),) * (1 if swap else 2),
        scratch_shapes=[
            pltpu.VMEM((FIELDS, NZ, NX, NY), F32),
            pltpu.SemaphoreType.DMA((FIELDS,)),
            pltpu.SemaphoreType.DMA((2 * FIELDS,)),
        ],
        compiler_params=params(LIMIT),
        cost_estimate=cost(2.5),
    )(place, odd_z, *fields)
    face_one, face_two = swap_pairs(z_one, "gz", 0), swap_pairs(z_two, "gz", 1)
    if swap:
        x_parts = (lax.ppermute(xmsgs[0], "gx", [(0, 1), (1, 0)]),)
    else:
        x_parts = (move(xmsgs[0], "gx", -1), move(xmsgs[1], "gx", 1))

    own_shape, halo_shape = shape(NX, NY), shape(ROWS - NX, NY)
    own_one, own_two = pl.pallas_call(
        pack_own_rims,
        out_shape=(own_shape, own_shape),
        in_specs=[smem()] + [vmem()] * 5,
        compiler_params=params(LIMIT),
        cost_estimate=cost(2.5),
    )(odd_y, *fields)
    halo_one, halo_two = pl.pallas_call(
        functools.partial(pack_rims, swap),
        out_shape=(halo_shape, halo_shape),
        in_specs=[smem()] * 2 + [vmem()] * len(x_parts),
        compiler_params=params(16),
        cost_estimate=cost(1),
    )(place, odd_y, *x_parts)
    y_one = swap_pairs(jnp.concatenate([own_one, halo_one], 0), "gy", 0)
    y_two = swap_pairs(jnp.concatenate([own_two, halo_two], 0), "gy", 1)
    yup, ydn = jnp.where(odd_y == 1, y_two, y_one), jnp.where(odd_y == 1, y_one, y_two)

    def rim(half):
        near, far, odd = ((0, 1, 0), (3, 2, 1))[half]
        rows = []
        for part in x_parts:
            rows.append(part[:, near].reshape(NEAR, NY))
            rows.append(part[: FAR // 4, far, 4 * odd : 4 * odd + 4].reshape(FAR, NY))
        lanes = slice(128 * half, 128 * half + 128)
        return jnp.concatenate(rows + [jnp.concatenate([yup[:, lanes], ydn[:, lanes]], 1)], 0)

    low, high = rim(0), rim(1)
    rim_one = swap_pairs(jnp.where(odd_z == 1, low, high), "gz", 0)
    rim_two = swap_pairs(jnp.where(odd_z == 1, high, low), "gz", 1)

    inner_shape = shape(sum(GROUPS[:-1]), NZ, EROWS, 128)
    inner_faces_shape = shape(7, NZ - 2, LT, ROWS, 128)
    inner, inner_faces = pl.pallas_call(
        functools.partial(krylov_inner, swap),
        out_shape=(inner_shape, inner_faces_shape),
        in_specs=[smem()] + [hbm()] * 5 + [vmem()] * (len(x_parts) + 2),
        out_specs=(hbm(), hbm()),
        scratch_shapes=[
            *[pltpu.VMEM((tiles, NZ, EROWS, 128), F32) for tiles in GROUPS[:-1]],
            pltpu.VMEM(inner_faces_shape.shape, F32),
            pltpu.SemaphoreType.DMA((2 * FIELDS,)),
            pltpu.SemaphoreType.DMA((9,)),
        ],
        compiler_params=params(LIMIT),
        cost_estimate=cost(7),
    )(place, *fields, *x_parts, yup, ydn)

    block = shape(2 * COLS, NZ, NX, 128)
    basis, message = pl.pallas_call(
        functools.partial(krylov_outer, swap),
        out_shape=(block, shape(devices, 2, 128)),
        in_specs=[hbm(), hbm(), smem(), smem(), hbm(), hbm(), vmem(), vmem()],
        out_specs=(hbm(), vmem()),
        scratch_shapes=[
            *[pltpu.VMEM((tiles, EZ, EROWS, 128), F32) for tiles in GROUPS],
            pltpu.VMEM((7, EZ, LT, ROWS, 128), F32),
            pltpu.VMEM((2, STACK, STACK), F32),
            pltpu.VMEM((2,) + rim_one.shape, F32),
            pltpu.SemaphoreType.DMA((4 * FIELDS,)),
            pltpu.SemaphoreType.DMA((9,)),
            pltpu.SemaphoreType.DMA((STEPS + 1,)),
        ],
        compiler_params=params(ROOMY),
        cost_estimate=cost(15),
    )(face_one, face_two, place, odd_z, inner, inner_faces, rim_one, rim_two)

    message = exchange(message)
    first, message, factor_one = pl.pallas_call(
        functools.partial(first_pass, cells),
        out_shape=(block, shape(devices, 2, 128), shape(24, 128)),
        in_specs=[vmem(), hbm()],
        out_specs=(hbm(), vmem(), vmem()),
        scratch_shapes=[
            pltpu.VMEM(block.shape, F32),
            pltpu.VMEM(block.shape, F32),
            pltpu.VMEM((COLS, 24, 128), F32),
            pltpu.VMEM((2, STACK, STACK), F32),
            pltpu.SemaphoreType.DMA((NZ,)),
            pltpu.SemaphoreType.DMA((NZ,)),
        ],
        compiler_params=params(ROOMY),
    )(message, basis)

    message = exchange(message)
    return pl.pallas_call(
        functools.partial(second_pass, cells),
        out_shape=(shape(COLS, NZ, NX, NY), shape(COLS, COLS)),
        in_specs=[vmem(), vmem(), hbm()],
        out_specs=(hbm(), vmem()),
        scratch_shapes=[
            pltpu.VMEM(block.shape, F32),
            pltpu.VMEM((COLS, NZ, NX, NY), F32),
            pltpu.VMEM((COLS, 24, 128), F32),
            pltpu.SemaphoreType.DMA((NZ,)),
            pltpu.SemaphoreType.DMA((NZ,)),
        ],
        compiler_params=params(ROOMY),
    )(message, factor_one, first)


def solution(mesh):
    return jax.shard_map(
        body,
        mesh=mesh,
        in_specs=(
            P(None, "gz", "gx", "gy"),
            P("gz", "gx", "gy"),
            P("gz", "gx", "gy"),
            P("gz", "gx", "gy"),
            P("gz", "gx", "gy"),
        ),
        out_specs=(P(None, "gz", "gx", "gy"), P()),
        check_vma=False,
    )
```

```python
import functools

import jax
import jax.numpy as jnp
from jax import lax
from jax.experimental import pallas as pl
from jax.experimental.pallas import tpu as pltpu
from jax.sharding import PartitionSpec as P

NRHS = 4
STEPS = 4
COLS = NRHS * (STEPS + 1)
SHIFTS = (3.0, 11.0, 7.0, 1.5)
SCALE = 1.0 / 6.0
FIELDS = NRHS + 4
AXES = ("gx", "gy", "gz")
HIGHEST = lax.Precision.HIGHEST

DEPTH = 4
NZ, NX, NY = 8, 32, 256
EZ = NZ + 2 * DEPTH
ROWS = NX + 8
EROWS = ROWS + 16
LT = 3
FACE = NRHS * 4 + 3 * 4 + 1
F32 = jnp.float32
LIMIT, ROOMY = 63, 52


def params(mb):
    return pltpu.CompilerParams(vmem_limit_bytes=mb << 20)


def cost(us):
    return pl.CostEstimate(flops=0, bytes_accessed=int(us * 3.6e6), transcendentals=0)


def vmem():
    return pl.BlockSpec(memory_space=pltpu.VMEM)


def smem():
    return pl.BlockSpec(memory_space=pltpu.SMEM)


def hbm():
    return pl.BlockSpec(memory_space=pl.ANY)


def row_ids(shape):
    return lax.broadcasted_iota(jnp.int32, shape, 0)


def lane_ids(shape):
    return lax.broadcasted_iota(jnp.int32, shape, 1)


def field_of(rhs, cz, cx, cy, dg, f, z):
    return rhs.at[f, z] if f < NRHS else (cz, cx, cy, dg)[f - NRHS].at[z]


def pack_faces(swap, place, odd_z, rhs, cz, cx, cy, dg, z_one, z_two, *rest):
    xmsgs, (xrows, whole, loads, saves, xsaves) = rest[:-5], rest[-5:]
    copies = []
    for f in range(FIELDS):
        src = rhs.at[f] if f < NRHS else (cz, cx, cy, dg)[f - NRHS]
        copies.append(pltpu.make_async_copy(src, whole.at[f], loads.at[f]))
        copies[-1].start()
    low = row_ids((8, NY)) < 4
    up = place[0] == 0
    planes = []
    at = 0
    for f in range(FIELDS):
        copies[f].wait()
        depth = DEPTH if f <= NRHS else DEPTH - 1
        for side, out in ((0, z_one), (1, z_two)):
            start = jnp.where(odd_z[0] == side, NZ - depth, 0)
            planes.append(
                pltpu.make_async_copy(
                    whole.at[f, pl.ds(start, depth)], out.at[pl.ds(at, depth)], saves.at[2 * f + side]
                )
            )
            planes[-1].start()
        at += depth
        for m in range(NZ // 2):
            a, b = whole.at[f, 2 * m], whole.at[f, 2 * m + 1]
            first = jnp.where(low, a[0:8], pltpu.roll(b[0:8], 4, 0))
            last = jnp.where(low, pltpu.roll(a[NX - 8 : NX], 4, 0), b[NX - 8 : NX])
            if swap:
                xrows[0, f, m] = jnp.where(up, last, first)
            else:
                xrows[0, f, m] = first
                xrows[1, f, m] = last
        for n, xmsg in enumerate(xmsgs):
            planes.append(pltpu.make_async_copy(xrows.at[n, f], xmsg.at[f], xsaves.at[n, f]))
            planes[-1].start()
    for copy in planes:
        copy.wait()


def halo_tile(above, below, odd, keep_up, keep_dn):
    low = row_ids(above.shape) < 4
    if odd:
        up, dn = pltpu.roll(above, 4, 0), below
    else:
        up, dn = above, pltpu.roll(below, 4, 0)
    return jnp.where(low, up * keep_up, dn * keep_dn)


def keep_sides(swap, place):
    if not swap:
        return 1.0, 1.0
    first = place[0] == 0
    return jnp.where(first, 1.0, 0.0), jnp.where(first, 0.0, 1.0)


def pack_lanes(tile_of, side):
    lane = lane_ids((8, 128))
    source = 124 * side
    acc = jnp.zeros((8, 128), F32)
    for zz in range(4):
        for f in range(FIELDS):
            tile = tile_of(f, zz)
            spot = (zz * FIELDS + f) * 4
            shift = (spot - source) % 128
            if shift:
                tile = pltpu.roll(tile, shift, 1)
            acc = jnp.where((lane >= spot) & (lane < spot + 4), tile, acc)
    return acc


def pack_own_rims(odd_y, rhs, cz, cx, cy, dg, one, two):
    odd = odd_y[0] == 1
    for t in range(NX // 8):
        for half in range(2):
            lo, hi = (
                pack_lanes(
                    lambda f, zz: field_of(rhs, cz, cx, cy, dg, f, 4 * half + zz)[
                        8 * t : 8 * t + 8, 128 * side : 128 * side + 128
                    ],
                    side,
                )
                for side in range(2)
            )
            one[8 * t : 8 * t + 8, 128 * half : 128 * half + 128] = jnp.where(odd, lo, hi)
            two[8 * t : 8 * t + 8, 128 * half : 128 * half + 128] = jnp.where(odd, hi, lo)


def pack_rims(swap, place, odd_y, *refs):
    above, below, one, two = refs if not swap else (refs[0],) + refs
    keep_up, keep_dn = keep_sides(swap, place)
    odd = odd_y[0] == 1
    for half in range(2):
        halves = []
        for side in range(2):
            lanes = slice(128 * side, 128 * side + 128)
            halves.append(
                pack_lanes(
                    lambda f, zz: halo_tile(
                        above[f, 2 * half + zz // 2, :, lanes],
                        below[f, 2 * half + zz // 2, :, lanes],
                        zz % 2,
                        keep_up,
                        keep_dn,
                    ),
                    side,
                )
            )
        lo, hi = halves
        one[:, 128 * half : 128 * half + 128] = jnp.where(odd, lo, hi)
        two[:, 128 * half : 128 * half + 128] = jnp.where(odd, hi, lo)


STACK = 8 * COLS


def gram_zero(accs):
    accs[...] = jnp.zeros_like(accs)


def gram_add(stacks, accs):
    left, right = [], []
    cross_left, cross_right = [], []
    for stack in stacks:
        high = stack.astype(jnp.bfloat16)
        rest = stack - high.astype(F32)
        mid = rest.astype(jnp.bfloat16)
        low = (rest - mid.astype(F32)).astype(jnp.bfloat16)
        left += [high, mid]
        cross_left += [high, high]
        cross_right += [mid, low]
    contract = (((1,), (1,)), ((), ()))

    def product(a, b):
        return lax.dot_general(jnp.concatenate(a, 1), jnp.concatenate(b, 1), contract, preferred_element_type=F32)

    accs[0] += product(left, left)
    accs[1] += product(cross_left, cross_right)


def gram_message(accs, out):
    same = (row_ids((STACK, STACK)) & 7) == (lane_ids((STACK, STACK)) & 7)
    pick = jnp.where((row_ids((STACK, 128)) >> 3) == lane_ids((STACK, 128)), 1.0, 0.0)

    def traces(product):
        picked = jnp.where(same, product, 0.0)
        rows = [jnp.sum(picked[8 * i : 8 * i + 8], axis=0, keepdims=True) for i in range(COLS)]
        rows = jnp.concatenate(rows + [jnp.zeros((128 - COLS, STACK), F32)], 0)
        return lax.dot_general(
            rows, pick, (((1,), (0,)), ((), ())), precision=HIGHEST, preferred_element_type=F32
        )

    cross = traces(accs[1])
    gram = traces(accs[0]) + cross + cross.T
    tops = [gram[8 * k : 8 * k + 8] for k in range(3)]
    rows, lanes = row_ids((8, 128)), lane_ids((8, 128))
    tile = jnp.where(lanes < COLS, tops[0], pltpu.roll(tops[1], 12, 1))
    corner = pltpu.roll(pltpu.roll(tops[2], 128 - 16, 1), 4, 0)
    tile = jnp.where((rows >= 4) & (lanes < 4), corner, tile)
    packed = tile
    for q in range(1, 4):
        turned = pltpu.roll(pltpu.roll(tile, 32 * q, 1), 8 - 2 * q, 0)
        packed = jnp.where((lanes >> 5) == q, turned, packed)
    packed = packed[0:2]
    for n in range(out.shape[0]):
        out[n] = packed


def gram_of(messages):
    parts = [messages[n] for n in range(messages.shape[0])]
    while len(parts) > 1:
        parts = [sum(parts[n : n + 2][1:], parts[n]) for n in range(0, len(parts), 2)]
    total = jnp.concatenate(parts * 4, 0)
    rows, lanes = row_ids((8, 128)), lane_ids((8, 128))
    tile = total
    for q in range(1, 4):
        tile = jnp.where((rows >> 1) == q, pltpu.roll(total, 128 - 32 * q, 1), tile)
    corner = pltpu.roll(pltpu.roll(tile, 4, 0), 16, 1)
    tops = [
        jnp.where((lanes < COLS) & (lanes >= rows), tile, 0.0),
        jnp.where((lanes < COLS) & (lanes >= rows + 8), pltpu.roll(tile, 128 - 12, 1), 0.0),
        jnp.where((lanes < COLS) & (lanes >= rows + 16), corner, 0.0),
    ]
    return jnp.concatenate(tops, 0)


GROUPS = (9, 12, 9, 9, 9, 9)


def group(k):
    return k + 1 if k else 0


class Block:
    def __init__(self, stores, base, faces, faces_base, one):
        self.one = one
        self.stores, self.base, self.faces, self.faces_base = stores, base, faces, faces_base
        self.lane = lane_ids((8, 128))

    def where(self, f, l):
        return (0, 2 * f + l) if f < NRHS else (1, 3 * (f - NRHS) + l)

    def put(self, g, n, z, t, value):
        store, z = self.stores[g], z - self.base
        store[n, z, 8 + 8 * t : 16 + 8 * t, :] = value
        if t == 0:
            store[n, z, 8 + ROWS : 16 + ROWS, :] = value
        if t == ROWS // 8 - 1:
            store[n, z, 0:8, :] = value

    def get(self, g, n, z, t, off=0):
        row = 8 + 8 * t + (off * self.one if off else 0)
        return self.stores[g][n, z - self.base, pl.ds(row, 8), :]

    def close_ring(self, f, z):
        z = z - self.base
        for l in range(2):
            g, n = self.where(f, l)
            self.stores[g][n, z, 8 + ROWS : 16 + ROWS, :] = self.stores[g][n, z, 8:16, :]

    def place_y(self, z, up, dn):
        part, place = self.lane & 31, self.lane >> 5
        upper, lower = part < 4, part >= 28
        for t in range(ROWS // 8):
            u_all, d_all = up[8 * t : 8 * t + 8, :], dn[8 * t : 8 * t + 8, :]

            def turned(value, shift):
                return pltpu.roll(value, shift % 128, 1) if shift % 128 else value

            def copies(f):
                result = []
                for m in range(4):
                    u, d = turned(u_all, 32 * m - 4 * f), turned(d_all, 32 * m + 28 - 4 * f)
                    result.append(jnp.where(upper, u, jnp.where(lower, d, 0.0)))
                return result

            def pick(tiles):
                value = tiles[0]
                for r in range(1, 4):
                    value = jnp.where(place == r, tiles[r], value)
                return value

            fields = [copies(r) for r in range(NRHS)]
            for zz in range(4):
                self.put(0, 2 * NRHS, z + zz, t, pick([fields[r][(r - zz) % 4] for r in range(4)]))
            for c in range(4):
                mine = copies(NRHS + c)
                for zz in range(4):
                    self.put(1, 3 * c + 2, z + zz, t, pick([mine[(r - zz) % 4] for r in range(4)]))

    def coefficients(self, z):
        lane = self.lane
        for t in range(ROWS // 8):

            def tiles(c, z, off=0):
                return [self.get(1, 3 * c + l, z, t, off) for l in range(LT)]

            center_z, center_x, center_y, diag = (tiles(c, z) for c in range(4))
            up = [pltpu.roll(v, 127, 1) for v in center_y]
            dn = [pltpu.roll(v, 1, 1) for v in center_y]
            first = jnp.broadcast_to(center_y[0][:, 0:1], (8, 128))
            last = jnp.broadcast_to(center_y[1][:, 127:128], (8, 128))
            sides = [
                (center_z, tiles(0, z + 1)),
                (center_z, tiles(0, z - 1)),
                (center_x, tiles(1, z, 1)),
                (center_x, tiles(1, z, -1)),
                (
                    center_y,
                    [
                        jnp.where(lane == 127, up[1], up[0]),
                        jnp.where(lane == 127, up[2], up[1]),
                        jnp.where((lane & 31) == 31, first, up[2]),
                    ],
                ),
                (
                    center_y,
                    [
                        jnp.where(lane == 0, dn[2], dn[0]),
                        jnp.where(lane == 0, dn[0], dn[1]),
                        jnp.where((lane & 31) == 0, last, dn[2]),
                    ],
                ),
            ]
            at = z - self.faces_base
            for l in range(LT):
                inside = diag[l] > 0.0
                total = diag[l] * SCALE
                for k, (mid, side) in enumerate(sides):
                    face = (mid[l] + side[l]) * (0.5 * SCALE)
                    total = total + face
                    self.faces[k, at, l, 8 * t : 8 * t + 8, :] = jnp.where(inside, face, 0.0)
                self.faces[6, at, l, 8 * t : 8 * t + 8, :] = jnp.where(inside, total, 0.0)

    def apply(self, k, z):
        last = k == STEPS - 1
        at, lane, edge = z - self.faces_base, self.lane, 2 * NRHS
        src, dst = group(k), group(k + 1)
        for t in range(NX // 8 if last else ROWS // 8):
            face = [
                [self.faces[c, at, l, 8 * t : 8 * t + 8, :] for l in range(2 if last else LT)] for c in range(7)
            ]
            diag = [d - SHIFTS[k] * SCALE for d in face[6]]

            def image(n, l, mid, up, dn):
                sides = (
                    self.get(src, n, z + 1, t),
                    self.get(src, n, z - 1, t),
                    self.get(src, n, z, t, 1),
                    self.get(src, n, z, t, -1),
                    up,
                    dn,
                )
                value = diag[l] * mid
                for c, side in enumerate(sides):
                    value = value - face[c][l] * side
                self.put(dst, n, z, t, value)

            rim = self.get(src, edge, z, t)
            rim_up, rim_dn = pltpu.roll(rim, 127, 1), pltpu.roll(rim, 1, 1)
            edge_up, edge_dn = rim_up, rim_dn
            for r in range(NRHS):
                one, two = self.get(src, 2 * r, z, t), self.get(src, 2 * r + 1, z, t)
                one_up, two_up = pltpu.roll(one, 127, 1), pltpu.roll(two, 127, 1)
                one_dn, two_dn = pltpu.roll(one, 1, 1), pltpu.roll(two, 1, 1)
                above = rim_up if r == 0 else pltpu.roll(rim, 127 - 32 * r, 1)
                below = rim_dn if r == NRHS - 1 else pltpu.roll(rim, 97 - 32 * r, 1)
                image(2 * r, 0, one, jnp.where(lane == 127, two_up, one_up), jnp.where(lane == 0, below, one_dn))
                image(2 * r + 1, 1, two, jnp.where(lane == 127, above, two_up), jnp.where(lane == 0, one_dn, two_dn))
                if not last:
                    start = one_up if r == NRHS - 1 else pltpu.roll(one, 32 * r + 31, 1)
                    end = two_dn if r == 0 else pltpu.roll(two, 32 * r + 1, 1)
                    edge_up = jnp.where(lane == 32 * r + 31, start, edge_up)
                    edge_dn = jnp.where(lane == 32 * r, end, edge_dn)
            if not last:
                image(edge, 2, rim, edge_up, edge_dn)


def dynamic_one(place):
    return (place[0] >> 24) + 1


def loop(start, stop, do):
    def step(n, carry):
        do(n)
        return carry

    lax.fori_loop(start, stop, step, 0)


def inner_planes(k):
    return DEPTH + k, DEPTH + NZ - k


def inner_copies(inner, inner_faces, stores, base, faces, faces_base, sems, out):
    def copy(n, there, here):
        src, dst = (here, there) if out else (there, here)
        return pltpu.make_async_copy(src, dst, sems.at[n])

    result = []
    for n, (g, start, stop) in enumerate(
        [(g, z, z + 2) for g in (0, 1) for z in (DEPTH, DEPTH + NZ - 2)]
        + [(0, DEPTH + 2, DEPTH + NZ - 2)]
        + [(group(k), *inner_planes(k)) for k in range(1, STEPS)]
    ):
        there = inner.at[pl.ds(sum(GROUPS[:g]), GROUPS[g]), pl.ds(start - DEPTH, stop - start)]
        result.append(copy(n, there, stores[g].at[:, pl.ds(start - base, stop - start)]))
    start, stop = inner_planes(1)
    result.append(copy(len(result), inner_faces, faces.at[:, pl.ds(start - faces_base, stop - start)]))
    return result


def krylov_inner(swap, place, rhs, cz, cx, cy, dg, *rest):
    above, below, yup, ydn, inner, inner_faces, *stores, faces, load_sems, sems = rest if not swap else rest[:1] + rest
    keep_up, keep_dn = keep_sides(swap, place)
    block = Block(stores, DEPTH, faces, DEPTH + 1, dynamic_one(place))
    loads = []
    for f in range(FIELDS):
        src = rhs.at[f] if f < NRHS else (cz, cx, cy, dg)[f - NRHS]
        for l in range(2):
            g, n = block.where(f, l)
            loads.append(
                pltpu.make_async_copy(
                    src.at[:, :, pl.ds(128 * l, 128)], stores[g].at[n, :, pl.ds(8, NX), :], load_sems.at[2 * f + l]
                )
            )
            loads[-1].start()
    for f in range(FIELDS):
        for z in range(DEPTH, DEPTH + NZ):
            m = (z - DEPTH) // 2
            for l in range(2):
                lanes = pl.ds(128 * l, 128)
                tile = halo_tile(above[f, m, :, lanes], below[f, m, :, lanes], z % 2, keep_up, keep_dn)
                block.put(*block.where(f, l), z, NX // 8, tile)
    for half in range(2):
        lanes = pl.ds(128 * half, 128)
        block.place_y(DEPTH + 4 * half, yup.at[:, lanes], ydn.at[:, lanes])
    for copy in loads:
        copy.wait()
    for f in range(FIELDS):
        for z in range(DEPTH, DEPTH + NZ):
            block.close_ring(f, z)
    copies = inner_copies(inner, inner_faces, stores, DEPTH, faces, DEPTH + 1, sems, True)
    for n in range(5):
        copies[n].start()
    loop(*inner_planes(1), block.coefficients)
    copies[-1].start()
    for k in range(STEPS - 1):
        loop(*inner_planes(k + 1), functools.partial(block.apply, k))
        copies[5 + k].start()
    for copy in copies:
        copy.wait()


NEAR, FAR = 8 * FIELDS, 24


def krylov_outer(
    swap, face_one, face_two, place, odd_z, inner, inner_faces, rim_one, rim_two,
    basis, message,
    *rest,
):
    keep_up, keep_dn = keep_sides(swap, place)
    n_x = 1 if swap else 2
    *stores, faces, accs, rims, plane_sems, loads, saves = rest
    odd = odd_z[0] == 1
    block = Block(stores, 0, faces, 0, dynamic_one(place))
    copies = inner_copies(inner, inner_faces, stores, 0, faces, 0, loads, False)
    def plane_copies(lower, upper):
        planes = []
        start = 0
        for f in range(FIELDS):
            depth = DEPTH if f <= NRHS else DEPTH - 1
            for side, (face, z) in enumerate(((lower, DEPTH - depth), (upper, DEPTH + NZ))):
                for l in range(2):
                    g, n = block.where(f, l)
                    planes.append(
                        pltpu.make_async_copy(
                            face.at[pl.ds(start, depth), :, pl.ds(128 * l, 128)],
                            stores[g].at[n, pl.ds(z, depth), pl.ds(8, NX), :],
                            plane_sems.at[4 * f + 2 * side + l],
                        )
                    )
            start += depth
        return planes

    for copy in copies[:4]:
        copy.start()

    @pl.when(odd)
    def _():
        for copy in plane_copies(face_one, face_two):
            copy.start()

    @pl.when(jnp.logical_not(odd))
    def _():
        for copy in plane_copies(face_two, face_one):
            copy.start()

    one, two = rim_one[...], rim_two[...]
    rims[0] = jnp.where(odd, one, two)
    rims[1] = jnp.where(odd, two, one)
    rimlo, rimhi = rims.at[0], rims.at[1]

    zero = jnp.zeros((8, 128), F32)
    for f in range(FIELDS):
        for rim, first in ((rimlo, 0), (rimhi, DEPTH + NZ)):
            for z in range(first, first + DEPTH):
                far = DEPTH - z if first == 0 else z - first + 1
                for l in range(2):
                    lanes = pl.ds(128 * l, 128)
                    if far <= 2:
                        at, odd = 8 * f, z % 2
                    elif far == 3 and 8 * (f // 2) < FAR:
                        at, odd = NEAR + 8 * (f // 2), f % 2
                    else:
                        block.put(*block.where(f, l), z, NX // 8, zero)
                        continue
                    other = at + (n_x - 1) * (NEAR + FAR)
                    tile = halo_tile(rim[at : at + 8, lanes], rim[other : other + 8, lanes], odd, keep_up, keep_dn)
                    block.put(*block.where(f, l), z, NX // 8, tile)
    rows = pl.ds(n_x * (NEAR + FAR), ROWS)
    for rim, z in ((rimlo, 0), (rimhi, DEPTH + NZ)):
        block.place_y(z, rim.at[rows, pl.ds(0, 128)], rim.at[rows, pl.ds(128, 128)])

    for copy in copies[:4] + plane_copies(face_one, face_two):
        copy.wait()
    for copy in [copies[5], copies[-1], copies[6], copies[7], copies[4]]:
        copy.start()
    for f in range(FIELDS):
        depth = DEPTH if f <= NRHS else DEPTH - 1
        for d in range(depth):
            block.close_ring(f, DEPTH - 1 - d)
            block.close_ring(f, DEPTH + NZ + d)
    loop(1, DEPTH + 1, block.coefficients)
    loop(DEPTH + NZ - 1, EZ - 1, block.coefficients)

    sends = []

    def send_block(k):
        copy = pltpu.make_async_copy(
            stores[group(k)].at[pl.ds(0, 2 * NRHS), pl.ds(DEPTH, NZ), pl.ds(8, NX), :],
            basis.at[pl.ds(k * 2 * NRHS, 2 * NRHS)],
            saves.at[k],
        )
        copy.start()
        sends.append(copy)

    for k in range(STEPS):
        if k == 1:
            copies[-1].wait()
        loop(
            0,
            2 * DEPTH,
            lambda n, k=k: block.apply(k, n + k + 1 + jnp.where(n >= DEPTH, NZ - 2 - 2 * k, 0)),
        )
        if k < STEPS - 1:
            copies[5 + k].wait()
        send_block(k + 1)
    copies[4].wait()
    send_block(0)
    gram_zero(accs)

    def products(z):
        def tile(i, t):
            store = stores[group(i // NRHS)]
            return jnp.concatenate([store[2 * (i % NRHS) + l, z, 8 + 8 * t : 16 + 8 * t, :] for l in range(2)], 1)

        gram_add([jnp.concatenate([tile(i, t) for i in range(COLS)], 0) for t in range(NX // 8)], accs)

    loop(DEPTH, DEPTH + NZ, products)
    gram_message(accs, message)
    for copy in sends:
        copy.wait()


def factor_gram(messages, cells, table):
    rows = row_ids((24, 128))
    lanes = lane_ids((24, 128))
    upper = gram_of(messages) / cells
    square = jnp.concatenate([upper, jnp.zeros((104, 128), F32)], 0).T
    whole = jnp.where(rows <= lanes, upper, square[0:24, :])

    tile_rows = row_ids((8, 128))
    tiles = range(3)

    def split(value):
        return [value[8 * k : 8 * k + 8] for k in tiles]

    def row_of(column, j):
        return jnp.broadcast_to(column[j // 8][j % 8 : j % 8 + 1, :], (8, 128))

    columns = [split(jnp.broadcast_to(whole[:, c : c + 1], (24, 128))) for c in range(COLS)]
    inverse = [[jnp.where(tile_rows + 8 * k == c, 1.0, 0.0) for k in tiles] for c in range(COLS)]
    pivots = [jnp.ones((8, 128), F32) for k in tiles]
    for j in range(COLS):
        pivot = row_of(columns[j], j)
        first = j // 8
        pivots[first] = jnp.where(tile_rows == j % 8, pivot, pivots[first])
        below = {k: columns[j][k] / pivot for k in tiles if k >= first}
        below[first] = jnp.where(tile_rows > j % 8, below[first], 0.0)
        for c in range(COLS):
            change = columns[c] if c > j else inverse[c]
            row = row_of(change, j)
            for k in below:
                change[k] = change[k] - below[k] * row
    scales = [1.0 / jnp.sqrt(p) for p in pivots]
    factor = jnp.zeros((24, 128), F32)
    for c in range(COLS):
        scaled = [inverse[c][k] * scales[k] for k in tiles]
        for i in range(c, COLS):
            table[c, i] = row_of(scaled, i)
        factor = jnp.where(lanes == c, jnp.concatenate(columns[c], 0), factor)
    return jnp.where((rows <= lanes) & (rows < COLS), factor * jnp.concatenate(scales, 0), 0.0)


def apply_rows(table, read, write):
    group = 5
    pieces = NX // 8
    for g in reversed(range(COLS // group)):
        mine = range(group * g, group * g + group)
        sums = {i: None for i in mine}
        for j in range(group * g + group):
            value = [read(j, p) for p in range(pieces)]
            for i in mine:
                if j <= i:
                    weight = table[j, i]
                    terms = [weight * v for v in value]
                    sums[i] = terms if sums[i] is None else [s + t for s, t in zip(sums[i], terms)]
        for i in mine:
            for p in range(pieces):
                write(i, p, sums[i][p])


def plane_copy(src, dst, sems, z):
    return pltpu.make_async_copy(src.at[:, z], dst.at[:, z], sems.at[z])


def first_pass(
    cells, message, basis_hbm, first_hbm, next_message, factor_out, basis, first, table, accs, loads, saves
):
    for z in range(NZ):
        plane_copy(basis_hbm, basis, loads, z).start()
    factor_out[...] = factor_gram(message, cells, table)
    gram_zero(accs)

    def products(z):
        def tile(i, t):
            return jnp.concatenate([first[2 * i + l, z, 8 * t : 8 * t + 8, :] for l in range(2)], 1)

        gram_add([jnp.concatenate([tile(i, t) for i in range(COLS)], 0) for t in range(NX // 8)], accs)

    def apply(z):
        for l in range(2):

            def read(j, p):
                return basis[2 * j + l, z, 8 * p : 8 * p + 8, :]

            def write(i, p, value):
                first[2 * i + l, z, 8 * p : 8 * p + 8, :] = value

            apply_rows(table, read, write)
        plane_copy(first, first_hbm, saves, z).start()

    def both(z):
        plane_copy(basis_hbm, basis, loads, z).wait()
        products(z - 1)
        apply(z)

    plane_copy(basis_hbm, basis, loads, 0).wait()
    apply(0)
    loop(1, NZ, both)
    products(NZ - 1)
    gram_message(accs, next_message)
    for z in range(NZ):
        plane_copy(first, first_hbm, saves, z).wait()


def second_pass(cells, message, factor_one, first_hbm, out_hbm, triangle, first, out, table, loads, saves):
    for z in range(NZ):
        plane_copy(first_hbm, first, loads, z).start()
    left = factor_gram(message, cells, table)[:, 0:24]
    product = lax.dot_general(
        left, factor_one[...], (((1,), (0,)), ((), ())), precision=HIGHEST, preferred_element_type=F32
    )
    triangle[...] = product[0:COLS, 0:COLS]

    def chunk(z, carry):
        plane_copy(first_hbm, first, loads, z).wait()
        for l in range(2):

            def read(j, p):
                return first[2 * j + l, z, 8 * p : 8 * p + 8, :]

            def write(i, p, value):
                out[i, z, 8 * p : 8 * p + 8, 128 * l : 128 * l + 128] = value

            apply_rows(table, read, write)
        plane_copy(out, out_hbm, saves, z).start()
        return carry

    lax.fori_loop(0, NZ, chunk, 0)
    for z in range(NZ):
        plane_copy(out, out_hbm, saves, z).wait()


def shape(*dims):
    return jax.ShapeDtypeStruct(dims, F32)


def move(value, axis, delta):
    count = lax.axis_size(axis)
    pairs = [(i, i + delta) for i in range(count) if 0 <= i + delta < count]
    return lax.ppermute(value, axis, pairs)


def swap_pairs(value, axis, first):
    pairs = [(i, i + 1) for i in range(first, lax.axis_size(axis) - 1, 2)]
    return lax.ppermute(value, axis, pairs + [(j, i) for i, j in pairs])


def exchange(messages):
    return lax.all_to_all(messages, AXES, 0, 0, tiled=True)


def body(rhs, coef_x, coef_y, coef_z, diag_term):
    n_x = lax.axis_size("gx")
    devices = n_x * lax.axis_size("gy") * lax.axis_size("gz")
    cells = float(NZ * NX * NY * devices)
    at_x = lax.axis_index("gx")
    swap = n_x == 2
    fields = (rhs, coef_z, coef_x, coef_y, diag_term)

    place = at_x.astype(jnp.int32).reshape(1)
    odd_z, odd_y = ((lax.axis_index(axis) & 1).astype(jnp.int32).reshape(1) for axis in ("gz", "gy"))
    face_shape = shape(FACE, NX, NY)
    x_shape = shape(FIELDS, NZ // 2, 8, NY)
    z_one, z_two, *xmsgs = pl.pallas_call(
        functools.partial(pack_faces, swap),
        out_shape=(face_shape, face_shape) + (x_shape,) * (1 if swap else 2),
        in_specs=[smem()] * 2 + [hbm()] * 5,
        out_specs=(hbm(), hbm()) + (hbm(),) * (1 if swap else 2),
        scratch_shapes=[
            pltpu.VMEM((1 if swap else 2,) + x_shape.shape, F32),
            pltpu.VMEM((FIELDS, NZ, NX, NY), F32),
            pltpu.SemaphoreType.DMA((FIELDS,)),
            pltpu.SemaphoreType.DMA((2 * FIELDS,)),
            pltpu.SemaphoreType.DMA((1 if swap else 2, FIELDS)),
        ],
        compiler_params=params(LIMIT),
        cost_estimate=cost(2.5),
    )(place, odd_z, *fields)
    face_one, face_two = swap_pairs(z_one, "gz", 0), swap_pairs(z_two, "gz", 1)
    if swap:
        x_parts = (lax.ppermute(xmsgs[0], "gx", [(0, 1), (1, 0)]),)
    else:
        x_parts = (move(xmsgs[0], "gx", -1), move(xmsgs[1], "gx", 1))

    own_shape, halo_shape = shape(NX, NY), shape(ROWS - NX, NY)
    own_one, own_two = pl.pallas_call(
        pack_own_rims,
        out_shape=(own_shape, own_shape),
        in_specs=[smem()] + [vmem()] * 5,
        compiler_params=params(LIMIT),
        cost_estimate=cost(2.5),
    )(odd_y, *fields)
    halo_one, halo_two = pl.pallas_call(
        functools.partial(pack_rims, swap),
        out_shape=(halo_shape, halo_shape),
        in_specs=[smem()] * 2 + [vmem()] * len(x_parts),
        compiler_params=params(16),
        cost_estimate=cost(1),
    )(place, odd_y, *x_parts)
    y_one = swap_pairs(jnp.concatenate([own_one, halo_one], 0), "gy", 0)
    y_two = swap_pairs(jnp.concatenate([own_two, halo_two], 0), "gy", 1)
    yup, ydn = jnp.where(odd_y == 1, y_two, y_one), jnp.where(odd_y == 1, y_one, y_two)

    def rim(half):
        near, far, odd = ((0, 1, 0), (3, 2, 1))[half]
        rows = []
        for part in x_parts:
            rows.append(part[:, near].reshape(NEAR, NY))
            rows.append(part[: FAR // 4, far, 4 * odd : 4 * odd + 4].reshape(FAR, NY))
        lanes = slice(128 * half, 128 * half + 128)
        return jnp.concatenate(rows + [jnp.concatenate([yup[:, lanes], ydn[:, lanes]], 1)], 0)

    low, high = rim(0), rim(1)
    rim_one = swap_pairs(jnp.where(odd_z == 1, low, high), "gz", 0)
    rim_two = swap_pairs(jnp.where(odd_z == 1, high, low), "gz", 1)

    inner_shape = shape(sum(GROUPS[:-1]), NZ, EROWS, 128)
    inner_faces_shape = shape(7, NZ - 2, LT, ROWS, 128)
    inner, inner_faces = pl.pallas_call(
        functools.partial(krylov_inner, swap),
        out_shape=(inner_shape, inner_faces_shape),
        in_specs=[smem()] + [hbm()] * 5 + [vmem()] * (len(x_parts) + 2),
        out_specs=(hbm(), hbm()),
        scratch_shapes=[
            *[pltpu.VMEM((tiles, NZ, EROWS, 128), F32) for tiles in GROUPS[:-1]],
            pltpu.VMEM(inner_faces_shape.shape, F32),
            pltpu.SemaphoreType.DMA((2 * FIELDS,)),
            pltpu.SemaphoreType.DMA((9,)),
        ],
        compiler_params=params(LIMIT),
        cost_estimate=cost(7),
    )(place, *fields, *x_parts, yup, ydn)

    block = shape(2 * COLS, NZ, NX, 128)
    basis, message = pl.pallas_call(
        functools.partial(krylov_outer, swap),
        out_shape=(block, shape(devices, 2, 128)),
        in_specs=[hbm(), hbm(), smem(), smem(), hbm(), hbm(), vmem(), vmem()],
        out_specs=(hbm(), vmem()),
        scratch_shapes=[
            *[pltpu.VMEM((tiles, EZ, EROWS, 128), F32) for tiles in GROUPS],
            pltpu.VMEM((7, EZ, LT, ROWS, 128), F32),
            pltpu.VMEM((2, STACK, STACK), F32),
            pltpu.VMEM((2,) + rim_one.shape, F32),
            pltpu.SemaphoreType.DMA((4 * FIELDS,)),
            pltpu.SemaphoreType.DMA((9,)),
            pltpu.SemaphoreType.DMA((STEPS + 1,)),
        ],
        compiler_params=params(ROOMY),
        cost_estimate=cost(15),
    )(face_one, face_two, place, odd_z, inner, inner_faces, rim_one, rim_two)

    message = exchange(message)
    first, message, factor_one = pl.pallas_call(
        functools.partial(first_pass, cells),
        out_shape=(block, shape(devices, 2, 128), shape(24, 128)),
        in_specs=[vmem(), hbm()],
        out_specs=(hbm(), vmem(), vmem()),
        scratch_shapes=[
            pltpu.VMEM(block.shape, F32),
            pltpu.VMEM(block.shape, F32),
            pltpu.VMEM((COLS, COLS, 8, 128), F32),
            pltpu.VMEM((2, STACK, STACK), F32),
            pltpu.SemaphoreType.DMA((NZ,)),
            pltpu.SemaphoreType.DMA((NZ,)),
        ],
        compiler_params=params(ROOMY),
    )(message, basis)

    message = exchange(message)
    return pl.pallas_call(
        functools.partial(second_pass, cells),
        out_shape=(shape(COLS, NZ, NX, NY), shape(COLS, COLS)),
        in_specs=[vmem(), vmem(), hbm()],
        out_specs=(hbm(), vmem()),
        scratch_shapes=[
            pltpu.VMEM(block.shape, F32),
            pltpu.VMEM((COLS, NZ, NX, NY), F32),
            pltpu.VMEM((COLS, COLS, 8, 128), F32),
            pltpu.SemaphoreType.DMA((NZ,)),
            pltpu.SemaphoreType.DMA((NZ,)),
        ],
        compiler_params=params(ROOMY),
    )(message, factor_one, first)


def solution(mesh):
    return jax.shard_map(
        body,
        mesh=mesh,
        in_specs=(
            P(None, "gz", "gx", "gy"),
            P("gz", "gx", "gy"),
            P("gz", "gx", "gy"),
            P("gz", "gx", "gy"),
            P("gz", "gx", "gy"),
        ),
        out_specs=(P(None, "gz", "gx", "gy"), P()),
        check_vma=False,
    )
```

```python
import functools

import jax
import jax.numpy as jnp
from jax import lax
from jax.experimental import pallas as pl
from jax.experimental.pallas import tpu as pltpu
from jax.sharding import PartitionSpec as P

NRHS = 4
STEPS = 4
COLS = NRHS * (STEPS + 1)
SHIFTS = (3.0, 11.0, 7.0, 1.5)
SCALE = 1.0 / 6.0
FIELDS = NRHS + 4
AXES = ("gx", "gy", "gz")
HIGHEST = lax.Precision.HIGHEST

DEPTH = 4
NZ, NX, NY = 8, 32, 256
EZ = NZ + 2 * DEPTH
ROWS = NX + 8
EROWS = ROWS + 16
LT = 3
FACE = NRHS * 4 + 3 * 4 + 1
F32 = jnp.float32
LIMIT, ROOMY = 63, 52


def params(mb):
    return pltpu.CompilerParams(vmem_limit_bytes=mb << 20)


def cost(us):
    return pl.CostEstimate(flops=0, bytes_accessed=int(us * 3.6e6), transcendentals=0)


def vmem():
    return pl.BlockSpec(memory_space=pltpu.VMEM)


def smem():
    return pl.BlockSpec(memory_space=pltpu.SMEM)


def hbm():
    return pl.BlockSpec(memory_space=pl.ANY)


def row_ids(shape):
    return lax.broadcasted_iota(jnp.int32, shape, 0)


def lane_ids(shape):
    return lax.broadcasted_iota(jnp.int32, shape, 1)


def field_of(rhs, cz, cx, cy, dg, f, z):
    return rhs.at[f, z] if f < NRHS else (cz, cx, cy, dg)[f - NRHS].at[z]


def pack_faces(swap, place, odd_z, rhs, cz, cx, cy, dg, z_one, z_two, *rest):
    xmsgs, (xrows, whole, loads, saves, xsaves) = rest[:-5], rest[-5:]
    copies = []
    for f in range(FIELDS):
        src = rhs.at[f] if f < NRHS else (cz, cx, cy, dg)[f - NRHS]
        copies.append(pltpu.make_async_copy(src, whole.at[f], loads.at[f]))
        copies[-1].start()
    low = row_ids((8, NY)) < 4
    up = place[0] == 0
    planes = []
    at = 0
    for f in range(FIELDS):
        copies[f].wait()
        depth = DEPTH if f <= NRHS else DEPTH - 1
        for side, out in ((0, z_one), (1, z_two)):
            start = jnp.where(odd_z[0] == side, NZ - depth, 0)
            planes.append(
                pltpu.make_async_copy(
                    whole.at[f, pl.ds(start, depth)], out.at[pl.ds(at, depth)], saves.at[2 * f + side]
                )
            )
            planes[-1].start()
        at += depth
        for m in range(NZ // 2):
            a, b = whole.at[f, 2 * m], whole.at[f, 2 * m + 1]
            first = jnp.where(low, a[0:8], pltpu.roll(b[0:8], 4, 0))
            last = jnp.where(low, pltpu.roll(a[NX - 8 : NX], 4, 0), b[NX - 8 : NX])
            if swap:
                xrows[0, f, m] = jnp.where(up, last, first)
            else:
                xrows[0, f, m] = first
                xrows[1, f, m] = last
        for n, xmsg in enumerate(xmsgs):
            planes.append(pltpu.make_async_copy(xrows.at[n, f], xmsg.at[f], xsaves.at[n, f]))
            planes[-1].start()
    for copy in planes:
        copy.wait()


def halo_tile(above, below, odd, keep_up, keep_dn):
    low = row_ids(above.shape) < 4
    if odd:
        up, dn = pltpu.roll(above, 4, 0), below
    else:
        up, dn = above, pltpu.roll(below, 4, 0)
    return jnp.where(low, up * keep_up, dn * keep_dn)


def keep_sides(swap, place):
    if not swap:
        return 1.0, 1.0
    first = place[0] == 0
    return jnp.where(first, 1.0, 0.0), jnp.where(first, 0.0, 1.0)


def pack_lanes(tile_of, side):
    lane = lane_ids((8, 128))
    source = 124 * side
    acc = jnp.zeros((8, 128), F32)
    for zz in range(4):
        for f in range(FIELDS):
            tile = tile_of(f, zz)
            spot = (zz * FIELDS + f) * 4
            shift = (spot - source) % 128
            if shift:
                tile = pltpu.roll(tile, shift, 1)
            acc = jnp.where((lane >= spot) & (lane < spot + 4), tile, acc)
    return acc


def pack_own_rims(odd_y, rhs, cz, cx, cy, dg, one, two):
    odd = odd_y[0] == 1
    for t in range(NX // 8):
        for half in range(2):
            lo, hi = (
                pack_lanes(
                    lambda f, zz: field_of(rhs, cz, cx, cy, dg, f, 4 * half + zz)[
                        8 * t : 8 * t + 8, 128 * side : 128 * side + 128
                    ],
                    side,
                )
                for side in range(2)
            )
            one[8 * t : 8 * t + 8, 128 * half : 128 * half + 128] = jnp.where(odd, lo, hi)
            two[8 * t : 8 * t + 8, 128 * half : 128 * half + 128] = jnp.where(odd, hi, lo)


def pack_rims(swap, place, odd_y, *refs):
    above, below, one, two = refs if not swap else (refs[0],) + refs
    keep_up, keep_dn = keep_sides(swap, place)
    odd = odd_y[0] == 1
    for half in range(2):
        halves = []
        for side in range(2):
            lanes = slice(128 * side, 128 * side + 128)
            halves.append(
                pack_lanes(
                    lambda f, zz: halo_tile(
                        above[f, 2 * half + zz // 2, :, lanes],
                        below[f, 2 * half + zz // 2, :, lanes],
                        zz % 2,
                        keep_up,
                        keep_dn,
                    ),
                    side,
                )
            )
        lo, hi = halves
        one[:, 128 * half : 128 * half + 128] = jnp.where(odd, lo, hi)
        two[:, 128 * half : 128 * half + 128] = jnp.where(odd, hi, lo)


STACK = 8 * COLS


def gram_zero(accs):
    accs[...] = jnp.zeros_like(accs)


def gram_add(stacks, accs):
    left, right = [], []
    cross_left, cross_right = [], []
    for stack in stacks:
        high = stack.astype(jnp.bfloat16)
        rest = stack - high.astype(F32)
        mid = rest.astype(jnp.bfloat16)
        low = (rest - mid.astype(F32)).astype(jnp.bfloat16)
        left += [high, mid]
        cross_left += [high, high]
        cross_right += [mid, low]
    contract = (((1,), (1,)), ((), ()))

    def product(a, b):
        return lax.dot_general(jnp.concatenate(a, 1), jnp.concatenate(b, 1), contract, preferred_element_type=F32)

    accs[0] += product(left, left)
    accs[1] += product(cross_left, cross_right)


def gram_message(accs, out):
    same = (row_ids((STACK, STACK)) & 7) == (lane_ids((STACK, STACK)) & 7)
    pick = jnp.where((row_ids((STACK, 128)) >> 3) == lane_ids((STACK, 128)), 1.0, 0.0)

    def traces(product):
        picked = jnp.where(same, product, 0.0)
        rows = [jnp.sum(picked[8 * i : 8 * i + 8], axis=0, keepdims=True) for i in range(COLS)]
        rows = jnp.concatenate(rows + [jnp.zeros((128 - COLS, STACK), F32)], 0)
        return lax.dot_general(
            rows, pick, (((1,), (0,)), ((), ())), precision=HIGHEST, preferred_element_type=F32
        )

    cross = traces(accs[1])
    gram = traces(accs[0]) + cross + cross.T
    tops = [gram[8 * k : 8 * k + 8] for k in range(3)]
    rows, lanes = row_ids((8, 128)), lane_ids((8, 128))
    tile = jnp.where(lanes < COLS, tops[0], pltpu.roll(tops[1], 12, 1))
    corner = pltpu.roll(pltpu.roll(tops[2], 128 - 16, 1), 4, 0)
    tile = jnp.where((rows >= 4) & (lanes < 4), corner, tile)
    packed = tile
    for q in range(1, 4):
        turned = pltpu.roll(pltpu.roll(tile, 32 * q, 1), 8 - 2 * q, 0)
        packed = jnp.where((lanes >> 5) == q, turned, packed)
    packed = packed[0:2]
    for n in range(out.shape[0]):
        out[n] = packed


def gram_of(messages):
    parts = [messages[n] for n in range(messages.shape[0])]
    while len(parts) > 1:
        parts = [sum(parts[n : n + 2][1:], parts[n]) for n in range(0, len(parts), 2)]
    total = jnp.concatenate(parts * 4, 0)
    rows, lanes = row_ids((8, 128)), lane_ids((8, 128))
    tile = total
    for q in range(1, 4):
        tile = jnp.where((rows >> 1) == q, pltpu.roll(total, 128 - 32 * q, 1), tile)
    corner = pltpu.roll(pltpu.roll(tile, 4, 0), 16, 1)
    tops = [
        jnp.where((lanes < COLS) & (lanes >= rows), tile, 0.0),
        jnp.where((lanes < COLS) & (lanes >= rows + 8), pltpu.roll(tile, 128 - 12, 1), 0.0),
        jnp.where((lanes < COLS) & (lanes >= rows + 16), corner, 0.0),
    ]
    return jnp.concatenate(tops, 0)


GROUPS = (9, 12, 9, 9, 9, 9)


def group(k):
    return k + 1 if k else 0


class Block:
    def __init__(self, stores, base, faces, faces_base, one):
        self.one = one
        self.stores, self.base, self.faces, self.faces_base = stores, base, faces, faces_base
        self.lane = lane_ids((8, 128))

    def where(self, f, l):
        return (0, 2 * f + l) if f < NRHS else (1, 3 * (f - NRHS) + l)

    def put(self, g, n, z, t, value):
        store, z = self.stores[g], z - self.base
        store[n, z, 8 + 8 * t : 16 + 8 * t, :] = value
        if t == 0:
            store[n, z, 8 + ROWS : 16 + ROWS, :] = value
        if t == ROWS // 8 - 1:
            store[n, z, 0:8, :] = value

    def get(self, g, n, z, t, off=0):
        row = 8 + 8 * t + (off * self.one if off else 0)
        return self.stores[g][n, z - self.base, pl.ds(row, 8), :]

    def close_ring(self, f, z):
        z = z - self.base
        for l in range(2):
            g, n = self.where(f, l)
            self.stores[g][n, z, 8 + ROWS : 16 + ROWS, :] = self.stores[g][n, z, 8:16, :]

    def place_y(self, z, up, dn):
        part, place = self.lane & 31, self.lane >> 5
        upper, lower = part < 4, part >= 28
        for t in range(ROWS // 8):
            u_all, d_all = up[8 * t : 8 * t + 8, :], dn[8 * t : 8 * t + 8, :]

            def turned(value, shift):
                return pltpu.roll(value, shift % 128, 1) if shift % 128 else value

            def copies(f):
                result = []
                for m in range(4):
                    u, d = turned(u_all, 32 * m - 4 * f), turned(d_all, 32 * m + 28 - 4 * f)
                    result.append(jnp.where(upper, u, jnp.where(lower, d, 0.0)))
                return result

            def pick(tiles):
                value = tiles[0]
                for r in range(1, 4):
                    value = jnp.where(place == r, tiles[r], value)
                return value

            fields = [copies(r) for r in range(NRHS)]
            for zz in range(4):
                self.put(0, 2 * NRHS, z + zz, t, pick([fields[r][(r - zz) % 4] for r in range(4)]))
            for c in range(4):
                mine = copies(NRHS + c)
                for zz in range(4):
                    self.put(1, 3 * c + 2, z + zz, t, pick([mine[(r - zz) % 4] for r in range(4)]))

    def coefficients(self, z):
        lane = self.lane
        for t in range(ROWS // 8):

            def tiles(c, z, off=0):
                return [self.get(1, 3 * c + l, z, t, off) for l in range(LT)]

            center_z, center_x, center_y, diag = (tiles(c, z) for c in range(4))
            up = [pltpu.roll(v, 127, 1) for v in center_y]
            dn = [pltpu.roll(v, 1, 1) for v in center_y]
            first = jnp.broadcast_to(center_y[0][:, 0:1], (8, 128))
            last = jnp.broadcast_to(center_y[1][:, 127:128], (8, 128))
            sides = [
                (center_z, tiles(0, z + 1)),
                (center_z, tiles(0, z - 1)),
                (center_x, tiles(1, z, 1)),
                (center_x, tiles(1, z, -1)),
                (
                    center_y,
                    [
                        jnp.where(lane == 127, up[1], up[0]),
                        jnp.where(lane == 127, up[2], up[1]),
                        jnp.where((lane & 31) == 31, first, up[2]),
                    ],
                ),
                (
                    center_y,
                    [
                        jnp.where(lane == 0, dn[2], dn[0]),
                        jnp.where(lane == 0, dn[0], dn[1]),
                        jnp.where((lane & 31) == 0, last, dn[2]),
                    ],
                ),
            ]
            at = z - self.faces_base
            for l in range(LT):
                inside = diag[l] > 0.0
                total = diag[l] * SCALE
                for k, (mid, side) in enumerate(sides):
                    face = (mid[l] + side[l]) * (0.5 * SCALE)
                    total = total + face
                    self.faces[k, at, l, 8 * t : 8 * t + 8, :] = jnp.where(inside, face, 0.0)
                self.faces[6, at, l, 8 * t : 8 * t + 8, :] = jnp.where(inside, total, 0.0)

    def apply(self, k, z):
        last = k == STEPS - 1
        at, lane, edge = z - self.faces_base, self.lane, 2 * NRHS
        src, dst = group(k), group(k + 1)
        for t in range(NX // 8 if last else ROWS // 8):
            face = [
                [self.faces[c, at, l, 8 * t : 8 * t + 8, :] for l in range(2 if last else LT)] for c in range(7)
            ]
            diag = [d - SHIFTS[k] * SCALE for d in face[6]]

            def image(n, l, mid, up, dn):
                sides = (
                    self.get(src, n, z + 1, t),
                    self.get(src, n, z - 1, t),
                    self.get(src, n, z, t, 1),
                    self.get(src, n, z, t, -1),
                    up,
                    dn,
                )
                value = diag[l] * mid
                for c, side in enumerate(sides):
                    value = value - face[c][l] * side
                self.put(dst, n, z, t, value)

            rim = self.get(src, edge, z, t)
            rim_up, rim_dn = pltpu.roll(rim, 127, 1), pltpu.roll(rim, 1, 1)
            edge_up, edge_dn = rim_up, rim_dn
            for r in range(NRHS):
                one, two = self.get(src, 2 * r, z, t), self.get(src, 2 * r + 1, z, t)
                one_up, two_up = pltpu.roll(one, 127, 1), pltpu.roll(two, 127, 1)
                one_dn, two_dn = pltpu.roll(one, 1, 1), pltpu.roll(two, 1, 1)
                above = rim_up if r == 0 else pltpu.roll(rim, 127 - 32 * r, 1)
                below = rim_dn if r == NRHS - 1 else pltpu.roll(rim, 97 - 32 * r, 1)
                image(2 * r, 0, one, jnp.where(lane == 127, two_up, one_up), jnp.where(lane == 0, below, one_dn))
                image(2 * r + 1, 1, two, jnp.where(lane == 127, above, two_up), jnp.where(lane == 0, one_dn, two_dn))
                if not last:
                    start = one_up if r == NRHS - 1 else pltpu.roll(one, 32 * r + 31, 1)
                    end = two_dn if r == 0 else pltpu.roll(two, 32 * r + 1, 1)
                    edge_up = jnp.where(lane == 32 * r + 31, start, edge_up)
                    edge_dn = jnp.where(lane == 32 * r, end, edge_dn)
            if not last:
                image(edge, 2, rim, edge_up, edge_dn)


def dynamic_one(place):
    return (place[0] >> 24) + 1


def loop(start, stop, do):
    def step(n, carry):
        do(n)
        return carry

    lax.fori_loop(start, stop, step, 0)


def inner_planes(k):
    return DEPTH + k, DEPTH + NZ - k


def inner_copies(inner, inner_faces, stores, base, faces, faces_base, sems, out):
    def copy(n, there, here):
        src, dst = (here, there) if out else (there, here)
        return pltpu.make_async_copy(src, dst, sems.at[n])

    result = []
    for n, (g, start, stop) in enumerate(
        [(g, z, z + 2) for g in (0, 1) for z in (DEPTH, DEPTH + NZ - 2)]
        + [(0, DEPTH + 2, DEPTH + NZ - 2)]
        + [(group(k), *inner_planes(k)) for k in range(1, STEPS)]
    ):
        there = inner.at[pl.ds(sum(GROUPS[:g]), GROUPS[g]), pl.ds(start - DEPTH, stop - start)]
        result.append(copy(n, there, stores[g].at[:, pl.ds(start - base, stop - start)]))
    start, stop = inner_planes(1)
    result.append(copy(len(result), inner_faces, faces.at[:, pl.ds(start - faces_base, stop - start)]))
    return result


def krylov_inner(swap, place, rhs, cz, cx, cy, dg, *rest):
    above, below, yup, ydn, inner, inner_faces, *stores, faces, load_sems, sems = rest if not swap else rest[:1] + rest
    keep_up, keep_dn = keep_sides(swap, place)
    block = Block(stores, DEPTH, faces, DEPTH + 1, dynamic_one(place))
    loads = []
    for f in range(FIELDS):
        src = rhs.at[f] if f < NRHS else (cz, cx, cy, dg)[f - NRHS]
        for l in range(2):
            g, n = block.where(f, l)
            loads.append(
                pltpu.make_async_copy(
                    src.at[:, :, pl.ds(128 * l, 128)], stores[g].at[n, :, pl.ds(8, NX), :], load_sems.at[2 * f + l]
                )
            )
            loads[-1].start()
    for f in range(FIELDS):
        for z in range(DEPTH, DEPTH + NZ):
            m = (z - DEPTH) // 2
            for l in range(2):
                lanes = pl.ds(128 * l, 128)
                tile = halo_tile(above[f, m, :, lanes], below[f, m, :, lanes], z % 2, keep_up, keep_dn)
                block.put(*block.where(f, l), z, NX // 8, tile)
    for half in range(2):
        lanes = pl.ds(128 * half, 128)
        block.place_y(DEPTH + 4 * half, yup.at[:, lanes], ydn.at[:, lanes])
    for copy in loads:
        copy.wait()
    for f in range(FIELDS):
        for z in range(DEPTH, DEPTH + NZ):
            block.close_ring(f, z)
    copies = inner_copies(inner, inner_faces, stores, DEPTH, faces, DEPTH + 1, sems, True)
    for n in range(5):
        copies[n].start()
    loop(*inner_planes(1), block.coefficients)
    copies[-1].start()
    for k in range(STEPS - 1):
        loop(*inner_planes(k + 1), functools.partial(block.apply, k))
        copies[5 + k].start()
    for copy in copies:
        copy.wait()


NEAR, FAR = 8 * FIELDS, 24


def krylov_outer(
    swap, face_one, face_two, place, odd_z, inner, inner_faces, rim_one, rim_two,
    basis, message,
    *rest,
):
    keep_up, keep_dn = keep_sides(swap, place)
    n_x = 1 if swap else 2
    *stores, faces, accs, rims, plane_sems, loads, saves = rest
    odd = odd_z[0] == 1
    block = Block(stores, 0, faces, 0, dynamic_one(place))
    copies = inner_copies(inner, inner_faces, stores, 0, faces, 0, loads, False)
    def plane_copies(lower, upper):
        planes = []
        start = 0
        for f in range(FIELDS):
            depth = DEPTH if f <= NRHS else DEPTH - 1
            for side, (face, z) in enumerate(((lower, DEPTH - depth), (upper, DEPTH + NZ))):
                for l in range(2):
                    g, n = block.where(f, l)
                    planes.append(
                        pltpu.make_async_copy(
                            face.at[pl.ds(start, depth), :, pl.ds(128 * l, 128)],
                            stores[g].at[n, pl.ds(z, depth), pl.ds(8, NX), :],
                            plane_sems.at[4 * f + 2 * side + l],
                        )
                    )
            start += depth
        return planes

    for copy in copies[:4]:
        copy.start()

    @pl.when(odd)
    def _():
        for copy in plane_copies(face_one, face_two):
            copy.start()

    @pl.when(jnp.logical_not(odd))
    def _():
        for copy in plane_copies(face_two, face_one):
            copy.start()

    one, two = rim_one[...], rim_two[...]
    rims[0] = jnp.where(odd, one, two)
    rims[1] = jnp.where(odd, two, one)
    rimlo, rimhi = rims.at[0], rims.at[1]

    zero = jnp.zeros((8, 128), F32)
    for f in range(FIELDS):
        for rim, first in ((rimlo, 0), (rimhi, DEPTH + NZ)):
            for z in range(first, first + DEPTH):
                far = DEPTH - z if first == 0 else z - first + 1
                for l in range(2):
                    lanes = pl.ds(128 * l, 128)
                    if far <= 2:
                        at, odd = 8 * f, z % 2
                    elif far == 3 and 8 * (f // 2) < FAR:
                        at, odd = NEAR + 8 * (f // 2), f % 2
                    else:
                        block.put(*block.where(f, l), z, NX // 8, zero)
                        continue
                    other = at + (n_x - 1) * (NEAR + FAR)
                    tile = halo_tile(rim[at : at + 8, lanes], rim[other : other + 8, lanes], odd, keep_up, keep_dn)
                    block.put(*block.where(f, l), z, NX // 8, tile)
    rows = pl.ds(n_x * (NEAR + FAR), ROWS)
    for rim, z in ((rimlo, 0), (rimhi, DEPTH + NZ)):
        block.place_y(z, rim.at[rows, pl.ds(0, 128)], rim.at[rows, pl.ds(128, 128)])

    for copy in copies[:4] + plane_copies(face_one, face_two):
        copy.wait()
    for copy in [copies[5], copies[-1], copies[6], copies[7], copies[4]]:
        copy.start()
    for f in range(FIELDS):
        depth = DEPTH if f <= NRHS else DEPTH - 1
        for d in range(depth):
            block.close_ring(f, DEPTH - 1 - d)
            block.close_ring(f, DEPTH + NZ + d)
    loop(1, DEPTH + 1, block.coefficients)
    loop(DEPTH + NZ - 1, EZ - 1, block.coefficients)

    sends = []

    def send_block(k):
        copy = pltpu.make_async_copy(
            stores[group(k)].at[pl.ds(0, 2 * NRHS), pl.ds(DEPTH, NZ), pl.ds(8, NX), :],
            basis.at[pl.ds(k * 2 * NRHS, 2 * NRHS)],
            saves.at[k],
        )
        copy.start()
        sends.append(copy)

    for k in range(STEPS):
        if k == 1:
            copies[-1].wait()
        loop(
            0,
            2 * DEPTH,
            lambda n, k=k: block.apply(k, n + k + 1 + jnp.where(n >= DEPTH, NZ - 2 - 2 * k, 0)),
        )
        if k < STEPS - 1:
            copies[5 + k].wait()
        send_block(k + 1)
    copies[4].wait()
    send_block(0)
    gram_zero(accs)

    def products(z):
        def tile(i, t):
            store = stores[group(i // NRHS)]
            return jnp.concatenate([store[2 * (i % NRHS) + l, z, 8 + 8 * t : 16 + 8 * t, :] for l in range(2)], 1)

        gram_add([jnp.concatenate([tile(i, t) for i in range(COLS)], 0) for t in range(NX // 8)], accs)

    loop(DEPTH, DEPTH + NZ, products)
    gram_message(accs, message)
    for copy in sends:
        copy.wait()


def factor_gram(messages, cells, table):
    rows = row_ids((24, 128))
    lanes = lane_ids((24, 128))
    upper = gram_of(messages) / cells
    square = jnp.concatenate([upper, jnp.zeros((104, 128), F32)], 0).T
    whole = jnp.where(rows <= lanes, upper, square[0:24, :])

    tile_rows = row_ids((8, 128))
    tiles = range(3)

    def split(value):
        return [value[8 * k : 8 * k + 8] for k in tiles]

    def row_of(column, j):
        return jnp.broadcast_to(column[j // 8][j % 8 : j % 8 + 1, :], (8, 128))

    columns = [split(jnp.broadcast_to(whole[:, c : c + 1], (24, 128))) for c in range(COLS)]
    inverse = [[jnp.where(tile_rows + 8 * k == c, 1.0, 0.0) for k in tiles] for c in range(COLS)]
    pivots = [jnp.ones((8, 128), F32) for k in tiles]
    for j in range(COLS):
        pivot = row_of(columns[j], j)
        first = j // 8
        pivots[first] = jnp.where(tile_rows == j % 8, pivot, pivots[first])
        below = {k: columns[j][k] / pivot for k in tiles if k >= first}
        below[first] = jnp.where(tile_rows > j % 8, below[first], 0.0)
        for c in range(COLS):
            change = columns[c] if c > j else inverse[c]
            row = row_of(change, j)
            for k in below:
                change[k] = change[k] - below[k] * row
    scales = [1.0 / jnp.sqrt(p) for p in pivots]
    factor = jnp.zeros((24, 128), F32)
    for c in range(COLS):
        table[c] = jnp.concatenate([inverse[c][k] * scales[k] for k in tiles], 0)
        factor = jnp.where(lanes == c, jnp.concatenate(columns[c], 0), factor)
    return jnp.where((rows <= lanes) & (rows < COLS), factor * jnp.concatenate(scales, 0), 0.0)


def apply_rows(table, read, write):
    group = 5
    pieces = NX // 4
    for g in reversed(range(COLS // group)):
        mine = range(group * g, group * g + group)
        sums = {i: None for i in mine}
        for j in range(group * g + group):
            value = [read(j, p) for p in range(pieces)]
            for i in mine:
                if j <= i:
                    weight = jnp.broadcast_to(table[j, i : i + 1, :], (8, 128))
                    terms = [weight * v for v in value]
                    sums[i] = terms if sums[i] is None else [s + t for s, t in zip(sums[i], terms)]
        for i in mine:
            for p in range(pieces):
                write(i, p, sums[i][p])


def plane_copy(src, dst, sems, z):
    return pltpu.make_async_copy(src.at[:, z], dst.at[:, z], sems.at[z])


def first_pass(
    cells, message, basis_hbm, first_hbm, next_message, factor_out, basis, first, table, accs, loads, saves
):
    for z in range(NZ):
        plane_copy(basis_hbm, basis, loads, z).start()
    factor_out[...] = factor_gram(message, cells, table)
    gram_zero(accs)

    def products(z):
        def tile(i, t):
            return jnp.concatenate([first[2 * i + l, z, 8 * t : 8 * t + 8, :] for l in range(2)], 1)

        gram_add([jnp.concatenate([tile(i, t) for i in range(COLS)], 0) for t in range(NX // 8)], accs)

    def apply(z):
        def read(j, n):
            l, p = n % 2, n // 2
            return basis[2 * j + l, z, 8 * p : 8 * p + 8, :]

        def write(i, n, value):
            l, p = n % 2, n // 2
            first[2 * i + l, z, 8 * p : 8 * p + 8, :] = value

        apply_rows(table, read, write)
        plane_copy(first, first_hbm, saves, z).start()

    def both(z):
        plane_copy(basis_hbm, basis, loads, z).wait()
        products(z - 1)
        apply(z)

    plane_copy(basis_hbm, basis, loads, 0).wait()
    apply(0)
    loop(1, NZ, both)
    products(NZ - 1)
    gram_message(accs, next_message)
    for z in range(NZ):
        plane_copy(first, first_hbm, saves, z).wait()


def second_pass(cells, message, factor_one, first_hbm, out_hbm, triangle, first, out, table, loads, saves):
    for z in range(NZ):
        plane_copy(first_hbm, first, loads, z).start()
    left = factor_gram(message, cells, table)[:, 0:24]
    product = lax.dot_general(
        left, factor_one[...], (((1,), (0,)), ((), ())), precision=HIGHEST, preferred_element_type=F32
    )
    triangle[...] = product[0:COLS, 0:COLS]

    def chunk(z, carry):
        plane_copy(first_hbm, first, loads, z).wait()

        def read(j, n):
            l, p = n % 2, n // 2
            return first[2 * j + l, z, 8 * p : 8 * p + 8, :]

        def write(i, n, value):
            l, p = n % 2, n // 2
            out[i, z, 8 * p : 8 * p + 8, 128 * l : 128 * l + 128] = value

        apply_rows(table, read, write)
        plane_copy(out, out_hbm, saves, z).start()
        return carry

    lax.fori_loop(0, NZ, chunk, 0)
    for z in range(NZ):
        plane_copy(out, out_hbm, saves, z).wait()


def shape(*dims):
    return jax.ShapeDtypeStruct(dims, F32)


def move(value, axis, delta):
    count = lax.axis_size(axis)
    pairs = [(i, i + delta) for i in range(count) if 0 <= i + delta < count]
    return lax.ppermute(value, axis, pairs)


def swap_pairs(value, axis, first):
    pairs = [(i, i + 1) for i in range(first, lax.axis_size(axis) - 1, 2)]
    return lax.ppermute(value, axis, pairs + [(j, i) for i, j in pairs])


def exchange(messages):
    return lax.all_to_all(messages, AXES, 0, 0, tiled=True)


def body(rhs, coef_x, coef_y, coef_z, diag_term):
    n_x = lax.axis_size("gx")
    devices = n_x * lax.axis_size("gy") * lax.axis_size("gz")
    cells = float(NZ * NX * NY * devices)
    at_x = lax.axis_index("gx")
    swap = n_x == 2
    fields = (rhs, coef_z, coef_x, coef_y, diag_term)

    place = at_x.astype(jnp.int32).reshape(1)
    odd_z, odd_y = ((lax.axis_index(axis) & 1).astype(jnp.int32).reshape(1) for axis in ("gz", "gy"))
    face_shape = shape(FACE, NX, NY)
    x_shape = shape(FIELDS, NZ // 2, 8, NY)
    z_one, z_two, *xmsgs = pl.pallas_call(
        functools.partial(pack_faces, swap),
        out_shape=(face_shape, face_shape) + (x_shape,) * (1 if swap else 2),
        in_specs=[smem()] * 2 + [hbm()] * 5,
        out_specs=(hbm(), hbm()) + (hbm(),) * (1 if swap else 2),
        scratch_shapes=[
            pltpu.VMEM((1 if swap else 2,) + x_shape.shape, F32),
            pltpu.VMEM((FIELDS, NZ, NX, NY), F32),
            pltpu.SemaphoreType.DMA((FIELDS,)),
            pltpu.SemaphoreType.DMA((2 * FIELDS,)),
            pltpu.SemaphoreType.DMA((1 if swap else 2, FIELDS)),
        ],
        compiler_params=params(LIMIT),
        cost_estimate=cost(2.5),
    )(place, odd_z, *fields)
    face_one, face_two = swap_pairs(z_one, "gz", 0), swap_pairs(z_two, "gz", 1)
    if swap:
        x_parts = (lax.ppermute(xmsgs[0], "gx", [(0, 1), (1, 0)]),)
    else:
        x_parts = (move(xmsgs[0], "gx", -1), move(xmsgs[1], "gx", 1))

    own_shape, halo_shape = shape(NX, NY), shape(ROWS - NX, NY)
    own_one, own_two = pl.pallas_call(
        pack_own_rims,
        out_shape=(own_shape, own_shape),
        in_specs=[smem()] + [vmem()] * 5,
        compiler_params=params(LIMIT),
        cost_estimate=cost(2.5),
    )(odd_y, *fields)
    halo_one, halo_two = pl.pallas_call(
        functools.partial(pack_rims, swap),
        out_shape=(halo_shape, halo_shape),
        in_specs=[smem()] * 2 + [vmem()] * len(x_parts),
        compiler_params=params(16),
        cost_estimate=cost(1),
    )(place, odd_y, *x_parts)
    y_one = swap_pairs(jnp.concatenate([own_one, halo_one], 0), "gy", 0)
    y_two = swap_pairs(jnp.concatenate([own_two, halo_two], 0), "gy", 1)
    yup, ydn = jnp.where(odd_y == 1, y_two, y_one), jnp.where(odd_y == 1, y_one, y_two)

    def rim(half):
        near, far, odd = ((0, 1, 0), (3, 2, 1))[half]
        rows = []
        for part in x_parts:
            rows.append(part[:, near].reshape(NEAR, NY))
            rows.append(part[: FAR // 4, far, 4 * odd : 4 * odd + 4].reshape(FAR, NY))
        lanes = slice(128 * half, 128 * half + 128)
        return jnp.concatenate(rows + [jnp.concatenate([yup[:, lanes], ydn[:, lanes]], 1)], 0)

    low, high = rim(0), rim(1)
    rim_one = swap_pairs(jnp.where(odd_z == 1, low, high), "gz", 0)
    rim_two = swap_pairs(jnp.where(odd_z == 1, high, low), "gz", 1)

    inner_shape = shape(sum(GROUPS[:-1]), NZ, EROWS, 128)
    inner_faces_shape = shape(7, NZ - 2, LT, ROWS, 128)
    inner, inner_faces = pl.pallas_call(
        functools.partial(krylov_inner, swap),
        out_shape=(inner_shape, inner_faces_shape),
        in_specs=[smem()] + [hbm()] * 5 + [vmem()] * (len(x_parts) + 2),
        out_specs=(hbm(), hbm()),
        scratch_shapes=[
            *[pltpu.VMEM((tiles, NZ, EROWS, 128), F32) for tiles in GROUPS[:-1]],
            pltpu.VMEM(inner_faces_shape.shape, F32),
            pltpu.SemaphoreType.DMA((2 * FIELDS,)),
            pltpu.SemaphoreType.DMA((9,)),
        ],
        compiler_params=params(LIMIT),
        cost_estimate=cost(7),
    )(place, *fields, *x_parts, yup, ydn)

    block = shape(2 * COLS, NZ, NX, 128)
    basis, message = pl.pallas_call(
        functools.partial(krylov_outer, swap),
        out_shape=(block, shape(devices, 2, 128)),
        in_specs=[hbm(), hbm(), smem(), smem(), hbm(), hbm(), vmem(), vmem()],
        out_specs=(hbm(), vmem()),
        scratch_shapes=[
            *[pltpu.VMEM((tiles, EZ, EROWS, 128), F32) for tiles in GROUPS],
            pltpu.VMEM((7, EZ, LT, ROWS, 128), F32),
            pltpu.VMEM((2, STACK, STACK), F32),
            pltpu.VMEM((2,) + rim_one.shape, F32),
            pltpu.SemaphoreType.DMA((4 * FIELDS,)),
            pltpu.SemaphoreType.DMA((9,)),
            pltpu.SemaphoreType.DMA((STEPS + 1,)),
        ],
        compiler_params=params(ROOMY),
        cost_estimate=cost(15),
    )(face_one, face_two, place, odd_z, inner, inner_faces, rim_one, rim_two)

    message = exchange(message)
    first, message, factor_one = pl.pallas_call(
        functools.partial(first_pass, cells),
        out_shape=(block, shape(devices, 2, 128), shape(24, 128)),
        in_specs=[vmem(), hbm()],
        out_specs=(hbm(), vmem(), vmem()),
        scratch_shapes=[
            pltpu.VMEM(block.shape, F32),
            pltpu.VMEM(block.shape, F32),
            pltpu.VMEM((COLS, 24, 128), F32),
            pltpu.VMEM((2, STACK, STACK), F32),
            pltpu.SemaphoreType.DMA((NZ,)),
            pltpu.SemaphoreType.DMA((NZ,)),
        ],
        compiler_params=params(ROOMY),
    )(message, basis)

    message = exchange(message)
    return pl.pallas_call(
        functools.partial(second_pass, cells),
        out_shape=(shape(COLS, NZ, NX, NY), shape(COLS, COLS)),
        in_specs=[vmem(), vmem(), hbm()],
        out_specs=(hbm(), vmem()),
        scratch_shapes=[
            pltpu.VMEM(block.shape, F32),
            pltpu.VMEM((COLS, NZ, NX, NY), F32),
            pltpu.VMEM((COLS, 24, 128), F32),
            pltpu.SemaphoreType.DMA((NZ,)),
            pltpu.SemaphoreType.DMA((NZ,)),
        ],
        compiler_params=params(ROOMY),
    )(message, factor_one, first)


def solution(mesh):
    return jax.shard_map(
        body,
        mesh=mesh,
        in_specs=(
            P(None, "gz", "gx", "gy"),
            P("gz", "gx", "gy"),
            P("gz", "gx", "gy"),
            P("gz", "gx", "gy"),
            P("gz", "gx", "gy"),
        ),
        out_specs=(P(None, "gz", "gx", "gy"), P()),
        check_vma=False,
    )
```

```python
import functools

import jax
import jax.numpy as jnp
from jax import lax
from jax.experimental import pallas as pl
from jax.experimental.pallas import tpu as pltpu
from jax.sharding import PartitionSpec as P

NRHS = 4
STEPS = 4
COLS = NRHS * (STEPS + 1)
SHIFTS = (3.0, 11.0, 7.0, 1.5)
SCALE = 1.0 / 6.0
FIELDS = NRHS + 4
AXES = ("gx", "gy", "gz")
HIGHEST = lax.Precision.HIGHEST

DEPTH = 4
NZ, NX, NY = 8, 32, 256
EZ = NZ + 2 * DEPTH
ROWS = NX + 8
EROWS = ROWS + 16
LT = 3
FACE = NRHS * 4 + 3 * 4 + 1
F32 = jnp.float32
LIMIT, ROOMY = 63, 52


def params(mb):
    return pltpu.CompilerParams(vmem_limit_bytes=mb << 20)


def cost(us):
    return pl.CostEstimate(flops=0, bytes_accessed=int(us * 3.6e6), transcendentals=0)


def vmem():
    return pl.BlockSpec(memory_space=pltpu.VMEM)


def smem():
    return pl.BlockSpec(memory_space=pltpu.SMEM)


def hbm():
    return pl.BlockSpec(memory_space=pl.ANY)


def row_ids(shape):
    return lax.broadcasted_iota(jnp.int32, shape, 0)


def lane_ids(shape):
    return lax.broadcasted_iota(jnp.int32, shape, 1)


def field_of(rhs, cz, cx, cy, dg, f, z):
    return rhs.at[f, z] if f < NRHS else (cz, cx, cy, dg)[f - NRHS].at[z]


def pack_faces(swap, place, odd_z, rhs, cz, cx, cy, dg, z_one, z_two, *rest):
    xmsgs, (xrows, whole, loads, saves, xsaves) = rest[:-5], rest[-5:]
    copies = []
    for f in range(FIELDS):
        src = rhs.at[f] if f < NRHS else (cz, cx, cy, dg)[f - NRHS]
        copies.append(pltpu.make_async_copy(src, whole.at[f], loads.at[f]))
        copies[-1].start()
    low = row_ids((8, NY)) < 4
    up = place[0] == 0
    planes = []
    at = 0
    for f in range(FIELDS):
        copies[f].wait()
        depth = DEPTH if f <= NRHS else DEPTH - 1
        for side, out in ((0, z_one), (1, z_two)):
            start = jnp.where(odd_z[0] == side, NZ - depth, 0)
            planes.append(
                pltpu.make_async_copy(
                    whole.at[f, pl.ds(start, depth)], out.at[pl.ds(at, depth)], saves.at[2 * f + side]
                )
            )
            planes[-1].start()
        at += depth
        for m in range(NZ // 2):
            a, b = whole.at[f, 2 * m], whole.at[f, 2 * m + 1]
            first = jnp.where(low, a[0:8], pltpu.roll(b[0:8], 4, 0))
            last = jnp.where(low, pltpu.roll(a[NX - 8 : NX], 4, 0), b[NX - 8 : NX])
            if swap:
                xrows[0, f, m] = jnp.where(up, last, first)
            else:
                xrows[0, f, m] = first
                xrows[1, f, m] = last
        for n, xmsg in enumerate(xmsgs):
            planes.append(pltpu.make_async_copy(xrows.at[n, f], xmsg.at[f], xsaves.at[n, f]))
            planes[-1].start()
    for copy in planes:
        copy.wait()


def halo_tile(above, below, odd, keep_up, keep_dn):
    low = row_ids(above.shape) < 4
    if odd:
        up, dn = pltpu.roll(above, 4, 0), below
    else:
        up, dn = above, pltpu.roll(below, 4, 0)
    return jnp.where(low, up * keep_up, dn * keep_dn)


def keep_sides(swap, place):
    if not swap:
        return 1.0, 1.0
    first = place[0] == 0
    return jnp.where(first, 1.0, 0.0), jnp.where(first, 0.0, 1.0)


def pack_lanes(tile_of, side):
    lane = lane_ids((8, 128))
    source = 124 * side
    acc = jnp.zeros((8, 128), F32)
    for zz in range(4):
        for f in range(FIELDS):
            tile = tile_of(f, zz)
            spot = (zz * FIELDS + f) * 4
            shift = (spot - source) % 128
            if shift:
                tile = pltpu.roll(tile, shift, 1)
            acc = jnp.where((lane >= spot) & (lane < spot + 4), tile, acc)
    return acc


def pack_own_rims(odd_y, rhs, cz, cx, cy, dg, one, two):
    odd = odd_y[0] == 1
    for t in range(NX // 8):
        for half in range(2):
            lo, hi = (
                pack_lanes(
                    lambda f, zz: field_of(rhs, cz, cx, cy, dg, f, 4 * half + zz)[
                        8 * t : 8 * t + 8, 128 * side : 128 * side + 128
                    ],
                    side,
                )
                for side in range(2)
            )
            one[8 * t : 8 * t + 8, 128 * half : 128 * half + 128] = jnp.where(odd, lo, hi)
            two[8 * t : 8 * t + 8, 128 * half : 128 * half + 128] = jnp.where(odd, hi, lo)


def pack_rims(swap, place, odd_y, *refs):
    above, below, one, two = refs if not swap else (refs[0],) + refs
    keep_up, keep_dn = keep_sides(swap, place)
    odd = odd_y[0] == 1
    for half in range(2):
        halves = []
        for side in range(2):
            lanes = slice(128 * side, 128 * side + 128)
            halves.append(
                pack_lanes(
                    lambda f, zz: halo_tile(
                        above[f, 2 * half + zz // 2, :, lanes],
                        below[f, 2 * half + zz // 2, :, lanes],
                        zz % 2,
                        keep_up,
                        keep_dn,
                    ),
                    side,
                )
            )
        lo, hi = halves
        one[:, 128 * half : 128 * half + 128] = jnp.where(odd, lo, hi)
        two[:, 128 * half : 128 * half + 128] = jnp.where(odd, hi, lo)


STACK = 8 * COLS


def gram_zero(accs):
    accs[...] = jnp.zeros_like(accs)


def gram_add(stacks, accs):
    left, right = [], []
    cross_left, cross_right = [], []
    for stack in stacks:
        high = stack.astype(jnp.bfloat16)
        rest = stack - high.astype(F32)
        mid = rest.astype(jnp.bfloat16)
        low = (rest - mid.astype(F32)).astype(jnp.bfloat16)
        left += [high, mid]
        cross_left += [high, high]
        cross_right += [mid, low]
    contract = (((1,), (1,)), ((), ()))

    def product(a, b):
        return lax.dot_general(jnp.concatenate(a, 1), jnp.concatenate(b, 1), contract, preferred_element_type=F32)

    accs[0] += product(left, left)
    accs[1] += product(cross_left, cross_right)


def gram_message(accs, out):
    same = (row_ids((STACK, STACK)) & 7) == (lane_ids((STACK, STACK)) & 7)
    pick = jnp.where((row_ids((STACK, 128)) >> 3) == lane_ids((STACK, 128)), 1.0, 0.0)

    def traces(product):
        picked = jnp.where(same, product, 0.0)
        rows = [jnp.sum(picked[8 * i : 8 * i + 8], axis=0, keepdims=True) for i in range(COLS)]
        rows = jnp.concatenate(rows + [jnp.zeros((128 - COLS, STACK), F32)], 0)
        return lax.dot_general(
            rows, pick, (((1,), (0,)), ((), ())), precision=HIGHEST, preferred_element_type=F32
        )

    cross = traces(accs[1])
    gram = traces(accs[0]) + cross + cross.T
    tops = [gram[8 * k : 8 * k + 8] for k in range(3)]
    rows, lanes = row_ids((8, 128)), lane_ids((8, 128))
    tile = jnp.where(lanes < COLS, tops[0], pltpu.roll(tops[1], 12, 1))
    corner = pltpu.roll(pltpu.roll(tops[2], 128 - 16, 1), 4, 0)
    tile = jnp.where((rows >= 4) & (lanes < 4), corner, tile)
    packed = tile
    for q in range(1, 4):
        turned = pltpu.roll(pltpu.roll(tile, 32 * q, 1), 8 - 2 * q, 0)
        packed = jnp.where((lanes >> 5) == q, turned, packed)
    packed = packed[0:2]
    for n in range(out.shape[0]):
        out[n] = packed


def gram_of(messages):
    parts = [messages[n] for n in range(messages.shape[0])]
    while len(parts) > 1:
        parts = [sum(parts[n : n + 2][1:], parts[n]) for n in range(0, len(parts), 2)]
    total = jnp.concatenate(parts * 4, 0)
    rows, lanes = row_ids((8, 128)), lane_ids((8, 128))
    tile = total
    for q in range(1, 4):
        tile = jnp.where((rows >> 1) == q, pltpu.roll(total, 128 - 32 * q, 1), tile)
    corner = pltpu.roll(pltpu.roll(tile, 4, 0), 16, 1)
    tops = [
        jnp.where((lanes < COLS) & (lanes >= rows), tile, 0.0),
        jnp.where((lanes < COLS) & (lanes >= rows + 8), pltpu.roll(tile, 128 - 12, 1), 0.0),
        jnp.where((lanes < COLS) & (lanes >= rows + 16), corner, 0.0),
    ]
    return jnp.concatenate(tops, 0)


GROUPS = (9, 12, 9, 9, 9, 9)


def group(k):
    return k + 1 if k else 0


class Block:
    def __init__(self, stores, base, faces, faces_base, one):
        self.one = one
        self.stores, self.base, self.faces, self.faces_base = stores, base, faces, faces_base
        self.lane = lane_ids((8, 128))

    def where(self, f, l):
        return (0, 2 * f + l) if f < NRHS else (1, 3 * (f - NRHS) + l)

    def put(self, g, n, z, t, value):
        store, z = self.stores[g], z - self.base
        store[n, z, 8 + 8 * t : 16 + 8 * t, :] = value
        if t == 0:
            store[n, z, 8 + ROWS : 16 + ROWS, :] = value
        if t == ROWS // 8 - 1:
            store[n, z, 0:8, :] = value

    def get(self, g, n, z, t, off=0):
        row = 8 + 8 * t + (off * self.one if off else 0)
        return self.stores[g][n, z - self.base, pl.ds(row, 8), :]

    def close_ring(self, f, z):
        z = z - self.base
        for l in range(2):
            g, n = self.where(f, l)
            self.stores[g][n, z, 8 + ROWS : 16 + ROWS, :] = self.stores[g][n, z, 8:16, :]

    def place_y(self, z, up, dn):
        part, place = self.lane & 31, self.lane >> 5
        upper, lower = part < 4, part >= 28
        for t in range(ROWS // 8):
            u_all, d_all = up[8 * t : 8 * t + 8, :], dn[8 * t : 8 * t + 8, :]

            def turned(value, shift):
                return pltpu.roll(value, shift % 128, 1) if shift % 128 else value

            def copies(f):
                result = []
                for m in range(4):
                    u, d = turned(u_all, 32 * m - 4 * f), turned(d_all, 32 * m + 28 - 4 * f)
                    result.append(jnp.where(upper, u, jnp.where(lower, d, 0.0)))
                return result

            def pick(tiles):
                value = tiles[0]
                for r in range(1, 4):
                    value = jnp.where(place == r, tiles[r], value)
                return value

            fields = [copies(r) for r in range(NRHS)]
            for zz in range(4):
                self.put(0, 2 * NRHS, z + zz, t, pick([fields[r][(r - zz) % 4] for r in range(4)]))
            for c in range(4):
                mine = copies(NRHS + c)
                for zz in range(4):
                    self.put(1, 3 * c + 2, z + zz, t, pick([mine[(r - zz) % 4] for r in range(4)]))

    def coefficients(self, z):
        lane = self.lane
        for t in range(ROWS // 8):

            def tiles(c, z, off=0):
                return [self.get(1, 3 * c + l, z, t, off) for l in range(LT)]

            center_z, center_x, center_y, diag = (tiles(c, z) for c in range(4))
            up = [pltpu.roll(v, 127, 1) for v in center_y]
            dn = [pltpu.roll(v, 1, 1) for v in center_y]
            first = jnp.broadcast_to(center_y[0][:, 0:1], (8, 128))
            last = jnp.broadcast_to(center_y[1][:, 127:128], (8, 128))
            sides = [
                (center_z, tiles(0, z + 1)),
                (center_z, tiles(0, z - 1)),
                (center_x, tiles(1, z, 1)),
                (center_x, tiles(1, z, -1)),
                (
                    center_y,
                    [
                        jnp.where(lane == 127, up[1], up[0]),
                        jnp.where(lane == 127, up[2], up[1]),
                        jnp.where((lane & 31) == 31, first, up[2]),
                    ],
                ),
                (
                    center_y,
                    [
                        jnp.where(lane == 0, dn[2], dn[0]),
                        jnp.where(lane == 0, dn[0], dn[1]),
                        jnp.where((lane & 31) == 0, last, dn[2]),
                    ],
                ),
            ]
            at = z - self.faces_base
            for l in range(LT):
                inside = diag[l] > 0.0
                total = diag[l] * SCALE
                for k, (mid, side) in enumerate(sides):
                    face = (mid[l] + side[l]) * (0.5 * SCALE)
                    total = total + face
                    self.faces[k, at, l, 8 * t : 8 * t + 8, :] = jnp.where(inside, face, 0.0)
                self.faces[6, at, l, 8 * t : 8 * t + 8, :] = jnp.where(inside, total, 0.0)

    def apply(self, k, z):
        last = k == STEPS - 1
        at, lane, edge = z - self.faces_base, self.lane, 2 * NRHS
        src, dst = group(k), group(k + 1)
        for t in range(NX // 8 if last else ROWS // 8):
            face = [
                [self.faces[c, at, l, 8 * t : 8 * t + 8, :] for l in range(2 if last else LT)] for c in range(7)
            ]
            diag = [d - SHIFTS[k] * SCALE for d in face[6]]

            def image(n, l, mid, up, dn):
                sides = (
                    self.get(src, n, z + 1, t),
                    self.get(src, n, z - 1, t),
                    self.get(src, n, z, t, 1),
                    self.get(src, n, z, t, -1),
                    up,
                    dn,
                )
                value = diag[l] * mid
                for c, side in enumerate(sides):
                    value = value - face[c][l] * side
                self.put(dst, n, z, t, value)

            rim = self.get(src, edge, z, t)
            rim_up, rim_dn = pltpu.roll(rim, 127, 1), pltpu.roll(rim, 1, 1)
            edge_up, edge_dn = rim_up, rim_dn
            for r in range(NRHS):
                one, two = self.get(src, 2 * r, z, t), self.get(src, 2 * r + 1, z, t)
                one_up, two_up = pltpu.roll(one, 127, 1), pltpu.roll(two, 127, 1)
                one_dn, two_dn = pltpu.roll(one, 1, 1), pltpu.roll(two, 1, 1)
                above = rim_up if r == 0 else pltpu.roll(rim, 127 - 32 * r, 1)
                below = rim_dn if r == NRHS - 1 else pltpu.roll(rim, 97 - 32 * r, 1)
                image(2 * r, 0, one, jnp.where(lane == 127, two_up, one_up), jnp.where(lane == 0, below, one_dn))
                image(2 * r + 1, 1, two, jnp.where(lane == 127, above, two_up), jnp.where(lane == 0, one_dn, two_dn))
                if not last:
                    start = one_up if r == NRHS - 1 else pltpu.roll(one, 32 * r + 31, 1)
                    end = two_dn if r == 0 else pltpu.roll(two, 32 * r + 1, 1)
                    edge_up = jnp.where(lane == 32 * r + 31, start, edge_up)
                    edge_dn = jnp.where(lane == 32 * r, end, edge_dn)
            if not last:
                image(edge, 2, rim, edge_up, edge_dn)


def dynamic_one(place):
    return (place[0] >> 24) + 1


def loop(start, stop, do):
    def step(n, carry):
        do(n)
        return carry

    lax.fori_loop(start, stop, step, 0)


def inner_planes(k):
    return DEPTH + k, DEPTH + NZ - k


def inner_copies(inner, inner_faces, stores, base, faces, faces_base, sems, out):
    def copy(n, there, here):
        src, dst = (here, there) if out else (there, here)
        return pltpu.make_async_copy(src, dst, sems.at[n])

    result = []
    for n, (g, start, stop) in enumerate(
        [(g, z, z + 2) for g in (0, 1) for z in (DEPTH, DEPTH + NZ - 2)]
        + [(0, DEPTH + 2, DEPTH + NZ - 2)]
        + [(group(k), *inner_planes(k)) for k in range(1, STEPS)]
    ):
        there = inner.at[pl.ds(sum(GROUPS[:g]), GROUPS[g]), pl.ds(start - DEPTH, stop - start)]
        result.append(copy(n, there, stores[g].at[:, pl.ds(start - base, stop - start)]))
    start, stop = inner_planes(1)
    result.append(copy(len(result), inner_faces, faces.at[:, pl.ds(start - faces_base, stop - start)]))
    return result


def krylov_inner(swap, place, rhs, cz, cx, cy, dg, *rest):
    above, below, yup, ydn, inner, inner_faces, *stores, faces, load_sems, sems = rest if not swap else rest[:1] + rest
    keep_up, keep_dn = keep_sides(swap, place)
    block = Block(stores, DEPTH, faces, DEPTH + 1, dynamic_one(place))
    loads = []
    for f in range(FIELDS):
        src = rhs.at[f] if f < NRHS else (cz, cx, cy, dg)[f - NRHS]
        for l in range(2):
            g, n = block.where(f, l)
            loads.append(
                pltpu.make_async_copy(
                    src.at[:, :, pl.ds(128 * l, 128)], stores[g].at[n, :, pl.ds(8, NX), :], load_sems.at[2 * f + l]
                )
            )
            loads[-1].start()
    for f in range(FIELDS):
        for z in range(DEPTH, DEPTH + NZ):
            m = (z - DEPTH) // 2
            for l in range(2):
                lanes = pl.ds(128 * l, 128)
                tile = halo_tile(above[f, m, :, lanes], below[f, m, :, lanes], z % 2, keep_up, keep_dn)
                block.put(*block.where(f, l), z, NX // 8, tile)
    for half in range(2):
        lanes = pl.ds(128 * half, 128)
        block.place_y(DEPTH + 4 * half, yup.at[:, lanes], ydn.at[:, lanes])
    for copy in loads:
        copy.wait()
    for f in range(FIELDS):
        for z in range(DEPTH, DEPTH + NZ):
            block.close_ring(f, z)
    copies = inner_copies(inner, inner_faces, stores, DEPTH, faces, DEPTH + 1, sems, True)
    for n in range(5):
        copies[n].start()
    loop(*inner_planes(1), block.coefficients)
    copies[-1].start()
    for k in range(STEPS - 1):
        loop(*inner_planes(k + 1), functools.partial(block.apply, k))
        copies[5 + k].start()
    for copy in copies:
        copy.wait()


NEAR, FAR = 8 * FIELDS, 24


def krylov_outer(
    swap, face_one, face_two, place, odd_z, inner, inner_faces, rim_one, rim_two,
    basis, message,
    *rest,
):
    keep_up, keep_dn = keep_sides(swap, place)
    n_x = 1 if swap else 2
    *stores, faces, accs, rims, plane_sems, loads, saves = rest
    odd = odd_z[0] == 1
    block = Block(stores, 0, faces, 0, dynamic_one(place))
    copies = inner_copies(inner, inner_faces, stores, 0, faces, 0, loads, False)
    def plane_copies(lower, upper):
        planes = []
        start = 0
        for f in range(FIELDS):
            depth = DEPTH if f <= NRHS else DEPTH - 1
            for side, (face, z) in enumerate(((lower, DEPTH - depth), (upper, DEPTH + NZ))):
                for l in range(2):
                    g, n = block.where(f, l)
                    planes.append(
                        pltpu.make_async_copy(
                            face.at[pl.ds(start, depth), :, pl.ds(128 * l, 128)],
                            stores[g].at[n, pl.ds(z, depth), pl.ds(8, NX), :],
                            plane_sems.at[4 * f + 2 * side + l],
                        )
                    )
            start += depth
        return planes

    for copy in copies[:4]:
        copy.start()

    @pl.when(odd)
    def _():
        for copy in plane_copies(face_one, face_two):
            copy.start()

    @pl.when(jnp.logical_not(odd))
    def _():
        for copy in plane_copies(face_two, face_one):
            copy.start()

    one, two = rim_one[...], rim_two[...]
    rims[0] = jnp.where(odd, one, two)
    rims[1] = jnp.where(odd, two, one)
    rimlo, rimhi = rims.at[0], rims.at[1]

    zero = jnp.zeros((8, 128), F32)
    for f in range(FIELDS):
        for rim, first in ((rimlo, 0), (rimhi, DEPTH + NZ)):
            for z in range(first, first + DEPTH):
                far = DEPTH - z if first == 0 else z - first + 1
                for l in range(2):
                    lanes = pl.ds(128 * l, 128)
                    if far <= 2:
                        at, odd = 8 * f, z % 2
                    elif far == 3 and 8 * (f // 2) < FAR:
                        at, odd = NEAR + 8 * (f // 2), f % 2
                    else:
                        block.put(*block.where(f, l), z, NX // 8, zero)
                        continue
                    other = at + (n_x - 1) * (NEAR + FAR)
                    tile = halo_tile(rim[at : at + 8, lanes], rim[other : other + 8, lanes], odd, keep_up, keep_dn)
                    block.put(*block.where(f, l), z, NX // 8, tile)
    rows = pl.ds(n_x * (NEAR + FAR), ROWS)
    for rim, z in ((rimlo, 0), (rimhi, DEPTH + NZ)):
        block.place_y(z, rim.at[rows, pl.ds(0, 128)], rim.at[rows, pl.ds(128, 128)])

    for copy in copies[:4] + plane_copies(face_one, face_two):
        copy.wait()
    for copy in [copies[5], copies[-1], copies[6], copies[7], copies[4]]:
        copy.start()
    for f in range(FIELDS):
        depth = DEPTH if f <= NRHS else DEPTH - 1
        for d in range(depth):
            block.close_ring(f, DEPTH - 1 - d)
            block.close_ring(f, DEPTH + NZ + d)
    loop(1, DEPTH + 1, block.coefficients)
    loop(DEPTH + NZ - 1, EZ - 1, block.coefficients)

    sends = []

    def send_block(k):
        copy = pltpu.make_async_copy(
            stores[group(k)].at[pl.ds(0, 2 * NRHS), pl.ds(DEPTH, NZ), pl.ds(8, NX), :],
            basis.at[pl.ds(k * 2 * NRHS, 2 * NRHS)],
            saves.at[k],
        )
        copy.start()
        sends.append(copy)

    for k in range(STEPS):
        if k == 1:
            copies[-1].wait()
        loop(
            0,
            2 * DEPTH,
            lambda n, k=k: block.apply(k, n + k + 1 + jnp.where(n >= DEPTH, NZ - 2 - 2 * k, 0)),
        )
        if k < STEPS - 1:
            copies[5 + k].wait()
        send_block(k + 1)
    copies[4].wait()
    send_block(0)
    gram_zero(accs)

    def products(z):
        def tile(i, t):
            store = stores[group(i // NRHS)]
            return jnp.concatenate([store[2 * (i % NRHS) + l, z, 8 + 8 * t : 16 + 8 * t, :] for l in range(2)], 1)

        gram_add([jnp.concatenate([tile(i, t) for i in range(COLS)], 0) for t in range(NX // 8)], accs)

    loop(DEPTH, DEPTH + NZ, products)
    gram_message(accs, message)
    for copy in sends:
        copy.wait()


def factor_gram(messages, cells, table):
    rows = row_ids((24, 128))
    lanes = lane_ids((24, 128))
    upper = gram_of(messages) / cells
    square = jnp.concatenate([upper, jnp.zeros((104, 128), F32)], 0).T
    whole = jnp.where(rows <= lanes, upper, square[0:24, :])

    tile_rows = row_ids((8, 128))
    tiles = range(3)

    def split(value):
        return [value[8 * k : 8 * k + 8] for k in tiles]

    def row_of(column, j):
        return jnp.broadcast_to(column[j // 8][j % 8 : j % 8 + 1, :], (8, 128))

    columns = [split(jnp.broadcast_to(whole[:, c : c + 1], (24, 128))) for c in range(COLS)]
    inverse = [[jnp.where(tile_rows + 8 * k == c, 1.0, 0.0) for k in tiles] for c in range(COLS)]
    pivots = [jnp.ones((8, 128), F32) for k in tiles]
    for j in range(COLS):
        pivot = row_of(columns[j], j)
        first = j // 8
        pivots[first] = jnp.where(tile_rows == j % 8, pivot, pivots[first])
        below = {k: columns[j][k] / pivot for k in tiles if k >= first}
        below[first] = jnp.where(tile_rows > j % 8, below[first], 0.0)
        for c in range(COLS):
            change = columns[c] if c > j else inverse[c]
            row = row_of(change, j)
            for k in below:
                change[k] = change[k] - below[k] * row
    scales = [1.0 / jnp.sqrt(p) for p in pivots]
    factor = jnp.zeros((24, 128), F32)
    for c in range(COLS):
        table[c] = jnp.concatenate([inverse[c][k] * scales[k] for k in tiles], 0)
        factor = jnp.where(lanes == c, jnp.concatenate(columns[c], 0), factor)
    return jnp.where((rows <= lanes) & (rows < COLS), factor * jnp.concatenate(scales, 0), 0.0)


def apply_rows(table, group, read, write):
    pieces = NX // 8
    for g in reversed(range(COLS // group)):
        mine = range(group * g, group * g + group)
        sums = {i: None for i in mine}
        for j in range(group * g + group):
            value = [read(j, p) for p in range(pieces)]
            for i in mine:
                if j <= i:
                    weight = jnp.broadcast_to(table[j, i : i + 1, :], (8, 128))
                    terms = [weight * v for v in value]
                    sums[i] = terms if sums[i] is None else [s + t for s, t in zip(sums[i], terms)]
        for i in mine:
            for p in range(pieces):
                write(i, p, sums[i][p])


def plane_copy(src, dst, sems, z):
    return pltpu.make_async_copy(src.at[:, z], dst.at[:, z], sems.at[z])


def first_pass(
    cells, message, basis_hbm, first_hbm, next_message, factor_out, basis, first, table, accs, loads, saves
):
    for z in range(NZ):
        plane_copy(basis_hbm, basis, loads, z).start()
    factor_out[...] = factor_gram(message, cells, table)
    gram_zero(accs)

    def products(z):
        def tile(i, t):
            return jnp.concatenate([first[2 * i + l, z, 8 * t : 8 * t + 8, :] for l in range(2)], 1)

        gram_add([jnp.concatenate([tile(i, t) for i in range(COLS)], 0) for t in range(NX // 8)], accs)

    def apply(z):
        for l in range(2):

            def read(j, p):
                return basis[2 * j + l, z, 8 * p : 8 * p + 8, :]

            def write(i, p, value):
                first[2 * i + l, z, 8 * p : 8 * p + 8, :] = value

            apply_rows(table, 5, read, write)
        plane_copy(first, first_hbm, saves, z).start()

    def both(z):
        plane_copy(basis_hbm, basis, loads, z).wait()
        products(z - 1)
        apply(z)

    plane_copy(basis_hbm, basis, loads, 0).wait()
    apply(0)
    loop(1, NZ, both)
    products(NZ - 1)
    gram_message(accs, next_message)
    for z in range(NZ):
        plane_copy(first, first_hbm, saves, z).wait()


def second_pass(cells, message, factor_one, first_hbm, out_hbm, triangle, first, out, table, loads, saves):
    for z in range(NZ):
        plane_copy(first_hbm, first, loads, z).start()
    left = factor_gram(message, cells, table)[:, 0:24]
    product = lax.dot_general(
        left, factor_one[...], (((1,), (0,)), ((), ())), precision=HIGHEST, preferred_element_type=F32
    )
    triangle[...] = product[0:COLS, 0:COLS]

    def chunk(z, carry):
        plane_copy(first_hbm, first, loads, z).wait()
        for l in range(2):

            def read(j, p):
                return first[2 * j + l, z, 8 * p : 8 * p + 8, :]

            def write(i, p, value):
                out[i, z, 8 * p : 8 * p + 8, 128 * l : 128 * l + 128] = value

            apply_rows(table, 4, read, write)
        plane_copy(out, out_hbm, saves, z).start()
        return carry

    lax.fori_loop(0, NZ, chunk, 0)
    for z in range(NZ):
        plane_copy(out, out_hbm, saves, z).wait()


def shape(*dims):
    return jax.ShapeDtypeStruct(dims, F32)


def move(value, axis, delta):
    count = lax.axis_size(axis)
    pairs = [(i, i + delta) for i in range(count) if 0 <= i + delta < count]
    return lax.ppermute(value, axis, pairs)


def swap_pairs(value, axis, first):
    pairs = [(i, i + 1) for i in range(first, lax.axis_size(axis) - 1, 2)]
    return lax.ppermute(value, axis, pairs + [(j, i) for i, j in pairs])


def exchange(messages):
    return lax.all_to_all(messages, AXES, 0, 0, tiled=True)


def body(rhs, coef_x, coef_y, coef_z, diag_term):
    n_x = lax.axis_size("gx")
    devices = n_x * lax.axis_size("gy") * lax.axis_size("gz")
    cells = float(NZ * NX * NY * devices)
    at_x = lax.axis_index("gx")
    swap = n_x == 2
    fields = (rhs, coef_z, coef_x, coef_y, diag_term)

    place = at_x.astype(jnp.int32).reshape(1)
    odd_z, odd_y = ((lax.axis_index(axis) & 1).astype(jnp.int32).reshape(1) for axis in ("gz", "gy"))
    face_shape = shape(FACE, NX, NY)
    x_shape = shape(FIELDS, NZ // 2, 8, NY)
    z_one, z_two, *xmsgs = pl.pallas_call(
        functools.partial(pack_faces, swap),
        out_shape=(face_shape, face_shape) + (x_shape,) * (1 if swap else 2),
        in_specs=[smem()] * 2 + [hbm()] * 5,
        out_specs=(hbm(), hbm()) + (hbm(),) * (1 if swap else 2),
        scratch_shapes=[
            pltpu.VMEM((1 if swap else 2,) + x_shape.shape, F32),
            pltpu.VMEM((FIELDS, NZ, NX, NY), F32),
            pltpu.SemaphoreType.DMA((FIELDS,)),
            pltpu.SemaphoreType.DMA((2 * FIELDS,)),
            pltpu.SemaphoreType.DMA((1 if swap else 2, FIELDS)),
        ],
        compiler_params=params(LIMIT),
        cost_estimate=cost(2.5),
    )(place, odd_z, *fields)
    face_one, face_two = swap_pairs(z_one, "gz", 0), swap_pairs(z_two, "gz", 1)
    if swap:
        x_parts = (lax.ppermute(xmsgs[0], "gx", [(0, 1), (1, 0)]),)
    else:
        x_parts = (move(xmsgs[0], "gx", -1), move(xmsgs[1], "gx", 1))

    own_shape, halo_shape = shape(NX, NY), shape(ROWS - NX, NY)
    own_one, own_two = pl.pallas_call(
        pack_own_rims,
        out_shape=(own_shape, own_shape),
        in_specs=[smem()] + [vmem()] * 5,
        compiler_params=params(LIMIT),
        cost_estimate=cost(2.5),
    )(odd_y, *fields)
    halo_one, halo_two = pl.pallas_call(
        functools.partial(pack_rims, swap),
        out_shape=(halo_shape, halo_shape),
        in_specs=[smem()] * 2 + [vmem()] * len(x_parts),
        compiler_params=params(16),
        cost_estimate=cost(1),
    )(place, odd_y, *x_parts)
    y_one = swap_pairs(jnp.concatenate([own_one, halo_one], 0), "gy", 0)
    y_two = swap_pairs(jnp.concatenate([own_two, halo_two], 0), "gy", 1)
    yup, ydn = jnp.where(odd_y == 1, y_two, y_one), jnp.where(odd_y == 1, y_one, y_two)

    def rim(half):
        near, far, odd = ((0, 1, 0), (3, 2, 1))[half]
        rows = []
        for part in x_parts:
            rows.append(part[:, near].reshape(NEAR, NY))
            rows.append(part[: FAR // 4, far, 4 * odd : 4 * odd + 4].reshape(FAR, NY))
        lanes = slice(128 * half, 128 * half + 128)
        return jnp.concatenate(rows + [jnp.concatenate([yup[:, lanes], ydn[:, lanes]], 1)], 0)

    low, high = rim(0), rim(1)
    rim_one = swap_pairs(jnp.where(odd_z == 1, low, high), "gz", 0)
    rim_two = swap_pairs(jnp.where(odd_z == 1, high, low), "gz", 1)

    inner_shape = shape(sum(GROUPS[:-1]), NZ, EROWS, 128)
    inner_faces_shape = shape(7, NZ - 2, LT, ROWS, 128)
    inner, inner_faces = pl.pallas_call(
        functools.partial(krylov_inner, swap),
        out_shape=(inner_shape, inner_faces_shape),
        in_specs=[smem()] + [hbm()] * 5 + [vmem()] * (len(x_parts) + 2),
        out_specs=(hbm(), hbm()),
        scratch_shapes=[
            *[pltpu.VMEM((tiles, NZ, EROWS, 128), F32) for tiles in GROUPS[:-1]],
            pltpu.VMEM(inner_faces_shape.shape, F32),
            pltpu.SemaphoreType.DMA((2 * FIELDS,)),
            pltpu.SemaphoreType.DMA((9,)),
        ],
        compiler_params=params(LIMIT),
        cost_estimate=cost(7),
    )(place, *fields, *x_parts, yup, ydn)

    block = shape(2 * COLS, NZ, NX, 128)
    basis, message = pl.pallas_call(
        functools.partial(krylov_outer, swap),
        out_shape=(block, shape(devices, 2, 128)),
        in_specs=[hbm(), hbm(), smem(), smem(), hbm(), hbm(), vmem(), vmem()],
        out_specs=(hbm(), vmem()),
        scratch_shapes=[
            *[pltpu.VMEM((tiles, EZ, EROWS, 128), F32) for tiles in GROUPS],
            pltpu.VMEM((7, EZ, LT, ROWS, 128), F32),
            pltpu.VMEM((2, STACK, STACK), F32),
            pltpu.VMEM((2,) + rim_one.shape, F32),
            pltpu.SemaphoreType.DMA((4 * FIELDS,)),
            pltpu.SemaphoreType.DMA((9,)),
            pltpu.SemaphoreType.DMA((STEPS + 1,)),
        ],
        compiler_params=params(ROOMY),
        cost_estimate=cost(15),
    )(face_one, face_two, place, odd_z, inner, inner_faces, rim_one, rim_two)

    message = exchange(message)
    first, message, factor_one = pl.pallas_call(
        functools.partial(first_pass, cells),
        out_shape=(block, shape(devices, 2, 128), shape(24, 128)),
        in_specs=[vmem(), hbm()],
        out_specs=(hbm(), vmem(), vmem()),
        scratch_shapes=[
            pltpu.VMEM(block.shape, F32),
            pltpu.VMEM(block.shape, F32),
            pltpu.VMEM((COLS, 24, 128), F32),
            pltpu.VMEM((2, STACK, STACK), F32),
            pltpu.SemaphoreType.DMA((NZ,)),
            pltpu.SemaphoreType.DMA((NZ,)),
        ],
        compiler_params=params(ROOMY),
    )(message, basis)

    message = exchange(message)
    return pl.pallas_call(
        functools.partial(second_pass, cells),
        out_shape=(shape(COLS, NZ, NX, NY), shape(COLS, COLS)),
        in_specs=[vmem(), vmem(), hbm()],
        out_specs=(hbm(), vmem()),
        scratch_shapes=[
            pltpu.VMEM(block.shape, F32),
            pltpu.VMEM((COLS, NZ, NX, NY), F32),
            pltpu.VMEM((COLS, 24, 128), F32),
            pltpu.SemaphoreType.DMA((NZ,)),
            pltpu.SemaphoreType.DMA((NZ,)),
        ],
        compiler_params=params(ROOMY),
    )(message, factor_one, first)


def solution(mesh):
    return jax.shard_map(
        body,
        mesh=mesh,
        in_specs=(
            P(None, "gz", "gx", "gy"),
            P("gz", "gx", "gy"),
            P("gz", "gx", "gy"),
            P("gz", "gx", "gy"),
            P("gz", "gx", "gy"),
        ),
        out_specs=(P(None, "gz", "gx", "gy"), P()),
        check_vma=False,
    )
```

```python
import functools

import jax
import jax.numpy as jnp
from jax import lax
from jax.experimental import pallas as pl
from jax.experimental.pallas import tpu as pltpu
from jax.sharding import PartitionSpec as P

NRHS = 4
STEPS = 4
COLS = NRHS * (STEPS + 1)
SHIFTS = (3.0, 11.0, 7.0, 1.5)
SCALE = 1.0 / 6.0
FIELDS = NRHS + 4
AXES = ("gx", "gy", "gz")
HIGHEST = lax.Precision.HIGHEST

DEPTH = 4
NZ, NX, NY = 8, 32, 256
EZ = NZ + 2 * DEPTH
ROWS = NX + 8
EROWS = ROWS + 16
LT = 3
FACE = NRHS * 4 + 3 * 4 + 1
F32 = jnp.float32
LIMIT, ROOMY = 63, 52


def params(mb):
    return pltpu.CompilerParams(vmem_limit_bytes=mb << 20)


def cost(us):
    return pl.CostEstimate(flops=0, bytes_accessed=int(us * 3.6e6), transcendentals=0)


def vmem():
    return pl.BlockSpec(memory_space=pltpu.VMEM)


def smem():
    return pl.BlockSpec(memory_space=pltpu.SMEM)


def hbm():
    return pl.BlockSpec(memory_space=pl.ANY)


def row_ids(shape):
    return lax.broadcasted_iota(jnp.int32, shape, 0)


def lane_ids(shape):
    return lax.broadcasted_iota(jnp.int32, shape, 1)


def field_of(rhs, cz, cx, cy, dg, f, z):
    return rhs.at[f, z] if f < NRHS else (cz, cx, cy, dg)[f - NRHS].at[z]


def pack_faces(swap, place, odd_z, rhs, cz, cx, cy, dg, z_one, z_two, *rest):
    xmsgs, (xrows, whole, loads, saves, xsaves) = rest[:-5], rest[-5:]
    copies = []
    for f in range(FIELDS):
        src = rhs.at[f] if f < NRHS else (cz, cx, cy, dg)[f - NRHS]
        copies.append(pltpu.make_async_copy(src, whole.at[f], loads.at[f]))
        copies[-1].start()
    low = row_ids((8, NY)) < 4
    up = place[0] == 0
    planes = []
    at = 0
    for f in range(FIELDS):
        copies[f].wait()
        depth = DEPTH if f <= NRHS else DEPTH - 1
        for side, out in ((0, z_one), (1, z_two)):
            start = jnp.where(odd_z[0] == side, NZ - depth, 0)
            planes.append(
                pltpu.make_async_copy(
                    whole.at[f, pl.ds(start, depth)], out.at[pl.ds(at, depth)], saves.at[2 * f + side]
                )
            )
            planes[-1].start()
        at += depth
        for m in range(NZ // 2):
            a, b = whole.at[f, 2 * m], whole.at[f, 2 * m + 1]
            first = jnp.where(low, a[0:8], pltpu.roll(b[0:8], 4, 0))
            last = jnp.where(low, pltpu.roll(a[NX - 8 : NX], 4, 0), b[NX - 8 : NX])
            if swap:
                xrows[0, f, m] = jnp.where(up, last, first)
            else:
                xrows[0, f, m] = first
                xrows[1, f, m] = last
        for n, xmsg in enumerate(xmsgs):
            planes.append(pltpu.make_async_copy(xrows.at[n, f], xmsg.at[f], xsaves.at[n, f]))
            planes[-1].start()
    for copy in planes:
        copy.wait()


def halo_tile(above, below, odd, keep_up, keep_dn):
    low = row_ids(above.shape) < 4
    if odd:
        up, dn = pltpu.roll(above, 4, 0), below
    else:
        up, dn = above, pltpu.roll(below, 4, 0)
    return jnp.where(low, up * keep_up, dn * keep_dn)


def keep_sides(swap, place):
    if not swap:
        return 1.0, 1.0
    first = place[0] == 0
    return jnp.where(first, 1.0, 0.0), jnp.where(first, 0.0, 1.0)


def pack_lanes(tile_of, side):
    lane = lane_ids((8, 128))
    source = 124 * side
    acc = jnp.zeros((8, 128), F32)
    for zz in range(4):
        for f in range(FIELDS):
            tile = tile_of(f, zz)
            spot = (zz * FIELDS + f) * 4
            shift = (spot - source) % 128
            if shift:
                tile = pltpu.roll(tile, shift, 1)
            acc = jnp.where((lane >= spot) & (lane < spot + 4), tile, acc)
    return acc


def pack_own_rims(odd_y, rhs, cz, cx, cy, dg, one, two):
    odd = odd_y[0] == 1
    for t in range(NX // 8):
        for half in range(2):
            lo, hi = (
                pack_lanes(
                    lambda f, zz: field_of(rhs, cz, cx, cy, dg, f, 4 * half + zz)[
                        8 * t : 8 * t + 8, 128 * side : 128 * side + 128
                    ],
                    side,
                )
                for side in range(2)
            )
            one[8 * t : 8 * t + 8, 128 * half : 128 * half + 128] = jnp.where(odd, lo, hi)
            two[8 * t : 8 * t + 8, 128 * half : 128 * half + 128] = jnp.where(odd, hi, lo)


def pack_rims(swap, place, odd_y, *refs):
    above, below, one, two = refs if not swap else (refs[0],) + refs
    keep_up, keep_dn = keep_sides(swap, place)
    odd = odd_y[0] == 1
    for half in range(2):
        halves = []
        for side in range(2):
            lanes = slice(128 * side, 128 * side + 128)
            halves.append(
                pack_lanes(
                    lambda f, zz: halo_tile(
                        above[f, 2 * half + zz // 2, :, lanes],
                        below[f, 2 * half + zz // 2, :, lanes],
                        zz % 2,
                        keep_up,
                        keep_dn,
                    ),
                    side,
                )
            )
        lo, hi = halves
        one[:, 128 * half : 128 * half + 128] = jnp.where(odd, lo, hi)
        two[:, 128 * half : 128 * half + 128] = jnp.where(odd, hi, lo)


STACK = 8 * COLS


def gram_zero(accs):
    accs[...] = jnp.zeros_like(accs)


def gram_add(stacks, accs):
    left, right = [], []
    cross_left, cross_right = [], []
    for stack in stacks:
        high = stack.astype(jnp.bfloat16)
        rest = stack - high.astype(F32)
        mid = rest.astype(jnp.bfloat16)
        low = (rest - mid.astype(F32)).astype(jnp.bfloat16)
        left += [high, mid]
        cross_left += [high, high]
        cross_right += [mid, low]
    contract = (((1,), (1,)), ((), ()))

    def product(a, b):
        return lax.dot_general(jnp.concatenate(a, 1), jnp.concatenate(b, 1), contract, preferred_element_type=F32)

    accs[0] += product(left, left)
    accs[1] += product(cross_left, cross_right)


def gram_message(accs, out):
    same = (row_ids((STACK, STACK)) & 7) == (lane_ids((STACK, STACK)) & 7)
    pick = jnp.where((row_ids((STACK, 128)) >> 3) == lane_ids((STACK, 128)), 1.0, 0.0)

    def traces(product):
        picked = jnp.where(same, product, 0.0)
        rows = [jnp.sum(picked[8 * i : 8 * i + 8], axis=0, keepdims=True) for i in range(COLS)]
        rows = jnp.concatenate(rows + [jnp.zeros((128 - COLS, STACK), F32)], 0)
        return lax.dot_general(
            rows, pick, (((1,), (0,)), ((), ())), precision=HIGHEST, preferred_element_type=F32
        )

    cross = traces(accs[1])
    gram = traces(accs[0]) + cross + cross.T
    tops = [gram[8 * k : 8 * k + 8] for k in range(3)]
    rows, lanes = row_ids((8, 128)), lane_ids((8, 128))
    tile = jnp.where(lanes < COLS, tops[0], pltpu.roll(tops[1], 12, 1))
    corner = pltpu.roll(pltpu.roll(tops[2], 128 - 16, 1), 4, 0)
    tile = jnp.where((rows >= 4) & (lanes < 4), corner, tile)
    packed = tile
    for q in range(1, 4):
        turned = pltpu.roll(pltpu.roll(tile, 32 * q, 1), 8 - 2 * q, 0)
        packed = jnp.where((lanes >> 5) == q, turned, packed)
    packed = packed[0:2]
    for n in range(out.shape[0]):
        out[n] = packed


def gram_of(messages):
    parts = [messages[n] for n in range(messages.shape[0])]
    while len(parts) > 1:
        parts = [sum(parts[n : n + 2][1:], parts[n]) for n in range(0, len(parts), 2)]
    total = jnp.concatenate(parts * 4, 0)
    rows, lanes = row_ids((8, 128)), lane_ids((8, 128))
    tile = total
    for q in range(1, 4):
        tile = jnp.where((rows >> 1) == q, pltpu.roll(total, 128 - 32 * q, 1), tile)
    corner = pltpu.roll(pltpu.roll(tile, 4, 0), 16, 1)
    tops = [
        jnp.where((lanes < COLS) & (lanes >= rows), tile, 0.0),
        jnp.where((lanes < COLS) & (lanes >= rows + 8), pltpu.roll(tile, 128 - 12, 1), 0.0),
        jnp.where((lanes < COLS) & (lanes >= rows + 16), corner, 0.0),
    ]
    return jnp.concatenate(tops, 0)


GROUPS = (9, 12, 9, 9, 9, 9)


def group(k):
    return k + 1 if k else 0


class Block:
    def __init__(self, stores, base, faces, faces_base, one):
        self.one = one
        self.stores, self.base, self.faces, self.faces_base = stores, base, faces, faces_base
        self.lane = lane_ids((8, 128))

    def where(self, f, l):
        return (0, 2 * f + l) if f < NRHS else (1, 3 * (f - NRHS) + l)

    def put(self, g, n, z, t, value):
        store, z = self.stores[g], z - self.base
        store[n, z, 8 + 8 * t : 16 + 8 * t, :] = value
        if t == 0:
            store[n, z, 8 + ROWS : 16 + ROWS, :] = value
        if t == ROWS // 8 - 1:
            store[n, z, 0:8, :] = value

    def get(self, g, n, z, t, off=0):
        row = 8 + 8 * t + (off * self.one if off else 0)
        return self.stores[g][n, z - self.base, pl.ds(row, 8), :]

    def close_ring(self, f, z):
        z = z - self.base
        for l in range(2):
            g, n = self.where(f, l)
            self.stores[g][n, z, 8 + ROWS : 16 + ROWS, :] = self.stores[g][n, z, 8:16, :]

    def place_y(self, z, up, dn):
        part, place = self.lane & 31, self.lane >> 5
        upper, lower = part < 4, part >= 28
        for t in range(ROWS // 8):
            u_all, d_all = up[8 * t : 8 * t + 8, :], dn[8 * t : 8 * t + 8, :]

            def turned(value, shift):
                return pltpu.roll(value, shift % 128, 1) if shift % 128 else value

            def copies(f):
                result = []
                for m in range(4):
                    u, d = turned(u_all, 32 * m - 4 * f), turned(d_all, 32 * m + 28 - 4 * f)
                    result.append(jnp.where(upper, u, jnp.where(lower, d, 0.0)))
                return result

            def pick(tiles):
                value = tiles[0]
                for r in range(1, 4):
                    value = jnp.where(place == r, tiles[r], value)
                return value

            fields = [copies(r) for r in range(NRHS)]
            for zz in range(4):
                self.put(0, 2 * NRHS, z + zz, t, pick([fields[r][(r - zz) % 4] for r in range(4)]))
            for c in range(4):
                mine = copies(NRHS + c)
                for zz in range(4):
                    self.put(1, 3 * c + 2, z + zz, t, pick([mine[(r - zz) % 4] for r in range(4)]))

    def coefficients(self, z):
        lane = self.lane
        for t in range(ROWS // 8):

            def tiles(c, z, off=0):
                return [self.get(1, 3 * c + l, z, t, off) for l in range(LT)]

            center_z, center_x, center_y, diag = (tiles(c, z) for c in range(4))
            up = [pltpu.roll(v, 127, 1) for v in center_y]
            dn = [pltpu.roll(v, 1, 1) for v in center_y]
            first = jnp.broadcast_to(center_y[0][:, 0:1], (8, 128))
            last = jnp.broadcast_to(center_y[1][:, 127:128], (8, 128))
            sides = [
                (center_z, tiles(0, z + 1)),
                (center_z, tiles(0, z - 1)),
                (center_x, tiles(1, z, 1)),
                (center_x, tiles(1, z, -1)),
                (
                    center_y,
                    [
                        jnp.where(lane == 127, up[1], up[0]),
                        jnp.where(lane == 127, up[2], up[1]),
                        jnp.where((lane & 31) == 31, first, up[2]),
                    ],
                ),
                (
                    center_y,
                    [
                        jnp.where(lane == 0, dn[2], dn[0]),
                        jnp.where(lane == 0, dn[0], dn[1]),
                        jnp.where((lane & 31) == 0, last, dn[2]),
                    ],
                ),
            ]
            at = z - self.faces_base
            for l in range(LT):
                inside = diag[l] > 0.0
                total = diag[l] * SCALE
                for k, (mid, side) in enumerate(sides):
                    face = (mid[l] + side[l]) * (0.5 * SCALE)
                    total = total + face
                    self.faces[k, at, l, 8 * t : 8 * t + 8, :] = jnp.where(inside, face, 0.0)
                self.faces[6, at, l, 8 * t : 8 * t + 8, :] = jnp.where(inside, total, 0.0)

    def apply(self, k, z):
        last = k == STEPS - 1
        at, lane, edge = z - self.faces_base, self.lane, 2 * NRHS
        src, dst = group(k), group(k + 1)
        for t in range(NX // 8 if last else ROWS // 8):
            face = [
                [self.faces[c, at, l, 8 * t : 8 * t + 8, :] for l in range(2 if last else LT)] for c in range(7)
            ]
            diag = [d - SHIFTS[k] * SCALE for d in face[6]]

            def image(n, l, mid, up, dn):
                sides = (
                    self.get(src, n, z + 1, t),
                    self.get(src, n, z - 1, t),
                    self.get(src, n, z, t, 1),
                    self.get(src, n, z, t, -1),
                    up,
                    dn,
                )
                value = diag[l] * mid
                for c, side in enumerate(sides):
                    value = value - face[c][l] * side
                self.put(dst, n, z, t, value)

            rim = self.get(src, edge, z, t)
            rim_up, rim_dn = pltpu.roll(rim, 127, 1), pltpu.roll(rim, 1, 1)
            edge_up, edge_dn = rim_up, rim_dn
            for r in range(NRHS):
                one, two = self.get(src, 2 * r, z, t), self.get(src, 2 * r + 1, z, t)
                one_up, two_up = pltpu.roll(one, 127, 1), pltpu.roll(two, 127, 1)
                one_dn, two_dn = pltpu.roll(one, 1, 1), pltpu.roll(two, 1, 1)
                above = rim_up if r == 0 else pltpu.roll(rim, 127 - 32 * r, 1)
                below = rim_dn if r == NRHS - 1 else pltpu.roll(rim, 97 - 32 * r, 1)
                image(2 * r, 0, one, jnp.where(lane == 127, two_up, one_up), jnp.where(lane == 0, below, one_dn))
                image(2 * r + 1, 1, two, jnp.where(lane == 127, above, two_up), jnp.where(lane == 0, one_dn, two_dn))
                if not last:
                    start = one_up if r == NRHS - 1 else pltpu.roll(one, 32 * r + 31, 1)
                    end = two_dn if r == 0 else pltpu.roll(two, 32 * r + 1, 1)
                    edge_up = jnp.where(lane == 32 * r + 31, start, edge_up)
                    edge_dn = jnp.where(lane == 32 * r, end, edge_dn)
            if not last:
                image(edge, 2, rim, edge_up, edge_dn)


def dynamic_one(place):
    return (place[0] >> 24) + 1


def loop(start, stop, do):
    def step(n, carry):
        do(n)
        return carry

    lax.fori_loop(start, stop, step, 0)


def inner_planes(k):
    return DEPTH + k, DEPTH + NZ - k


def inner_copies(inner, inner_faces, stores, base, faces, faces_base, sems, out):
    def copy(n, there, here):
        src, dst = (here, there) if out else (there, here)
        return pltpu.make_async_copy(src, dst, sems.at[n])

    result = []
    for n, (g, start, stop) in enumerate(
        [(g, z, z + 2) for g in (0, 1) for z in (DEPTH, DEPTH + NZ - 2)]
        + [(0, DEPTH + 2, DEPTH + NZ - 2)]
        + [(group(k), *inner_planes(k)) for k in range(1, STEPS)]
    ):
        there = inner.at[pl.ds(sum(GROUPS[:g]), GROUPS[g]), pl.ds(start - DEPTH, stop - start)]
        result.append(copy(n, there, stores[g].at[:, pl.ds(start - base, stop - start)]))
    start, stop = inner_planes(1)
    result.append(copy(len(result), inner_faces, faces.at[:, pl.ds(start - faces_base, stop - start)]))
    return result


def krylov_inner(swap, place, rhs, cz, cx, cy, dg, *rest):
    above, below, yup, ydn, inner, inner_faces, *stores, faces, load_sems, sems = rest if not swap else rest[:1] + rest
    keep_up, keep_dn = keep_sides(swap, place)
    block = Block(stores, DEPTH, faces, DEPTH + 1, dynamic_one(place))
    loads = []
    for f in range(FIELDS):
        src = rhs.at[f] if f < NRHS else (cz, cx, cy, dg)[f - NRHS]
        for l in range(2):
            g, n = block.where(f, l)
            loads.append(
                pltpu.make_async_copy(
                    src.at[:, :, pl.ds(128 * l, 128)], stores[g].at[n, :, pl.ds(8, NX), :], load_sems.at[2 * f + l]
                )
            )
            loads[-1].start()
    for f in range(FIELDS):
        for z in range(DEPTH, DEPTH + NZ):
            m = (z - DEPTH) // 2
            for l in range(2):
                lanes = pl.ds(128 * l, 128)
                tile = halo_tile(above[f, m, :, lanes], below[f, m, :, lanes], z % 2, keep_up, keep_dn)
                block.put(*block.where(f, l), z, NX // 8, tile)
    for half in range(2):
        lanes = pl.ds(128 * half, 128)
        block.place_y(DEPTH + 4 * half, yup.at[:, lanes], ydn.at[:, lanes])
    for copy in loads:
        copy.wait()
    for f in range(FIELDS):
        for z in range(DEPTH, DEPTH + NZ):
            block.close_ring(f, z)
    copies = inner_copies(inner, inner_faces, stores, DEPTH, faces, DEPTH + 1, sems, True)
    for n in range(5):
        copies[n].start()
    loop(*inner_planes(1), block.coefficients)
    copies[-1].start()
    for k in range(STEPS - 1):
        loop(*inner_planes(k + 1), functools.partial(block.apply, k))
        copies[5 + k].start()
    for copy in copies:
        copy.wait()


NEAR, FAR = 8 * FIELDS, 24


def krylov_outer(
    swap, face_one, face_two, place, odd_z, inner, inner_faces, rim_one, rim_two,
    basis, message,
    *rest,
):
    keep_up, keep_dn = keep_sides(swap, place)
    n_x = 1 if swap else 2
    *stores, faces, accs, rims, plane_sems, loads, saves = rest
    odd = odd_z[0] == 1
    block = Block(stores, 0, faces, 0, dynamic_one(place))
    copies = inner_copies(inner, inner_faces, stores, 0, faces, 0, loads, False)
    def plane_copies(lower, upper):
        planes = []
        start = 0
        for f in range(FIELDS):
            depth = DEPTH if f <= NRHS else DEPTH - 1
            for side, (face, z) in enumerate(((lower, DEPTH - depth), (upper, DEPTH + NZ))):
                for l in range(2):
                    g, n = block.where(f, l)
                    planes.append(
                        pltpu.make_async_copy(
                            face.at[pl.ds(start, depth), :, pl.ds(128 * l, 128)],
                            stores[g].at[n, pl.ds(z, depth), pl.ds(8, NX), :],
                            plane_sems.at[4 * f + 2 * side + l],
                        )
                    )
            start += depth
        return planes

    for copy in copies[:4]:
        copy.start()

    @pl.when(odd)
    def _():
        for copy in plane_copies(face_one, face_two):
            copy.start()

    @pl.when(jnp.logical_not(odd))
    def _():
        for copy in plane_copies(face_two, face_one):
            copy.start()

    one, two = rim_one[...], rim_two[...]
    rims[0] = jnp.where(odd, one, two)
    rims[1] = jnp.where(odd, two, one)
    rimlo, rimhi = rims.at[0], rims.at[1]

    zero = jnp.zeros((8, 128), F32)
    for f in range(FIELDS):
        for rim, first in ((rimlo, 0), (rimhi, DEPTH + NZ)):
            for z in range(first, first + DEPTH):
                far = DEPTH - z if first == 0 else z - first + 1
                for l in range(2):
                    lanes = pl.ds(128 * l, 128)
                    if far <= 2:
                        at, odd = 8 * f, z % 2
                    elif far == 3 and 8 * (f // 2) < FAR:
                        at, odd = NEAR + 8 * (f // 2), f % 2
                    else:
                        block.put(*block.where(f, l), z, NX // 8, zero)
                        continue
                    other = at + (n_x - 1) * (NEAR + FAR)
                    tile = halo_tile(rim[at : at + 8, lanes], rim[other : other + 8, lanes], odd, keep_up, keep_dn)
                    block.put(*block.where(f, l), z, NX // 8, tile)
    rows = pl.ds(n_x * (NEAR + FAR), ROWS)
    for rim, z in ((rimlo, 0), (rimhi, DEPTH + NZ)):
        block.place_y(z, rim.at[rows, pl.ds(0, 128)], rim.at[rows, pl.ds(128, 128)])

    for copy in copies[:4] + plane_copies(face_one, face_two):
        copy.wait()
    for copy in [copies[5], copies[-1], copies[6], copies[7], copies[4]]:
        copy.start()
    for f in range(FIELDS):
        depth = DEPTH if f <= NRHS else DEPTH - 1
        for d in range(depth):
            block.close_ring(f, DEPTH - 1 - d)
            block.close_ring(f, DEPTH + NZ + d)
    loop(1, DEPTH + 1, block.coefficients)
    loop(DEPTH + NZ - 1, EZ - 1, block.coefficients)

    sends = []

    def send_block(k):
        copy = pltpu.make_async_copy(
            stores[group(k)].at[pl.ds(0, 2 * NRHS), pl.ds(DEPTH, NZ), pl.ds(8, NX), :],
            basis.at[pl.ds(k * 2 * NRHS, 2 * NRHS)],
            saves.at[k],
        )
        copy.start()
        sends.append(copy)

    for k in range(STEPS):
        if k == 1:
            copies[-1].wait()
        loop(
            0,
            2 * DEPTH,
            lambda n, k=k: block.apply(k, n + k + 1 + jnp.where(n >= DEPTH, NZ - 2 - 2 * k, 0)),
        )
        if k < STEPS - 1:
            copies[5 + k].wait()
        send_block(k + 1)
    copies[4].wait()
    send_block(0)
    gram_zero(accs)

    def products(z):
        def tile(i, t):
            store = stores[group(i // NRHS)]
            return jnp.concatenate([store[2 * (i % NRHS) + l, z, 8 + 8 * t : 16 + 8 * t, :] for l in range(2)], 1)

        gram_add([jnp.concatenate([tile(i, t) for i in range(COLS)], 0) for t in range(NX // 8)], accs)

    loop(DEPTH, DEPTH + NZ, products)
    gram_message(accs, message)
    for copy in sends:
        copy.wait()


def factor_gram(messages, cells, table):
    rows = row_ids((24, 128))
    lanes = lane_ids((24, 128))
    upper = gram_of(messages) / cells
    square = jnp.concatenate([upper, jnp.zeros((104, 128), F32)], 0).T
    whole = jnp.where(rows <= lanes, upper, square[0:24, :])

    tile_rows = row_ids((8, 128))
    tiles = range(3)

    def split(value):
        return [value[8 * k : 8 * k + 8] for k in tiles]

    def row_of(column, j):
        return jnp.broadcast_to(column[j // 8][j % 8 : j % 8 + 1, :], (8, 128))

    columns = [split(jnp.broadcast_to(whole[:, c : c + 1], (24, 128))) for c in range(COLS)]
    inverse = [[jnp.where(tile_rows + 8 * k == c, 1.0, 0.0) for k in tiles] for c in range(COLS)]
    pivots = [jnp.ones((8, 128), F32) for k in tiles]
    for j in range(COLS):
        pivot = row_of(columns[j], j)
        first = j // 8
        pivots[first] = jnp.where(tile_rows == j % 8, pivot, pivots[first])
        below = {k: columns[j][k] / pivot for k in tiles if k >= first}
        below[first] = jnp.where(tile_rows > j % 8, below[first], 0.0)
        for c in range(COLS):
            change = columns[c] if c > j else inverse[c]
            row = row_of(change, j)
            for k in below:
                change[k] = change[k] - below[k] * row
    scales = [1.0 / jnp.sqrt(p) for p in pivots]
    factor = jnp.zeros((24, 128), F32)
    for c in range(COLS):
        table[c] = jnp.concatenate([inverse[c][k] * scales[k] for k in tiles], 0)
        factor = jnp.where(lanes == c, jnp.concatenate(columns[c], 0), factor)
    return jnp.where((rows <= lanes) & (rows < COLS), factor * jnp.concatenate(scales, 0), 0.0)


def apply_rows(table, group, read, write):
    pieces = NX // 8
    for g in reversed(range(COLS // group)):
        mine = range(group * g, group * g + group)
        sums = {i: None for i in mine}
        for j in range(group * g + group):
            value = [read(j, p) for p in range(pieces)]
            for i in mine:
                if j <= i:
                    weight = jnp.broadcast_to(table[j, i : i + 1, :], (8, 128))
                    terms = [weight * v for v in value]
                    sums[i] = terms if sums[i] is None else [s + t for s, t in zip(sums[i], terms)]
        for i in mine:
            for p in range(pieces):
                write(i, p, sums[i][p])


def plane_copy(src, dst, sems, z):
    return pltpu.make_async_copy(src.at[:, z], dst.at[:, z], sems.at[z])


def first_pass(
    cells, message, basis_hbm, first_hbm, next_message, factor_out, basis, first, table, accs, loads, saves
):
    for z in range(NZ):
        plane_copy(basis_hbm, basis, loads, z).start()
    factor_out[...] = factor_gram(message, cells, table)
    gram_zero(accs)

    def products(z):
        def tile(i, t):
            return jnp.concatenate([first[2 * i + l, z, 8 * t : 8 * t + 8, :] for l in range(2)], 1)

        gram_add([jnp.concatenate([tile(i, t) for i in range(COLS)], 0) for t in range(NX // 8)], accs)

    def apply(z):
        for l in range(2):

            def read(j, p):
                return basis[2 * j + l, z, 8 * p : 8 * p + 8, :]

            def write(i, p, value):
                first[2 * i + l, z, 8 * p : 8 * p + 8, :] = value

            apply_rows(table, 4, read, write)
        plane_copy(first, first_hbm, saves, z).start()

    def both(z):
        plane_copy(basis_hbm, basis, loads, z).wait()
        products(z - 1)
        apply(z)

    plane_copy(basis_hbm, basis, loads, 0).wait()
    apply(0)
    loop(1, NZ, both)
    products(NZ - 1)
    gram_message(accs, next_message)
    for z in range(NZ):
        plane_copy(first, first_hbm, saves, z).wait()


def second_pass(cells, message, factor_one, first_hbm, out_hbm, triangle, first, out, table, loads, saves):
    for z in range(NZ):
        plane_copy(first_hbm, first, loads, z).start()
    left = factor_gram(message, cells, table)[:, 0:24]
    product = lax.dot_general(
        left, factor_one[...], (((1,), (0,)), ((), ())), precision=HIGHEST, preferred_element_type=F32
    )
    triangle[...] = product[0:COLS, 0:COLS]

    def chunk(z, carry):
        plane_copy(first_hbm, first, loads, z).wait()
        for l in range(2):

            def read(j, p):
                return first[2 * j + l, z, 8 * p : 8 * p + 8, :]

            def write(i, p, value):
                out[i, z, 8 * p : 8 * p + 8, 128 * l : 128 * l + 128] = value

            apply_rows(table, 4, read, write)
        plane_copy(out, out_hbm, saves, z).start()
        return carry

    lax.fori_loop(0, NZ, chunk, 0)
    for z in range(NZ):
        plane_copy(out, out_hbm, saves, z).wait()


def shape(*dims):
    return jax.ShapeDtypeStruct(dims, F32)


def move(value, axis, delta):
    count = lax.axis_size(axis)
    pairs = [(i, i + delta) for i in range(count) if 0 <= i + delta < count]
    return lax.ppermute(value, axis, pairs)


def swap_pairs(value, axis, first):
    pairs = [(i, i + 1) for i in range(first, lax.axis_size(axis) - 1, 2)]
    return lax.ppermute(value, axis, pairs + [(j, i) for i, j in pairs])


def exchange(messages):
    return lax.all_to_all(messages, AXES, 0, 0, tiled=True)


def body(rhs, coef_x, coef_y, coef_z, diag_term):
    n_x = lax.axis_size("gx")
    devices = n_x * lax.axis_size("gy") * lax.axis_size("gz")
    cells = float(NZ * NX * NY * devices)
    at_x = lax.axis_index("gx")
    swap = n_x == 2
    fields = (rhs, coef_z, coef_x, coef_y, diag_term)

    place = at_x.astype(jnp.int32).reshape(1)
    odd_z = ((lax.axis_index("gz") + 1) & 1).astype(jnp.int32).reshape(1)
    odd_y = (lax.axis_index("gy") & 1).astype(jnp.int32).reshape(1)
    face_shape = shape(FACE, NX, NY)
    x_shape = shape(FIELDS, NZ // 2, 8, NY)
    z_one, z_two, *xmsgs = pl.pallas_call(
        functools.partial(pack_faces, swap),
        out_shape=(face_shape, face_shape) + (x_shape,) * (1 if swap else 2),
        in_specs=[smem()] * 2 + [hbm()] * 5,
        out_specs=(hbm(), hbm()) + (hbm(),) * (1 if swap else 2),
        scratch_shapes=[
            pltpu.VMEM((1 if swap else 2,) + x_shape.shape, F32),
            pltpu.VMEM((FIELDS, NZ, NX, NY), F32),
            pltpu.SemaphoreType.DMA((FIELDS,)),
            pltpu.SemaphoreType.DMA((2 * FIELDS,)),
            pltpu.SemaphoreType.DMA((1 if swap else 2, FIELDS)),
        ],
        compiler_params=params(LIMIT),
        cost_estimate=cost(2.5),
    )(place, odd_z, *fields)
    face_one, face_two = swap_pairs(z_one, "gz", 1), swap_pairs(z_two, "gz", 0)
    if swap:
        x_parts = (lax.ppermute(xmsgs[0], "gx", [(0, 1), (1, 0)]),)
    else:
        x_parts = (move(xmsgs[0], "gx", -1), move(xmsgs[1], "gx", 1))

    own_shape, halo_shape = shape(NX, NY), shape(ROWS - NX, NY)
    own_one, own_two = pl.pallas_call(
        pack_own_rims,
        out_shape=(own_shape, own_shape),
        in_specs=[smem()] + [vmem()] * 5,
        compiler_params=params(LIMIT),
        cost_estimate=cost(2.5),
    )(odd_y, *fields)
    halo_one, halo_two = pl.pallas_call(
        functools.partial(pack_rims, swap),
        out_shape=(halo_shape, halo_shape),
        in_specs=[smem()] * 2 + [vmem()] * len(x_parts),
        compiler_params=params(16),
        cost_estimate=cost(1),
    )(place, odd_y, *x_parts)
    y_one = swap_pairs(jnp.concatenate([own_one, halo_one], 0), "gy", 0)
    y_two = swap_pairs(jnp.concatenate([own_two, halo_two], 0), "gy", 1)
    yup, ydn = jnp.where(odd_y == 1, y_two, y_one), jnp.where(odd_y == 1, y_one, y_two)

    def rim(half):
        near, far, odd = ((0, 1, 0), (3, 2, 1))[half]
        rows = []
        for part in x_parts:
            rows.append(part[:, near].reshape(NEAR, NY))
            rows.append(part[: FAR // 4, far, 4 * odd : 4 * odd + 4].reshape(FAR, NY))
        lanes = slice(128 * half, 128 * half + 128)
        return jnp.concatenate(rows + [jnp.concatenate([yup[:, lanes], ydn[:, lanes]], 1)], 0)

    low, high = rim(0), rim(1)
    rim_one = swap_pairs(jnp.where(odd_z == 1, low, high), "gz", 1)
    rim_two = swap_pairs(jnp.where(odd_z == 1, high, low), "gz", 0)

    inner_shape = shape(sum(GROUPS[:-1]), NZ, EROWS, 128)
    inner_faces_shape = shape(7, NZ - 2, LT, ROWS, 128)
    inner, inner_faces = pl.pallas_call(
        functools.partial(krylov_inner, swap),
        out_shape=(inner_shape, inner_faces_shape),
        in_specs=[smem()] + [hbm()] * 5 + [vmem()] * (len(x_parts) + 2),
        out_specs=(hbm(), hbm()),
        scratch_shapes=[
            *[pltpu.VMEM((tiles, NZ, EROWS, 128), F32) for tiles in GROUPS[:-1]],
            pltpu.VMEM(inner_faces_shape.shape, F32),
            pltpu.SemaphoreType.DMA((2 * FIELDS,)),
            pltpu.SemaphoreType.DMA((9,)),
        ],
        compiler_params=params(LIMIT),
        cost_estimate=cost(7),
    )(place, *fields, *x_parts, yup, ydn)

    block = shape(2 * COLS, NZ, NX, 128)
    basis, message = pl.pallas_call(
        functools.partial(krylov_outer, swap),
        out_shape=(block, shape(devices, 2, 128)),
        in_specs=[hbm(), hbm(), smem(), smem(), hbm(), hbm(), vmem(), vmem()],
        out_specs=(hbm(), vmem()),
        scratch_shapes=[
            *[pltpu.VMEM((tiles, EZ, EROWS, 128), F32) for tiles in GROUPS],
            pltpu.VMEM((7, EZ, LT, ROWS, 128), F32),
            pltpu.VMEM((2, STACK, STACK), F32),
            pltpu.VMEM((2,) + rim_one.shape, F32),
            pltpu.SemaphoreType.DMA((4 * FIELDS,)),
            pltpu.SemaphoreType.DMA((9,)),
            pltpu.SemaphoreType.DMA((STEPS + 1,)),
        ],
        compiler_params=params(ROOMY),
        cost_estimate=cost(15),
    )(face_one, face_two, place, odd_z, inner, inner_faces, rim_one, rim_two)

    message = exchange(message)
    first, message, factor_one = pl.pallas_call(
        functools.partial(first_pass, cells),
        out_shape=(block, shape(devices, 2, 128), shape(24, 128)),
        in_specs=[vmem(), hbm()],
        out_specs=(hbm(), vmem(), vmem()),
        scratch_shapes=[
            pltpu.VMEM(block.shape, F32),
            pltpu.VMEM(block.shape, F32),
            pltpu.VMEM((COLS, 24, 128), F32),
            pltpu.VMEM((2, STACK, STACK), F32),
            pltpu.SemaphoreType.DMA((NZ,)),
            pltpu.SemaphoreType.DMA((NZ,)),
        ],
        compiler_params=params(ROOMY),
    )(message, basis)

    message = exchange(message)
    return pl.pallas_call(
        functools.partial(second_pass, cells),
        out_shape=(shape(COLS, NZ, NX, NY), shape(COLS, COLS)),
        in_specs=[vmem(), vmem(), hbm()],
        out_specs=(hbm(), vmem()),
        scratch_shapes=[
            pltpu.VMEM(block.shape, F32),
            pltpu.VMEM((COLS, NZ, NX, NY), F32),
            pltpu.VMEM((COLS, 24, 128), F32),
            pltpu.SemaphoreType.DMA((NZ,)),
            pltpu.SemaphoreType.DMA((NZ,)),
        ],
        compiler_params=params(ROOMY),
    )(message, factor_one, first)


def solution(mesh):
    return jax.shard_map(
        body,
        mesh=mesh,
        in_specs=(
            P(None, "gz", "gx", "gy"),
            P("gz", "gx", "gy"),
            P("gz", "gx", "gy"),
            P("gz", "gx", "gy"),
            P("gz", "gx", "gy"),
        ),
        out_specs=(P(None, "gz", "gx", "gy"), P()),
        check_vma=False,
    )
```
